32 devices in a mesh: feat: 4 (over z), tok: 8 (over y, x, core).
Axes of the slice: x: 2, y: 2, z: 4, core: 2. Of those that a mesh axis runs over, the one named last changes fastest.
Arguments:
- master: float32 [422144], P(('feat', 'tok')), may hold values from -2 to 2
- first_moment: float32 [422144], P(('feat', 'tok')), may hold values from -1 to 1
- second_moment: float32 [422144], P(('feat', 'tok')), may hold values from 0 to 1
- observations: bfloat16 [61440, 512], P('tok', 'feat'), may hold values from -6 to 6
- camera_counts: int32 [2048, 10], P('tok'), may hold values from 1 to 3, as said below
- code_targets: int32 [61440, 2], P('tok'), may hold values from 0 to 15
- action_targets: float32 [35, 61440], P(None, 'tok'), may hold values from -6 to 6
- action_valid: int32 [35, 61440], P(None, 'tok'), may hold values from 0 to 1
Outputs:
- master_new: float32 [422144], P(('feat', 'tok'))
- first_new: float32 [422144], P(('feat', 'tok'))
- second_new: float32 [422144], P(('feat', 'tok'))
- loss_parts: float32 [4], replicated
The draws below stay inside these ranges and needn't reach their ends.
Inputs may be any that keep to these rules, and one draw needn't show every extreme that they name: `camera_counts`: every timestep has at least one live camera token.
All inputs are finite; a program needn't handle non-finite values.
Results may differ from the reference program's by a relative error of at most 0.002.
The reference program's roundings to bfloat16 on the way count: a program that leaves them out, or rounds other values in their place, can miss the bound.
Values may be sent and summed in bfloat16 or wider, within the bound.
A program may use at most 192 MiB of HBM per device.

```python
import math
import jax
import jax.numpy as jnp
import numpy as np
from jax import lax

D = 120
H = 6
HD = 20
FF = 480
OBS = 512
LAYERS = 2
STEPS = 10
CAMS = 3
BOOKS = 2
CODES = 16
SPAN = 5
ACT = 7
STEP_NO = 10
WIN_DEV = 64
WIN = 30
GROUP_WIN = 256
WINDOWS = 2048
SLOTS = 61440
FLAT = 422144


def layout_scales():
    table_rows = [((OBS, D), OBS ** (-0.5), 0.0), ((D,), 0.1, 0.0), ((WIN, D), 0.3, 0.0)]
    for depth_index in range(LAYERS):
        table_rows += [((D,), 0.1, 1.0), ((D,), 0.1, 0.0), ((D, 3 * D), D ** (-0.5), 0.0), ((2 * D,), 0.1, 0.0), ((D, D), 3.0 * D ** (-0.5), 0.0), ((D,), 0.1, 0.0), ((D,), 0.1, 1.0), ((D,), 0.1, 0.0), ((D, FF), D ** (-0.5), 0.0), ((FF,), 0.1, 0.0), ((FF, D), FF ** (-0.5), 0.0), ((D,), 0.1, 0.0)]
    table_rows += [((D,), 0.1, 1.0), ((D,), 0.1, 0.0), ((D, BOOKS * CODES), D ** (-0.5), 0.0), ((BOOKS * CODES,), 0.1, 0.0), ((D, SPAN * ACT), D ** (-0.5), 0.0), ((SPAN * ACT,), 0.1, 0.0)]
    scales = np.full((FLAT,), 0.05, np.float32)
    shifts = np.zeros((FLAT,), np.float32)
    offset = 0
    for entry in table_rows:
        length_now = math.prod(entry[0])
        scales[offset:offset + length_now] = entry[1]
        shifts[offset:offset + length_now] = entry[2]
        offset += length_now
    return (jnp.asarray(scales), jnp.asarray(shifts))


def draw_master(key, part):
    key = jax.random.fold_in(key, 11)
    scales, shifts = layout_scales()
    noise = jnp.clip(jax.random.normal(key, (FLAT,), jnp.float32), -4.0, 4.0)
    return shifts + scales * noise


def draw_first_moment(key, part):
    key = jax.random.fold_in(key, 13)
    grad_size = 0.5 * SLOTS ** (-0.5)
    noise = jnp.clip(jax.random.normal(key, (FLAT,), jnp.float32), -4.0, 4.0)
    return 0.11 * grad_size * noise


def draw_second_moment(key, part):
    key = jax.random.fold_in(key, 17)
    grad_size = 0.5 * SLOTS ** (-0.5)
    factor = jnp.exp(jax.random.uniform(key, (FLAT,), jnp.float32, math.log(0.5), math.log(8.0)))
    return 0.001 * grad_size * grad_size * factor


def draw_camera_counts(key, part):
    key = jax.random.fold_in(key, 23)
    first_key, second_key = jax.random.split(key)
    window_ids = jnp.arange(WINDOWS, dtype=jnp.int32)[:, None]
    level = window_ids // GROUP_WIN * GROUP_WIN * GROUP_WIN + window_ids % GROUP_WIN // WIN_DEV * WIN_DEV * WINDOWS
    limit = 2 * WINDOWS * GROUP_WIN
    extra_one = (jax.random.randint(first_key, (WINDOWS, STEPS), 0, limit) < level).astype(jnp.int32)
    extra_two = (jax.random.randint(second_key, (WINDOWS, STEPS), 0, limit) < level).astype(jnp.int32)
    counts = 1 + extra_one + extra_two
    counts = counts.at[0, 0].set(1)
    counts = counts.at[WINDOWS - 1, 0].set(3)
    return counts


def draw_action_valid(key, part):
    key = jax.random.fold_in(key, 29)
    slot_ids = jnp.arange(SLOTS, dtype=jnp.int32)[None, :]
    drawn = jax.random.randint(key, (SPAN * ACT, SLOTS), 0, 4 * SLOTS)
    return (drawn < SLOTS + 3 * slot_ids).astype(jnp.int32)


def place_ends(values, key, smallest, top_value):
    dims = values.shape
    spot = [jax.random.randint(jax.random.fold_in(key, axis), (), 0, dims[axis]) for axis in range(len(dims))]
    values = values.at[tuple(spot)].set(smallest)
    longest = dims.index(max(dims))
    spot[longest] = (spot[longest] + 1) % dims[longest]
    return values.at[tuple(spot)].set(top_value)


def block_scale(stream_key, shape, shards, least, top_value):
    level = 1.0
    for axis_at, parts in shards:
        draws = jax.random.uniform(jax.random.fold_in(jax.random.fold_in(stream_key, 6), axis_at), (parts,), jnp.float32, least / len(shards), top_value / len(shards))
        level = level * jnp.repeat(jnp.exp(draws), shape[axis_at] // parts).reshape((-1,) + (1,) * (len(shape) - 1 - axis_at))
    return level


def normal_values(stream_key, extent, scale, most, cuts=(), held_as=jnp.bfloat16):
    values = jax.random.normal(stream_key, extent, jnp.float32) * scale
    if len(cuts) > 0:
        values = block_scale(stream_key, extent, cuts, -0.22, 0.18) * values
    return jnp.clip(values, min=-most, max=most).astype(held_as)


def setup_inputs(seed: int = 0) -> dict:
    seeds = jax.random.split(jax.random.key(seed), 9)
    master = draw_master(jax.random.fold_in(seeds[8], 71), 0)
    first_moment = draw_first_moment(jax.random.fold_in(seeds[8], 71), 0)
    second_moment = draw_second_moment(jax.random.fold_in(seeds[8], 71), 0)
    observations = normal_values(seeds[3], (SLOTS, OBS), 1.0, 6.0, ((0, 8), (1, 4)))
    camera_counts = draw_camera_counts(jax.random.fold_in(seeds[8], 71), 0)
    code_targets = place_ends(jax.random.randint(seeds[5], (SLOTS, BOOKS), 0, CODES), jax.random.fold_in(seeds[5], 1), 0, CODES - 1).astype(jnp.int32)
    action_targets = normal_values(seeds[6], (SPAN * ACT, SLOTS), 1.0, 6.0, ((1, 8),), jnp.float32)
    action_valid = draw_action_valid(jax.random.fold_in(seeds[8], 71), 0)
    return {"master": master, "first_moment": first_moment, "second_moment": second_moment, "observations": observations, "camera_counts": camera_counts, "code_targets": code_targets, "action_targets": action_targets, "action_valid": action_valid}


@jax.custom_vjp
def low(v):
    return lax.optimization_barrier(v.astype(jnp.bfloat16)).astype(jnp.float32)

@jax.custom_vjp
def low_back(v):
    return v

def low_keep(v):
    return (low(v), None)

def low_pass(kept, grad):
    return (grad,)

def back_keep(v):
    return (v, None)

def back_low(kept, grad):
    return (low(grad),)
low.defvjp(low_keep, low_pass)
low_back.defvjp(back_keep, back_low)
NORM_EPS = 1e-05
BETA_ONE = 0.9
BETA_TWO = 0.999
ADAM_EPS = 1e-08
DECAY_RATE = 0.1
LEARN_RATE = 0.05

def layout_table():
    table_rows = [('obs_w', (OBS, D)), ('obs_b', (D,)), ('pos_table', (WIN, D))]
    for depth_index in range(LAYERS):
        table_rows += [('gain_one', (D,)), ('bias_one', (D,)), ('qkv_w', (D, 3 * D)), ('qv_b', (2 * D,)), ('out_w', (D, D)), ('out_b', (D,)), ('gain_two', (D,)), ('bias_two', (D,)), ('fc_w', (D, FF)), ('fc_b', (FF,)), ('proj_w', (FF, D)), ('proj_b', (D,))]
    table_rows += [('gain_final', (D,)), ('bias_final', (D,)), ('code_w', (D, BOOKS * CODES)), ('code_b', (BOOKS * CODES,)), ('off_w', (D, SPAN * ACT)), ('off_b', (SPAN * ACT,))]
    return table_rows

def unpack_flat(flat):
    pieces = []
    offset = 0
    for entry in layout_table():
        length_now = math.prod(entry[1])
        pieces.append(flat[offset:offset + length_now].reshape(entry[1]))
        offset += length_now
    return pieces

def slot_masks(counts):
    slot_ids = jnp.arange(WIN, dtype=jnp.int32)
    step_of = slot_ids // CAMS
    live_slots = (slot_ids % CAMS)[None, :] < jnp.repeat(counts, CAMS, axis=1)
    allowed = (step_of[:, None] >= step_of[None, :])[None, :, :] & live_slots[:, None, :]
    return (live_slots, allowed)

def layer_norm(values, gain, shift):
    center = values - lax.optimization_barrier(jnp.mean(values, axis=-1, keepdims=True))
    spread = lax.optimization_barrier(jnp.mean(center * center, axis=-1, keepdims=True))
    return center * lax.rsqrt(spread + NORM_EPS) * gain + shift

def attend_windows(mixed, allowed):
    windows = mixed.shape[0]
    queries = mixed[:, :, :D].reshape(windows, WIN, H, HD)
    keys_all = mixed[:, :, D:2 * D].reshape(windows, WIN, H, HD)
    values_all = mixed[:, :, 2 * D:].reshape(windows, WIN, H, HD)
    scores = jnp.einsum('wqhe,wkhe->whqk', queries, keys_all, precision=lax.Precision.HIGHEST) * HD ** (-0.5)
    scores = jnp.where(allowed[:, None, :, :], scores, -1e+30)
    highest = lax.optimization_barrier(jnp.max(scores, axis=-1, keepdims=True))
    probs = jnp.exp(scores - highest)
    probs = probs / lax.optimization_barrier(jnp.sum(probs, axis=-1, keepdims=True))
    output = jnp.einsum('whqk,wkhe->wqhe', probs, values_all, precision=lax.Precision.HIGHEST)
    return output.reshape(windows, WIN, D)

def head_sums(logits, offsets, live_rows, codes, actions, valid_rows):
    grouped = logits.reshape(-1, BOOKS, CODES)
    highest = lax.optimization_barrier(jnp.max(grouped, axis=-1, keepdims=True))
    total_exp = jnp.log(lax.optimization_barrier(jnp.sum(jnp.exp(grouped - highest), axis=-1))) + highest[..., 0]
    picked = lax.optimization_barrier(jnp.sum(jnp.where(codes[..., None] == jnp.arange(CODES, dtype=jnp.int32), grouped, 0.0), axis=-1))
    code_sum = jnp.sum((total_exp - picked) * live_rows[:, None])
    action_sum = jnp.sum(valid_rows * jnp.sqrt((offsets - actions) ** 2 + 1.0))
    return (code_sum, action_sum)

def matmul(left, right):
    return jnp.dot(left, right, precision=lax.Precision.HIGHEST, preferred_element_type=jnp.float32)

def block_sums(params, obs_block, counts_block, codes_block, actions_block, valid_block):
    live_slots, allowed = slot_masks(counts_block)
    windows = counts_block.shape[0]
    rows = windows * WIN
    live_rows = live_slots.reshape(-1).astype(jnp.float32)
    valid_rows = valid_block.astype(jnp.float32) * live_rows[:, None]
    hidden = low_back(matmul(obs_block, params[0])) + params[1] + jnp.tile(params[2], (windows, 1))
    for depth_index in range(LAYERS):
        first_slot = 3 + 12 * depth_index
        gain_one, bias_one, qkv_w, qv_b, out_w, out_b, gain_two, bias_two, fc_w, fc_b, proj_w, proj_b = params[first_slot:first_slot + 12]
        normed = low(layer_norm(hidden, gain_one, bias_one))
        qkv_bias = jnp.concatenate([qv_b[:D], jnp.zeros((D,), jnp.float32), qv_b[D:]])
        mixed = low_back(matmul(normed, qkv_w)) + qkv_bias
        attended = low(attend_windows(mixed.reshape(windows, WIN, 3 * D), allowed).reshape(rows, D))
        hidden = hidden + low_back(matmul(attended, out_w)) + out_b
        normed = low(layer_norm(hidden, gain_two, bias_two))
        inner = low(jax.nn.gelu(low_back(matmul(normed, fc_w) + fc_b), approximate=True))
        hidden = hidden + low_back(matmul(inner, proj_w)) + proj_b
    head_start = 3 + 12 * LAYERS
    final = low(layer_norm(hidden, params[head_start], params[head_start + 1]))
    logits = low_back(matmul(final, params[head_start + 2])) + params[head_start + 3]
    offsets = low_back(matmul(final, params[head_start + 4])) + params[head_start + 5]
    return head_sums(logits, offsets, live_rows, codes_block, actions_block, valid_rows)

def reference(master, first_moment, second_moment, observations, camera_counts, code_targets, action_targets, action_valid):
    actions_rows = jnp.transpose(action_targets)
    valid_ints = jnp.transpose(action_valid)
    live_slots = slot_masks(camera_counts)[0]
    live_rows = live_slots.reshape(-1).astype(jnp.float32)
    live_total = jnp.sum(live_rows)
    valid_total = jnp.sum(valid_ints.astype(jnp.float32) * live_rows[:, None])
    block_windows = min(WINDOWS, 32)
    blocks = WINDOWS // block_windows
    block_rows = block_windows * WIN
    inputs = (observations.astype(jnp.float32).reshape(blocks, block_rows, OBS), camera_counts.reshape(blocks, block_windows, STEPS), code_targets.reshape(blocks, block_rows, BOOKS), actions_rows.reshape(blocks, block_rows, SPAN * ACT), valid_ints.reshape(blocks, block_rows, SPAN * ACT))

    def total_loss(flat):
        params = unpack_flat(low(flat))

        def one_block(carry, pieces):
            sums = block_sums(params, *pieces)
            return ((carry[0] + sums[0], carry[1] + sums[1]), None)
        zero = jnp.zeros((), jnp.float32)
        sums, ignored = lax.scan(jax.checkpoint(one_block), (zero, zero), inputs)
        return (sums[0] / live_total + sums[1] / valid_total, sums)
    loss_value, back_fn, sums = jax.vjp(total_loss, master, has_aux=True)
    grad = back_fn(jnp.ones((), jnp.float32))[0]
    first_new = BETA_ONE * first_moment + (1.0 - BETA_ONE) * grad
    second_new = BETA_TWO * second_moment + (1.0 - BETA_TWO) * grad * grad
    first_hat = first_new / (1.0 - BETA_ONE ** STEP_NO)
    second_hat = second_new / (1.0 - BETA_TWO ** STEP_NO)
    master_new = master - LEARN_RATE * (first_hat / (jnp.sqrt(second_hat) + ADAM_EPS) + DECAY_RATE * master)
    loss_parts = jnp.stack([sums[0], live_total, sums[1], valid_total])
    return (master_new, first_new, second_new, loss_parts)
```

```python
import functools
import math

import jax
import jax.numpy as jnp
from jax import lax
from jax.experimental import pallas as pl
from jax.experimental.pallas import tpu as pltpu
from jax.sharding import PartitionSpec as PSpec

D = 120
H = 6
HD = 20
FF = 480
OBS = 512
LAYERS = 2
CAMS = 3
BOOKS = 2
CODES = 16
SPAN = 5
ACT = 7
WIN = 30
OFFS = SPAN * ACT
NORM_EPS = 1e-05
STEP_NO = 10
BETA_ONE = 0.9
BETA_TWO = 0.999
ADAM_EPS = 1e-08
DECAY_RATE = 0.1
LEARN_RATE = 0.05
GW = 4
GT = GW * WIN
CG = 4
L = CG * 128
CT = CG * GT
F32 = jnp.float32
BF = jnp.bfloat16
SCALE = HD ** (-0.5)
LROW = 2 * 1 + 3 * D + 2 + D + 1 + 2 + 4 * D + 4 + 4 * D + 1
BASE = OBS + 1 + WIN
HEAD = BASE + LAYERS * LROW
NV = 13
VROWS = [0, 1, 362, 363, 484, 485, 486, 967, 968, 969, 970, 1451]
(G1, B1, QB, VB, OB, G2, B2, FB0, FB1, FB2, FB3, PB) = range(12)


def nn(a, b):
    return lax.dot_general(a, b, (((1,), (0,)), ((), ())), preferred_element_type=F32)


def nt(a, b, precision=None):
    return lax.dot_general(a, b, (((1,), (1,)), ((), ())), preferred_element_type=F32, precision=precision)


def low(v):
    return v.astype(BF)


def pad8(v):
    return jnp.concatenate([v, jnp.zeros((8, v.shape[1]), v.dtype)], axis=0)


def tile4(v):
    return jnp.concatenate([v] * CG, axis=1)


def fold4(v):
    out = v[:, 0:128]
    for g in range(1, CG):
        out = out + v[:, 128 * g:128 * (g + 1)]
    return out


def iota(shape, axis):
    return lax.broadcasted_iota(jnp.int32, shape, axis)


def slab_at(h):
    return 20 * h - (4 if h % 2 else 0)


def head_stack(v):
    rows = iota((8, 128), 0)
    cols = []
    for h in range(H):
        a = slab_at(h)
        if h % 2 == 0:
            parts = [v[a:a + 16], jnp.where(rows < 4, v[a + 16:a + 24], 0.0)]
        else:
            parts = [jnp.where(rows >= 4, v[a:a + 8], 0.0), v[a + 8:a + 24]]
        if a > 0:
            parts = [jnp.zeros((a, 128), F32)] + parts
        if a + 24 < 128:
            parts = parts + [jnp.zeros((128 - a - 24, 128), F32)]
        cols.append(jnp.concatenate(parts, axis=0))
    return jnp.concatenate(cols, axis=1)


def join_slabs(slabs):
    rows = iota((8, 128), 0)
    parts = []
    for p in range(3):
        a, b = slabs[2 * p], slabs[2 * p + 1]
        parts += [a[0:16], jnp.where(rows < 4, a[16:24], b[0:8]), b[8:24]]
    return jnp.concatenate(parts, axis=0)


def slabs_of(v):
    return [v[slab_at(h):slab_at(h) + 24] for h in range(H)]


def hi_lo(v):
    hi = low(v)
    return hi, low(v - hi.astype(F32))


def normed(x):
    mean = jnp.sum(x, axis=0, keepdims=True) * (1.0 / D)
    c = x - mean
    var = jnp.sum(c * c, axis=0, keepdims=True) * (1.0 / D)
    r = lax.rsqrt(var + NORM_EPS)
    return c * r, r


def normed_back(d, xh, r):
    m0 = jnp.sum(d, axis=0, keepdims=True) * (1.0 / D)
    m1 = jnp.sum(d * xh, axis=0, keepdims=True) * (1.0 / D)
    return r * (d - m0 - xh * m1)


GA = math.sqrt(2.0 / math.pi)
GB = 0.044715


def gelu(x):
    t = jnp.tanh(GA * (x + GB * x * x * x))
    return 0.5 * x * (1.0 + t)


def gelu_back(x):
    x2 = x * x
    t = jnp.tanh(GA * x * (1.0 + GB * x2))
    return 0.5 * (1.0 + t) + (0.5 * GA) * x * (1.0 - t * t) * (1.0 + 3.0 * GB * x2)


PRECISE = True


class Refs:
    pass


def scratch_list(chunks):
    groups = chunks * CG
    return dict(
        w_obs=pltpu.VMEM((OBS, 128), BF),
        posb=pltpu.VMEM((GT, 128), F32),
        qkv_t=pltpu.VMEM((LAYERS, 384, 128), BF),
        qkv=pltpu.VMEM((LAYERS, 128, 384), BF),
        out_t=pltpu.VMEM((LAYERS, 128, 128), BF),
        out=pltpu.VMEM((LAYERS, 128, 128), BF),
        fc_t=pltpu.VMEM((LAYERS, 512, 128), BF),
        fc=pltpu.VMEM((LAYERS, 128, 512), BF),
        proj_t=pltpu.VMEM((LAYERS, 128, 512), BF),
        proj=pltpu.VMEM((LAYERS, 512, 128), BF),
        head_t=pltpu.VMEM((72, 128), BF),
        head=pltpu.VMEM((128, 128), BF),
        vec=pltpu.VMEM((32, 128), F32),
        bc=pltpu.VMEM((LAYERS, 12, GT, 128), F32),
        bcf=pltpu.VMEM((2, GT, 128), F32),
        bch=pltpu.VMEM((72, 128), F32),
        hc=pltpu.VMEM((128, 128), F32),
        ho=pltpu.VMEM((128, 128), F32),
        cnt=pltpu.VMEM((16, 256), F32),
        bias=pltpu.VMEM((groups, GT, 128), F32),
        live=pltpu.VMEM((chunks, 1, L), F32),
        act=pltpu.VMEM((chunks, 40, L), F32),
        val=pltpu.VMEM((chunks, 40, L), F32),
        code=pltpu.VMEM((chunks, 2, L), F32),
        x=pltpu.VMEM((chunks, D, L), F32),
        xh1=pltpu.VMEM((LAYERS, chunks, D, L), F32),
        r1=pltpu.VMEM((LAYERS, chunks, 1, L), F32),
        xh2=pltpu.VMEM((LAYERS, chunks, D, L), F32),
        r2=pltpu.VMEM((LAYERS, chunks, 1, L), F32),
        n1=pltpu.VMEM((LAYERS, chunks, 128, L), BF),
        n2=pltpu.VMEM((LAYERS, chunks, 128, L), BF),
        att=pltpu.VMEM((LAYERS, chunks, 128, L), BF),
        mix=pltpu.VMEM((LAYERS, chunks, 360, L), F32),
        prob=pltpu.VMEM((LAYERS, groups, GT, H * 128), F32),
        pre=pltpu.VMEM((LAYERS, chunks, FF, L), F32),
        inner=pltpu.VMEM((LAYERS, chunks, 512, L), BF),
        a_qkv=pltpu.VMEM((LAYERS, 128, 384), F32),
        a_out=pltpu.VMEM((LAYERS, 128, 128), F32),
        a_fc=pltpu.VMEM((LAYERS, 128, 512), F32),
        a_proj=pltpu.VMEM((LAYERS, 512, 128), F32),
        a_bias=pltpu.VMEM((LAYERS, 12, 128, 128), F32),
        a_obs=pltpu.VMEM((128, 512), F32),
        a_x=pltpu.VMEM((128, 128), F32),
        a_fin=pltpu.VMEM((2, 128, 128), F32),
        a_head=pltpu.VMEM((128, 128), F32),
        a_hb=pltpu.VMEM((128, 128), F32),
        loss=pltpu.VMEM((2, 8, 128), F32),
    )


def code_phases():
    for p in range(15):
        yield p, (32 * p) // D, (32 * p) % D


def off_phases():
    for p in range(24):
        yield p, (35 * p + 32) // D, (35 * p + 32) % D


def shifted(v, by):
    by %= 128
    return v if by == 0 else pltpu.roll(v, by, 1)


def take_phase(load, a, s, width, rows):
    lanes = iota((rows, 128), 1)
    first = shifted(load(a), -s)
    if s + width > D:
        second = shifted(load(a + 1), D - s)
        first = jnp.where(lanes < D - s, first, second)
    return jnp.where(lanes < width, first, 0.0)


def prep_weights(rg, R):
    R.w_obs[...] = low(rg[0:OBS, :])
    for w in range(GW):
        R.posb[pl.ds(WIN * w, WIN), :] = rg[OBS + 1:OBS + 1 + WIN, :] + rg[OBS:OBS + 1, :]
    R.vec[...] = jnp.zeros((32, 128), F32)
    for l in range(LAYERS):
        b = BASE + LROW * l
        for j in range(3):
            w = pad8(rg[pl.ds(b + 2 + j, D, stride=3), :])
            R.qkv[l, :, 128 * j:128 * (j + 1)] = low(w)
            R.qkv_t[l, 128 * j:128 * (j + 1), :] = low(w.T)
        w = pad8(rg[pl.ds(b + 364, D), :])
        R.out[l] = low(w)
        R.out_t[l] = low(w.T)
        for j in range(4):
            w = pad8(rg[pl.ds(b + 487 + j, D, stride=4), :])
            R.fc[l, :, 128 * j:128 * (j + 1)] = low(w)
            R.fc_t[l, 128 * j:128 * (j + 1), :] = low(w.T)
            w = pad8(rg[pl.ds(b + 971 + D * j, D), :])
            R.proj[l, 128 * j:128 * (j + 1), :] = low(w)
            R.proj_t[l, :, 128 * j:128 * (j + 1)] = low(w.T)
        for i, r in enumerate(VROWS):
            R.vec[pl.ds(12 * l + i, 1), :] = rg[pl.ds(b + r, 1), :]
    R.vec[24:26, :] = rg[pl.ds(HEAD, 2), :]
    R.hc[...] = jnp.zeros((128, 128), F32)
    R.ho[...] = jnp.zeros((128, 128), F32)
    c0 = HEAD + 2
    for p, a, s in code_phases():
        R.hc[pl.ds(p, 8, stride=15), :] = take_phase(
            lambda i: rg[pl.ds(c0 + i, 8, stride=4), :], a, s, 32, 8)
    o0 = c0 + 32
    for p, a, s in off_phases():
        R.ho[pl.ds(p, 5, stride=24), :] = take_phase(
            lambda i: rg[pl.ds(o0 + i, 5, stride=7), :], a, s, OFFS, 5)
    hw = R.hc[...] + shifted(R.ho[...], 32)
    R.head[...] = low(hw)
    R.head_t[...] = low(hw.T[0:72])
    lanes = iota((1, 128), 1)
    hb = jnp.where(lanes < 32, rg[pl.ds(o0, 1), :], 0.0)
    a, s = (D * OFFS + 32) // D, (D * OFFS + 32) % D
    ob = take_phase(lambda i: rg[pl.ds(o0 + i, 1), :], a, s, OFFS, 1)
    R.vec[26:27, :] = hb + shifted(ob, 32)
    columns = jnp.concatenate([R.vec[...], jnp.zeros((96, 128), F32)], axis=0).T
    for l in range(LAYERS):
        for i in range(12):
            R.bc[l, i] = jnp.broadcast_to(columns[0:D, 12 * l + i:12 * l + i + 1], (D, 128))
    for i in range(2):
        R.bcf[i] = jnp.broadcast_to(columns[0:D, 24 + i:25 + i], (D, 128))
    R.bch[...] = jnp.broadcast_to(columns[0:72, 26:27], (72, 128))


def spread_groups(v, groups, width):
    rows = v.shape[0]
    lanes = iota((rows, 128), 1)
    out = []
    for g in range(groups):
        t, o = (GT * g) // 128, (GT * g) % 128
        a = shifted(v[:, 128 * t:128 * (t + 1)], -o)
        if o + GT > 128:
            b = shifted(v[:, 128 * (t + 1):128 * (t + 2)], -o)
            a = jnp.where(lanes < 128 - o, a, b)
        out.append(jnp.where(lanes < GT, a, 0))
    return out


def prep_tokens(R, counts, codes, actions, valid, feat, chunks):
    groups = chunks * CG
    wins = counts.shape[1]
    R.cnt[...] = jnp.zeros(R.cnt.shape, F32)
    R.cnt[0:WIN // CAMS, :] = counts[...].astype(F32)
    k = iota((GT, 16), 0)
    step = (k % WIN) // CAMS
    sel = jnp.where(step == iota((GT, 16), 1), 1.0, 0.0)
    x = nn(low(sel), low(R.cnt[...]))
    y = jnp.where(iota((GT, wins), 1) % GW == iota((GT, wins), 0) // WIN, x, 0.0)
    pick = jnp.where(iota((wins, 128), 0) // GW == iota((wins, 128), 1) + groups * feat, 1.0, 0.0)
    z = nn(low(y), low(pick))
    kk = iota((GT, 128), 0)
    alive = jnp.where((kk % CAMS).astype(F32) < z, 1.0, 0.0)
    q = iota((GT, 128), 1)
    same = (kk // WIN == q // WIN) & ((kk % WIN) // CAMS <= (q % WIN) // CAMS) & (q < GT)
    base = jnp.where(same, 0.0, -1e30)
    for g in range(groups):
        R.bias[g] = jnp.where(jnp.broadcast_to(alive[:, g:g + 1], (GT, 128)) > 0.5, base, -1e30)
    rows = pad8(alive).T
    live_count = 0.0
    for g in range(groups):
        R.live[g // CG, :, 128 * (g % CG):128 * (g % CG + 1)] = rows[g:g + 1, :]
    for name, src in (("code", codes), ("act", actions), ("val", valid)):
        parts = spread_groups(src[...].astype(F32), groups, GT)
        dst = getattr(R, name)
        for g in range(groups):
            c, lo = g // CG, 128 * (g % CG)
            part = parts[g]
            if name == "val":
                part = part * rows[g:g + 1, :]
            if name != "code":
                dst[c, 32:40, lo:lo + 128] = jnp.zeros((8, 128), F32)
            dst[c, 0:part.shape[0], lo:lo + 128] = part
    lanes = iota((GT, 128), 1)
    live_total = jnp.sum(jnp.where(lanes < groups, alive, 0.0), keepdims=True)
    v = jnp.zeros((40, L), F32)
    for c in range(chunks):
        v = v + R.val[c]
    valid_total = jnp.sum(v, keepdims=True)
    return live_total, valid_total


def attend(q, k, v, bias):
    krow = pad8(k).T[0:GT]
    if PRECISE:
        kh, kl = hi_lo(krow)
        qh, ql = hi_lo(head_stack(q))
        s = nn(jnp.concatenate([kh, kl, kh], axis=1), jnp.concatenate([qh, qh, ql], axis=0))
    else:
        s = nn(low(krow), low(head_stack(q)))
    s = s + jnp.concatenate([bias] * H, axis=1)
    e = jnp.exp(s - jnp.max(s, axis=0, keepdims=True))
    p = e * (1.0 / jnp.sum(e, axis=0, keepdims=True))
    slabs = []
    vs = slabs_of(v)
    for h in range(H):
        ph = pad8(p[:, 128 * h:128 * (h + 1)])
        if PRECISE:
            pa, pb = hi_lo(ph)
            va, vb = hi_lo(vs[h])
            slabs.append(nn(jnp.concatenate([va, vb, va], axis=1), jnp.concatenate([pa, pa, pb], axis=0)))
        else:
            slabs.append(nn(low(vs[h]), low(ph)))
    return join_slabs(slabs), p


def attend_back(do, p, q, k, v):
    vrow = pad8(v).T[0:GT]
    dp = nn(low(vrow), low(head_stack(do)))
    t = p * dp
    ds = t - p * jnp.sum(t, axis=0, keepdims=True)
    dq, dk, dv = [], [], []
    qs, ks, os = slabs_of(q), slabs_of(k), slabs_of(do)
    for h in range(H):
        dsh = low(pad8(ds[:, 128 * h:128 * (h + 1)]))
        ph = low(pad8(p[:, 128 * h:128 * (h + 1)]))
        dq.append(nn(low(ks[h]), dsh))
        dk.append(nt(low(qs[h]), dsh))
        dv.append(nt(low(os[h]), ph))
    return join_slabs(dq) * SCALE, join_slabs(dk), join_slabs(dv)


def embed(R, obs, c):
    rows = nn(jnp.concatenate(obs, axis=1), R.w_obs[...])
    parts = []
    for g in range(CG):
        r = rows[GT * g:GT * (g + 1)] + R.posb[...]
        parts.append(pad8(r).T[0:D])
    return jnp.concatenate(parts, axis=1)


def layer_fwd(R, l, c, x):
    def vec(i):
        return tile4(R.bc[l, i])

    xh, r = normed(x)
    R.xh1[l, c] = xh
    R.r1[l, c] = r
    n1 = low(pad8(xh * vec(G1) + vec(B1)))
    R.n1[l, c] = n1
    mix = nn(R.qkv_t[l], n1)
    q = (mix[0:D] + vec(QB)) * SCALE
    k = mix[128:128 + D]
    v = mix[256:256 + D] + vec(VB)
    R.mix[l, c, 0:D] = q
    R.mix[l, c, D:2 * D] = k
    R.mix[l, c, 2 * D:3 * D] = v
    parts = []
    for g in range(CG):
        at = slice(128 * g, 128 * (g + 1))
        o, p = attend(q[:, at], k[:, at], v[:, at], R.bias[c * CG + g])
        R.prob[l, c * CG + g] = p
        parts.append(o)
    att = low(pad8(jnp.concatenate(parts, axis=1)))
    R.att[l, c] = att
    x1 = x + nn(R.out_t[l], att)[0:D] + vec(OB)
    xh, r = normed(x1)
    R.xh2[l, c] = xh
    R.r2[l, c] = r
    n2 = low(pad8(xh * vec(G2) + vec(B2)))
    R.n2[l, c] = n2
    pre = nn(R.fc_t[l], n2)
    parts = []
    for j in range(4):
        pj = pre[128 * j:128 * j + D] + vec(FB0 + j)
        R.pre[l, c, D * j:D * (j + 1)] = pj
        parts.append(low(pad8(gelu(pj))))
    inner = jnp.concatenate(parts, axis=0)
    R.inner[l, c] = inner
    return x1 + nn(R.proj_t[l], inner)[0:D] + vec(PB)


def head_step(R, c, x, live_total, valid_total):
    xh, r = normed(x)
    fin = low(pad8(xh * tile4(R.bcf[0]) + tile4(R.bcf[1])))
    hd = nn(R.head_t[...], fin) + tile4(R.bch[...])
    live = R.live[c]
    lw = live * (1.0 / live_total)
    rows = iota((CODES, L), 0).astype(F32)
    grads = []
    csum = jnp.zeros((1, L), F32)
    for b in range(BOOKS):
        lg = hd[CODES * b:CODES * (b + 1)]
        m = jnp.max(lg, axis=0, keepdims=True)
        e = jnp.exp(lg - m)
        s = jnp.sum(e, axis=0, keepdims=True)
        hot = rows == R.code[c, b:b + 1, :]
        picked = jnp.sum(jnp.where(hot, lg, 0.0), axis=0, keepdims=True)
        csum = csum + (jnp.log(s) + m - picked) * live
        grads.append((e * (1.0 / s) - jnp.where(hot, 1.0, 0.0)) * lw)
    diff = hd[32:72] - R.act[c]
    val = R.val[c]
    sq = diff * diff + 1.0
    ri = lax.rsqrt(sq)
    asum = val * (sq * ri)
    grads.append((val * (1.0 / valid_total)) * (diff * ri))
    R.loss[0, 0:1] += fold4(csum)
    af = fold4(asum)
    R.loss[1] += af[0:8] + af[8:16] + af[16:24] + af[24:32] + af[32:40]
    dh = jnp.concatenate(grads, axis=0)
    R.a_hb[0:72] += fold4(dh)
    dhl = low(jnp.concatenate([dh, jnp.zeros((56, L), F32)], axis=0))
    R.a_head[...] += nt(fin, dhl)
    df = nn(R.head[...], dhl)[0:D]
    R.a_fin[0, 0:D] += fold4(df * xh)
    R.a_fin[1, 0:D] += fold4(df)
    return normed_back(df * tile4(R.bcf[0]), xh, r)


def layer_bwd(R, l, c, dout):
    def vec(i):
        return tile4(R.bc[l, i])

    def add_bias(i, v):
        R.a_bias[l, i, 0:D] += fold4(v)

    outl = low(pad8(dout))
    R.a_proj[l] += nt(R.inner[l, c], outl)
    add_bias(PB, dout)
    di = nn(R.proj[l], outl)
    parts = []
    for j in range(4):
        pj = di[128 * j:128 * j + D] * gelu_back(R.pre[l, c, D * j:D * (j + 1)])
        plow = low(pad8(pj))
        add_bias(FB0 + j, plow.astype(F32)[0:D])
        parts.append(plow)
    prel = jnp.concatenate(parts, axis=0)
    R.a_fc[l] += nt(R.n2[l, c], prel)
    dn = nn(R.fc[l], prel)[0:D]
    xh = R.xh2[l, c]
    add_bias(G2, dn * xh)
    add_bias(B2, dn)
    dmid = normed_back(dn * vec(G2), xh, R.r2[l, c]) + dout
    midl = low(pad8(dmid))
    R.a_out[l] += nt(R.att[l, c], midl)
    add_bias(OB, dmid)
    da = nn(R.out[l], midl)[0:D]
    dq, dk, dv = [], [], []
    for g in range(CG):
        at = slice(128 * g, 128 * (g + 1))
        res = attend_back(da[:, at], R.prob[l, c * CG + g], R.mix[l, c, 0:D, at],
                          R.mix[l, c, D:2 * D, at], R.mix[l, c, 2 * D:3 * D, at])
        for lst, val in zip((dq, dk, dv), res):
            lst.append(val)
    dq, dk, dv = (jnp.concatenate(v, axis=1) for v in (dq, dk, dv))
    add_bias(QB, dq)
    add_bias(VB, dv)
    mixl = jnp.concatenate([low(pad8(dq)), low(pad8(dk)), low(pad8(dv))], axis=0)
    R.a_qkv[l] += nt(R.n1[l, c], mixl)
    dn = nn(R.qkv[l], mixl)[0:D]
    xh = R.xh1[l, c]
    add_bias(G1, dn * xh)
    add_bias(B1, dn)
    return normed_back(dn * vec(G1), xh, R.r1[l, c]) + dmid


def embed_bwd(R, obs, c, dx):
    R.a_x[0:D] += fold4(dx)
    lanes = iota((D, 128), 1)
    tiles = []
    gs = [dx[:, 128 * g:128 * (g + 1)] for g in range(CG)]
    for t in range(CG):
        a = shifted(gs[t], -8 * t)
        b = shifted(gs[t + 1], 120 - 8 * t) if t + 1 < CG else jnp.zeros((D, 128), F32)
        tiles.append(jnp.where(lanes < GT - 8 * t, a, b))
    gl = low(pad8(jnp.concatenate(tiles, axis=1)))
    R.a_obs[...] += nn(gl, jnp.concatenate(obs, axis=1))


def zero_grads(R):
    for name in ("a_qkv", "a_out", "a_fc", "a_proj", "a_bias", "a_obs", "a_x", "a_fin", "a_head", "a_hb", "loss"):
        ref = getattr(R, name)
        ref[...] = jnp.zeros(ref.shape, F32)


HIGH = lax.Precision.HIGHEST


def pack_layer(R, rg, l):
    b = BASE + LROW * l
    for j in range(3):
        rg[pl.ds(b + 2 + j, D, stride=3), :] = R.a_qkv[l, 0:D, 128 * j:128 * (j + 1)]
    rg[pl.ds(b + 364, D), :] = R.a_out[l, 0:D]
    for j in range(4):
        rg[pl.ds(b + 487 + j, D, stride=4), :] = R.a_fc[l, 0:D, 128 * j:128 * (j + 1)]
        rg[pl.ds(b + 971 + D * j, D), :] = R.a_proj[l, 128 * j:128 * j + D, :]
    rows = nt(jnp.ones((8, 128), F32), R.a_bias[l].reshape(12 * 128, 128), HIGH)
    for i, r in enumerate(VROWS):
        rg[pl.ds(b + r, 1), :] = rows[0:1, 128 * i:128 * (i + 1)]


def pack_embed(R, rg):
    for f in range(OBS // 128):
        rg[128 * f:128 * (f + 1), :] = R.a_obs[:, 128 * f:128 * (f + 1)].T
    slot, lane = iota((32, 128), 0), iota((32, 128), 1)
    sel = jnp.where((slot == 0) | (lane % WIN == slot - 1), 1.0, 0.0)
    sel = jnp.where(lane < GT, sel, 0.0)
    rows = nt(sel, R.a_x[...], HIGH)
    rg[pl.ds(OBS, 1 + WIN), :] = rows[0:1 + WIN]


def pack_head(R, rg):
    rows = nt(jnp.ones((8, 128), F32), R.a_fin[...].reshape(256, 128), HIGH)
    for i in range(2):
        rg[pl.ds(HEAD + i, 1), :] = rows[0:1, 128 * i:128 * (i + 1)]
    lanes8 = iota((8, 128), 1)
    grad = R.a_head[...]
    R.hc[...] = jnp.where(iota((128, 128), 1) < 32, grad, 0.0)
    R.ho[...] = jnp.where(iota((128, 128), 1) < OFFS, shifted(grad, -32), 0.0)
    c0 = HEAD + 2
    o0 = c0 + 32

    def put(phases, src, rows_n, stride, width, count):
        acc = [jnp.zeros((rows_n, 128), F32) for _ in range(count + 1)]
        lanes = iota((rows_n, 128), 1)
        for p, a, s in phases:
            v = src[pl.ds(p, rows_n, stride=stride), :]
            first = shifted(v, s)
            if s + width > D:
                acc[a] = acc[a] + jnp.where((lanes >= s) & (lanes < D), first, 0.0)
                acc[a + 1] = acc[a + 1] + jnp.where(lanes < s + width - D, shifted(v, s - D), 0.0)
            else:
                acc[a] = acc[a] + first
        return acc

    acc = put(code_phases(), R.hc, 8, 15, 32, 4)
    for a in range(4):
        rg[pl.ds(c0 + a, 8, stride=4), :] = acc[a]
    hb = nt(jnp.ones((8, 128), F32), R.a_hb[...], HIGH)[0:1]
    lane1 = iota((1, 128), 1)
    rg[pl.ds(o0, 48), :] = jnp.zeros((48, 128), F32)
    acc = put(off_phases(), R.ho, 5, 24, OFFS, 7)
    for a in range(7):
        rg[pl.ds(o0 + a, 5, stride=7), :] = acc[a]
    rg[pl.ds(o0 + 7, 5, stride=7), :] = rg[pl.ds(o0 + 7, 5, stride=7), :] + acc[7]
    rg[pl.ds(o0, 1), :] = rg[pl.ds(o0, 1), :] + jnp.where(lane1 < 32, hb, 0.0)
    a, s = (D * OFFS + 32) // D, (D * OFFS + 32) % D
    ob = jnp.where(lane1 < OFFS, shifted(hb, -32), 0.0)
    rg[pl.ds(o0 + a, 1), :] = rg[pl.ds(o0 + a, 1), :] + shifted(ob, s)


MESH = pl.DeviceIdType.MESH


def round_up(n, m):
    return -(-n // m) * m


class Plan:
    def __init__(self, feats, toks, shard, tok_rows):
        self.feats, self.toks, self.chips = feats, toks, toks // 2
        self.shard = shard
        self.block = round_up(-(-(shard + 112) // D), 16)
        self.flat_rows = self.block // 16 * 15
        self.local = round_up(-(-shard // 128), 8)
        self.work = round_up(max(self.flat_rows, self.local + 1), 8)
        self.own_rows = tok_rows // feats
        self.chunks = self.own_rows // CT
        self.grid = round_up(-(-(shard * feats * toks) // D) + self.block, 8)


def comm_scratch(P):
    dma = pltpu.SemaphoreType.DMA
    B, C, Fn = P.block, P.chips, P.feats
    return dict(
        rg=pltpu.VMEM((P.grid, 128), F32),
        ob=pltpu.VMEM((P.chunks, Fn, L, 128), BF),
        pg=pltpu.VMEM((2, C, Fn, B, 128), BF),
        loc=pltpu.VMEM((P.work, 128), F32),
        rblk=pltpu.VMEM((B, 128), F32),
        codes_in=pltpu.VMEM((BOOKS, P.own_rows), jnp.int32),
        act_in=pltpu.VMEM((OFFS, P.own_rows), F32),
        val_in=pltpu.VMEM((OFFS, P.own_rows), jnp.int32),
        tz=pltpu.VMEM((2, Fn, 8, 128), F32),
        tc=pltpu.VMEM((2, C, 8, 128), F32),
        ts=pltpu.VMEM((2, 2, 8, 128), F32),
        sb1=pltpu.VMEM((C, Fn, B, 128), F32),
        rb1=pltpu.VMEM((C, Fn, B, 128), F32),
        sb2=pltpu.VMEM((C, Fn, B, 128), F32),
        rb2=pltpu.VMEM((C, Fn, B, 128), F32),
        sb3=pltpu.VMEM((Fn, B, 128), F32),
        rb3=pltpu.VMEM((Fn, B, 128), F32),
        s_p1=dma((2, Fn)), s_p2=dma((2, C)), s_p3=dma((2, C)),
        s_tz=dma((2, 2, Fn)), s_tc=dma((2, 2, C)), s_ts=dma((2, 2)),
        s_ob=dma((2, P.chunks, Fn)),
        s_in=dma((3,)),
        s_r1=dma((2, C)), s_r2=dma((2, C)), s_r3=dma((2, Fn)),
    )


def to_rows(loc, rblk, delta, P):
    v = loc[...]
    lanes = iota(v.shape, 1)
    moved = pltpu.roll(v, delta, 1)
    loc[...] = jnp.where(lanes >= delta, moved, pltpu.roll(moved, 1, 0))
    n = P.block // 16
    lane = iota((n, 128), 1)
    for j in range(16):
        if j < 15:
            a = shifted(loc[pl.ds(j, n, stride=15), :], 8 * j)
        if j > 0:
            b = shifted(loc[pl.ds(j - 1, n, stride=15), :], 8 * j)
            a = jnp.where(lane < 8 * j, b, a) if j < 15 else b
        rblk[pl.ds(j, n, stride=16), :] = jnp.where(lane < D, a, 0.0)


def from_rows(rblk, loc, delta, P):
    n = P.block // 16
    lane = iota((n, 128), 1)
    loc[...] = jnp.zeros(loc.shape, F32)
    for i in range(15):
        a = shifted(rblk[pl.ds(i, n, stride=16), :], -8 * i)
        b = shifted(rblk[pl.ds(i + 1, n, stride=16), :], D - 8 * i)
        loc[pl.ds(i, n, stride=15), :] = jnp.where(lane < D - 8 * i, a, b)
    v = loc[...]
    lanes = iota(v.shape, 1)
    moved = pltpu.roll(v, lax.rem(128 - delta, 128), 1)
    v = jnp.where(lanes < 128 - delta, moved, pltpu.roll(moved, P.work - 1, 0))
    return v[0:P.local]


def step_kernel(P, names, master, first, second, obs, counts, codes, actions, valid,
                new_master, new_first, new_second, sums, *scratch):
    R = Refs()
    for name, ref in zip(names, scratch):
        setattr(R, name, ref)
    Fn, C, B = P.feats, P.chips, P.block
    feat = lax.axis_index("feat")
    tok = lax.axis_index("tok")
    chip = tok // 2
    core = tok % 2
    me = feat * P.toks + tok
    delta = lax.rem(me * P.shard, D)

    def z_peer(i):
        return lax.rem(feat + i, Fn)

    def z_from(i):
        return lax.rem(feat + Fn - i, Fn)

    def c_peer(i):
        return lax.rem(chip + i, C)

    def c_from(i):
        return lax.rem(chip + C - i, C)

    def to_z(i):
        return (z_peer(i), tok)

    def to_c(i):
        return (feat, 2 * c_peer(i) + core)

    sibling = (feat, 2 * chip + 1 - core)

    def send(src, dst, sems, at, dev):
        return pltpu.make_async_remote_copy(
            src_ref=src, dst_ref=dst, send_sem=sems.at[(0,) + at], recv_sem=sems.at[(1,) + at],
            device_id=dev, device_id_type=MESH)

    n = P.own_rows
    ins = []
    for i, (src, dst) in enumerate(((codes, R.codes_in), (actions, R.act_in), (valid, R.val_in))):
        ins.append(pltpu.make_async_copy(src.at[:, pl.ds(pl.multiple_of(feat * n, 128), n)], dst, R.s_in.at[i]))
        ins[-1].start()

    barrier = pltpu.get_barrier_semaphore()
    peers = [to_z(i) for i in range(1, Fn)] + [to_c(i) for i in range(1, C)] + [sibling]
    for dev in peers:
        pl.semaphore_signal(barrier, inc=1, device_id=dev, device_id_type=MESH)

    R.loc[...] = jnp.zeros(R.loc.shape, F32)
    R.loc[0:P.local, :] = master[...]
    to_rows(R.loc, R.rblk, delta, P)
    R.pg[core, chip, feat] = low(R.rblk[...])
    pl.semaphore_wait(barrier, len(peers))

    p1 = []
    for i in range(1, Fn):
        blk = R.pg.at[core, chip, feat]
        p1.append(send(blk, blk, R.s_p1, (i,), to_z(i)))
        p1[-1].start()

    own = []
    others = []

    def start_obs(c):
        for i in range(1, Fn):
            src = obs.at[pl.ds(pl.multiple_of(z_peer(i) * n + CT * c, 16), CT), :]
            cp = send(src, R.ob.at[c, feat, pl.ds(0, CT), :], R.s_ob, (c, i), to_z(i))
            cp.start()
            others.append(cp)
        src = obs.at[pl.ds(pl.multiple_of(feat * n + CT * c, 16), CT), :]
        cp = pltpu.make_async_copy(src, R.ob.at[c, feat, pl.ds(0, CT), :], R.s_ob.at[0, c, 0])
        cp.start()
        own.append(cp)

    start_obs(0)
    for cp in ins:
        cp.wait()
    zero_grads(R)
    for c in range(P.chunks):
        for f in range(Fn):
            R.ob[c, f, CT:L, :] = jnp.zeros((L - CT, 128), BF)
    live_n, valid_n = prep_tokens(R, counts, R.codes_in, R.act_in, R.val_in, feat, P.chunks)

    def two_rows(a, b):
        return jnp.concatenate([jnp.broadcast_to(a, (1, 128)), jnp.broadcast_to(b, (1, 128)),
                                jnp.zeros((6, 128), F32)], axis=0)

    def hop_z(w, value):
        R.tz[w, feat] = value
        cps = []
        for i in range(1, Fn):
            cps.append(send(R.tz.at[w, feat], R.tz.at[w, feat], R.s_tz.at[w], (i,), to_z(i)))
            cps[-1].start()
        return cps

    def hop_c(w, value):
        R.tc[w, chip] = value
        cps = []
        for i in range(1, C):
            cps.append(send(R.tc.at[w, chip], R.tc.at[w, chip], R.s_tc.at[w], (i,), to_c(i)))
            cps[-1].start()
        return cps

    def hop_s(w, value):
        R.ts[w, core] = value
        cp = send(R.ts.at[w, core], R.ts.at[w, core], R.s_ts.at[w], (), sibling)
        cp.start()
        return [cp]

    def total(ref, w, count):
        v = ref[w, 0]
        for i in range(1, count):
            v = v + ref[w, i]
        return v

    def wait_all(cps):
        for cp in cps:
            cp.wait()

    tz = hop_z(0, two_rows(live_n, valid_n))
    wait_all(p1)
    p2 = []
    for i in range(1, C):
        blk = R.pg.at[core, chip]
        p2.append(send(blk, blk, R.s_p2, (i,), to_c(i)))
        p2[-1].start()
    p3 = [send(R.pg.at[core, chip], R.pg.at[core, chip], R.s_p3, (0,), sibling)]
    p3[0].start()
    wait_all(tz)
    tc = hop_c(0, total(R.tz, 0, Fn))
    for i in range(1, C):
        p2[i - 1].wait_recv()
        blk = R.pg.at[core, c_from(i)]
        p3.append(send(blk, blk, R.s_p3, (i,), sibling))
        p3[-1].start()
    for c in range(1, P.chunks):
        start_obs(c)
    wait_all(tc)
    ts = hop_s(0, total(R.tc, 0, C))
    for cp in p2:
        cp.wait_send()
    wait_all(p3)
    wait_all(ts)
    counted = total(R.ts, 0, 2)
    live_total = counted[0:1, 0:1]
    valid_total = counted[1:2, 0:1]

    R.rg[0:8, :] = jnp.zeros((8, 128), F32)

    def place(d, _):
        r0 = (P.shard * d) // D
        f, t = d // P.toks, d % P.toks
        blk = R.pg[t % 2, t // 2, f].astype(F32)
        before = R.rg[pl.ds(r0, 1), :]
        R.rg[pl.ds(r0, B), :] = blk
        R.rg[pl.ds(r0, 1), :] = blk[0:1] + before
        return 0

    lax.fori_loop(0, Fn * P.toks, place, 0)
    prep_weights(R.rg, R)

    def fwd(c, _):
        for i in range(1, Fn):
            send(R.ob.at[c, feat, pl.ds(0, CT), :], R.ob.at[c, feat, pl.ds(0, CT), :],
                 R.s_ob, (c, i), to_z(i)).wait_recv()
        pltpu.make_async_copy(obs.at[pl.ds(0, CT), :], R.ob.at[c, feat, pl.ds(0, CT), :],
                              R.s_ob.at[0, c, 0]).wait()
        R.x[c] = embed(R, [R.ob[c, f, 0:CT, :] for f in range(Fn)], c)

        def lay(l, _):
            R.x[c] = layer_fwd(R, l, c, R.x[c])
            return 0

        lax.fori_loop(0, LAYERS, lay, 0)
        return 0

    lax.fori_loop(0, P.chunks, fwd, 0)

    def heads(c, _):
        R.x[c] = head_step(R, c, R.x[c], live_total, valid_total)
        return 0

    lax.fori_loop(0, P.chunks, heads, 0)
    lz = hop_z(1, two_rows(jnp.sum(R.loss[0], keepdims=True), jnp.sum(R.loss[1], keepdims=True)))

    def back(i, _):
        def chunk(c, _):
            R.x[c] = layer_bwd(R, LAYERS - 1 - i, c, R.x[c])
            return 0

        lax.fori_loop(0, P.chunks, chunk, 0)
        return 0

    lax.fori_loop(0, LAYERS, back, 0)

    def last(c, _):
        embed_bwd(R, [R.ob[c, f] for f in range(Fn)], c, R.x[c])
        return 0

    lax.fori_loop(0, P.chunks, last, 0)
    wait_all(lz)
    lc = hop_c(1, total(R.tz, 1, Fn))
    R.rg[pl.ds(HEAD + 32, P.grid - HEAD - 32), :] = jnp.zeros((P.grid - HEAD - 32, 128), F32)
    for l in range(LAYERS):
        pack_layer(R, R.rg, l)
    pack_embed(R, R.rg)
    pack_head(R, R.rg)

    def rows_of(f, ch, co):
        return (P.shard * (f * P.toks + 2 * ch + co)) // D

    r1 = []
    for i in range(1, C + 1):
        ch = c_peer(i)
        for f in range(Fn):
            R.sb1[i - 1, f] = R.rg[pl.ds(rows_of(f, ch, 1 - core), B), :]
        r1.append(send(R.sb1.at[i - 1], R.rb1.at[i - 1], R.s_r1, (i - 1,), sibling))
        r1[-1].start()
    wait_all(lc)
    ls = hop_s(1, total(R.tc, 1, C))
    r2 = []
    for i in range(1, C):
        ch = c_peer(i)
        r1[i - 1].wait_recv()
        for f in range(Fn):
            R.sb2[i, f] = R.rg[pl.ds(rows_of(f, ch, core), B), :] + R.rb1[i - 1, f]
        r2.append(send(R.sb2.at[i], R.rb2.at[i], R.s_r2, (i,), to_c(i)))
        r2[-1].start()
    r1[C - 1].wait_recv()
    for f in range(Fn):
        R.sb2[0, f] = R.rg[pl.ds(rows_of(f, chip, core), B), :] + R.rb1[C - 1, f]
    for cp in r2:
        cp.wait_recv()
    r3 = []
    for i in range(1, Fn):
        f = z_peer(i)
        v = R.sb2[0, f]
        for j in range(1, C):
            v = v + R.rb2[j, f]
        R.sb3[i] = v
        r3.append(send(R.sb3.at[i], R.rb3.at[i], R.s_r3, (i,), to_z(i)))
        r3[-1].start()
    v = R.sb2[0, feat]
    for j in range(1, C):
        v = v + R.rb2[j, feat]
    for i in range(1, Fn):
        r3[i - 1].wait_recv()
        v = v + R.rb3[i]
    R.rblk[...] = v
    grad = from_rows(R.rblk, R.loc, delta, P)
    f_new = BETA_ONE * first[...] + (1.0 - BETA_ONE) * grad
    s_new = BETA_TWO * second[...] + (1.0 - BETA_TWO) * grad * grad
    f_hat = f_new / (1.0 - BETA_ONE ** STEP_NO)
    s_hat = s_new / (1.0 - BETA_TWO ** STEP_NO)
    old = master[...]
    new_first[...] = f_new
    new_second[...] = s_new
    new_master[...] = old - LEARN_RATE * (f_hat / (jnp.sqrt(s_hat) + ADAM_EPS) + DECAY_RATE * old)
    wait_all(ls)
    lost = total(R.ts, 1, 2)
    sums[...] = jnp.concatenate([lost[0:1], counted[0:1], lost[1:2], counted[1:2], jnp.zeros((4, 128), F32)], axis=0)
    for cps in (others, r1, r2, r3):
        for cp in cps:
            cp.wait_send()


def solution(mesh):
    feats, toks = mesh.shape["feat"], mesh.shape["tok"]

    def shards(master, first, second, obs, counts, codes, actions, valid):
        P_ = Plan(feats, toks, master.shape[0], obs.shape[0])
        scratch = dict(scratch_list(P_.chunks))
        scratch.update(comm_scratch(P_))
        pad = P_.local * 128 - P_.shard
        flat = [jnp.pad(v, (0, pad)).reshape(P_.local, 128) for v in (master, first, second)]
        vmem = pl.BlockSpec(memory_space=pltpu.VMEM)
        hbm = pl.BlockSpec(memory_space=pl.ANY)
        out = jax.ShapeDtypeStruct((P_.local, 128), F32)
        outs = pl.pallas_call(
            functools.partial(step_kernel, P_, list(scratch)),
            out_shape=(out, out, out, jax.ShapeDtypeStruct((8, 128), F32)),
            in_specs=[vmem, vmem, vmem, hbm, vmem, hbm, hbm, hbm],
            out_specs=(vmem,) * 4,
            scratch_shapes=list(scratch.values()),
            compiler_params=pltpu.CompilerParams(
                collective_id=0, has_side_effects=True, vmem_limit_bytes=60 * 2 ** 20),
        )(*flat, obs, counts.T, codes.T, actions, valid)
        cut = [v.reshape(-1)[:P_.shard] for v in outs[:3]]
        return (*cut, outs[3][0:4, 0])

    weights = PSpec(("feat", "tok"))
    return jax.shard_map(
        shards, mesh=mesh,
        in_specs=(weights, weights, weights, PSpec("tok", "feat"), PSpec("tok", None), PSpec("tok", None),
                  PSpec(None, "tok"), PSpec(None, "tok")),
        out_specs=(weights, weights, weights, PSpec()), check_vma=False)
```

```python
import functools
import math

import jax
import jax.numpy as jnp
from jax import lax
from jax.experimental import pallas as pl
from jax.experimental.pallas import tpu as pltpu
from jax.sharding import PartitionSpec as PSpec

D = 120
H = 6
HD = 20
FF = 480
OBS = 512
LAYERS = 2
CAMS = 3
BOOKS = 2
CODES = 16
SPAN = 5
ACT = 7
WIN = 30
OFFS = SPAN * ACT
NORM_EPS = 1e-05
STEP_NO = 10
BETA_ONE = 0.9
BETA_TWO = 0.999
ADAM_EPS = 1e-08
DECAY_RATE = 0.1
LEARN_RATE = 0.05
GW = 4
GT = GW * WIN
CG = 4
L = CG * 128
CT = CG * GT
F32 = jnp.float32
BF = jnp.bfloat16
SCALE = HD ** (-0.5)
LROW = 2 * 1 + 3 * D + 2 + D + 1 + 2 + 4 * D + 4 + 4 * D + 1
BASE = OBS + 1 + WIN
HEAD = BASE + LAYERS * LROW
NV = 13
VROWS = [0, 1, 362, 363, 484, 485, 486, 967, 968, 969, 970, 1451]
(G1, B1, QB, VB, OB, G2, B2, FB0, FB1, FB2, FB3, PB) = range(12)


def nn(a, b):
    return lax.dot_general(a, b, (((1,), (0,)), ((), ())), preferred_element_type=F32)


def nt(a, b, precision=None):
    return lax.dot_general(a, b, (((1,), (1,)), ((), ())), preferred_element_type=F32, precision=precision)


def low(v):
    return v.astype(BF)


def pad8(v):
    return jnp.concatenate([v, jnp.zeros((8, v.shape[1]), v.dtype)], axis=0)


def tile4(v):
    return jnp.concatenate([v] * CG, axis=1)


def fold4(v):
    out = v[:, 0:128]
    for g in range(1, CG):
        out = out + v[:, 128 * g:128 * (g + 1)]
    return out


def iota(shape, axis):
    return lax.broadcasted_iota(jnp.int32, shape, axis)


def slab_at(h):
    return 20 * h - (4 if h % 2 else 0)


def head_stack(v):
    rows = iota((8, 128), 0)
    cols = []
    for h in range(H):
        a = slab_at(h)
        if h % 2 == 0:
            parts = [v[a:a + 16], jnp.where(rows < 4, v[a + 16:a + 24], 0.0)]
        else:
            parts = [jnp.where(rows >= 4, v[a:a + 8], 0.0), v[a + 8:a + 24]]
        if a > 0:
            parts = [jnp.zeros((a, 128), F32)] + parts
        if a + 24 < 128:
            parts = parts + [jnp.zeros((128 - a - 24, 128), F32)]
        cols.append(jnp.concatenate(parts, axis=0))
    return jnp.concatenate(cols, axis=1)


def join_slabs(slabs):
    rows = iota((8, 128), 0)
    parts = []
    for p in range(3):
        a, b = slabs[2 * p], slabs[2 * p + 1]
        parts += [a[0:16], jnp.where(rows < 4, a[16:24], b[0:8]), b[8:24]]
    return jnp.concatenate(parts, axis=0)


def slabs_of(v):
    return [v[slab_at(h):slab_at(h) + 24] for h in range(H)]


def hi_lo(v):
    hi = low(v)
    return hi, low(v - hi.astype(F32))


def normed(x):
    mean = jnp.sum(x, axis=0, keepdims=True) * (1.0 / D)
    c = x - mean
    var = jnp.sum(c * c, axis=0, keepdims=True) * (1.0 / D)
    r = lax.rsqrt(var + NORM_EPS)
    return c * r, r


def normed_back(d, xh, r):
    m0 = jnp.sum(d, axis=0, keepdims=True) * (1.0 / D)
    m1 = jnp.sum(d * xh, axis=0, keepdims=True) * (1.0 / D)
    return r * (d - m0 - xh * m1)


GA = math.sqrt(2.0 / math.pi)
GB = 0.044715


def gelu_half(x):
    return 0.5 + 0.5 * jnp.tanh(x * (GA + (GA * GB) * (x * x)))


def gelu_slope(x, s):
    return s + (x * s) * (1.0 - s) * (2.0 * GA + (6.0 * GA * GB) * (x * x))


LOG2E = math.log2(math.e)
BIG = 1e30


class Refs:
    pass


def scratch_list(chunks):
    groups = chunks * CG
    return dict(
        w_obs=pltpu.VMEM((OBS, 128), BF),
        posb=pltpu.VMEM((GT, 128), F32),
        qkv_t=pltpu.VMEM((LAYERS, 384, 128), BF),
        qkv=pltpu.VMEM((LAYERS, 128, 384), BF),
        out_t=pltpu.VMEM((LAYERS, 128, 128), BF),
        out=pltpu.VMEM((LAYERS, 128, 128), BF),
        fc_t=pltpu.VMEM((LAYERS, 512, 128), BF),
        fc=pltpu.VMEM((LAYERS, 128, 512), BF),
        proj_t=pltpu.VMEM((LAYERS, 128, 512), BF),
        proj=pltpu.VMEM((LAYERS, 512, 128), BF),
        head_t=pltpu.VMEM((72, 128), BF),
        head=pltpu.VMEM((128, 128), BF),
        vec=pltpu.VMEM((32, 128), F32),
        bc=pltpu.VMEM((LAYERS, 12, GT, 128), F32),
        bcf=pltpu.VMEM((2, GT, 128), F32),
        bch=pltpu.VMEM((72, 128), F32),
        hc=pltpu.VMEM((128, 128), F32),
        ho=pltpu.VMEM((128, 128), F32),
        cnt=pltpu.VMEM((16, 256), F32),
        live=pltpu.VMEM((chunks, 1, L), F32),
        act=pltpu.VMEM((chunks, 40, L), F32),
        val=pltpu.VMEM((chunks, 40, L), F32),
        code=pltpu.VMEM((chunks, 2, L), F32),
        x=pltpu.VMEM((D, L), F32),
        xh1=pltpu.VMEM((LAYERS, D, L), F32),
        r1=pltpu.VMEM((LAYERS, 1, L), F32),
        xh2=pltpu.VMEM((LAYERS, D, L), F32),
        r2=pltpu.VMEM((LAYERS, 1, L), F32),
        n1=pltpu.VMEM((LAYERS, 128, L), BF),
        n2=pltpu.VMEM((LAYERS, 128, L), BF),
        att=pltpu.VMEM((LAYERS, 128, L), BF),
        q_low=pltpu.VMEM((LAYERS, H, 24, L), BF),
        k_low=pltpu.VMEM((LAYERS, H, 24, L), BF),
        v_low=pltpu.VMEM((LAYERS, 128, L), BF),
        rsum=pltpu.VMEM((LAYERS, H, 1, L), F32),
        prob=pltpu.VMEM((LAYERS, CG, GT, H * 128), F32),
        prob_low=pltpu.VMEM((LAYERS, CG, 128, H * 128), BF),
        k_mask=pltpu.VMEM((48, 128), BF),
        q_mask=pltpu.VMEM((48, 128), BF),
        dead=pltpu.VMEM((groups, 8, 128), F32),
        pre=pltpu.VMEM((LAYERS, FF, L), F32),
        half=pltpu.VMEM((LAYERS, FF, L), F32),
        inner=pltpu.VMEM((LAYERS, 512, L), BF),
        a_qkv=pltpu.VMEM((LAYERS, 128, 384), F32),
        a_out=pltpu.VMEM((LAYERS, 128, 128), F32),
        a_fc=pltpu.VMEM((LAYERS, 128, 512), F32),
        a_proj=pltpu.VMEM((LAYERS, 128, 512), F32),
        a_bias=pltpu.VMEM((LAYERS, 12, 128, 128), F32),
        a_obs=pltpu.VMEM((128, 512), F32),
        a_x=pltpu.VMEM((128, 128), F32),
        a_fin=pltpu.VMEM((2, 128, 128), F32),
        a_head=pltpu.VMEM((128, 128), F32),
        a_hb=pltpu.VMEM((128, 128), F32),
        loss=pltpu.VMEM((2, 8, 128), F32),
    )


def code_phases():
    for p in range(15):
        yield p, (32 * p) // D, (32 * p) % D


def off_phases():
    for p in range(24):
        yield p, (35 * p + 32) // D, (35 * p + 32) % D


def shifted(v, by):
    by %= 128
    return v if by == 0 else pltpu.roll(v, by, 1)


def take_phase(load, a, s, width, rows):
    lanes = iota((rows, 128), 1)
    first = shifted(load(a), -s)
    if s + width > D:
        second = shifted(load(a + 1), D - s)
        first = jnp.where(lanes < D - s, first, second)
    return jnp.where(lanes < width, first, 0.0)


def with_bias(w, bias):
    if bias is not None:
        w = jnp.where(iota((128, 128), 0) == D, bias, w)
    return low(w.T)


def ones8(v):
    return jnp.concatenate([v, jnp.where(iota((8, v.shape[1]), 0) == 0, 1.0, 0.0)], axis=0)


def prep_weights(rg, R):
    R.w_obs[...] = low(rg[0:OBS, :])
    for w in range(GW):
        R.posb[pl.ds(WIN * w, WIN), :] = rg[OBS + 1:OBS + 1 + WIN, :] + rg[OBS:OBS + 1, :]
    R.vec[...] = jnp.zeros((32, 128), F32)
    for l in range(LAYERS):
        b = BASE + LROW * l
        for j in range(3):
            w = pad8(rg[pl.ds(b + 2 + j, D, stride=3), :])
            R.qkv[l, :, 128 * j:128 * (j + 1)] = low(w)
            R.qkv_t[l, 128 * j:128 * (j + 1), :] = with_bias(w, None if j == 1 else rg[pl.ds(b + 362 + j // 2, 1), :])
        w = pad8(rg[pl.ds(b + 364, D), :])
        R.out[l] = low(w)
        R.out_t[l] = with_bias(w, rg[pl.ds(b + 484, 1), :])
        for j in range(4):
            w = pad8(rg[pl.ds(b + 487 + j, D, stride=4), :])
            R.fc[l, :, 128 * j:128 * (j + 1)] = low(w)
            R.fc_t[l, 128 * j:128 * (j + 1), :] = with_bias(w, rg[pl.ds(b + 967 + j, 1), :])
            w = pad8(rg[pl.ds(b + 971 + D * j, D), :])
            R.proj[l, 128 * j:128 * (j + 1), :] = low(w)
            R.proj_t[l, :, 128 * j:128 * (j + 1)] = with_bias(w, None if j else rg[pl.ds(b + 1451, 1), :])
        for i, r in enumerate(VROWS):
            R.vec[pl.ds(12 * l + i, 1), :] = rg[pl.ds(b + r, 1), :]
    R.vec[24:26, :] = rg[pl.ds(HEAD, 2), :]
    R.hc[...] = jnp.zeros((128, 128), F32)
    R.ho[...] = jnp.zeros((128, 128), F32)
    c0 = HEAD + 2
    for p, a, s in code_phases():
        R.hc[pl.ds(p, 8, stride=15), :] = take_phase(
            lambda i: rg[pl.ds(c0 + i, 8, stride=4), :], a, s, 32, 8)
    o0 = c0 + 32
    for p, a, s in off_phases():
        R.ho[pl.ds(p, 5, stride=24), :] = take_phase(
            lambda i: rg[pl.ds(o0 + i, 5, stride=7), :], a, s, OFFS, 5)
    hw = R.hc[...] + shifted(R.ho[...], 32)
    R.head[...] = low(hw)
    R.head_t[...] = low(hw.T[0:72])
    lanes = iota((1, 128), 1)
    hb = jnp.where(lanes < 32, rg[pl.ds(o0, 1), :], 0.0)
    a, s = (D * OFFS + 32) // D, (D * OFFS + 32) % D
    ob = take_phase(lambda i: rg[pl.ds(o0 + i, 1), :], a, s, OFFS, 1)
    R.vec[26:27, :] = hb + shifted(ob, 32)
    columns = jnp.concatenate([R.vec[...], jnp.zeros((96, 128), F32)], axis=0).T
    for l in range(LAYERS):
        for i in range(12):
            R.bc[l, i] = jnp.broadcast_to(columns[0:D, 12 * l + i:12 * l + i + 1], (D, 128))
    for i in range(2):
        R.bcf[i] = jnp.broadcast_to(columns[0:D, 24 + i:25 + i], (D, 128))
    R.bch[...] = jnp.broadcast_to(columns[0:72, 26:27], (72, 128))


def spread_groups(v, groups, width):
    rows = v.shape[0]
    lanes = iota((rows, 128), 1)
    out = []
    for g in range(groups):
        t, o = (GT * g) // 128, (GT * g) % 128
        a = shifted(v[:, 128 * t:128 * (t + 1)], -o)
        if o + GT > 128:
            b = shifted(v[:, 128 * (t + 1):128 * (t + 2)], -o)
            a = jnp.where(lanes < 128 - o, a, b)
        out.append(jnp.where(lanes < GT, a, 0))
    return out


def prep_tokens(R, counts, codes, actions, valid, feat, chunks):
    groups = chunks * CG
    wins = counts.shape[1]
    R.cnt[...] = jnp.zeros(R.cnt.shape, F32)
    R.cnt[0:WIN // CAMS, :] = counts[...].astype(F32)
    k = iota((GT, 16), 0)
    step = (k % WIN) // CAMS
    sel = jnp.where(step == iota((GT, 16), 1), 1.0, 0.0)
    x = nn(low(sel), low(R.cnt[...]))
    y = jnp.where(iota((GT, wins), 1) % GW == iota((GT, wins), 0) // WIN, x, 0.0)
    pick = jnp.where(iota((wins, 128), 0) // GW == iota((wins, 128), 1) + groups * feat, 1.0, 0.0)
    z = nn(low(y), low(pick))
    kk = iota((GT, 128), 0)
    alive = jnp.where((kk % CAMS).astype(F32) < z, 1.0, 0.0)
    steps = WIN // CAMS
    j, at = iota((48, 128), 0), iota((48, 128), 1)
    own = (at // WIN == j // steps) & ((at % WIN) // CAMS == j % steps) & (at < GT)
    R.k_mask[...] = low(jnp.where(own, 1.0, 0.0))
    may = (at // WIN == j // steps) & ((at % WIN) // CAMS >= j % steps)
    R.q_mask[...] = low(jnp.where(may | (j >= GW * steps), 0.0, -BIG))
    rows = pad8(alive).T
    for g in range(groups):
        R.live[g // CG, :, 128 * (g % CG):128 * (g % CG + 1)] = rows[g:g + 1, :]
        R.dead[g] = jnp.where(iota((8, 128), 0) == 0, 1.0 - rows[g:g + 1, :], 0.0)
    for name, src in (("code", codes), ("act", actions), ("val", valid)):
        parts = spread_groups(src[...].astype(F32), groups, GT)
        dst = getattr(R, name)
        for g in range(groups):
            c, lo = g // CG, 128 * (g % CG)
            part = parts[g]
            if name == "val":
                part = part * rows[g:g + 1, :]
            if name != "code":
                dst[c, 32:40, lo:lo + 128] = jnp.zeros((8, 128), F32)
            dst[c, 0:part.shape[0], lo:lo + 128] = part
    lanes = iota((GT, 128), 1)
    live_total = jnp.sum(jnp.where(lanes < groups, alive, 0.0), keepdims=True)
    v = jnp.zeros((40, L), F32)
    for c in range(chunks):
        v = v + R.val[c]
    valid_total = jnp.sum(v, keepdims=True)
    return live_total, valid_total


def own_rows(slab, h):
    rows = iota((8, 128), 0)
    if h % 2 == 0:
        return jnp.concatenate([slab[0:16], jnp.where(rows < 4, slab[16:24], 0.0)], axis=0)
    return jnp.concatenate([jnp.where(rows >= 4, slab[0:8], 0.0), slab[8:24]], axis=0)


def split(v):
    hi = low(v).astype(F32)
    return hi, v - hi


def attend(R, l, c, q, k, v):
    qh, ql = split(q)
    kh, kl = split(k)
    vh, vl = split(v)
    minus = jnp.where(iota((8, 128), 0) == 0, -BIG, 0.0)

    none = jnp.zeros((128, 128), BF)

    def scores(g, p):
        at = slice(128 * g, 128 * (g + 1))
        qs, ks = [], []
        for h in (2 * p, 2 * p + 1):
            sl = slice(slab_at(h), slab_at(h) + 24)
            hi = own_rows(qh[sl, at], h)
            qd = low(jnp.concatenate([hi, hi, own_rows(ql[sl, at], h), minus], axis=0))
            kd = low(jnp.concatenate([kh[sl, at], kl[sl, at], kh[sl, at], R.dead[c * CG + g]], axis=0))
            qs.append(jnp.concatenate([qd, R.q_mask[...]], axis=0))
            ks.append(jnp.concatenate([kd, R.k_mask[...]], axis=0).T)
        if PAIR:
            both = jnp.concatenate([jnp.concatenate([qs[0], none], axis=1),
                                    jnp.concatenate([none, qs[1]], axis=1)], axis=0)
            return nn(jnp.concatenate(ks, axis=1), both)[0:GT]
        return jnp.concatenate([nn(ks[0], qs[0])[0:GT], nn(ks[1], qs[1])[0:GT]], axis=1)

    def soft(g, p, s):
        at = slice(128 * g, 128 * (g + 1))
        e = jnp.exp2(s - jnp.max(s, axis=0, keepdims=True))
        r = 1.0 / jnp.sum(e, axis=0, keepdims=True)
        e8 = pad8(e)
        eh = low(e8)
        el = low(e8 - eh.astype(F32))
        cols = slice(256 * p, 256 * (p + 1))
        R.prob[l, g, :, cols] = e
        R.prob_low[l, g, :, cols] = eh
        R.rsum[l, 2 * p, :, at] = r[:, 0:128]
        R.rsum[l, 2 * p + 1, :, at] = r[:, 128:256]
        return r, eh, el

    def values(g, p, r, eh, el):
        at = slice(128 * g, 128 * (g + 1))
        out = []
        for i in range(2):
            sl = slice(slab_at(2 * p + i), slab_at(2 * p + i) + 24)
            cols = slice(128 * i, 128 * (i + 1))
            vs = low(jnp.concatenate([vh[sl, at], vl[sl, at]], axis=0))
            o = nn(jnp.concatenate([vs, vs], axis=1), jnp.concatenate([eh[:, cols], el[:, cols]], axis=0))
            out.append((o[0:24] + o[24:48]) * r[:, cols])
        return out

    items = [(g, p) for g in range(CG) for p in range(H // 2)]
    slabs = pipeline(items, scores, soft, values, FAHEAD)
    slabs = [t for pair in slabs for t in pair]
    return jnp.concatenate([join_slabs(slabs[H * g:H * (g + 1)]) for g in range(CG)], axis=1)


PAIR = True
FAHEAD = 2
BAHEAD = 2


def pipeline(items, first, second, third, ahead, between=()):
    n = len(items)
    a, b, out = {}, {}, []
    between = list(between)
    done = 0
    for t in range(n + ahead):
        if t < n:
            a[t] = first(*items[t])
        m = t - ahead + 1
        if 0 <= m < n:
            b[m] = second(*items[m], *(a.pop(m) if isinstance(a[m], tuple) else (a.pop(m),)))
        m = t - ahead
        if 0 <= m < n:
            out.append(third(*items[m], *b.pop(m)))
        while done < len(between) * (t + 1) // (n + ahead):
            between[done]()
            done += 1
    return out


def attend_back(R, l, do, between=()):
    vrows = [R.v_low[l, :, 128 * g:128 * (g + 1)].T for g in range(CG)]

    def probs(g, p):
        at = slice(128 * g, 128 * (g + 1))
        ds, stack = [], []
        for h in (2 * p, 2 * p + 1):
            a = slab_at(h)
            d = own_rows(do[a:a + 24, at], h) * R.rsum[l, h, :, at]
            parts = ([jnp.zeros((a, 128), F32)] if a else []) + [d] + ([jnp.zeros((104 - a, 128), F32)])
            ds.append(low(d))
            stack.append(low(jnp.concatenate(parts, axis=0)))
        return ds, nn(vrows[g], jnp.concatenate(stack, axis=1))[0:GT]

    def inner(g, p, d, dp):
        at = slice(128 * g, 128 * (g + 1))
        e = R.prob[l, g, :, 256 * p:256 * (p + 1)]
        r = jnp.concatenate([R.rsum[l, 2 * p, :, at], R.rsum[l, 2 * p + 1, :, at]], axis=1)
        total = jnp.sum(e * dp, axis=0, keepdims=True) * r
        return d, low(pad8(e * (dp - total)))

    def outer(g, p, d, ds):
        at = slice(128 * g, 128 * (g + 1))
        out = []
        for i in range(2):
            h = 2 * p + i
            dsh = ds[:, 128 * i:128 * (i + 1)]
            out.append((nn(R.k_low[l, h, :, at], dsh), nt(R.q_low[l, h, :, at], dsh),
                        nt(d[i], R.prob_low[l, g, :, 128 * h:128 * (h + 1)])))
        return out

    items = [(g, p) for g in range(CG) for p in range(H // 2)]
    slabs = pipeline(items, probs, inner, outer, BAHEAD, between)
    slabs = [t for pair in slabs for t in pair]
    out = []
    for i in range(3):
        out.append(jnp.concatenate(
            [join_slabs([t[i] for t in slabs[H * g:H * (g + 1)]]) for g in range(CG)], axis=1))
    return out[0] * SCALE, out[1], out[2]


def embed(R, obs, c):
    rows = nn(jnp.concatenate(obs, axis=1), R.w_obs[...])
    parts = []
    for g in range(CG):
        r = rows[GT * g:GT * (g + 1)] + R.posb[...]
        parts.append(pad8(r).T[0:D])
    return jnp.concatenate(parts, axis=1)


def layer_fwd(R, l, c, x):
    def vec(i):
        return tile4(R.bc[l, i])

    xh, r = normed(x)
    R.xh1[l] = xh
    R.r1[l] = r
    n1 = low(ones8(xh * vec(G1) + vec(B1)))
    R.n1[l] = n1
    mix = nn(R.qkv_t[l], n1)
    q = mix[0:D] * SCALE
    k = mix[128:128 + D]
    v = mix[256:256 + D]
    for h in range(H):
        a = slab_at(h)
        R.q_low[l, h] = low(q[a:a + 24])
        R.k_low[l, h] = low(k[a:a + 24])
    R.v_low[l] = low(pad8(v))
    att = low(ones8(attend(R, l, c, q * LOG2E, k, v)))
    R.att[l] = att
    x1 = x + nn(R.out_t[l], att)[0:D]
    xh, r = normed(x1)
    R.xh2[l] = xh
    R.r2[l] = r
    n2 = low(ones8(xh * vec(G2) + vec(B2)))
    R.n2[l] = n2
    pre = nn(R.fc_t[l], n2)
    parts = []
    for j in range(4):
        pj = pre[128 * j:128 * j + D]
        half = gelu_half(pj)
        R.pre[l, D * j:D * (j + 1)] = pj
        R.half[l, D * j:D * (j + 1)] = half
        parts.append(low(ones8(pj * half) if j == 0 else pad8(pj * half)))
    inner = jnp.concatenate(parts, axis=0)
    R.inner[l] = inner
    return x1 + nn(R.proj_t[l], inner)[0:D]


def head_step(R, c, x, live_total, valid_total):
    xh, r = normed(x)
    fin = low(pad8(xh * tile4(R.bcf[0]) + tile4(R.bcf[1])))
    hd = nn(R.head_t[...], fin) + tile4(R.bch[...])
    live = R.live[c]
    lw = live * (1.0 / live_total)
    rows = iota((CODES, L), 0).astype(F32)
    grads = []
    csum = jnp.zeros((1, L), F32)
    for b in range(BOOKS):
        lg = hd[CODES * b:CODES * (b + 1)]
        m = jnp.max(lg, axis=0, keepdims=True)
        e = jnp.exp(lg - m)
        s = jnp.sum(e, axis=0, keepdims=True)
        hot = rows == R.code[c, b:b + 1, :]
        picked = jnp.sum(jnp.where(hot, lg, 0.0), axis=0, keepdims=True)
        csum = csum + (jnp.log(s) + m - picked) * live
        grads.append((e * (1.0 / s) - jnp.where(hot, 1.0, 0.0)) * lw)
    diff = hd[32:72] - R.act[c]
    val = R.val[c]
    sq = diff * diff + 1.0
    ri = lax.rsqrt(sq)
    asum = val * (sq * ri)
    grads.append((val * (1.0 / valid_total)) * (diff * ri))
    R.loss[0, 0:1] += fold4(csum)
    af = fold4(asum)
    R.loss[1] += af[0:8] + af[8:16] + af[16:24] + af[24:32] + af[32:40]
    dh = jnp.concatenate(grads, axis=0)
    R.a_hb[0:72] += fold4(dh)
    dhl = low(jnp.concatenate([dh, jnp.zeros((56, L), F32)], axis=0))
    R.a_head[...] += nt(fin, dhl)
    df = nn(R.head[...], dhl)[0:D]
    R.a_fin[0, 0:D] += fold4(df * xh)
    R.a_fin[1, 0:D] += fold4(df)
    return normed_back(df * tile4(R.bcf[0]), xh, r)


def layer_bwd(R, l, c, dout):
    def vec(i):
        return tile4(R.bc[l, i])

    def add_bias(i, v):
        R.a_bias[l, i, 0:D] += fold4(v)

    outl = low(pad8(dout))
    add_bias(PB, dout)
    parts = []
    for j in range(4):
        rows = slice(D * j, D * (j + 1))
        dj = nn(R.proj[l, 128 * j:128 * (j + 1)], outl)
        parts.append(low(pad8(dj[0:D] * gelu_slope(R.pre[l, rows], R.half[l, rows]))))
    prel = jnp.concatenate(parts, axis=0)
    dn = nn(R.fc[l], prel)[0:D]
    xh = R.xh2[l]
    add_bias(G2, dn * xh)
    add_bias(B2, dn)
    dmid = normed_back(dn * vec(G2), xh, R.r2[l]) + dout
    midl = low(pad8(dmid))
    add_bias(OB, dmid)
    da = nn(R.out[l], midl)[0:D]
    later = []

    def a_proj(j):
        def run():
            cols = slice(256 * j, 256 * (j + 1))
            R.a_proj[l, :, cols] += nt(outl, R.inner[l, cols])
        return run

    def a_fc(j):
        def run():
            cols = slice(256 * j, 256 * (j + 1))
            R.a_fc[l, :, cols] += nt(R.n2[l], prel[cols])
        return run

    def a_out():
        R.a_out[l] += nt(R.att[l], midl)

    dq, dk, dv = attend_back(R, l, da, [a_proj(0), a_proj(1), a_fc(0), a_fc(1), a_out])
    mixl = jnp.concatenate([low(pad8(dq)), low(pad8(dk)), low(pad8(dv))], axis=0)
    dn = nn(R.qkv[l], mixl)[0:D]
    add_bias(QB, dq)
    add_bias(VB, dv)
    R.a_qkv[l] += nt(R.n1[l], mixl)
    xh = R.xh1[l]
    add_bias(G1, dn * xh)
    add_bias(B1, dn)
    return normed_back(dn * vec(G1), xh, R.r1[l]) + dmid


def embed_bwd(R, obs, c, dx):
    R.a_x[0:D] += fold4(dx)
    lanes = iota((D, 128), 1)
    tiles = []
    gs = [dx[:, 128 * g:128 * (g + 1)] for g in range(CG)]
    for t in range(CG):
        a = shifted(gs[t], -8 * t)
        b = shifted(gs[t + 1], 120 - 8 * t) if t + 1 < CG else jnp.zeros((D, 128), F32)
        tiles.append(jnp.where(lanes < GT - 8 * t, a, b))
    gl = low(pad8(jnp.concatenate(tiles, axis=1)))
    R.a_obs[...] += nn(gl, jnp.concatenate(obs, axis=1))


def zero_grads(R):
    for name in ("a_qkv", "a_out", "a_fc", "a_proj", "a_bias", "a_obs", "a_x", "a_fin", "a_head", "a_hb", "loss"):
        ref = getattr(R, name)
        ref[...] = jnp.zeros(ref.shape, F32)


HIGH = lax.Precision.HIGHEST


def pack_layer(R, rg, l):
    b = BASE + LROW * l
    for j in range(3):
        rg[pl.ds(b + 2 + j, D, stride=3), :] = R.a_qkv[l, 0:D, 128 * j:128 * (j + 1)]
    rg[pl.ds(b + 364, D), :] = R.a_out[l, 0:D]
    for j in range(4):
        rg[pl.ds(b + 487 + j, D, stride=4), :] = R.a_fc[l, 0:D, 128 * j:128 * (j + 1)]
        rg[pl.ds(b + 971 + D * j, D), :] = R.a_proj[l, :, 128 * j:128 * (j + 1)].T[0:D]
    rows = nt(jnp.ones((8, 128), F32), R.a_bias[l].reshape(12 * 128, 128), HIGH)
    for i, r in enumerate(VROWS):
        if FB0 <= i <= FB3:
            rg[pl.ds(b + r, 1), :] = R.a_fc[l, D:D + 1, 128 * (i - FB0):128 * (i - FB0 + 1)]
        else:
            rg[pl.ds(b + r, 1), :] = rows[0:1, 128 * i:128 * (i + 1)]


def pack_embed(R, rg):
    for f in range(OBS // 128):
        rg[128 * f:128 * (f + 1), :] = R.a_obs[:, 128 * f:128 * (f + 1)].T
    slot, lane = iota((32, 128), 0), iota((32, 128), 1)
    sel = jnp.where((slot == 0) | (lane % WIN == slot - 1), 1.0, 0.0)
    sel = jnp.where(lane < GT, sel, 0.0)
    rows = nt(sel, R.a_x[...], HIGH)
    rg[pl.ds(OBS, 1 + WIN), :] = rows[0:1 + WIN]


def pack_head(R, rg):
    rows = nt(jnp.ones((8, 128), F32), R.a_fin[...].reshape(256, 128), HIGH)
    for i in range(2):
        rg[pl.ds(HEAD + i, 1), :] = rows[0:1, 128 * i:128 * (i + 1)]
    lanes8 = iota((8, 128), 1)
    grad = R.a_head[...]
    R.hc[...] = jnp.where(iota((128, 128), 1) < 32, grad, 0.0)
    R.ho[...] = jnp.where(iota((128, 128), 1) < OFFS, shifted(grad, -32), 0.0)
    c0 = HEAD + 2
    o0 = c0 + 32

    def put(phases, src, rows_n, stride, width, count):
        acc = [jnp.zeros((rows_n, 128), F32) for _ in range(count + 1)]
        lanes = iota((rows_n, 128), 1)
        for p, a, s in phases:
            v = src[pl.ds(p, rows_n, stride=stride), :]
            first = shifted(v, s)
            if s + width > D:
                acc[a] = acc[a] + jnp.where((lanes >= s) & (lanes < D), first, 0.0)
                acc[a + 1] = acc[a + 1] + jnp.where(lanes < s + width - D, shifted(v, s - D), 0.0)
            else:
                acc[a] = acc[a] + first
        return acc

    acc = put(code_phases(), R.hc, 8, 15, 32, 4)
    for a in range(4):
        rg[pl.ds(c0 + a, 8, stride=4), :] = acc[a]
    hb = nt(jnp.ones((8, 128), F32), R.a_hb[...], HIGH)[0:1]
    lane1 = iota((1, 128), 1)
    rg[pl.ds(o0, 48), :] = jnp.zeros((48, 128), F32)
    acc = put(off_phases(), R.ho, 5, 24, OFFS, 7)
    for a in range(7):
        rg[pl.ds(o0 + a, 5, stride=7), :] = acc[a]
    rg[pl.ds(o0 + 7, 5, stride=7), :] = rg[pl.ds(o0 + 7, 5, stride=7), :] + acc[7]
    rg[pl.ds(o0, 1), :] = rg[pl.ds(o0, 1), :] + jnp.where(lane1 < 32, hb, 0.0)
    a, s = (D * OFFS + 32) // D, (D * OFFS + 32) % D
    ob = jnp.where(lane1 < OFFS, shifted(hb, -32), 0.0)
    rg[pl.ds(o0 + a, 1), :] = rg[pl.ds(o0 + a, 1), :] + shifted(ob, s)


MESH = pl.DeviceIdType.MESH


def round_up(n, m):
    return -(-n // m) * m


class Plan:
    def __init__(self, feats, toks, shard, tok_rows):
        self.feats, self.toks, self.chips = feats, toks, toks // 2
        self.shard = shard
        self.block = round_up(-(-(shard + 112) // D), 16)
        self.flat_rows = self.block // 16 * 15
        self.local = round_up(-(-shard // 128), 8)
        self.work = round_up(max(self.flat_rows, self.local + 1), 8)
        self.own_rows = tok_rows // feats
        self.chunks = self.own_rows // CT
        self.grid = round_up(-(-(shard * feats * toks) // D) + self.block, 8)


def comm_scratch(P):
    dma = pltpu.SemaphoreType.DMA
    B, C, Fn = P.block, P.chips, P.feats
    return dict(
        rg=pltpu.VMEM((P.grid, 128), F32),
        ob=pltpu.VMEM((P.chunks, Fn, L, 128), BF),
        pg=pltpu.VMEM((2, C, Fn, B, 128), BF),
        loc=pltpu.VMEM((P.work, 128), F32),
        rblk=pltpu.VMEM((B, 128), F32),
        codes_in=pltpu.VMEM((BOOKS, P.own_rows), jnp.int32),
        act_in=pltpu.VMEM((OFFS, P.own_rows), F32),
        val_in=pltpu.VMEM((OFFS, P.own_rows), jnp.int32),
        tz=pltpu.VMEM((2, Fn, 8, 128), F32),
        tc=pltpu.VMEM((2, C, 8, 128), F32),
        ts=pltpu.VMEM((2, 2, 8, 128), F32),
        sb1=pltpu.VMEM((C, Fn, B, 128), F32),
        rb1=pltpu.VMEM((C, Fn, B, 128), F32),
        sb2=pltpu.VMEM((C, Fn, B, 128), F32),
        rb2=pltpu.VMEM((C, Fn, B, 128), F32),
        sb3=pltpu.VMEM((Fn, B, 128), F32),
        rb3=pltpu.VMEM((Fn, B, 128), F32),
        s_p1=dma((2, Fn)), s_p2=dma((2, C)), s_p3=dma((2, C)),
        s_tz=dma((2, 2, Fn)), s_tc=dma((2, 2, C)), s_ts=dma((2, 2)),
        s_ob=dma((2, P.chunks, Fn)),
        s_in=dma((3,)),
        s_r1=dma((2, C)), s_r2=dma((2, C)), s_r3=dma((2, Fn)),
    )


def to_rows(loc, rblk, delta, P):
    v = loc[...]
    lanes = iota(v.shape, 1)
    moved = pltpu.roll(v, delta, 1)
    loc[...] = jnp.where(lanes >= delta, moved, pltpu.roll(moved, 1, 0))
    n = P.block // 16
    lane = iota((n, 128), 1)
    for j in range(16):
        if j < 15:
            a = shifted(loc[pl.ds(j, n, stride=15), :], 8 * j)
        if j > 0:
            b = shifted(loc[pl.ds(j - 1, n, stride=15), :], 8 * j)
            a = jnp.where(lane < 8 * j, b, a) if j < 15 else b
        rblk[pl.ds(j, n, stride=16), :] = jnp.where(lane < D, a, 0.0)


def from_rows(rblk, loc, delta, P):
    n = P.block // 16
    lane = iota((n, 128), 1)
    loc[...] = jnp.zeros(loc.shape, F32)
    for i in range(15):
        a = shifted(rblk[pl.ds(i, n, stride=16), :], -8 * i)
        b = shifted(rblk[pl.ds(i + 1, n, stride=16), :], D - 8 * i)
        loc[pl.ds(i, n, stride=15), :] = jnp.where(lane < D - 8 * i, a, b)
    v = loc[...]
    lanes = iota(v.shape, 1)
    moved = pltpu.roll(v, lax.rem(128 - delta, 128), 1)
    v = jnp.where(lanes < 128 - delta, moved, pltpu.roll(moved, P.work - 1, 0))
    return v[0:P.local]


def step_kernel(P, names, master, first, second, obs, counts, codes, actions, valid,
                new_master, new_first, new_second, sums, *scratch):
    R = Refs()
    for name, ref in zip(names, scratch):
        setattr(R, name, ref)
    Fn, C, B = P.feats, P.chips, P.block
    feat = lax.axis_index("feat")
    tok = lax.axis_index("tok")
    chip = tok // 2
    core = tok % 2
    me = feat * P.toks + tok
    delta = lax.rem(me * P.shard, D)

    def z_peer(i):
        return lax.rem(feat + i, Fn)

    def z_from(i):
        return lax.rem(feat + Fn - i, Fn)

    def c_peer(i):
        return lax.rem(chip + i, C)

    def c_from(i):
        return lax.rem(chip + C - i, C)

    def to_z(i):
        return (z_peer(i), tok)

    def to_c(i):
        return (feat, 2 * c_peer(i) + core)

    sibling = (feat, 2 * chip + 1 - core)

    def send(src, dst, sems, at, dev):
        return pltpu.make_async_remote_copy(
            src_ref=src, dst_ref=dst, send_sem=sems.at[(0,) + at], recv_sem=sems.at[(1,) + at],
            device_id=dev, device_id_type=MESH)

    n = P.own_rows
    ins = []
    for i, (src, dst) in enumerate(((codes, R.codes_in), (actions, R.act_in), (valid, R.val_in))):
        ins.append(pltpu.make_async_copy(src.at[:, pl.ds(pl.multiple_of(feat * n, 128), n)], dst, R.s_in.at[i]))
        ins[-1].start()

    barrier = pltpu.get_barrier_semaphore()
    peers = [to_z(i) for i in range(1, Fn)] + [to_c(i) for i in range(1, C)] + [sibling]
    for dev in peers:
        pl.semaphore_signal(barrier, inc=1, device_id=dev, device_id_type=MESH)

    R.loc[...] = jnp.zeros(R.loc.shape, F32)
    R.loc[0:P.local, :] = master[...]
    to_rows(R.loc, R.rblk, delta, P)
    R.pg[core, chip, feat] = low(R.rblk[...])
    pl.semaphore_wait(barrier, len(peers))

    p1 = []
    for i in range(1, Fn):
        blk = R.pg.at[core, chip, feat]
        p1.append(send(blk, blk, R.s_p1, (i,), to_z(i)))
        p1[-1].start()

    def obs_copies(c):
        cps = []
        for i in range(1, Fn):
            src = obs.at[pl.ds(pl.multiple_of(z_peer(i) * n + CT * c, 16), CT), :]
            cps.append(send(src, R.ob.at[c, feat, pl.ds(0, CT), :], R.s_ob, (c, i), to_z(i)))
        src = obs.at[pl.ds(pl.multiple_of(feat * n + CT * c, 16), CT), :]
        cps.append(pltpu.make_async_copy(src, R.ob.at[c, feat, pl.ds(0, CT), :], R.s_ob.at[0, c, 0]))
        return cps

    def start_obs(c):
        for cp in obs_copies(c):
            cp.start()

    start_obs(0)
    for cp in ins:
        cp.wait()
    zero_grads(R)
    for c in range(P.chunks):
        for f in range(Fn):
            R.ob[c, f, CT:L, :] = jnp.zeros((L - CT, 128), BF)
    live_n, valid_n = prep_tokens(R, counts, R.codes_in, R.act_in, R.val_in, feat, P.chunks)

    def two_rows(a, b):
        return jnp.concatenate([jnp.broadcast_to(a, (1, 128)), jnp.broadcast_to(b, (1, 128)),
                                jnp.zeros((6, 128), F32)], axis=0)

    def hop_z(w, value):
        R.tz[w, feat] = value
        cps = []
        for i in range(1, Fn):
            cps.append(send(R.tz.at[w, feat], R.tz.at[w, feat], R.s_tz.at[w], (i,), to_z(i)))
            cps[-1].start()
        return cps

    def hop_c(w, value):
        R.tc[w, chip] = value
        cps = []
        for i in range(1, C):
            cps.append(send(R.tc.at[w, chip], R.tc.at[w, chip], R.s_tc.at[w], (i,), to_c(i)))
            cps[-1].start()
        return cps

    def hop_s(w, value):
        R.ts[w, core] = value
        cp = send(R.ts.at[w, core], R.ts.at[w, core], R.s_ts.at[w], (), sibling)
        cp.start()
        return [cp]

    def total(ref, w, count):
        v = ref[w, 0]
        for i in range(1, count):
            v = v + ref[w, i]
        return v

    def wait_all(cps):
        for cp in cps:
            cp.wait()

    tz = hop_z(0, two_rows(live_n, valid_n))
    wait_all(p1)
    p2 = []
    for i in range(1, C):
        blk = R.pg.at[core, chip]
        p2.append(send(blk, blk, R.s_p2, (i,), to_c(i)))
        p2[-1].start()
    p3 = [send(R.pg.at[core, chip], R.pg.at[core, chip], R.s_p3, (0,), sibling)]
    p3[0].start()
    wait_all(tz)
    tc = hop_c(0, total(R.tz, 0, Fn))
    for i in range(1, C):
        p2[i - 1].wait_recv()
        blk = R.pg.at[core, c_from(i)]
        p3.append(send(blk, blk, R.s_p3, (i,), sibling))
        p3[-1].start()
    wait_all(tc)
    ts = hop_s(0, total(R.tc, 0, C))
    for cp in p2:
        cp.wait_send()
    wait_all(p3)
    wait_all(ts)
    counted = total(R.ts, 0, 2)
    live_total = counted[0:1, 0:1]
    valid_total = counted[1:2, 0:1]

    R.rg[0:8, :] = jnp.zeros((8, 128), F32)

    def place(d, _):
        r0 = (P.shard * d) // D
        f, t = d // P.toks, d % P.toks
        blk = R.pg[t % 2, t // 2, f].astype(F32)
        before = R.rg[pl.ds(r0, 1), :]
        R.rg[pl.ds(r0, B), :] = blk
        R.rg[pl.ds(r0, 1), :] = blk[0:1] + before
        return 0

    lax.fori_loop(0, Fn * P.toks, place, 0)
    prep_weights(R.rg, R)

    def chunk(c, _):
        cps = obs_copies(c)
        for cp in cps[:-1]:
            cp.wait_recv()
        cps[-1].wait()

        @pl.when(c + 1 < P.chunks)
        def _():
            start_obs(c + 1)

        R.x[...] = embed(R, [R.ob[c, f, 0:CT, :] for f in range(Fn)], c)

        def lay(l, _):
            R.x[...] = layer_fwd(R, l, c, R.x[...])
            return 0

        lax.fori_loop(0, LAYERS, lay, 0)
        R.x[...] = head_step(R, c, R.x[...], live_total, valid_total)

        def back(i, _):
            R.x[...] = layer_bwd(R, LAYERS - 1 - i, c, R.x[...])
            return 0

        lax.fori_loop(0, LAYERS, back, 0)
        embed_bwd(R, [R.ob[c, f] for f in range(Fn)], c, R.x[...])
        return 0

    lax.fori_loop(0, P.chunks, chunk, 0)
    lz = hop_z(1, two_rows(jnp.sum(R.loss[0], keepdims=True), jnp.sum(R.loss[1], keepdims=True)))
    wait_all(lz)
    lc = hop_c(1, total(R.tz, 1, Fn))
    R.rg[pl.ds(HEAD + 32, P.grid - HEAD - 32), :] = jnp.zeros((P.grid - HEAD - 32, 128), F32)
    for l in range(LAYERS):
        pack_layer(R, R.rg, l)
    pack_embed(R, R.rg)
    pack_head(R, R.rg)

    def rows_of(f, ch, co):
        return (P.shard * (f * P.toks + 2 * ch + co)) // D

    r1 = []
    for i in range(1, C + 1):
        ch = c_peer(i)
        for f in range(Fn):
            R.sb1[i - 1, f] = R.rg[pl.ds(rows_of(f, ch, 1 - core), B), :]
        r1.append(send(R.sb1.at[i - 1], R.rb1.at[i - 1], R.s_r1, (i - 1,), sibling))
        r1[-1].start()
    wait_all(lc)
    ls = hop_s(1, total(R.tc, 1, C))
    r2 = []
    for i in range(1, C):
        ch = c_peer(i)
        r1[i - 1].wait_recv()
        for f in range(Fn):
            R.sb2[i, f] = R.rg[pl.ds(rows_of(f, ch, core), B), :] + R.rb1[i - 1, f]
        r2.append(send(R.sb2.at[i], R.rb2.at[i], R.s_r2, (i,), to_c(i)))
        r2[-1].start()
    r1[C - 1].wait_recv()
    for f in range(Fn):
        R.sb2[0, f] = R.rg[pl.ds(rows_of(f, chip, core), B), :] + R.rb1[C - 1, f]
    for cp in r2:
        cp.wait_recv()
    r3 = []
    for i in range(1, Fn):
        f = z_peer(i)
        v = R.sb2[0, f]
        for j in range(1, C):
            v = v + R.rb2[j, f]
        R.sb3[i] = v
        r3.append(send(R.sb3.at[i], R.rb3.at[i], R.s_r3, (i,), to_z(i)))
        r3[-1].start()
    v = R.sb2[0, feat]
    for j in range(1, C):
        v = v + R.rb2[j, feat]
    for i in range(1, Fn):
        r3[i - 1].wait_recv()
        v = v + R.rb3[i]
    R.rblk[...] = v
    grad = from_rows(R.rblk, R.loc, delta, P)
    f_new = BETA_ONE * first[...] + (1.0 - BETA_ONE) * grad
    s_new = BETA_TWO * second[...] + (1.0 - BETA_TWO) * grad * grad
    f_hat = f_new / (1.0 - BETA_ONE ** STEP_NO)
    s_hat = s_new / (1.0 - BETA_TWO ** STEP_NO)
    old = master[...]
    new_first[...] = f_new
    new_second[...] = s_new
    new_master[...] = old - LEARN_RATE * (f_hat / (jnp.sqrt(s_hat) + ADAM_EPS) + DECAY_RATE * old)
    wait_all(ls)
    lost = total(R.ts, 1, 2)
    sums[...] = jnp.concatenate([lost[0:1], counted[0:1], lost[1:2], counted[1:2], jnp.zeros((4, 128), F32)], axis=0)
    for c in range(P.chunks):
        for cp in obs_copies(c)[:-1]:
            cp.wait_send()
    for cps in (r1, r2, r3):
        for cp in cps:
            cp.wait_send()


def solution(mesh):
    feats, toks = mesh.shape["feat"], mesh.shape["tok"]

    def shards(master, first, second, obs, counts, codes, actions, valid):
        P_ = Plan(feats, toks, master.shape[0], obs.shape[0])
        scratch = dict(scratch_list(P_.chunks))
        scratch.update(comm_scratch(P_))
        pad = P_.local * 128 - P_.shard
        flat = [jnp.pad(v, (0, pad)).reshape(P_.local, 128) for v in (master, first, second)]
        vmem = pl.BlockSpec(memory_space=pltpu.VMEM)
        hbm = pl.BlockSpec(memory_space=pl.ANY)
        out = jax.ShapeDtypeStruct((P_.local, 128), F32)
        outs = pl.pallas_call(
            functools.partial(step_kernel, P_, list(scratch)),
            out_shape=(out, out, out, jax.ShapeDtypeStruct((8, 128), F32)),
            in_specs=[vmem, vmem, vmem, hbm, vmem, hbm, hbm, hbm],
            out_specs=(vmem,) * 4,
            scratch_shapes=list(scratch.values()),
            compiler_params=pltpu.CompilerParams(
                collective_id=0, has_side_effects=True, vmem_limit_bytes=60 * 2 ** 20),
        )(*flat, obs, counts.T, codes.T, actions, valid)
        cut = [v.reshape(-1)[:P_.shard] for v in outs[:3]]
        return (*cut, outs[3][0:4, 0])

    weights = PSpec(("feat", "tok"))
    return jax.shard_map(
        shards, mesh=mesh,
        in_specs=(weights, weights, weights, PSpec("tok", "feat"), PSpec("tok", None), PSpec("tok", None),
                  PSpec(None, "tok"), PSpec(None, "tok")),
        out_specs=(weights, weights, weights, PSpec()), check_vma=False)
```

```python
import functools
import math

import jax
import jax.numpy as jnp
from jax import lax
from jax.experimental import pallas as pl
from jax.experimental.pallas import tpu as pltpu
from jax.sharding import PartitionSpec as PSpec

D = 120
H = 6
HD = 20
FF = 480
OBS = 512
LAYERS = 2
CAMS = 3
BOOKS = 2
CODES = 16
SPAN = 5
ACT = 7
WIN = 30
OFFS = SPAN * ACT
NORM_EPS = 1e-05
STEP_NO = 10
BETA_ONE = 0.9
BETA_TWO = 0.999
ADAM_EPS = 1e-08
DECAY_RATE = 0.1
LEARN_RATE = 0.05
GW = 4
GT = GW * WIN
CG = 4
L = CG * 128
CT = CG * GT
F32 = jnp.float32
BF = jnp.bfloat16
SCALE = HD ** (-0.5)
LROW = 2 * 1 + 3 * D + 2 + D + 1 + 2 + 4 * D + 4 + 4 * D + 1
BASE = OBS + 1 + WIN
HEAD = BASE + LAYERS * LROW
NV = 13
VROWS = [0, 1, 362, 363, 484, 485, 486, 967, 968, 969, 970, 1451]
(G1, B1, QB, VB, OB, G2, B2, FB0, FB1, FB2, FB3, PB) = range(12)


def nn(a, b):
    return lax.dot_general(a, b, (((1,), (0,)), ((), ())), preferred_element_type=F32)


def nt(a, b, precision=None):
    return lax.dot_general(a, b, (((1,), (1,)), ((), ())), preferred_element_type=F32, precision=precision)


def low(v):
    return v.astype(BF)


def pad8(v):
    return jnp.concatenate([v, jnp.zeros((8, v.shape[1]), v.dtype)], axis=0)


def tile4(v):
    return jnp.concatenate([v] * CG, axis=1)


def fold4(v):
    out = v[:, 0:128]
    for g in range(1, CG):
        out = out + v[:, 128 * g:128 * (g + 1)]
    return out


def iota(shape, axis):
    return lax.broadcasted_iota(jnp.int32, shape, axis)


def slab_at(h):
    return 20 * h - (4 if h % 2 else 0)


def head_stack(v):
    rows = iota((8, 128), 0)
    cols = []
    for h in range(H):
        a = slab_at(h)
        if h % 2 == 0:
            parts = [v[a:a + 16], jnp.where(rows < 4, v[a + 16:a + 24], 0.0)]
        else:
            parts = [jnp.where(rows >= 4, v[a:a + 8], 0.0), v[a + 8:a + 24]]
        if a > 0:
            parts = [jnp.zeros((a, 128), F32)] + parts
        if a + 24 < 128:
            parts = parts + [jnp.zeros((128 - a - 24, 128), F32)]
        cols.append(jnp.concatenate(parts, axis=0))
    return jnp.concatenate(cols, axis=1)


def join_slabs(slabs):
    rows = iota((8, 128), 0)
    parts = []
    for p in range(3):
        a, b = slabs[2 * p], slabs[2 * p + 1]
        parts += [a[0:16], jnp.where(rows < 4, a[16:24], b[0:8]), b[8:24]]
    return jnp.concatenate(parts, axis=0)


def slabs_of(v):
    return [v[slab_at(h):slab_at(h) + 24] for h in range(H)]


def hi_lo(v):
    hi = low(v)
    return hi, low(v - hi.astype(F32))


def normed(x):
    mean = jnp.sum(x, axis=0, keepdims=True) * (1.0 / D)
    c = x - mean
    var = jnp.sum(c * c, axis=0, keepdims=True) * (1.0 / D)
    r = lax.rsqrt(var + NORM_EPS)
    return c * r, r


def normed_back(d, xh, r):
    m0 = jnp.sum(d, axis=0, keepdims=True) * (1.0 / D)
    m1 = jnp.sum(d * xh, axis=0, keepdims=True) * (1.0 / D)
    return r * (d - m0 - xh * m1)


GA = math.sqrt(2.0 / math.pi)
GB = 0.044715


def gelu_half(x):
    return 0.5 + 0.5 * jnp.tanh(x * (GA + (GA * GB) * (x * x)))


def gelu_slope(x, s):
    return s + (x * s) * (1.0 - s) * (2.0 * GA + (6.0 * GA * GB) * (x * x))


LOG2E = math.log2(math.e)
BIG = 1e30


class Refs:
    pass


def scratch_list(chunks):
    groups = chunks * CG
    return dict(
        w_obs=pltpu.VMEM((OBS, 128), BF),
        posb=pltpu.VMEM((GT, 128), F32),
        qkv_t=pltpu.VMEM((LAYERS, 384, 128), BF),
        qkv=pltpu.VMEM((LAYERS, 128, 384), BF),
        out_t=pltpu.VMEM((LAYERS, 128, 128), BF),
        out=pltpu.VMEM((LAYERS, 128, 128), BF),
        fc_t=pltpu.VMEM((LAYERS, 512, 128), BF),
        fc=pltpu.VMEM((LAYERS, 128, 512), BF),
        proj_t=pltpu.VMEM((LAYERS, 128, 512), BF),
        proj=pltpu.VMEM((LAYERS, 512, 128), BF),
        head_t=pltpu.VMEM((72, 128), BF),
        head=pltpu.VMEM((128, 128), BF),
        vec=pltpu.VMEM((32, 128), F32),
        bc=pltpu.VMEM((LAYERS, 12, GT, 128), F32),
        bcf=pltpu.VMEM((2, GT, 128), F32),
        bch=pltpu.VMEM((72, 128), F32),
        hc=pltpu.VMEM((128, 128), F32),
        ho=pltpu.VMEM((128, 128), F32),
        cnt=pltpu.VMEM((16, 256), F32),
        live=pltpu.VMEM((chunks, 1, L), F32),
        act=pltpu.VMEM((chunks, 40, L), F32),
        val=pltpu.VMEM((chunks, 40, L), F32),
        code=pltpu.VMEM((chunks, 2, L), F32),
        x=pltpu.VMEM((D, L), F32),
        dmid=pltpu.VMEM((D, L), F32),
        da=pltpu.VMEM((D, L), F32),
        xh1=pltpu.VMEM((LAYERS, D, L), F32),
        r1=pltpu.VMEM((LAYERS, 1, L), F32),
        xh2=pltpu.VMEM((LAYERS, D, L), F32),
        r2=pltpu.VMEM((LAYERS, 1, L), F32),
        n1=pltpu.VMEM((LAYERS, 128, L), BF),
        n2=pltpu.VMEM((LAYERS, 128, L), BF),
        att=pltpu.VMEM((LAYERS, 128, L), BF),
        q_low=pltpu.VMEM((LAYERS, H, 24, L), BF),
        k_low=pltpu.VMEM((LAYERS, H, 24, L), BF),
        v_low=pltpu.VMEM((LAYERS, 128, L), BF),
        rsum=pltpu.VMEM((LAYERS, H, 1, L), F32),
        prob=pltpu.VMEM((LAYERS, CG, GT, H * 128), F32),
        prob_low=pltpu.VMEM((LAYERS, CG, 128, H * 128), BF),
        k_mask=pltpu.VMEM((48, 128), BF),
        q_mask=pltpu.VMEM((48, 128), BF),
        dead=pltpu.VMEM((groups, 8, 128), F32),
        pre=pltpu.VMEM((LAYERS, FF, L), F32),
        half=pltpu.VMEM((LAYERS, FF, L), F32),
        inner=pltpu.VMEM((LAYERS, 512, L), BF),
        a_qkv=pltpu.VMEM((LAYERS, 128, 384), F32),
        a_out=pltpu.VMEM((LAYERS, 128, 128), F32),
        a_fc=pltpu.VMEM((LAYERS, 128, 512), F32),
        a_proj=pltpu.VMEM((LAYERS, 128, 512), F32),
        a_bias=pltpu.VMEM((LAYERS, 12, 128, 128), F32),
        a_obs=pltpu.VMEM((128, 512), F32),
        a_x=pltpu.VMEM((128, 128), F32),
        a_fin=pltpu.VMEM((2, 128, 128), F32),
        a_head=pltpu.VMEM((128, 128), F32),
        a_hb=pltpu.VMEM((128, 128), F32),
        loss=pltpu.VMEM((2, 8, 128), F32),
    )


def code_phases():
    for p in range(15):
        yield p, (32 * p) // D, (32 * p) % D


def off_phases():
    for p in range(24):
        yield p, (35 * p + 32) // D, (35 * p + 32) % D


def shifted(v, by):
    by %= 128
    return v if by == 0 else pltpu.roll(v, by, 1)


def take_phase(load, a, s, width, rows):
    lanes = iota((rows, 128), 1)
    first = shifted(load(a), -s)
    if s + width > D:
        second = shifted(load(a + 1), D - s)
        first = jnp.where(lanes < D - s, first, second)
    return jnp.where(lanes < width, first, 0.0)


def with_bias(w, bias):
    if bias is not None:
        w = jnp.where(iota((128, 128), 0) == D, bias, w)
    return low(w.T)


def ones8(v):
    return jnp.concatenate([v, jnp.where(iota((8, v.shape[1]), 0) == 0, 1.0, 0.0)], axis=0)


def prep_weights(rg, R):
    R.w_obs[...] = low(rg[0:OBS, :])
    for w in range(GW):
        R.posb[pl.ds(WIN * w, WIN), :] = rg[OBS + 1:OBS + 1 + WIN, :] + rg[OBS:OBS + 1, :]
    R.vec[...] = jnp.zeros((32, 128), F32)
    for l in range(LAYERS):
        b = BASE + LROW * l
        for j in range(3):
            w = pad8(rg[pl.ds(b + 2 + j, D, stride=3), :])
            R.qkv[l, :, 128 * j:128 * (j + 1)] = low(w)
            R.qkv_t[l, 128 * j:128 * (j + 1), :] = with_bias(w, None if j == 1 else rg[pl.ds(b + 362 + j // 2, 1), :])
        w = pad8(rg[pl.ds(b + 364, D), :])
        R.out[l] = low(w)
        R.out_t[l] = with_bias(w, rg[pl.ds(b + 484, 1), :])
        for j in range(4):
            w = pad8(rg[pl.ds(b + 487 + j, D, stride=4), :])
            R.fc[l, :, 128 * j:128 * (j + 1)] = low(w)
            R.fc_t[l, 128 * j:128 * (j + 1), :] = with_bias(w, rg[pl.ds(b + 967 + j, 1), :])
            w = pad8(rg[pl.ds(b + 971 + D * j, D), :])
            R.proj[l, 128 * j:128 * (j + 1), :] = low(w)
            R.proj_t[l, :, 128 * j:128 * (j + 1)] = with_bias(w, None if j else rg[pl.ds(b + 1451, 1), :])
        for i, r in enumerate(VROWS):
            R.vec[pl.ds(12 * l + i, 1), :] = rg[pl.ds(b + r, 1), :]
    R.vec[24:26, :] = rg[pl.ds(HEAD, 2), :]
    R.hc[...] = jnp.zeros((128, 128), F32)
    R.ho[...] = jnp.zeros((128, 128), F32)
    c0 = HEAD + 2
    for p, a, s in code_phases():
        R.hc[pl.ds(p, 8, stride=15), :] = take_phase(
            lambda i: rg[pl.ds(c0 + i, 8, stride=4), :], a, s, 32, 8)
    o0 = c0 + 32
    for p, a, s in off_phases():
        R.ho[pl.ds(p, 5, stride=24), :] = take_phase(
            lambda i: rg[pl.ds(o0 + i, 5, stride=7), :], a, s, OFFS, 5)
    hw = R.hc[...] + shifted(R.ho[...], 32)
    R.head[...] = low(hw)
    R.head_t[...] = low(hw.T[0:72])
    lanes = iota((1, 128), 1)
    hb = jnp.where(lanes < 32, rg[pl.ds(o0, 1), :], 0.0)
    a, s = (D * OFFS + 32) // D, (D * OFFS + 32) % D
    ob = take_phase(lambda i: rg[pl.ds(o0 + i, 1), :], a, s, OFFS, 1)
    R.vec[26:27, :] = hb + shifted(ob, 32)
    columns = jnp.concatenate([R.vec[...], jnp.zeros((96, 128), F32)], axis=0).T
    for l in range(LAYERS):
        for i in range(12):
            R.bc[l, i] = jnp.broadcast_to(columns[0:D, 12 * l + i:12 * l + i + 1], (D, 128))
    for i in range(2):
        R.bcf[i] = jnp.broadcast_to(columns[0:D, 24 + i:25 + i], (D, 128))
    R.bch[...] = jnp.broadcast_to(columns[0:72, 26:27], (72, 128))


def spread_groups(v, groups, width):
    rows = v.shape[0]
    lanes = iota((rows, 128), 1)
    out = []
    for g in range(groups):
        t, o = (GT * g) // 128, (GT * g) % 128
        a = shifted(v[:, 128 * t:128 * (t + 1)], -o)
        if o + GT > 128:
            b = shifted(v[:, 128 * (t + 1):128 * (t + 2)], -o)
            a = jnp.where(lanes < 128 - o, a, b)
        out.append(jnp.where(lanes < GT, a, 0))
    return out


def prep_tokens(R, counts, codes, actions, valid, feat, chunks):
    groups = chunks * CG
    wins = counts.shape[1]
    R.cnt[...] = jnp.zeros(R.cnt.shape, F32)
    R.cnt[0:WIN // CAMS, :] = counts[...].astype(F32)
    k = iota((GT, 16), 0)
    step = (k % WIN) // CAMS
    sel = jnp.where(step == iota((GT, 16), 1), 1.0, 0.0)
    x = nn(low(sel), low(R.cnt[...]))
    y = jnp.where(iota((GT, wins), 1) % GW == iota((GT, wins), 0) // WIN, x, 0.0)
    pick = jnp.where(iota((wins, 128), 0) // GW == iota((wins, 128), 1) + groups * feat, 1.0, 0.0)
    z = nn(low(y), low(pick))
    kk = iota((GT, 128), 0)
    alive = jnp.where((kk % CAMS).astype(F32) < z, 1.0, 0.0)
    steps = WIN // CAMS
    j, at = iota((48, 128), 0), iota((48, 128), 1)
    own = (at // WIN == j // steps) & ((at % WIN) // CAMS == j % steps) & (at < GT)
    R.k_mask[...] = low(jnp.where(own, 1.0, 0.0))
    may = (at // WIN == j // steps) & ((at % WIN) // CAMS >= j % steps)
    R.q_mask[...] = low(jnp.where(may | (j >= GW * steps), 0.0, -BIG))
    rows = pad8(alive).T
    for g in range(groups):
        R.live[g // CG, :, 128 * (g % CG):128 * (g % CG + 1)] = rows[g:g + 1, :]
        R.dead[g] = jnp.where(iota((8, 128), 0) == 0, 1.0 - rows[g:g + 1, :], 0.0)
    for name, src in (("code", codes), ("act", actions), ("val", valid)):
        parts = spread_groups(src[...].astype(F32), groups, GT)
        dst = getattr(R, name)
        for g in range(groups):
            c, lo = g // CG, 128 * (g % CG)
            part = parts[g]
            if name == "val":
                part = part * rows[g:g + 1, :]
            if name != "code":
                dst[c, 32:40, lo:lo + 128] = jnp.zeros((8, 128), F32)
            dst[c, 0:part.shape[0], lo:lo + 128] = part
    lanes = iota((GT, 128), 1)
    live_total = jnp.sum(jnp.where(lanes < groups, alive, 0.0), keepdims=True)
    v = jnp.zeros((40, L), F32)
    for c in range(chunks):
        v = v + R.val[c]
    valid_total = jnp.sum(v, keepdims=True)
    return live_total, valid_total


def own_rows(slab, h):
    rows = iota((8, 128), 0)
    if h % 2 == 0:
        return jnp.concatenate([slab[0:16], jnp.where(rows < 4, slab[16:24], 0.0)], axis=0)
    return jnp.concatenate([jnp.where(rows >= 4, slab[0:8], 0.0), slab[8:24]], axis=0)


def split(v):
    hi = low(v).astype(F32)
    return hi, v - hi


def attend(R, s, c, q, k, v):
    qh, ql = split(q)
    kh, kl = split(k)
    vh, vl = split(v)
    minus = jnp.where(iota((8, 128), 0) == 0, -BIG, 0.0)

    none = jnp.zeros((128, 128), BF)

    def scores(g, p):
        at = slice(128 * g, 128 * (g + 1))
        qs, ks = [], []
        for h in (2 * p, 2 * p + 1):
            sl = slice(slab_at(h), slab_at(h) + 24)
            hi = own_rows(qh[sl, at], h)
            qd = low(jnp.concatenate([hi, hi, own_rows(ql[sl, at], h), minus], axis=0))
            kd = low(jnp.concatenate([kh[sl, at], kl[sl, at], kh[sl, at], R.dead[c * CG + g]], axis=0))
            qs.append(jnp.concatenate([qd, R.q_mask[...]], axis=0))
            ks.append(jnp.concatenate([kd, R.k_mask[...]], axis=0).T)
        if PAIR:
            both = jnp.concatenate([jnp.concatenate([qs[0], none], axis=1),
                                    jnp.concatenate([none, qs[1]], axis=1)], axis=0)
            return nn(jnp.concatenate(ks, axis=1), both)[0:GT]
        return jnp.concatenate([nn(ks[0], qs[0])[0:GT], nn(ks[1], qs[1])[0:GT]], axis=1)

    def soft(g, p, sc):
        at = slice(128 * g, 128 * (g + 1))
        e = jnp.exp2(sc - jnp.max(sc, axis=0, keepdims=True))
        r = 1.0 / jnp.sum(e, axis=0, keepdims=True)
        e8 = pad8(e)
        eh = low(e8)
        el = low(e8 - eh.astype(F32))
        cols = slice(256 * p, 256 * (p + 1))
        R.prob[s, g, :, cols] = e
        R.prob_low[s, g, :, cols] = eh
        R.rsum[s, 2 * p, :, at] = r[:, 0:128]
        R.rsum[s, 2 * p + 1, :, at] = r[:, 128:256]
        return r, eh, el

    def values(g, p, r, eh, el):
        at = slice(128 * g, 128 * (g + 1))
        out = []
        for i in range(2):
            sl = slice(slab_at(2 * p + i), slab_at(2 * p + i) + 24)
            cols = slice(128 * i, 128 * (i + 1))
            vs = low(jnp.concatenate([vh[sl, at], vl[sl, at]], axis=0))
            o = nn(jnp.concatenate([vs, vs], axis=1), jnp.concatenate([eh[:, cols], el[:, cols]], axis=0))
            out.append((o[0:24] + o[24:48]) * r[:, cols])
        return out

    items = [(g, p) for g in range(CG) for p in range(H // 2)]
    slabs = pipeline(items, scores, soft, values, FAHEAD)
    slabs = [t for pair in slabs for t in pair]
    return jnp.concatenate([join_slabs(slabs[H * g:H * (g + 1)]) for g in range(CG)], axis=1)


PAIR = True
FAHEAD = 2
BAHEAD = 2


def pipeline(items, first, second, third, ahead, between=()):
    n = len(items)
    a, b, out = {}, {}, []
    between = list(between)
    done = 0
    for t in range(n + ahead):
        if t < n:
            a[t] = first(*items[t])
        m = t - ahead + 1
        if 0 <= m < n:
            b[m] = second(*items[m], *(a.pop(m) if isinstance(a[m], tuple) else (a.pop(m),)))
        m = t - ahead
        if 0 <= m < n:
            out.append(third(*items[m], *b.pop(m)))
        while done < len(between) * (t + 1) // (n + ahead):
            between[done]()
            done += 1
    return out


def attend_back(R, s, do, between=()):
    vrows = [R.v_low[s, :, 128 * g:128 * (g + 1)].T for g in range(CG)]

    def probs(g, p):
        at = slice(128 * g, 128 * (g + 1))
        ds, stack = [], []
        for h in (2 * p, 2 * p + 1):
            a = slab_at(h)
            d = own_rows(do[a:a + 24, at], h) * R.rsum[s, h, :, at]
            parts = ([jnp.zeros((a, 128), F32)] if a else []) + [d] + ([jnp.zeros((104 - a, 128), F32)])
            ds.append(low(d))
            stack.append(low(jnp.concatenate(parts, axis=0)))
        return ds, nn(vrows[g], jnp.concatenate(stack, axis=1))[0:GT]

    def inner(g, p, d, dp):
        at = slice(128 * g, 128 * (g + 1))
        e = R.prob[s, g, :, 256 * p:256 * (p + 1)]
        r = jnp.concatenate([R.rsum[s, 2 * p, :, at], R.rsum[s, 2 * p + 1, :, at]], axis=1)
        total = jnp.sum(e * dp, axis=0, keepdims=True) * r
        return d, low(pad8(e * (dp - total)))

    def outer(g, p, d, ds):
        at = slice(128 * g, 128 * (g + 1))
        out = []
        for i in range(2):
            h = 2 * p + i
            dsh = ds[:, 128 * i:128 * (i + 1)]
            out.append((nn(R.k_low[s, h, :, at], dsh), nt(R.q_low[s, h, :, at], dsh),
                        nt(d[i], R.prob_low[s, g, :, 128 * h:128 * (h + 1)])))
        return out

    items = [(g, p) for g in range(CG) for p in range(H // 2)]
    slabs = pipeline(items, probs, inner, outer, BAHEAD, between)
    slabs = [t for pair in slabs for t in pair]
    out = []
    for i in range(3):
        out.append(jnp.concatenate(
            [join_slabs([t[i] for t in slabs[H * g:H * (g + 1)]]) for g in range(CG)], axis=1))
    return out[0] * SCALE, out[1], out[2]


def embed(R, obs, c):
    rows = nn(jnp.concatenate(obs, axis=1), R.w_obs[...])
    parts = []
    for g in range(CG):
        r = rows[GT * g:GT * (g + 1)] + R.posb[...]
        parts.append(pad8(r).T[0:D])
    return jnp.concatenate(parts, axis=1)


def layer_fwd(R, l, c, s, x):
    def vec(i):
        return tile4(R.bc[l, i])

    xh, r = normed(x)
    R.xh1[s] = xh
    R.r1[s] = r
    n1 = low(ones8(xh * vec(G1) + vec(B1)))
    R.n1[s] = n1
    mix = nn(R.qkv_t[l], n1)
    q = mix[0:D] * SCALE
    k = mix[128:128 + D]
    v = mix[256:256 + D]
    for h in range(H):
        a = slab_at(h)
        R.q_low[s, h] = low(q[a:a + 24])
        R.k_low[s, h] = low(k[a:a + 24])
    R.v_low[s] = low(pad8(v))
    att = low(ones8(attend(R, s, c, q * LOG2E, k, v)))
    R.att[l] = att
    x1 = x + nn(R.out_t[l], att)[0:D]
    xh, r = normed(x1)
    R.xh2[l] = xh
    R.r2[l] = r
    n2 = low(ones8(xh * vec(G2) + vec(B2)))
    R.n2[l] = n2
    pre = nn(R.fc_t[l], n2)
    parts = []
    for j in range(4):
        pj = pre[128 * j:128 * j + D]
        half = gelu_half(pj)
        R.pre[l, D * j:D * (j + 1)] = pj
        R.half[l, D * j:D * (j + 1)] = half
        parts.append(low(ones8(pj * half) if j == 0 else pad8(pj * half)))
    inner = jnp.concatenate(parts, axis=0)
    R.inner[l] = inner
    return x1 + nn(R.proj_t[l], inner)[0:D]


def head_step(R, c, x, live_total, valid_total):
    xh, r = normed(x)
    fin = low(pad8(xh * tile4(R.bcf[0]) + tile4(R.bcf[1])))
    hd = nn(R.head_t[...], fin) + tile4(R.bch[...])
    live = R.live[c]
    lw = live * (1.0 / live_total)
    rows = iota((CODES, L), 0).astype(F32)
    grads = []
    csum = jnp.zeros((1, L), F32)
    for b in range(BOOKS):
        lg = hd[CODES * b:CODES * (b + 1)]
        m = jnp.max(lg, axis=0, keepdims=True)
        e = jnp.exp(lg - m)
        s = jnp.sum(e, axis=0, keepdims=True)
        hot = rows == R.code[c, b:b + 1, :]
        picked = jnp.sum(jnp.where(hot, lg, 0.0), axis=0, keepdims=True)
        csum = csum + (jnp.log(s) + m - picked) * live
        grads.append((e * (1.0 / s) - jnp.where(hot, 1.0, 0.0)) * lw)
    diff = hd[32:72] - R.act[c]
    val = R.val[c]
    sq = diff * diff + 1.0
    ri = lax.rsqrt(sq)
    asum = val * (sq * ri)
    grads.append((val * (1.0 / valid_total)) * (diff * ri))
    R.loss[0, 0:1] += fold4(csum)
    af = fold4(asum)
    R.loss[1] += af[0:8] + af[8:16] + af[16:24] + af[24:32] + af[32:40]
    dh = jnp.concatenate(grads, axis=0)
    R.a_hb[0:72] += fold4(dh)
    dhl = low(jnp.concatenate([dh, jnp.zeros((56, L), F32)], axis=0))
    R.a_head[...] += nt(fin, dhl)
    df = nn(R.head[...], dhl)[0:D]
    R.a_fin[0, 0:D] += fold4(df * xh)
    R.a_fin[1, 0:D] += fold4(df)
    return normed_back(df * tile4(R.bcf[0]), xh, r)


def add_bias(R, l, i, v):
    R.a_bias[l, i, 0:D] += fold4(v)


def mlp_bwd(R, l, dout):
    outl = low(pad8(dout))
    add_bias(R, l, PB, dout)
    parts = []
    for j in range(4):
        rows = slice(D * j, D * (j + 1))
        dj = nn(R.proj[l, 128 * j:128 * (j + 1)], outl)
        parts.append(low(pad8(dj[0:D] * gelu_slope(R.pre[l, rows], R.half[l, rows]))))
    prel = jnp.concatenate(parts, axis=0)
    dn = nn(R.fc[l], prel)[0:D]
    xh = R.xh2[l]
    add_bias(R, l, G2, dn * xh)
    add_bias(R, l, B2, dn)
    dmid = normed_back(dn * tile4(R.bc[l, G2]), xh, R.r2[l]) + dout
    midl = low(pad8(dmid))
    add_bias(R, l, OB, dmid)
    da = nn(R.out[l], midl)[0:D]

    def a_proj(j):
        def run():
            cols = slice(256 * j, 256 * (j + 1))
            R.a_proj[l, :, cols] += nt(outl, R.inner[l, cols])
        return run

    def a_fc(j):
        def run():
            cols = slice(256 * j, 256 * (j + 1))
            R.a_fc[l, :, cols] += nt(R.n2[l], prel[cols])
        return run

    def a_out():
        R.a_out[l] += nt(R.att[l], midl)

    return dmid, da, [a_proj(0), a_proj(1), a_fc(0), a_fc(1), a_out]


def att_bwd(R, l, s, dmid, da, between):
    dq, dk, dv = attend_back(R, s, da, between)
    mixl = jnp.concatenate([low(pad8(dq)), low(pad8(dk)), low(pad8(dv))], axis=0)
    dn = nn(R.qkv[l], mixl)[0:D]
    add_bias(R, l, QB, dq)
    add_bias(R, l, VB, dv)
    R.a_qkv[l] += nt(R.n1[s], mixl)
    xh = R.xh1[s]
    add_bias(R, l, G1, dn * xh)
    add_bias(R, l, B1, dn)
    return normed_back(dn * tile4(R.bc[l, G1]), xh, R.r1[s]) + dmid


def embed_bwd(R, obs, c, dx):
    R.a_x[0:D] += fold4(dx)
    lanes = iota((D, 128), 1)
    tiles = []
    gs = [dx[:, 128 * g:128 * (g + 1)] for g in range(CG)]
    for t in range(CG):
        a = shifted(gs[t], -8 * t)
        b = shifted(gs[t + 1], 120 - 8 * t) if t + 1 < CG else jnp.zeros((D, 128), F32)
        tiles.append(jnp.where(lanes < GT - 8 * t, a, b))
    gl = low(pad8(jnp.concatenate(tiles, axis=1)))
    R.a_obs[...] += nn(gl, jnp.concatenate(obs, axis=1))


def zero_grads(R):
    for name in ("a_qkv", "a_out", "a_fc", "a_proj", "a_bias", "a_obs", "a_x", "a_fin", "a_head", "a_hb", "loss"):
        ref = getattr(R, name)
        ref[...] = jnp.zeros(ref.shape, F32)


HIGH = lax.Precision.HIGHEST


LATE = 364
EARLY_ROWS = (OB, G2, B2, FB0, FB1, FB2, FB3, PB)


def pack_vectors(R, rg, l, which):
    b = BASE + LROW * l
    for i in which:
        if FB0 <= i <= FB3:
            row = R.a_fc[l, D:D + 1, 128 * (i - FB0):128 * (i - FB0 + 1)]
        else:
            row = nt(jnp.ones((8, 128), F32), R.a_bias[l, i], HIGH)[0:1]
        rg[pl.ds(b + VROWS[i], 1), :] = row


def pack_early(R, rg, l):
    b = BASE + LROW * l
    rg[pl.ds(b + 364, D), :] = R.a_out[l, 0:D]
    for j in range(4):
        rg[pl.ds(b + 487 + j, D, stride=4), :] = R.a_fc[l, 0:D, 128 * j:128 * (j + 1)]
        rg[pl.ds(b + 971 + D * j, D), :] = R.a_proj[l, :, 128 * j:128 * (j + 1)].T[0:D]
    pack_vectors(R, rg, l, EARLY_ROWS)


def pack_late(R, rg, l):
    b = BASE + LROW * l
    for j in range(3):
        rg[pl.ds(b + 2 + j, D, stride=3), :] = R.a_qkv[l, 0:D, 128 * j:128 * (j + 1)]
    pack_vectors(R, rg, l, (G1, B1, QB, VB))


def pack_embed(R, rg):
    for f in range(OBS // 128):
        rg[128 * f:128 * (f + 1), :] = R.a_obs[:, 128 * f:128 * (f + 1)].T
    slot, lane = iota((32, 128), 0), iota((32, 128), 1)
    sel = jnp.where((slot == 0) | (lane % WIN == slot - 1), 1.0, 0.0)
    sel = jnp.where(lane < GT, sel, 0.0)
    rows = nt(sel, R.a_x[...], HIGH)
    rg[pl.ds(OBS, 1 + WIN), :] = rows[0:1 + WIN]


def pack_head(R, rg):
    rows = nt(jnp.ones((8, 128), F32), R.a_fin[...].reshape(256, 128), HIGH)
    for i in range(2):
        rg[pl.ds(HEAD + i, 1), :] = rows[0:1, 128 * i:128 * (i + 1)]
    lanes8 = iota((8, 128), 1)
    grad = R.a_head[...]
    R.hc[...] = jnp.where(iota((128, 128), 1) < 32, grad, 0.0)
    R.ho[...] = jnp.where(iota((128, 128), 1) < OFFS, shifted(grad, -32), 0.0)
    c0 = HEAD + 2
    o0 = c0 + 32

    def put(phases, src, rows_n, stride, width, count):
        acc = [jnp.zeros((rows_n, 128), F32) for _ in range(count + 1)]
        lanes = iota((rows_n, 128), 1)
        for p, a, s in phases:
            v = src[pl.ds(p, rows_n, stride=stride), :]
            first = shifted(v, s)
            if s + width > D:
                acc[a] = acc[a] + jnp.where((lanes >= s) & (lanes < D), first, 0.0)
                acc[a + 1] = acc[a + 1] + jnp.where(lanes < s + width - D, shifted(v, s - D), 0.0)
            else:
                acc[a] = acc[a] + first
        return acc

    acc = put(code_phases(), R.hc, 8, 15, 32, 4)
    for a in range(4):
        rg[pl.ds(c0 + a, 8, stride=4), :] = acc[a]
    hb = nt(jnp.ones((8, 128), F32), R.a_hb[...], HIGH)[0:1]
    lane1 = iota((1, 128), 1)
    rg[pl.ds(o0, 48), :] = jnp.zeros((48, 128), F32)
    acc = put(off_phases(), R.ho, 5, 24, OFFS, 7)
    for a in range(7):
        rg[pl.ds(o0 + a, 5, stride=7), :] = acc[a]
    rg[pl.ds(o0 + 7, 5, stride=7), :] = rg[pl.ds(o0 + 7, 5, stride=7), :] + acc[7]
    rg[pl.ds(o0, 1), :] = rg[pl.ds(o0, 1), :] + jnp.where(lane1 < 32, hb, 0.0)
    a, s = (D * OFFS + 32) // D, (D * OFFS + 32) % D
    ob = jnp.where(lane1 < OFFS, shifted(hb, -32), 0.0)
    rg[pl.ds(o0 + a, 1), :] = rg[pl.ds(o0 + a, 1), :] + shifted(ob, s)


MESH = pl.DeviceIdType.MESH


def round_up(n, m):
    return -(-n // m) * m


class Plan:
    def __init__(self, feats, toks, shard, tok_rows):
        self.feats, self.toks, self.chips = feats, toks, toks // 2
        self.shard = shard
        self.block = round_up(-(-(shard + 112) // D), 16)
        self.flat_rows = self.block // 16 * 15
        self.local = round_up(-(-shard // 1024), 1) * 8
        self.work = round_up(max(self.flat_rows, self.local + 1), 8)
        self.own_rows = tok_rows // feats
        self.chunks = self.own_rows // CT
        self.early = [f for f in range(feats) if shard * toks * f // D >= BASE + LATE]
        self.grid = round_up(-(-(shard * feats * toks) // D) + self.block, 8)


def comm_scratch(P):
    dma = pltpu.SemaphoreType.DMA
    B, C, Fn = P.block, P.chips, P.feats
    return dict(
        rg=pltpu.VMEM((P.grid, 128), F32),
        ob=pltpu.VMEM((P.chunks, Fn, L, 128), BF),
        pg=pltpu.VMEM((2, C, Fn, B, 128), BF),
        loc=pltpu.VMEM((P.work, 128), F32),
        rblk=pltpu.VMEM((B, 128), F32),
        codes_in=pltpu.VMEM((BOOKS, P.own_rows), jnp.int32),
        act_in=pltpu.VMEM((OFFS, P.own_rows), F32),
        val_in=pltpu.VMEM((OFFS, P.own_rows), jnp.int32),
        tz=pltpu.VMEM((2, Fn, 8, 128), F32),
        tc=pltpu.VMEM((2, C, 8, 128), F32),
        ts=pltpu.VMEM((2, 2, 8, 128), F32),
        sb1=pltpu.VMEM((C, Fn, B, 128), F32),
        rb1=pltpu.VMEM((C, Fn, B, 128), F32),
        sb2=pltpu.VMEM((C, Fn, B, 128), BF),
        rb2=pltpu.VMEM((C, Fn, B, 128), BF),
        col=pltpu.VMEM((Fn, B, 128), F32),
        sb3=pltpu.VMEM((Fn, B, 128), F32),
        rb3=pltpu.VMEM((Fn, B, 128), F32),
        s_p1=dma((2, Fn)), s_p2=dma((2, C)), s_p3=dma((2, C)),
        s_tz=dma((2, 2, Fn)), s_tc=dma((2, 2, C)), s_ts=dma((2, 2)),
        s_ob=dma((2, 2 * P.chunks, Fn)),
        s_own=dma((P.chunks,)),
        s_in=dma((3,)),
        s_r1=dma((2, 2, C)), s_r2=dma((2, Fn, C)), s_r3=dma((2, Fn)),
    )


def to_rows(loc, rblk, delta, P):
    v = loc[...]
    lanes = iota(v.shape, 1)
    moved = pltpu.roll(v, delta, 1)
    loc[...] = jnp.where(lanes >= delta, moved, pltpu.roll(moved, 1, 0))
    n = P.block // 16
    lane = iota((n, 128), 1)
    for j in range(16):
        if j < 15:
            a = shifted(loc[pl.ds(j, n, stride=15), :], 8 * j)
        if j > 0:
            b = shifted(loc[pl.ds(j - 1, n, stride=15), :], 8 * j)
            a = jnp.where(lane < 8 * j, b, a) if j < 15 else b
        rblk[pl.ds(j, n, stride=16), :] = jnp.where(lane < D, a, 0.0)


def from_rows(rblk, loc, delta, P):
    n = P.block // 16
    lane = iota((n, 128), 1)
    loc[...] = jnp.zeros(loc.shape, F32)
    for i in range(15):
        a = shifted(rblk[pl.ds(i, n, stride=16), :], -8 * i)
        b = shifted(rblk[pl.ds(i + 1, n, stride=16), :], D - 8 * i)
        loc[pl.ds(i, n, stride=15), :] = jnp.where(lane < D - 8 * i, a, b)
    v = loc[...]
    lanes = iota(v.shape, 1)
    moved = pltpu.roll(v, lax.rem(128 - delta, 128), 1)
    v = jnp.where(lanes < 128 - delta, moved, pltpu.roll(moved, P.work - 1, 0))
    return v[0:P.local]


def step_kernel(P, names, master, obs, counts, codes, actions, valid, grad, sums, *scratch):
    R = Refs()
    for name, ref in zip(names, scratch):
        setattr(R, name, ref)
    Fn, C, B = P.feats, P.chips, P.block
    feat = lax.axis_index("feat")
    tok = lax.axis_index("tok")
    chip = tok // 2
    core = tok % 2
    me = feat * P.toks + tok
    delta = lax.rem(me * P.shard, D)

    def z_peer(i):
        return lax.rem(feat + i, Fn)

    def z_from(i):
        return lax.rem(feat + Fn - i, Fn)

    def c_peer(i):
        return lax.rem(chip + i, C)

    def c_from(i):
        return lax.rem(chip + C - i, C)

    def to_z(i):
        return (z_peer(i), tok)

    def to_c(i):
        return (feat, 2 * c_peer(i) + core)

    sibling = (feat, 2 * chip + 1 - core)

    def send(src, dst, sems, at, dev):
        return pltpu.make_async_remote_copy(
            src_ref=src, dst_ref=dst, send_sem=sems.at[(0,) + at], recv_sem=sems.at[(1,) + at],
            device_id=dev, device_id_type=MESH)

    n = P.own_rows
    ins = []
    for i, (src, dst) in enumerate(((codes, R.codes_in), (actions, R.act_in), (valid, R.val_in))):
        ins.append(pltpu.make_async_copy(src.at[:, pl.ds(pl.multiple_of(feat * n, 128), n)], dst, R.s_in.at[i]))
        ins[-1].start()

    barrier = pltpu.get_barrier_semaphore()
    peers = [to_z(i) for i in range(1, Fn)] + [to_c(i) for i in range(1, C)] + [sibling]
    for dev in peers:
        pl.semaphore_signal(barrier, inc=1, device_id=dev, device_id_type=MESH)

    R.loc[...] = jnp.zeros(R.loc.shape, F32)
    whole = P.shard // 1024
    R.loc[0:8 * whole, :] = master[pl.ds(0, 1024 * whole)].reshape(8 * whole, 128)
    rest = P.shard - 1024 * whole
    last = jnp.concatenate([master[pl.ds(1024 * whole, rest)], jnp.zeros((1024 - rest,), F32)])
    R.loc[8 * whole:8 * whole + 8, :] = last.reshape(8, 128)
    to_rows(R.loc, R.rblk, delta, P)
    R.pg[core, chip, feat] = low(R.rblk[...])
    pl.semaphore_wait(barrier, len(peers))

    p1 = []
    for i in range(1, Fn):
        blk = R.pg.at[core, chip, feat]
        p1.append(send(blk, blk, R.s_p1, (i,), to_z(i)))
        p1[-1].start()

    half = CT // 2

    def obs_copies(p):
        cps = []
        for i in range(1, Fn):
            src = obs.at[pl.ds(pl.multiple_of(z_peer(i) * n + half * p, 16), half), :]
            dst = R.ob.at[p // 2, feat, pl.ds(pl.multiple_of(half * (p % 2), 16), half), :]
            cps.append(send(src, dst, R.s_ob, (p, i), to_z(i)))
        return cps

    def start_obs(p):
        for cp in obs_copies(p):
            cp.start()

    own = []
    for c in range(P.chunks):
        src = obs.at[pl.ds(pl.multiple_of(feat * n + CT * c, 16), CT), :]
        own.append(pltpu.make_async_copy(src, R.ob.at[c, feat, pl.ds(0, CT), :], R.s_own.at[c]))
        own[-1].start()
    start_obs(0)
    start_obs(1)
    for cp in ins:
        cp.wait()
    zero_grads(R)
    for c in range(P.chunks):
        for f in range(Fn):
            R.ob[c, f, CT:L, :] = jnp.zeros((L - CT, 128), BF)
    live_n, valid_n = prep_tokens(R, counts, R.codes_in, R.act_in, R.val_in, feat, P.chunks)

    def two_rows(a, b):
        return jnp.concatenate([jnp.broadcast_to(a, (1, 128)), jnp.broadcast_to(b, (1, 128)),
                                jnp.zeros((6, 128), F32)], axis=0)

    def z_copies(w):
        return [send(R.tz.at[w, feat], R.tz.at[w, feat], R.s_tz.at[w], (i,), to_z(i)) for i in range(1, Fn)]

    def c_copies(w):
        return [send(R.tc.at[w, chip], R.tc.at[w, chip], R.s_tc.at[w], (i,), to_c(i)) for i in range(1, C)]

    def s_copies(w):
        return [send(R.ts.at[w, core], R.ts.at[w, core], R.s_ts.at[w], (), sibling)]

    def start_all(cps):
        for cp in cps:
            cp.start()

    def total(ref, w, count):
        v = ref[w, 0]
        for i in range(1, count):
            v = v + ref[w, i]
        return v

    def wait_all(cps):
        for cp in cps:
            cp.wait()

    R.tz[0, feat] = two_rows(live_n, valid_n)
    start_all(z_copies(0))
    wait_all(p1)
    start_obs(2)
    p2 = []
    for i in range(1, C):
        blk = R.pg.at[core, chip]
        p2.append(send(blk, blk, R.s_p2, (i,), to_c(i)))
        p2[-1].start()
    p3 = [send(R.pg.at[core, chip], R.pg.at[core, chip], R.s_p3, (0,), sibling)]
    p3[0].start()
    wait_all(z_copies(0))
    R.tc[0, chip] = total(R.tz, 0, Fn)
    start_all(c_copies(0))
    for i in range(1, C):
        p2[i - 1].wait_recv()
        blk = R.pg.at[core, c_from(i)]
        p3.append(send(blk, blk, R.s_p3, (i,), sibling))
        p3[-1].start()
    start_obs(3)
    wait_all(c_copies(0))
    R.ts[0, core] = total(R.tc, 0, C)
    start_all(s_copies(0))
    for cp in p2:
        cp.wait_send()
    wait_all(p3)
    R.rg[0:8, :] = jnp.zeros((8, 128), F32)

    def place(d, _):
        r0 = (P.shard * d) // D
        f, t = d // P.toks, d % P.toks
        blk = R.pg[t % 2, t // 2, f].astype(F32)
        before = R.rg[pl.ds(r0, 1), :]
        R.rg[pl.ds(r0, B), :] = blk
        R.rg[pl.ds(r0, 1), :] = blk[0:1] + before
        return 0

    lax.fori_loop(0, Fn * P.toks, place, 0)
    prep_weights(R.rg, R)
    wait_all(s_copies(0))
    counted = total(R.ts, 0, 2)
    live_total = counted[0:1, 0:1]
    valid_total = counted[1:2, 0:1]

    for cp in own:
        cp.wait()


    def rows_of(f, ch, co):
        return (P.shard * (f * P.toks + 2 * ch + co)) // D

    early = P.early[0] if P.early else Fn
    planes = [slice(early, Fn), slice(0, early)]

    def r1_copy(w, i):
        at = pl.ds(planes[w].start, planes[w].stop - planes[w].start)
        return send(R.sb1.at[i, at], R.rb1.at[i, at], R.s_r1.at[w], (i,), sibling)

    def r2_copy(f, i):
        return send(R.sb2.at[i, f], R.rb2.at[i, f], R.s_r2.at[:, f], (i,), to_c(i))

    def r3_copy(i):
        return send(R.sb3.at[i], R.rb3.at[i], R.s_r3, (i,), to_z(i))

    order = list(range(1, C)) + [0]

    def sum_cores(w):
        for i in order:
            for f in range(planes[w].start, planes[w].stop):
                R.sb1[i, f] = R.rg[pl.ds(rows_of(f, c_peer(i), 1 - core), B), :]
            r1_copy(w, i).start()

    def sum_chips(w):
        for i in order:
            r1_copy(w, i).wait_recv()
            for f in reversed(range(planes[w].start, planes[w].stop)):
                v = R.rg[pl.ds(rows_of(f, c_peer(i), core), B), :] + R.rb1[i, f]
                if i:
                    R.sb2[i, f] = low(v)
                    r2_copy(f, i).start()
                else:
                    R.col[f] = v

    def sum_column(f):
        v = R.col[f]
        for i in range(1, C):
            r2_copy(f, i).wait_recv()
            v = v + R.rb2[i, f].astype(F32)
        R.col[f] = v
        for i in range(1, Fn):
            @pl.when(z_peer(i) == f)
            def _():
                R.sb3[i] = v
                r3_copy(i).start()

    def chunk(c, _):
        for p in (2 * c, 2 * c + 1):
            for cp in obs_copies(p):
                cp.wait_recv()

        @pl.when(2 * c + 4 < 2 * P.chunks)
        def _():
            start_obs(2 * c + 4)

        R.x[...] = embed(R, [R.ob[c, f, 0:CT, :] for f in range(Fn)], c)

        def lay(l, _):
            R.x[...] = layer_fwd(R, l, c, l, R.x[...])
            return 0

        lax.fori_loop(0, LAYERS, lay, 0)

        @pl.when(2 * c + 5 < 2 * P.chunks)
        def _():
            start_obs(2 * c + 5)

        dx = head_step(R, c, R.x[...], live_total, valid_total)
        dmid, da, rest = mlp_bwd(R, 1, dx)
        R.x[...] = att_bwd(R, 1, 1, dmid, da, rest)
        dmid, da, rest = mlp_bwd(R, 0, R.x[...])
        R.dmid[...] = dmid
        R.da[...] = da
        for run in rest:
            run()

        @pl.when(c == P.chunks - 1)
        def _():
            R.rg[pl.ds(HEAD + 32, P.grid - HEAD - 32), :] = jnp.zeros((P.grid - HEAD - 32, 128), F32)
            pack_head(R, R.rg)
            pack_late(R, R.rg, 1)
            for l in range(LAYERS):
                pack_early(R, R.rg, l)
            R.ts[1, core] = two_rows(jnp.sum(R.loss[0], keepdims=True), jnp.sum(R.loss[1], keepdims=True))
            start_all(s_copies(1))
            sum_cores(0)

        dx = att_bwd(R, 0, 0, R.dmid[...], R.da[...], [])

        @pl.when(c == P.chunks - 1)
        def _():
            sum_chips(0)
            wait_all(s_copies(1))
            R.tc[1, chip] = total(R.ts, 1, 2)
            start_all(c_copies(1))

        embed_bwd(R, [R.ob[c, f] for f in range(Fn)], c, dx)
        return 0

    lax.fori_loop(0, P.chunks, chunk, 0)
    pack_embed(R, R.rg)
    pack_late(R, R.rg, 0)
    sum_cores(1)
    sum_chips(1)
    wait_all(c_copies(1))
    R.tz[1, feat] = total(R.tc, 1, C)
    start_all(z_copies(1))
    for f in reversed(range(Fn)):
        sum_column(f)
    for i in range(1, Fn):
        r3_copy(i).wait_recv()
    v = R.col[feat]
    for i in range(1, Fn):
        v = v + R.rb3[i]
    R.rblk[...] = v
    grad[...] = from_rows(R.rblk, R.loc, delta, P)
    wait_all(z_copies(1))
    lost = total(R.tz, 1, Fn)
    sums[...] = jnp.concatenate([lost[0:1], counted[0:1], lost[1:2], counted[1:2], jnp.zeros((4, 128), F32)], axis=0)
    for p in range(2 * P.chunks):
        for cp in obs_copies(p):
            cp.wait_send()
    for w in range(2):
        for i in range(C):
            r1_copy(w, i).wait_send()
    for i in range(1, C):
        for f in range(Fn):
            r2_copy(f, i).wait_send()
    for i in range(1, Fn):
        r3_copy(i).wait_send()


def solution(mesh):
    feats, toks = mesh.shape["feat"], mesh.shape["tok"]

    def shards(master, first, second, obs, counts, codes, actions, valid):
        P_ = Plan(feats, toks, master.shape[0], obs.shape[0])
        scratch = dict(scratch_list(P_.chunks))
        scratch.update(comm_scratch(P_))
        vmem = pl.BlockSpec(memory_space=pltpu.VMEM)
        hbm = pl.BlockSpec(memory_space=pl.ANY)
        grad, sums = pl.pallas_call(
            functools.partial(step_kernel, P_, list(scratch)),
            out_shape=(jax.ShapeDtypeStruct((P_.local, 128), F32), jax.ShapeDtypeStruct((8, 128), F32)),
            in_specs=[vmem, hbm, vmem, hbm, hbm, hbm],
            out_specs=(vmem, vmem),
            scratch_shapes=list(scratch.values()),
            compiler_params=pltpu.CompilerParams(
                collective_id=0, has_side_effects=True, vmem_limit_bytes=60 * 2 ** 20),
        )(master, obs, counts.T, codes.T, actions, valid)
        grad = grad.reshape(-1)[:P_.shard]
        f_new = BETA_ONE * first + (1.0 - BETA_ONE) * grad
        s_new = BETA_TWO * second + (1.0 - BETA_TWO) * grad * grad
        f_hat = f_new / (1.0 - BETA_ONE ** STEP_NO)
        s_hat = s_new / (1.0 - BETA_TWO ** STEP_NO)
        new = master - LEARN_RATE * (f_hat / (jnp.sqrt(s_hat) + ADAM_EPS) + DECAY_RATE * master)
        return new, f_new, s_new, sums[0:4, 0]

    weights = PSpec(("feat", "tok"))
    return jax.shard_map(
        shards, mesh=mesh,
        in_specs=(weights, weights, weights, PSpec("tok", "feat"), PSpec("tok", None), PSpec("tok", None),
                  PSpec(None, "tok"), PSpec(None, "tok")),
        out_specs=(weights, weights, weights, PSpec()), check_vma=False)
```

```python
import functools
import math

import jax
import jax.numpy as jnp
from jax import lax
from jax.experimental import pallas as pl
from jax.experimental.pallas import tpu as pltpu
from jax.sharding import PartitionSpec as PSpec

D = 120
H = 6
HD = 20
FF = 480
OBS = 512
LAYERS = 2
CAMS = 3
BOOKS = 2
CODES = 16
SPAN = 5
ACT = 7
WIN = 30
OFFS = SPAN * ACT
NORM_EPS = 1e-05
STEP_NO = 10
BETA_ONE = 0.9
BETA_TWO = 0.999
ADAM_EPS = 1e-08
DECAY_RATE = 0.1
LEARN_RATE = 0.05
GW = 4
GT = GW * WIN
CG = 4
L = CG * 128
CT = CG * GT
F32 = jnp.float32
BF = jnp.bfloat16
SCALE = HD ** (-0.5)
LROW = 2 * 1 + 3 * D + 2 + D + 1 + 2 + 4 * D + 4 + 4 * D + 1
BASE = OBS + 1 + WIN
HEAD = BASE + LAYERS * LROW
NV = 13
VROWS = [0, 1, 362, 363, 484, 485, 486, 967, 968, 969, 970, 1451]
(G1, B1, QB, VB, OB, G2, B2, FB0, FB1, FB2, FB3, PB) = range(12)


def nn(a, b):
    return lax.dot_general(a, b, (((1,), (0,)), ((), ())), preferred_element_type=F32)


def nt(a, b, precision=None):
    return lax.dot_general(a, b, (((1,), (1,)), ((), ())), preferred_element_type=F32, precision=precision)


def low(v):
    return v.astype(BF)


def pad8(v):
    return jnp.concatenate([v, jnp.zeros((8, v.shape[1]), v.dtype)], axis=0)


def tile4(v):
    return jnp.concatenate([v] * CG, axis=1)


def fold4(v):
    out = v[:, 0:128]
    for g in range(1, CG):
        out = out + v[:, 128 * g:128 * (g + 1)]
    return out


def iota(shape, axis):
    return lax.broadcasted_iota(jnp.int32, shape, axis)


def slab_at(h):
    return 20 * h - (4 if h % 2 else 0)


def head_stack(v):
    rows = iota((8, 128), 0)
    cols = []
    for h in range(H):
        a = slab_at(h)
        if h % 2 == 0:
            parts = [v[a:a + 16], jnp.where(rows < 4, v[a + 16:a + 24], 0.0)]
        else:
            parts = [jnp.where(rows >= 4, v[a:a + 8], 0.0), v[a + 8:a + 24]]
        if a > 0:
            parts = [jnp.zeros((a, 128), F32)] + parts
        if a + 24 < 128:
            parts = parts + [jnp.zeros((128 - a - 24, 128), F32)]
        cols.append(jnp.concatenate(parts, axis=0))
    return jnp.concatenate(cols, axis=1)


def join_slabs(slabs):
    rows = iota((8, 128), 0)
    parts = []
    for p in range(3):
        a, b = slabs[2 * p], slabs[2 * p + 1]
        parts += [a[0:16], jnp.where(rows < 4, a[16:24], b[0:8]), b[8:24]]
    return jnp.concatenate(parts, axis=0)


def slabs_of(v):
    return [v[slab_at(h):slab_at(h) + 24] for h in range(H)]


def hi_lo(v):
    hi = low(v)
    return hi, low(v - hi.astype(F32))


def normed(x):
    mean = jnp.sum(x, axis=0, keepdims=True) * (1.0 / D)
    c = x - mean
    var = jnp.sum(c * c, axis=0, keepdims=True) * (1.0 / D)
    r = lax.rsqrt(var + NORM_EPS)
    return c * r, r


def normed_back(d, xh, r):
    m0 = jnp.sum(d, axis=0, keepdims=True) * (1.0 / D)
    m1 = jnp.sum(d * xh, axis=0, keepdims=True) * (1.0 / D)
    return r * (d - m0 - xh * m1)


GA = math.sqrt(2.0 / math.pi)
GB = 0.044715


def gelu_half(x):
    return 0.5 + 0.5 * jnp.tanh(x * (GA + (GA * GB) * (x * x)))


def gelu_slope(x, s):
    return s + (x * s) * (1.0 - s) * (2.0 * GA + (6.0 * GA * GB) * (x * x))


LOG2E = math.log2(math.e)
BIG = 1e30


class Refs:
    pass


def scratch_list(chunks):
    groups = chunks * CG
    return dict(
        w_obs=pltpu.VMEM((OBS, 128), BF),
        posb=pltpu.VMEM((GT, 128), F32),
        qkv_t=pltpu.VMEM((LAYERS, 384, 128), BF),
        qkv=pltpu.VMEM((LAYERS, 128, 384), BF),
        out_t=pltpu.VMEM((LAYERS, 128, 128), BF),
        out=pltpu.VMEM((LAYERS, 128, 128), BF),
        fc_t=pltpu.VMEM((LAYERS, 512, 128), BF),
        fc=pltpu.VMEM((LAYERS, 128, 512), BF),
        proj_t=pltpu.VMEM((LAYERS, 128, 512), BF),
        proj=pltpu.VMEM((LAYERS, 512, 128), BF),
        head_t=pltpu.VMEM((72, 128), BF),
        head=pltpu.VMEM((128, 128), BF),
        vec=pltpu.VMEM((32, 128), F32),
        bc=pltpu.VMEM((LAYERS, 12, GT, 128), F32),
        bcf=pltpu.VMEM((2, GT, 128), F32),
        bch=pltpu.VMEM((72, 128), F32),
        hc=pltpu.VMEM((128, 128), F32),
        ho=pltpu.VMEM((128, 128), F32),
        cnt=pltpu.VMEM((16, 256), F32),
        live=pltpu.VMEM((chunks, 1, L), F32),
        act=pltpu.VMEM((chunks, 40, L), F32),
        val=pltpu.VMEM((chunks, 40, L), F32),
        code=pltpu.VMEM((chunks, 2, L), F32),
        x=pltpu.VMEM((D, L), F32),
        dmid=pltpu.VMEM((D, L), F32),
        da=pltpu.VMEM((D, L), F32),
        xh1=pltpu.VMEM((LAYERS, D, L), F32),
        r1=pltpu.VMEM((LAYERS, 1, L), F32),
        xh2=pltpu.VMEM((LAYERS, D, L), F32),
        r2=pltpu.VMEM((LAYERS, 1, L), F32),
        n1=pltpu.VMEM((LAYERS, 128, L), BF),
        n2=pltpu.VMEM((LAYERS, 128, L), BF),
        att=pltpu.VMEM((LAYERS, 128, L), BF),
        q_low=pltpu.VMEM((LAYERS, H, 24, L), BF),
        k_low=pltpu.VMEM((LAYERS, H, 24, L), BF),
        v_low=pltpu.VMEM((LAYERS, 128, L), BF),
        rsum=pltpu.VMEM((LAYERS, H, 1, L), F32),
        prob=pltpu.VMEM((LAYERS, CG, GT, H * 128), F32),
        prob_low=pltpu.VMEM((LAYERS, CG, 128, H * 128), BF),
        k_mask=pltpu.VMEM((48, 128), BF),
        q_mask=pltpu.VMEM((48, 128), BF),
        dead=pltpu.VMEM((groups, 8, 128), F32),
        pre=pltpu.VMEM((LAYERS, FF, L), F32),
        half=pltpu.VMEM((LAYERS, FF, L), F32),
        inner=pltpu.VMEM((LAYERS, 512, L), BF),
        a_qkv=pltpu.VMEM((LAYERS, 384, 128), F32),
        ds_t=pltpu.VMEM((CG * H // 2, 128, 256), BF),
        turned=pltpu.VMEM((5, L, 128), BF),
        a_out=pltpu.VMEM((LAYERS, 128, 128), F32),
        a_fc=pltpu.VMEM((LAYERS, 512, 128), F32),
        a_proj=pltpu.VMEM((LAYERS, 512, 128), F32),
        a_bias=pltpu.VMEM((LAYERS, 12, 128, 128), F32),
        a_obs=pltpu.VMEM((128, 512), F32),
        a_x=pltpu.VMEM((128, 128), F32),
        a_fin=pltpu.VMEM((2, 128, 128), F32),
        a_head=pltpu.VMEM((128, 128), F32),
        a_hb=pltpu.VMEM((128, 128), F32),
        loss=pltpu.VMEM((2, 8, 128), F32),
    )


def code_phases():
    for p in range(15):
        yield p, (32 * p) // D, (32 * p) % D


def off_phases():
    for p in range(24):
        yield p, (35 * p + 32) // D, (35 * p + 32) % D


def shifted(v, by):
    by %= 128
    return v if by == 0 else pltpu.roll(v, by, 1)


def take_phase(load, a, s, width, rows):
    lanes = iota((rows, 128), 1)
    first = shifted(load(a), -s)
    if s + width > D:
        second = shifted(load(a + 1), D - s)
        first = jnp.where(lanes < D - s, first, second)
    return jnp.where(lanes < width, first, 0.0)


def with_bias(w, bias):
    if bias is not None:
        w = jnp.where(iota((128, 128), 0) == D, bias, w)
    return low(w.T)


def ones8(v):
    return jnp.concatenate([v, jnp.where(iota((8, v.shape[1]), 0) == 0, 1.0, 0.0)], axis=0)


def prep_weights(rg, R):
    R.w_obs[...] = low(rg[0:OBS, :])
    for w in range(GW):
        R.posb[pl.ds(WIN * w, WIN), :] = rg[OBS + 1:OBS + 1 + WIN, :] + rg[OBS:OBS + 1, :]
    R.vec[...] = jnp.zeros((32, 128), F32)
    for l in range(LAYERS):
        b = BASE + LROW * l
        for j in range(3):
            w = pad8(rg[pl.ds(b + 2 + j, D, stride=3), :])
            R.qkv[l, :, 128 * j:128 * (j + 1)] = low(w)
            R.qkv_t[l, 128 * j:128 * (j + 1), :] = with_bias(w, None if j == 1 else rg[pl.ds(b + 362 + j // 2, 1), :])
        w = pad8(rg[pl.ds(b + 364, D), :])
        R.out[l] = low(w)
        R.out_t[l] = with_bias(w, rg[pl.ds(b + 484, 1), :])
        for j in range(4):
            w = pad8(rg[pl.ds(b + 487 + j, D, stride=4), :])
            R.fc[l, :, 128 * j:128 * (j + 1)] = low(w)
            R.fc_t[l, 128 * j:128 * (j + 1), :] = with_bias(w, rg[pl.ds(b + 967 + j, 1), :])
            w = pad8(rg[pl.ds(b + 971 + D * j, D), :])
            R.proj[l, 128 * j:128 * (j + 1), :] = low(w)
            R.proj_t[l, :, 128 * j:128 * (j + 1)] = with_bias(w, None if j else rg[pl.ds(b + 1451, 1), :])
        for i, r in enumerate(VROWS):
            R.vec[pl.ds(12 * l + i, 1), :] = rg[pl.ds(b + r, 1), :]
    R.vec[24:26, :] = rg[pl.ds(HEAD, 2), :]
    R.hc[...] = jnp.zeros((128, 128), F32)
    R.ho[...] = jnp.zeros((128, 128), F32)
    c0 = HEAD + 2
    for p, a, s in code_phases():
        R.hc[pl.ds(p, 8, stride=15), :] = take_phase(
            lambda i: rg[pl.ds(c0 + i, 8, stride=4), :], a, s, 32, 8)
    o0 = c0 + 32
    for p, a, s in off_phases():
        R.ho[pl.ds(p, 5, stride=24), :] = take_phase(
            lambda i: rg[pl.ds(o0 + i, 5, stride=7), :], a, s, OFFS, 5)
    hw = R.hc[...] + shifted(R.ho[...], 32)
    R.head[...] = low(hw)
    R.head_t[...] = low(hw.T[0:72])
    lanes = iota((1, 128), 1)
    hb = jnp.where(lanes < 32, rg[pl.ds(o0, 1), :], 0.0)
    a, s = (D * OFFS + 32) // D, (D * OFFS + 32) % D
    ob = take_phase(lambda i: rg[pl.ds(o0 + i, 1), :], a, s, OFFS, 1)
    R.vec[26:27, :] = hb + shifted(ob, 32)
    columns = jnp.concatenate([R.vec[...], jnp.zeros((96, 128), F32)], axis=0).T
    for l in range(LAYERS):
        for i in range(12):
            R.bc[l, i] = jnp.broadcast_to(columns[0:D, 12 * l + i:12 * l + i + 1], (D, 128))
    for i in range(2):
        R.bcf[i] = jnp.broadcast_to(columns[0:D, 24 + i:25 + i], (D, 128))
    R.bch[...] = jnp.broadcast_to(columns[0:72, 26:27], (72, 128))


def spread_groups(v, groups, width):
    rows = v.shape[0]
    lanes = iota((rows, 128), 1)
    out = []
    for g in range(groups):
        t, o = (GT * g) // 128, (GT * g) % 128
        a = shifted(v[:, 128 * t:128 * (t + 1)], -o)
        if o + GT > 128:
            b = shifted(v[:, 128 * (t + 1):128 * (t + 2)], -o)
            a = jnp.where(lanes < 128 - o, a, b)
        out.append(jnp.where(lanes < GT, a, 0))
    return out


def prep_tokens(R, counts, codes, actions, valid, feat, chunks):
    groups = chunks * CG
    wins = counts.shape[1]
    R.cnt[...] = jnp.zeros(R.cnt.shape, F32)
    R.cnt[0:WIN // CAMS, :] = counts[...].astype(F32)
    k = iota((GT, 16), 0)
    step = (k % WIN) // CAMS
    sel = jnp.where(step == iota((GT, 16), 1), 1.0, 0.0)
    x = nn(low(sel), low(R.cnt[...]))
    y = jnp.where(iota((GT, wins), 1) % GW == iota((GT, wins), 0) // WIN, x, 0.0)
    pick = jnp.where(iota((wins, 128), 0) // GW == iota((wins, 128), 1) + groups * feat, 1.0, 0.0)
    z = nn(low(y), low(pick))
    kk = iota((GT, 128), 0)
    alive = jnp.where((kk % CAMS).astype(F32) < z, 1.0, 0.0)
    steps = WIN // CAMS
    j, at = iota((48, 128), 0), iota((48, 128), 1)
    own = (at // WIN == j // steps) & ((at % WIN) // CAMS == j % steps) & (at < GT)
    R.k_mask[...] = low(jnp.where(own, 1.0, 0.0))
    may = (at // WIN == j // steps) & ((at % WIN) // CAMS >= j % steps)
    R.q_mask[...] = low(jnp.where(may | (j >= GW * steps), 0.0, -BIG))
    rows = pad8(alive).T
    for g in range(groups):
        R.live[g // CG, :, 128 * (g % CG):128 * (g % CG + 1)] = rows[g:g + 1, :]
        R.dead[g] = jnp.where(iota((8, 128), 0) == 0, 1.0 - rows[g:g + 1, :], 0.0)
    for name, src in (("code", codes), ("act", actions), ("val", valid)):
        parts = spread_groups(src[...].astype(F32), groups, GT)
        dst = getattr(R, name)
        for g in range(groups):
            c, lo = g // CG, 128 * (g % CG)
            part = parts[g]
            if name == "val":
                part = part * rows[g:g + 1, :]
            if name != "code":
                dst[c, 32:40, lo:lo + 128] = jnp.zeros((8, 128), F32)
            dst[c, 0:part.shape[0], lo:lo + 128] = part
    lanes = iota((GT, 128), 1)
    live_total = jnp.sum(jnp.where(lanes < groups, alive, 0.0), keepdims=True)
    v = jnp.zeros((40, L), F32)
    for c in range(chunks):
        v = v + R.val[c]
    valid_total = jnp.sum(v, keepdims=True)
    return live_total, valid_total


def own_rows(slab, h):
    rows = iota((8, 128), 0)
    if h % 2 == 0:
        return jnp.concatenate([slab[0:16], jnp.where(rows < 4, slab[16:24], 0.0)], axis=0)
    return jnp.concatenate([jnp.where(rows >= 4, slab[0:8], 0.0), slab[8:24]], axis=0)


def split(v):
    hi = low(v).astype(F32)
    return hi, v - hi


def attend(R, s, c, q, k, v):
    qh, ql = split(q)
    kh, kl = split(k)
    vh, vl = split(v)
    minus = jnp.where(iota((8, 128), 0) == 0, -BIG, 0.0)

    none = jnp.zeros((128, 128), BF)

    def scores(g, p):
        at = slice(128 * g, 128 * (g + 1))
        qs, ks = [], []
        for h in (2 * p, 2 * p + 1):
            sl = slice(slab_at(h), slab_at(h) + 24)
            hi = own_rows(qh[sl, at], h)
            qd = low(jnp.concatenate([hi, hi, own_rows(ql[sl, at], h), minus], axis=0))
            kd = low(jnp.concatenate([kh[sl, at], kl[sl, at], kh[sl, at], R.dead[c * CG + g]], axis=0))
            qs.append(jnp.concatenate([qd, R.q_mask[...]], axis=0))
            ks.append(jnp.concatenate([kd, R.k_mask[...]], axis=0).T)
        if PAIR:
            both = jnp.concatenate([jnp.concatenate([qs[0], none], axis=1),
                                    jnp.concatenate([none, qs[1]], axis=1)], axis=0)
            return nn(jnp.concatenate(ks, axis=1), both)[0:GT]
        return jnp.concatenate([nn(ks[0], qs[0])[0:GT], nn(ks[1], qs[1])[0:GT]], axis=1)

    def soft(g, p, sc):
        at = slice(128 * g, 128 * (g + 1))
        e = jnp.exp2(sc - jnp.max(sc, axis=0, keepdims=True))
        r = 1.0 / jnp.sum(e, axis=0, keepdims=True)
        e8 = pad8(e)
        eh = low(e8)
        el = low(e8 - eh.astype(F32))
        cols = slice(256 * p, 256 * (p + 1))
        R.prob[s, g, :, cols] = e
        for i in range(2):
            at_h = slice(256 * p + 128 * i, 256 * p + 128 * (i + 1))
            R.prob_low[s, g, :, at_h] = eh[:, 128 * i:128 * (i + 1)].T
        R.rsum[s, 2 * p, :, at] = r[:, 0:128]
        R.rsum[s, 2 * p + 1, :, at] = r[:, 128:256]
        return r, eh, el

    def values(g, p, r, eh, el):
        at = slice(128 * g, 128 * (g + 1))
        out = []
        for i in range(2):
            sl = slice(slab_at(2 * p + i), slab_at(2 * p + i) + 24)
            cols = slice(128 * i, 128 * (i + 1))
            vs = low(jnp.concatenate([vh[sl, at], vl[sl, at]], axis=0))
            o = nn(jnp.concatenate([vs, vs], axis=1), jnp.concatenate([eh[:, cols], el[:, cols]], axis=0))
            out.append((o[0:24] + o[24:48]) * r[:, cols])
        return out

    items = [(g, p) for g in range(CG) for p in range(H // 2)]
    slabs = pipeline(items, scores, soft, values, FAHEAD)
    slabs = [t for pair in slabs for t in pair]
    return jnp.concatenate([join_slabs(slabs[H * g:H * (g + 1)]) for g in range(CG)], axis=1)


PAIR = True
FAHEAD = 2
BAHEAD = 2


def pipeline(items, first, second, third, ahead, between=()):
    n = len(items)
    a, b, out = {}, {}, []
    between = list(between)
    done = 0
    for t in range(n + ahead):
        if t < n:
            a[t] = first(*items[t])
        m = t - ahead + 1
        if 0 <= m < n:
            b[m] = second(*items[m], *(a.pop(m) if isinstance(a[m], tuple) else (a.pop(m),)))
        m = t - ahead
        if 0 <= m < n:
            out.append(third(*items[m], *b.pop(m)))
        while done < len(between) * (t + 1) // (n + ahead):
            between[done]()
            done += 1
    return out


def attend_back(R, s, do, between=()):
    vrows = [R.v_low[s, :, 128 * g:128 * (g + 1)].T for g in range(CG)]

    def probs(g, p):
        at = slice(128 * g, 128 * (g + 1))
        ds, stack = [], []
        for h in (2 * p, 2 * p + 1):
            a = slab_at(h)
            d = own_rows(do[a:a + 24, at], h) * R.rsum[s, h, :, at]
            parts = ([jnp.zeros((a, 128), F32)] if a else []) + [d] + ([jnp.zeros((104 - a, 128), F32)])
            ds.append(low(d))
            stack.append(low(jnp.concatenate(parts, axis=0)))
        return ds, nn(vrows[g], jnp.concatenate(stack, axis=1))[0:GT]

    def inner(g, p, d, dp):
        at = slice(128 * g, 128 * (g + 1))
        e = R.prob[s, g, :, 256 * p:256 * (p + 1)]
        r = jnp.concatenate([R.rsum[s, 2 * p, :, at], R.rsum[s, 2 * p + 1, :, at]], axis=1)
        total = jnp.sum(e * dp, axis=0, keepdims=True) * r
        ds = low(pad8(e * (dp - total)))
        for i in range(2):
            cols = slice(128 * i, 128 * (i + 1))
            R.ds_t[3 * g + p, :, cols] = ds[:, cols].T
        return d, ds

    def outer(g, p, d, ds):
        at = slice(128 * g, 128 * (g + 1))
        out = []
        for i in range(2):
            h = 2 * p + i
            dsh = ds[:, 128 * i:128 * (i + 1)]
            out.append((nn(R.k_low[s, h, :, at], dsh), nn(R.q_low[s, h, :, at], R.ds_t[3 * g + p, :, 128 * i:128 * (i + 1)]),
                        nn(d[i], R.prob_low[s, g, :, 128 * h:128 * (h + 1)])))
        return out

    items = [(g, p) for g in range(CG) for p in range(H // 2)]
    slabs = pipeline(items, probs, inner, outer, BAHEAD, between)
    slabs = [t for pair in slabs for t in pair]
    out = []
    for i in range(3):
        out.append(jnp.concatenate(
            [join_slabs([t[i] for t in slabs[H * g:H * (g + 1)]]) for g in range(CG)], axis=1))
    return out[0] * SCALE, out[1], out[2]


def turn(R, i, v):
    for g in range(CG):
        R.turned[i, 128 * g:128 * (g + 1), :] = v[:, 128 * g:128 * (g + 1)].T


def embed(R, obs, c):
    rows = nn(jnp.concatenate(obs, axis=1), R.w_obs[...])
    parts = []
    for g in range(CG):
        r = rows[GT * g:GT * (g + 1)] + R.posb[...]
        parts.append(pad8(r).T[0:D])
    return jnp.concatenate(parts, axis=1)


def layer_fwd(R, l, c, s, x):
    def vec(i):
        return tile4(R.bc[l, i])

    xh, r = normed(x)
    R.xh1[s] = xh
    R.r1[s] = r
    n1 = low(ones8(xh * vec(G1) + vec(B1)))
    R.n1[s] = n1
    mix = nn(R.qkv_t[l], n1)
    q = mix[0:D] * SCALE
    k = mix[128:128 + D]
    v = mix[256:256 + D]
    for h in range(H):
        a = slab_at(h)
        R.q_low[s, h] = low(q[a:a + 24])
        R.k_low[s, h] = low(k[a:a + 24])
    R.v_low[s] = low(pad8(v))
    att = low(ones8(attend(R, s, c, q * LOG2E, k, v)))
    R.att[l] = att
    x1 = x + nn(R.out_t[l], att)[0:D]
    xh, r = normed(x1)
    R.xh2[l] = xh
    R.r2[l] = r
    n2 = low(ones8(xh * vec(G2) + vec(B2)))
    R.n2[l] = n2
    pre = nn(R.fc_t[l], n2)
    parts = []
    for j in range(4):
        pj = pre[128 * j:128 * j + D]
        half = gelu_half(pj)
        R.pre[l, D * j:D * (j + 1)] = pj
        R.half[l, D * j:D * (j + 1)] = half
        parts.append(low(ones8(pj * half) if j == 0 else pad8(pj * half)))
    inner = jnp.concatenate(parts, axis=0)
    R.inner[l] = inner
    return x1 + nn(R.proj_t[l], inner)[0:D]


def head_step(R, c, x, live_total, valid_total):
    xh, r = normed(x)
    fin = low(pad8(xh * tile4(R.bcf[0]) + tile4(R.bcf[1])))
    hd = nn(R.head_t[...], fin) + tile4(R.bch[...])
    live = R.live[c]
    lw = live * (1.0 / live_total)
    rows = iota((CODES, L), 0).astype(F32)
    grads = []
    csum = jnp.zeros((1, L), F32)
    for b in range(BOOKS):
        lg = hd[CODES * b:CODES * (b + 1)]
        m = jnp.max(lg, axis=0, keepdims=True)
        e = jnp.exp(lg - m)
        s = jnp.sum(e, axis=0, keepdims=True)
        hot = rows == R.code[c, b:b + 1, :]
        picked = jnp.sum(jnp.where(hot, lg, 0.0), axis=0, keepdims=True)
        csum = csum + (jnp.log(s) + m - picked) * live
        grads.append((e * (1.0 / s) - jnp.where(hot, 1.0, 0.0)) * lw)
    diff = hd[32:72] - R.act[c]
    val = R.val[c]
    sq = diff * diff + 1.0
    ri = lax.rsqrt(sq)
    asum = val * (sq * ri)
    grads.append((val * (1.0 / valid_total)) * (diff * ri))
    R.loss[0, 0:1] += fold4(csum)
    af = fold4(asum)
    R.loss[1] += af[0:8] + af[8:16] + af[16:24] + af[24:32] + af[32:40]
    dh = jnp.concatenate(grads, axis=0)
    R.a_hb[0:72] += fold4(dh)
    dhl = low(jnp.concatenate([dh, jnp.zeros((56, L), F32)], axis=0))
    turn(R, 4, dhl)
    R.a_head[...] += nn(fin, R.turned[4])
    df = nn(R.head[...], dhl)[0:D]
    R.a_fin[0, 0:D] += fold4(df * xh)
    R.a_fin[1, 0:D] += fold4(df)
    return normed_back(df * tile4(R.bcf[0]), xh, r)


def add_bias(R, l, i, v):
    R.a_bias[l, i, 0:D] += fold4(v)


def mlp_bwd(R, l, dout):
    outl = low(pad8(dout))
    add_bias(R, l, PB, dout)
    parts = []
    for j in range(4):
        rows = slice(D * j, D * (j + 1))
        dj = nn(R.proj[l, 128 * j:128 * (j + 1)], outl)
        parts.append(low(pad8(dj[0:D] * gelu_slope(R.pre[l, rows], R.half[l, rows]))))
    prel = jnp.concatenate(parts, axis=0)
    dn = nn(R.fc[l], prel)[0:D]
    xh = R.xh2[l]
    add_bias(R, l, G2, dn * xh)
    add_bias(R, l, B2, dn)
    dmid = normed_back(dn * tile4(R.bc[l, G2]), xh, R.r2[l]) + dout
    midl = low(pad8(dmid))
    add_bias(R, l, OB, dmid)
    da = nn(R.out[l], midl)[0:D]

    turn(R, 0, outl)
    turn(R, 1, R.n2[l])
    turn(R, 2, midl)

    def a_proj(j):
        def run():
            rows = slice(256 * j, 256 * (j + 1))
            R.a_proj[l, rows] += nn(R.inner[l, rows], R.turned[0])
        return run

    def a_fc(j):
        def run():
            rows = slice(256 * j, 256 * (j + 1))
            R.a_fc[l, rows] += nn(prel[rows], R.turned[1])
        return run

    def a_out():
        R.a_out[l] += nn(R.att[l], R.turned[2])

    return dmid, da, [a_proj(0), a_proj(1), a_fc(0), a_fc(1), a_out]


def att_bwd(R, l, s, dmid, da, between):
    turn(R, 3, R.n1[s])
    dq, dk, dv = attend_back(R, s, da, between)
    mixl = jnp.concatenate([low(pad8(dq)), low(pad8(dk)), low(pad8(dv))], axis=0)
    dn = nn(R.qkv[l], mixl)[0:D]
    add_bias(R, l, QB, dq)
    add_bias(R, l, VB, dv)
    R.a_qkv[l] += nn(mixl, R.turned[3])
    xh = R.xh1[s]
    add_bias(R, l, G1, dn * xh)
    add_bias(R, l, B1, dn)
    return normed_back(dn * tile4(R.bc[l, G1]), xh, R.r1[s]) + dmid


def embed_bwd(R, obs, c, dx):
    R.a_x[0:D] += fold4(dx)
    lanes = iota((D, 128), 1)
    tiles = []
    gs = [dx[:, 128 * g:128 * (g + 1)] for g in range(CG)]
    for t in range(CG):
        a = shifted(gs[t], -8 * t)
        b = shifted(gs[t + 1], 120 - 8 * t) if t + 1 < CG else jnp.zeros((D, 128), F32)
        tiles.append(jnp.where(lanes < GT - 8 * t, a, b))
    gl = low(pad8(jnp.concatenate(tiles, axis=1)))
    R.a_obs[...] += nn(gl, jnp.concatenate(obs, axis=1))


def zero_grads(R):
    for name in ("a_qkv", "a_out", "a_fc", "a_proj", "a_bias", "a_obs", "a_x", "a_fin", "a_head", "a_hb", "loss"):
        ref = getattr(R, name)
        ref[...] = jnp.zeros(ref.shape, F32)


HIGH = lax.Precision.HIGHEST


LATE = 364
EARLY_ROWS = (OB, G2, B2, PB)


def lane_sums(v):
    return jnp.sum(v.T, axis=0, keepdims=True)


def pack_vectors(R, rg, l, which):
    b = BASE + LROW * l
    for i in which:
        rg[pl.ds(b + VROWS[i], 1), :] = lane_sums(R.a_bias[l, i])


def pack_early(R, rg, l):
    b = BASE + LROW * l
    rg[pl.ds(b + 364, D), :] = R.a_out[l, 0:D]
    for j in range(4):
        fc = R.a_fc[l, 128 * j:128 * (j + 1), :].T
        rg[pl.ds(b + 487 + j, D, stride=4), :] = fc[0:D]
        rg[pl.ds(b + 967 + j, 1), :] = fc[D:D + 1]
        rg[pl.ds(b + 971 + D * j, D), :] = R.a_proj[l, 128 * j:128 * j + D, :]
    pack_vectors(R, rg, l, EARLY_ROWS)


def pack_late(R, rg, l):
    b = BASE + LROW * l
    for j in range(3):
        rg[pl.ds(b + 2 + j, D, stride=3), :] = R.a_qkv[l, 128 * j:128 * (j + 1), :].T[0:D]
    pack_vectors(R, rg, l, (G1, B1, QB, VB))


def pack_embed(R, rg):
    for f in range(OBS // 128):
        rg[128 * f:128 * (f + 1), :] = R.a_obs[:, 128 * f:128 * (f + 1)].T
    slot, lane = iota((32, 128), 0), iota((32, 128), 1)
    sel = jnp.where((slot == 0) | (lane % WIN == slot - 1), 1.0, 0.0)
    sel = jnp.where(lane < GT, sel, 0.0)
    rows = nt(sel, R.a_x[...], HIGH)
    rg[pl.ds(OBS, 1 + WIN), :] = rows[0:1 + WIN]


def pack_head(R, rg):
    for i in range(2):
        rg[pl.ds(HEAD + i, 1), :] = lane_sums(R.a_fin[i])
    lanes8 = iota((8, 128), 1)
    grad = R.a_head[...]
    R.hc[...] = jnp.where(iota((128, 128), 1) < 32, grad, 0.0)
    R.ho[...] = jnp.where(iota((128, 128), 1) < OFFS, shifted(grad, -32), 0.0)
    c0 = HEAD + 2
    o0 = c0 + 32

    def put(phases, src, rows_n, stride, width, count):
        acc = [jnp.zeros((rows_n, 128), F32) for _ in range(count + 1)]
        lanes = iota((rows_n, 128), 1)
        for p, a, s in phases:
            v = src[pl.ds(p, rows_n, stride=stride), :]
            first = shifted(v, s)
            if s + width > D:
                acc[a] = acc[a] + jnp.where((lanes >= s) & (lanes < D), first, 0.0)
                acc[a + 1] = acc[a + 1] + jnp.where(lanes < s + width - D, shifted(v, s - D), 0.0)
            else:
                acc[a] = acc[a] + first
        return acc

    acc = put(code_phases(), R.hc, 8, 15, 32, 4)
    for a in range(4):
        rg[pl.ds(c0 + a, 8, stride=4), :] = acc[a]
    hb = lane_sums(R.a_hb[...])
    lane1 = iota((1, 128), 1)
    rg[pl.ds(o0, 48), :] = jnp.zeros((48, 128), F32)
    acc = put(off_phases(), R.ho, 5, 24, OFFS, 7)
    for a in range(7):
        rg[pl.ds(o0 + a, 5, stride=7), :] = acc[a]
    rg[pl.ds(o0 + 7, 5, stride=7), :] = rg[pl.ds(o0 + 7, 5, stride=7), :] + acc[7]
    rg[pl.ds(o0, 1), :] = rg[pl.ds(o0, 1), :] + jnp.where(lane1 < 32, hb, 0.0)
    a, s = (D * OFFS + 32) // D, (D * OFFS + 32) % D
    ob = jnp.where(lane1 < OFFS, shifted(hb, -32), 0.0)
    rg[pl.ds(o0 + a, 1), :] = rg[pl.ds(o0 + a, 1), :] + shifted(ob, s)


MESH = pl.DeviceIdType.MESH


def round_up(n, m):
    return -(-n // m) * m


class Plan:
    def __init__(self, feats, toks, shard, tok_rows):
        self.feats, self.toks, self.chips = feats, toks, toks // 2
        self.shard = shard
        self.block = round_up(-(-(shard + 112) // D), 16)
        self.flat_rows = self.block // 16 * 15
        self.local = round_up(-(-shard // 1024), 1) * 8
        self.work = round_up(max(self.flat_rows, self.local + 1), 8)
        self.own_rows = tok_rows // feats
        self.chunks = self.own_rows // CT
        self.early = [f for f in range(feats) if shard * toks * f // D >= BASE + LATE]
        self.grid = round_up(-(-(shard * feats * toks) // D) + self.block, 8)


def comm_scratch(P):
    dma = pltpu.SemaphoreType.DMA
    B, C, Fn = P.block, P.chips, P.feats
    return dict(
        rg=pltpu.VMEM((P.grid, 128), F32),
        ob=pltpu.VMEM((P.chunks, Fn, L, 128), BF),
        pg=pltpu.VMEM((2, C, Fn, B, 128), BF),
        loc=pltpu.VMEM((P.work, 128), F32),
        rblk=pltpu.VMEM((B, 128), F32),
        codes_in=pltpu.VMEM((BOOKS, P.own_rows), jnp.int32),
        act_in=pltpu.VMEM((OFFS, P.own_rows), F32),
        val_in=pltpu.VMEM((OFFS, P.own_rows), jnp.int32),
        tz=pltpu.VMEM((2, Fn, 8, 128), F32),
        tc=pltpu.VMEM((2, C, 8, 128), F32),
        ts=pltpu.VMEM((2, 2, 8, 128), F32),
        sb1=pltpu.VMEM((C, Fn, B, 128), F32),
        rb1=pltpu.VMEM((C, Fn, B, 128), F32),
        sb2=pltpu.VMEM((C, Fn, B, 128), BF),
        rb2=pltpu.VMEM((C, Fn, B, 128), BF),
        col=pltpu.VMEM((Fn, B, 128), F32),
        sb3=pltpu.VMEM((Fn, B, 128), F32),
        rb3=pltpu.VMEM((Fn, B, 128), F32),
        s_p1=dma((2, Fn)), s_p2=dma((2, C)), s_p3=dma((2, C)),
        s_tz=dma((2, 2, Fn)), s_tc=dma((2, 2, C)), s_ts=dma((2, 2)),
        s_ob=dma((2, 2 * P.chunks, Fn)),
        s_own=dma((P.chunks,)),
        s_in=dma((3,)),
        s_r1=dma((2, 2, C)), s_r2=dma((2, Fn, C)), s_r3=dma((2, Fn)),
    )


def to_rows(loc, rblk, delta, P):
    v = loc[...]
    lanes = iota(v.shape, 1)
    moved = pltpu.roll(v, delta, 1)
    loc[...] = jnp.where(lanes >= delta, moved, pltpu.roll(moved, 1, 0))
    n = P.block // 16
    lane = iota((n, 128), 1)
    for j in range(16):
        if j < 15:
            a = shifted(loc[pl.ds(j, n, stride=15), :], 8 * j)
        if j > 0:
            b = shifted(loc[pl.ds(j - 1, n, stride=15), :], 8 * j)
            a = jnp.where(lane < 8 * j, b, a) if j < 15 else b
        rblk[pl.ds(j, n, stride=16), :] = jnp.where(lane < D, a, 0.0)


def from_rows(rblk, loc, delta, P):
    n = P.block // 16
    lane = iota((n, 128), 1)
    loc[...] = jnp.zeros(loc.shape, F32)
    for i in range(15):
        a = shifted(rblk[pl.ds(i, n, stride=16), :], -8 * i)
        b = shifted(rblk[pl.ds(i + 1, n, stride=16), :], D - 8 * i)
        loc[pl.ds(i, n, stride=15), :] = jnp.where(lane < D - 8 * i, a, b)
    v = loc[...]
    lanes = iota(v.shape, 1)
    moved = pltpu.roll(v, lax.rem(128 - delta, 128), 1)
    v = jnp.where(lanes < 128 - delta, moved, pltpu.roll(moved, P.work - 1, 0))
    return v[0:P.local]


def step_kernel(P, names, master, obs, counts, codes, actions, valid, grad, sums, *scratch):
    R = Refs()
    for name, ref in zip(names, scratch):
        setattr(R, name, ref)
    Fn, C, B = P.feats, P.chips, P.block
    feat = lax.axis_index("feat")
    tok = lax.axis_index("tok")
    chip = tok // 2
    core = tok % 2
    me = feat * P.toks + tok
    delta = lax.rem(me * P.shard, D)

    def z_peer(i):
        return lax.rem(feat + i, Fn)

    def z_from(i):
        return lax.rem(feat + Fn - i, Fn)

    def c_peer(i):
        return lax.rem(chip + i, C)

    def c_from(i):
        return lax.rem(chip + C - i, C)

    def to_z(i):
        return (z_peer(i), tok)

    def to_c(i):
        return (feat, 2 * c_peer(i) + core)

    sibling = (feat, 2 * chip + 1 - core)

    def send(src, dst, sems, at, dev):
        return pltpu.make_async_remote_copy(
            src_ref=src, dst_ref=dst, send_sem=sems.at[(0,) + at], recv_sem=sems.at[(1,) + at],
            device_id=dev, device_id_type=MESH)

    n = P.own_rows
    ins = []
    for i, (src, dst) in enumerate(((codes, R.codes_in), (actions, R.act_in), (valid, R.val_in))):
        ins.append(pltpu.make_async_copy(src.at[:, pl.ds(pl.multiple_of(feat * n, 128), n)], dst, R.s_in.at[i]))
        ins[-1].start()

    barrier = pltpu.get_barrier_semaphore()
    peers = [to_z(i) for i in range(1, Fn)] + [to_c(i) for i in range(1, C)] + [sibling]
    for dev in peers:
        pl.semaphore_signal(barrier, inc=1, device_id=dev, device_id_type=MESH)

    R.loc[...] = jnp.zeros(R.loc.shape, F32)
    whole = P.shard // 1024
    R.loc[0:8 * whole, :] = master[pl.ds(0, 1024 * whole)].reshape(8 * whole, 128)
    rest = P.shard - 1024 * whole
    last = jnp.concatenate([master[pl.ds(1024 * whole, rest)], jnp.zeros((1024 - rest,), F32)])
    R.loc[8 * whole:8 * whole + 8, :] = last.reshape(8, 128)
    to_rows(R.loc, R.rblk, delta, P)
    R.pg[core, chip, feat] = low(R.rblk[...])
    pl.semaphore_wait(barrier, len(peers))

    p1 = []
    for i in range(1, Fn):
        blk = R.pg.at[core, chip, feat]
        p1.append(send(blk, blk, R.s_p1, (i,), to_z(i)))
        p1[-1].start()

    half = CT // 2

    def obs_copies(p):
        cps = []
        for i in range(1, Fn):
            src = obs.at[pl.ds(pl.multiple_of(z_peer(i) * n + half * p, 16), half), :]
            dst = R.ob.at[p // 2, feat, pl.ds(pl.multiple_of(half * (p % 2), 16), half), :]
            cps.append(send(src, dst, R.s_ob, (p, i), to_z(i)))
        return cps

    def start_obs(p):
        for cp in obs_copies(p):
            cp.start()

    own = []
    for c in range(P.chunks):
        src = obs.at[pl.ds(pl.multiple_of(feat * n + CT * c, 16), CT), :]
        own.append(pltpu.make_async_copy(src, R.ob.at[c, feat, pl.ds(0, CT), :], R.s_own.at[c]))
        own[-1].start()
    for cp in ins:
        cp.wait()
    zero_grads(R)
    for c in range(P.chunks):
        for f in range(Fn):
            R.ob[c, f, CT:L, :] = jnp.zeros((L - CT, 128), BF)
    live_n, valid_n = prep_tokens(R, counts, R.codes_in, R.act_in, R.val_in, feat, P.chunks)

    def two_rows(a, b):
        return jnp.concatenate([jnp.broadcast_to(a, (1, 128)), jnp.broadcast_to(b, (1, 128)),
                                jnp.zeros((6, 128), F32)], axis=0)

    def z_copies(w):
        return [send(R.tz.at[w, feat], R.tz.at[w, feat], R.s_tz.at[w], (i,), to_z(i)) for i in range(1, Fn)]

    def c_copies(w):
        return [send(R.tc.at[w, chip], R.tc.at[w, chip], R.s_tc.at[w], (i,), to_c(i)) for i in range(1, C)]

    def s_copies(w):
        return [send(R.ts.at[w, core], R.ts.at[w, core], R.s_ts.at[w], (), sibling)]

    def start_all(cps):
        for cp in cps:
            cp.start()

    def total(ref, w, count):
        v = ref[w, 0]
        for i in range(1, count):
            v = v + ref[w, i]
        return v

    def wait_all(cps):
        for cp in cps:
            cp.wait()

    R.tz[0, feat] = two_rows(live_n, valid_n)
    start_all(z_copies(0))
    wait_all(p1)
    start_obs(0)
    start_obs(1)
    p2 = []
    for i in range(1, C):
        blk = R.pg.at[core, chip]
        p2.append(send(blk, blk, R.s_p2, (i,), to_c(i)))
        p2[-1].start()
    p3 = [send(R.pg.at[core, chip], R.pg.at[core, chip], R.s_p3, (0,), sibling)]
    p3[0].start()
    wait_all(z_copies(0))
    R.tc[0, chip] = total(R.tz, 0, Fn)
    start_all(c_copies(0))
    for i in range(1, C):
        p2[i - 1].wait_recv()
        blk = R.pg.at[core, c_from(i)]
        p3.append(send(blk, blk, R.s_p3, (i,), sibling))
        p3[-1].start()
    wait_all(c_copies(0))
    R.ts[0, core] = total(R.tc, 0, C)
    start_all(s_copies(0))
    for cp in p2:
        cp.wait_send()
    wait_all(p3)
    R.rg[0:8, :] = jnp.zeros((8, 128), F32)

    def place(d, _):
        r0 = (P.shard * d) // D
        f, t = d // P.toks, d % P.toks
        blk = R.pg[t % 2, t // 2, f].astype(F32)
        before = R.rg[pl.ds(r0, 1), :]
        R.rg[pl.ds(r0, B), :] = blk
        R.rg[pl.ds(r0, 1), :] = blk[0:1] + before
        return 0

    lax.fori_loop(0, Fn * P.toks, place, 0)
    prep_weights(R.rg, R)
    wait_all(s_copies(0))
    counted = total(R.ts, 0, 2)
    live_total = counted[0:1, 0:1]
    valid_total = counted[1:2, 0:1]

    for cp in own:
        cp.wait()


    def rows_of(f, ch, co):
        return (P.shard * (f * P.toks + 2 * ch + co)) // D

    early = P.early[0] if P.early else Fn
    planes = [slice(early, Fn), slice(0, early)]

    def r1_copy(w, i):
        at = pl.ds(planes[w].start, planes[w].stop - planes[w].start)
        return send(R.sb1.at[i, at], R.rb1.at[i, at], R.s_r1.at[w], (i,), sibling)

    def r2_copy(f, i):
        return send(R.sb2.at[i, f], R.rb2.at[i, f], R.s_r2.at[:, f], (i,), to_c(i))

    def r3_copy(i):
        return send(R.sb3.at[i], R.rb3.at[i], R.s_r3, (i,), to_z(i))

    order = list(range(1, C)) + [0]

    def sum_cores(w):
        for i in order:
            for f in range(planes[w].start, planes[w].stop):
                R.sb1[i, f] = R.rg[pl.ds(rows_of(f, c_peer(i), 1 - core), B), :]
            r1_copy(w, i).start()

    def sum_chips(w):
        for i in order:
            r1_copy(w, i).wait_recv()
            for f in reversed(range(planes[w].start, planes[w].stop)):
                v = R.rg[pl.ds(rows_of(f, c_peer(i), core), B), :] + R.rb1[i, f]
                if i:
                    R.sb2[i, f] = low(v)
                    r2_copy(f, i).start()
                else:
                    R.col[f] = v

    def sum_column(f):
        v = R.col[f]
        for i in range(1, C):
            r2_copy(f, i).wait_recv()
            v = v + R.rb2[i, f].astype(F32)
        R.col[f] = v
        for i in range(1, Fn):
            @pl.when(z_peer(i) == f)
            def _():
                R.sb3[i] = v
                r3_copy(i).start()

    def chunk(c, _):
        for p in (2 * c, 2 * c + 1):
            for cp in obs_copies(p):
                cp.wait_recv()

        @pl.when(c + 1 < P.chunks)
        def _():
            start_obs(2 * c + 2)
            start_obs(2 * c + 3)

        R.x[...] = embed(R, [R.ob[c, f, 0:CT, :] for f in range(Fn)], c)

        def lay(l, _):
            R.x[...] = layer_fwd(R, l, c, l, R.x[...])
            return 0

        lax.fori_loop(0, LAYERS, lay, 0)

        dx = head_step(R, c, R.x[...], live_total, valid_total)
        dmid, da, rest = mlp_bwd(R, 1, dx)
        R.x[...] = att_bwd(R, 1, 1, dmid, da, rest)
        dmid, da, rest = mlp_bwd(R, 0, R.x[...])
        R.dmid[...] = dmid
        R.da[...] = da
        for run in rest:
            run()

        @pl.when(c == P.chunks - 1)
        def _():
            R.rg[pl.ds(HEAD + 32, P.grid - HEAD - 32), :] = jnp.zeros((P.grid - HEAD - 32, 128), F32)
            pack_head(R, R.rg)
            pack_late(R, R.rg, 1)
            for l in range(LAYERS):
                pack_early(R, R.rg, l)
            R.ts[1, core] = two_rows(jnp.sum(R.loss[0], keepdims=True), jnp.sum(R.loss[1], keepdims=True))
            start_all(s_copies(1))
            sum_cores(0)

        dx = att_bwd(R, 0, 0, R.dmid[...], R.da[...], [])

        @pl.when(c == P.chunks - 1)
        def _():
            sum_chips(0)
            wait_all(s_copies(1))
            R.tc[1, chip] = total(R.ts, 1, 2)
            start_all(c_copies(1))

        embed_bwd(R, [R.ob[c, f] for f in range(Fn)], c, dx)
        return 0

    lax.fori_loop(0, P.chunks, chunk, 0)
    pack_embed(R, R.rg)
    pack_late(R, R.rg, 0)
    sum_cores(1)
    sum_chips(1)
    wait_all(c_copies(1))
    R.tz[1, feat] = total(R.tc, 1, C)
    start_all(z_copies(1))
    for f in reversed(range(Fn)):
        sum_column(f)
    for i in range(1, Fn):
        r3_copy(i).wait_recv()
    v = R.col[feat]
    for i in range(1, Fn):
        v = v + R.rb3[i]
    R.rblk[...] = v
    grad[...] = from_rows(R.rblk, R.loc, delta, P)
    wait_all(z_copies(1))
    lost = total(R.tz, 1, Fn)
    sums[...] = jnp.concatenate([lost[0:1], counted[0:1], lost[1:2], counted[1:2], jnp.zeros((4, 128), F32)], axis=0)
    for p in range(2 * P.chunks):
        for cp in obs_copies(p):
            cp.wait_send()
    for w in range(2):
        for i in range(C):
            r1_copy(w, i).wait_send()
    for i in range(1, C):
        for f in range(Fn):
            r2_copy(f, i).wait_send()
    for i in range(1, Fn):
        r3_copy(i).wait_send()


def solution(mesh):
    feats, toks = mesh.shape["feat"], mesh.shape["tok"]

    def shards(master, first, second, obs, counts, codes, actions, valid):
        P_ = Plan(feats, toks, master.shape[0], obs.shape[0])
        scratch = dict(scratch_list(P_.chunks))
        scratch.update(comm_scratch(P_))
        vmem = pl.BlockSpec(memory_space=pltpu.VMEM)
        hbm = pl.BlockSpec(memory_space=pl.ANY)
        grad, sums = pl.pallas_call(
            functools.partial(step_kernel, P_, list(scratch)),
            out_shape=(jax.ShapeDtypeStruct((P_.local, 128), F32), jax.ShapeDtypeStruct((8, 128), F32)),
            in_specs=[vmem, hbm, vmem, hbm, hbm, hbm],
            out_specs=(vmem, vmem),
            scratch_shapes=list(scratch.values()),
            compiler_params=pltpu.CompilerParams(
                collective_id=0, has_side_effects=True, vmem_limit_bytes=60 * 2 ** 20),
        )(master, obs, counts.T, codes.T, actions, valid)
        grad = grad.reshape(-1)[:P_.shard]
        f_new = BETA_ONE * first + (1.0 - BETA_ONE) * grad
        s_new = BETA_TWO * second + (1.0 - BETA_TWO) * grad * grad
        f_hat = f_new / (1.0 - BETA_ONE ** STEP_NO)
        s_hat = s_new / (1.0 - BETA_TWO ** STEP_NO)
        new = master - LEARN_RATE * (f_hat / (jnp.sqrt(s_hat) + ADAM_EPS) + DECAY_RATE * master)
        return new, f_new, s_new, sums[0:4, 0]

    weights = PSpec(("feat", "tok"))
    return jax.shard_map(
        shards, mesh=mesh,
        in_specs=(weights, weights, weights, PSpec("tok", "feat"), PSpec("tok", None), PSpec("tok", None),
                  PSpec(None, "tok"), PSpec(None, "tok")),
        out_specs=(weights, weights, weights, PSpec()), check_vma=False)
```

```python
import functools
import math

import jax
import jax.numpy as jnp
from jax import lax
from jax.experimental import pallas as pl
from jax.experimental.pallas import tpu as pltpu
from jax.sharding import PartitionSpec as PSpec

D = 120
H = 6
HD = 20
FF = 480
OBS = 512
LAYERS = 2
CAMS = 3
BOOKS = 2
CODES = 16
SPAN = 5
ACT = 7
WIN = 30
OFFS = SPAN * ACT
NORM_EPS = 1e-05
STEP_NO = 10
BETA_ONE = 0.9
BETA_TWO = 0.999
ADAM_EPS = 1e-08
DECAY_RATE = 0.1
LEARN_RATE = 0.05
GW = 4
GT = GW * WIN
CG = 4
L = CG * 128
CT = CG * GT
F32 = jnp.float32
BF = jnp.bfloat16
SCALE = HD ** (-0.5)
LROW = 2 * 1 + 3 * D + 2 + D + 1 + 2 + 4 * D + 4 + 4 * D + 1
BASE = OBS + 1 + WIN
HEAD = BASE + LAYERS * LROW
NV = 13
VROWS = [0, 1, 362, 363, 484, 485, 486, 967, 968, 969, 970, 1451]
(G1, B1, QB, VB, OB, G2, B2, FB0, FB1, FB2, FB3, PB) = range(12)


def nn(a, b):
    return lax.dot_general(a, b, (((1,), (0,)), ((), ())), preferred_element_type=F32)


def nt(a, b, precision=None):
    return lax.dot_general(a, b, (((1,), (1,)), ((), ())), preferred_element_type=F32, precision=precision)


def low(v):
    return v.astype(BF)


def pad8(v):
    return jnp.concatenate([v, jnp.zeros((8, v.shape[1]), v.dtype)], axis=0)


def tile4(v):
    return jnp.concatenate([v] * CG, axis=1)


def fold4(v):
    out = v[:, 0:128]
    for g in range(1, CG):
        out = out + v[:, 128 * g:128 * (g + 1)]
    return out


def iota(shape, axis):
    return lax.broadcasted_iota(jnp.int32, shape, axis)


def slab_at(h):
    return 20 * h - (4 if h % 2 else 0)


def head_stack(v):
    rows = iota((8, 128), 0)
    cols = []
    for h in range(H):
        a = slab_at(h)
        if h % 2 == 0:
            parts = [v[a:a + 16], jnp.where(rows < 4, v[a + 16:a + 24], 0.0)]
        else:
            parts = [jnp.where(rows >= 4, v[a:a + 8], 0.0), v[a + 8:a + 24]]
        if a > 0:
            parts = [jnp.zeros((a, 128), F32)] + parts
        if a + 24 < 128:
            parts = parts + [jnp.zeros((128 - a - 24, 128), F32)]
        cols.append(jnp.concatenate(parts, axis=0))
    return jnp.concatenate(cols, axis=1)


def join_slabs(slabs):
    rows = iota((8, 128), 0)
    parts = []
    for p in range(3):
        a, b = slabs[2 * p], slabs[2 * p + 1]
        parts += [a[0:16], jnp.where(rows < 4, a[16:24], b[0:8]), b[8:24]]
    return jnp.concatenate(parts, axis=0)


def slabs_of(v):
    return [v[slab_at(h):slab_at(h) + 24] for h in range(H)]


def hi_lo(v):
    hi = low(v)
    return hi, low(v - hi.astype(F32))


def normed(x):
    mean = jnp.sum(x, axis=0, keepdims=True) * (1.0 / D)
    c = x - mean
    var = jnp.sum(c * c, axis=0, keepdims=True) * (1.0 / D)
    r = lax.rsqrt(var + NORM_EPS)
    return c * r, r


def normed_back(d, xh, r):
    m0 = jnp.sum(d, axis=0, keepdims=True) * (1.0 / D)
    m1 = jnp.sum(d * xh, axis=0, keepdims=True) * (1.0 / D)
    return r * (d - m0 - xh * m1)


GA = math.sqrt(2.0 / math.pi)
GB = 0.044715


def gelu_half(x):
    return 0.5 + 0.5 * jnp.tanh(x * (GA + (GA * GB) * (x * x)))


def gelu_slope(x, s):
    return s + (x * s) * (1.0 - s) * (2.0 * GA + (6.0 * GA * GB) * (x * x))


LOG2E = math.log2(math.e)
BIG = 1e30


class Refs:
    pass


def scratch_list(chunks):
    groups = chunks * CG
    return dict(
        w_obs=pltpu.VMEM((OBS, 128), BF),
        posb=pltpu.VMEM((GT, 128), F32),
        qkv_t=pltpu.VMEM((LAYERS, 384, 128), BF),
        qkv=pltpu.VMEM((LAYERS, 128, 384), BF),
        out_t=pltpu.VMEM((LAYERS, 128, 128), BF),
        out=pltpu.VMEM((LAYERS, 128, 128), BF),
        fc_t=pltpu.VMEM((LAYERS, 512, 128), BF),
        fc=pltpu.VMEM((LAYERS, 128, 512), BF),
        proj_t=pltpu.VMEM((LAYERS, 128, 512), BF),
        proj=pltpu.VMEM((LAYERS, 512, 128), BF),
        head_t=pltpu.VMEM((72, 128), BF),
        head=pltpu.VMEM((128, 128), BF),
        vec=pltpu.VMEM((32, 128), F32),
        bc=pltpu.VMEM((LAYERS, 12, GT, 128), F32),
        bcf=pltpu.VMEM((2, GT, 128), F32),
        bch=pltpu.VMEM((72, 128), F32),
        hc=pltpu.VMEM((128, 128), F32),
        ho=pltpu.VMEM((128, 128), F32),
        cnt=pltpu.VMEM((16, 256), F32),
        live=pltpu.VMEM((chunks, 1, L), F32),
        act=pltpu.VMEM((chunks, 40, L), F32),
        val=pltpu.VMEM((chunks, 40, L), F32),
        code=pltpu.VMEM((chunks, 2, L), F32),
        x=pltpu.VMEM((D, L), F32),
        dmid=pltpu.VMEM((D, L), F32),
        da=pltpu.VMEM((D, L), F32),
        xh1=pltpu.VMEM((LAYERS, D, L), F32),
        r1=pltpu.VMEM((LAYERS, 1, L), F32),
        xh2=pltpu.VMEM((LAYERS, D, L), F32),
        r2=pltpu.VMEM((LAYERS, 1, L), F32),
        n1=pltpu.VMEM((LAYERS, 128, L), BF),
        n2=pltpu.VMEM((LAYERS, 128, L), BF),
        att=pltpu.VMEM((LAYERS, 128, L), BF),
        q_low=pltpu.VMEM((LAYERS, H, 24, L), BF),
        k_low=pltpu.VMEM((LAYERS, H, 24, L), BF),
        v_low=pltpu.VMEM((LAYERS, 128, L), BF),
        rsum=pltpu.VMEM((LAYERS, H, 1, L), F32),
        prob=pltpu.VMEM((LAYERS, CG, GT, H * 128), F32),
        prob_low=pltpu.VMEM((LAYERS, CG, 128, H * 128), BF),
        k_mask=pltpu.VMEM((48, 128), BF),
        q_mask=pltpu.VMEM((48, 128), BF),
        dead=pltpu.VMEM((groups, 8, 128), F32),
        pre=pltpu.VMEM((LAYERS, FF, L), F32),
        half=pltpu.VMEM((LAYERS, FF, L), F32),
        inner=pltpu.VMEM((LAYERS, 512, L), BF),
        a_qkv=pltpu.VMEM((LAYERS, 384, 128), F32),
        ds_t=pltpu.VMEM((CG * H // 2, 128, 256), BF),
        turned=pltpu.VMEM((5, L, 128), BF),
        a_out=pltpu.VMEM((LAYERS, 128, 128), F32),
        a_fc=pltpu.VMEM((LAYERS, 512, 128), F32),
        a_proj=pltpu.VMEM((LAYERS, 512, 128), F32),
        a_bias=pltpu.VMEM((LAYERS, 12, 128, 128), F32),
        a_obs=pltpu.VMEM((128, 512), F32),
        a_x=pltpu.VMEM((128, 128), F32),
        a_fin=pltpu.VMEM((2, 128, 128), F32),
        a_head=pltpu.VMEM((128, 128), F32),
        a_hb=pltpu.VMEM((128, 128), F32),
        loss=pltpu.VMEM((2, 8, 128), F32),
    )


def code_phases():
    for p in range(15):
        yield p, (32 * p) // D, (32 * p) % D


def off_phases():
    for p in range(24):
        yield p, (35 * p + 32) // D, (35 * p + 32) % D


def shifted(v, by):
    by %= 128
    return v if by == 0 else pltpu.roll(v, by, 1)


def take_phase(load, a, s, width, rows):
    lanes = iota((rows, 128), 1)
    first = shifted(load(a), -s)
    if s + width > D:
        second = shifted(load(a + 1), D - s)
        first = jnp.where(lanes < D - s, first, second)
    return jnp.where(lanes < width, first, 0.0)


def with_bias(w, bias):
    if bias is not None:
        w = jnp.where(iota((128, 128), 0) == D, bias, w)
    return low(w.T)


def ones8(v):
    return jnp.concatenate([v, jnp.where(iota((8, v.shape[1]), 0) == 0, 1.0, 0.0)], axis=0)


def prep_weights(rg, R):
    R.w_obs[...] = low(rg[0:OBS, :])
    for w in range(GW):
        R.posb[pl.ds(WIN * w, WIN), :] = rg[OBS + 1:OBS + 1 + WIN, :] + rg[OBS:OBS + 1, :]
    R.vec[...] = jnp.zeros((32, 128), F32)
    for l in range(LAYERS):
        b = BASE + LROW * l
        for j in range(3):
            w = pad8(rg[pl.ds(b + 2 + j, D, stride=3), :])
            R.qkv[l, :, 128 * j:128 * (j + 1)] = low(w)
            R.qkv_t[l, 128 * j:128 * (j + 1), :] = with_bias(w, None if j == 1 else rg[pl.ds(b + 362 + j // 2, 1), :])
        w = pad8(rg[pl.ds(b + 364, D), :])
        R.out[l] = low(w)
        R.out_t[l] = with_bias(w, rg[pl.ds(b + 484, 1), :])
        for j in range(4):
            w = pad8(rg[pl.ds(b + 487 + j, D, stride=4), :])
            R.fc[l, :, 128 * j:128 * (j + 1)] = low(w)
            R.fc_t[l, 128 * j:128 * (j + 1), :] = with_bias(w, rg[pl.ds(b + 967 + j, 1), :])
            w = pad8(rg[pl.ds(b + 971 + D * j, D), :])
            R.proj[l, 128 * j:128 * (j + 1), :] = low(w)
            R.proj_t[l, :, 128 * j:128 * (j + 1)] = with_bias(w, None if j else rg[pl.ds(b + 1451, 1), :])
        for i, r in enumerate(VROWS):
            R.vec[pl.ds(12 * l + i, 1), :] = rg[pl.ds(b + r, 1), :]
    R.vec[24:26, :] = rg[pl.ds(HEAD, 2), :]
    R.hc[...] = jnp.zeros((128, 128), F32)
    R.ho[...] = jnp.zeros((128, 128), F32)
    c0 = HEAD + 2
    for p, a, s in code_phases():
        R.hc[pl.ds(p, 8, stride=15), :] = take_phase(
            lambda i: rg[pl.ds(c0 + i, 8, stride=4), :], a, s, 32, 8)
    o0 = c0 + 32
    for p, a, s in off_phases():
        R.ho[pl.ds(p, 5, stride=24), :] = take_phase(
            lambda i: rg[pl.ds(o0 + i, 5, stride=7), :], a, s, OFFS, 5)
    hw = R.hc[...] + shifted(R.ho[...], 32)
    R.head[...] = low(hw)
    R.head_t[...] = low(hw.T[0:72])
    lanes = iota((1, 128), 1)
    hb = jnp.where(lanes < 32, rg[pl.ds(o0, 1), :], 0.0)
    a, s = (D * OFFS + 32) // D, (D * OFFS + 32) % D
    ob = take_phase(lambda i: rg[pl.ds(o0 + i, 1), :], a, s, OFFS, 1)
    R.vec[26:27, :] = hb + shifted(ob, 32)
    columns = jnp.concatenate([R.vec[...], jnp.zeros((96, 128), F32)], axis=0).T
    for l in range(LAYERS):
        for i in range(12):
            R.bc[l, i] = jnp.broadcast_to(columns[0:D, 12 * l + i:12 * l + i + 1], (D, 128))
    for i in range(2):
        R.bcf[i] = jnp.broadcast_to(columns[0:D, 24 + i:25 + i], (D, 128))
    R.bch[...] = jnp.broadcast_to(columns[0:72, 26:27], (72, 128))


def spread_groups(v, groups, width):
    rows = v.shape[0]
    lanes = iota((rows, 128), 1)
    out = []
    for g in range(groups):
        t, o = (GT * g) // 128, (GT * g) % 128
        a = shifted(v[:, 128 * t:128 * (t + 1)], -o)
        if o + GT > 128:
            b = shifted(v[:, 128 * (t + 1):128 * (t + 2)], -o)
            a = jnp.where(lanes < 128 - o, a, b)
        out.append(jnp.where(lanes < GT, a, 0))
    return out


def prep_tokens(R, counts, codes, actions, valid, feat, chunks):
    groups = chunks * CG
    wins = counts.shape[1]
    R.cnt[...] = jnp.zeros(R.cnt.shape, F32)
    R.cnt[0:WIN // CAMS, :] = counts[...].astype(F32)
    k = iota((GT, 16), 0)
    step = (k % WIN) // CAMS
    sel = jnp.where(step == iota((GT, 16), 1), 1.0, 0.0)
    x = nn(low(sel), low(R.cnt[...]))
    y = jnp.where(iota((GT, wins), 1) % GW == iota((GT, wins), 0) // WIN, x, 0.0)
    pick = jnp.where(iota((wins, 128), 0) // GW == iota((wins, 128), 1) + groups * feat, 1.0, 0.0)
    z = nn(low(y), low(pick))
    kk = iota((GT, 128), 0)
    alive = jnp.where((kk % CAMS).astype(F32) < z, 1.0, 0.0)
    steps = WIN // CAMS
    j, at = iota((48, 128), 0), iota((48, 128), 1)
    own = (at // WIN == j // steps) & ((at % WIN) // CAMS == j % steps) & (at < GT)
    R.k_mask[...] = low(jnp.where(own, 1.0, 0.0))
    may = (at // WIN == j // steps) & ((at % WIN) // CAMS >= j % steps)
    R.q_mask[...] = low(jnp.where(may | (j >= GW * steps), 0.0, -BIG))
    rows = pad8(alive).T
    for g in range(groups):
        R.live[g // CG, :, 128 * (g % CG):128 * (g % CG + 1)] = rows[g:g + 1, :]
        R.dead[g] = jnp.where(iota((8, 128), 0) == 0, 1.0 - rows[g:g + 1, :], 0.0)
    for name, src in (("code", codes), ("act", actions), ("val", valid)):
        parts = spread_groups(src[...].astype(F32), groups, GT)
        dst = getattr(R, name)
        for g in range(groups):
            c, lo = g // CG, 128 * (g % CG)
            part = parts[g]
            if name == "val":
                part = part * rows[g:g + 1, :]
            if name != "code":
                dst[c, 32:40, lo:lo + 128] = jnp.zeros((8, 128), F32)
            dst[c, 0:part.shape[0], lo:lo + 128] = part
    lanes = iota((GT, 128), 1)
    live_total = jnp.sum(jnp.where(lanes < groups, alive, 0.0), keepdims=True)
    v = jnp.zeros((40, L), F32)
    for c in range(chunks):
        v = v + R.val[c]
    valid_total = jnp.sum(v, keepdims=True)
    return live_total, valid_total


def own_rows(slab, h):
    rows = iota((8, 128), 0)
    if h % 2 == 0:
        return jnp.concatenate([slab[0:16], jnp.where(rows < 4, slab[16:24], 0.0)], axis=0)
    return jnp.concatenate([jnp.where(rows >= 4, slab[0:8], 0.0), slab[8:24]], axis=0)


def split(v):
    hi = low(v).astype(F32)
    return hi, v - hi


def attend(R, s, c, q, k, v):
    qh, ql = split(q)
    kh, kl = split(k)
    vh, vl = split(v)
    minus = jnp.where(iota((8, 128), 0) == 0, -BIG, 0.0)

    none = jnp.zeros((128, 128), BF)

    def scores(g, p):
        at = slice(128 * g, 128 * (g + 1))
        qs, ks = [], []
        for h in (2 * p, 2 * p + 1):
            sl = slice(slab_at(h), slab_at(h) + 24)
            hi = own_rows(qh[sl, at], h)
            qd = low(jnp.concatenate([hi, hi, own_rows(ql[sl, at], h), minus], axis=0))
            kd = low(jnp.concatenate([kh[sl, at], kl[sl, at], kh[sl, at], R.dead[c * CG + g]], axis=0))
            qs.append(jnp.concatenate([qd, R.q_mask[...]], axis=0))
            ks.append(jnp.concatenate([kd, R.k_mask[...]], axis=0).T)
        if PAIR:
            both = jnp.concatenate([jnp.concatenate([qs[0], none], axis=1),
                                    jnp.concatenate([none, qs[1]], axis=1)], axis=0)
            return nn(jnp.concatenate(ks, axis=1), both)[0:GT]
        return jnp.concatenate([nn(ks[0], qs[0])[0:GT], nn(ks[1], qs[1])[0:GT]], axis=1)

    def soft(g, p, sc):
        at = slice(128 * g, 128 * (g + 1))
        e = jnp.exp2(sc - jnp.max(sc, axis=0, keepdims=True))
        r = 1.0 / jnp.sum(e, axis=0, keepdims=True)
        e8 = pad8(e)
        eh = low(e8)
        cols = slice(256 * p, 256 * (p + 1))
        R.prob[s, g, :, cols] = e
        for i in range(2):
            at_h = slice(256 * p + 128 * i, 256 * p + 128 * (i + 1))
            R.prob_low[s, g, :, at_h] = eh[:, 128 * i:128 * (i + 1)].T
        R.rsum[s, 2 * p, :, at] = r[:, 0:128]
        R.rsum[s, 2 * p + 1, :, at] = r[:, 128:256]
        return r, eh

    def values(g, p, r, eh):
        at = slice(128 * g, 128 * (g + 1))
        out = []
        for i in range(2):
            sl = slice(slab_at(2 * p + i), slab_at(2 * p + i) + 24)
            cols = slice(128 * i, 128 * (i + 1))
            vs = low(jnp.concatenate([vh[sl, at], vl[sl, at]], axis=0))
            o = nn(vs, eh[:, cols])
            out.append((o[0:24] + o[24:48]) * r[:, cols])
        return out

    items = [(g, p) for g in range(CG) for p in range(H // 2)]
    slabs = pipeline(items, scores, soft, values, FAHEAD)
    slabs = [t for pair in slabs for t in pair]
    return jnp.concatenate([join_slabs(slabs[H * g:H * (g + 1)]) for g in range(CG)], axis=1)


PAIR = True
FAHEAD = 2
BAHEAD = 2


def pipeline(items, first, second, third, ahead, between=()):
    n = len(items)
    a, b, out = {}, {}, []
    between = list(between)
    done = 0
    for t in range(n + ahead):
        if t < n:
            a[t] = first(*items[t])
        m = t - ahead + 1
        if 0 <= m < n:
            b[m] = second(*items[m], *(a.pop(m) if isinstance(a[m], tuple) else (a.pop(m),)))
        m = t - ahead
        if 0 <= m < n:
            out.append(third(*items[m], *b.pop(m)))
        while done < len(between) * (t + 1) // (n + ahead):
            between[done]()
            done += 1
    return out


def attend_back(R, s, do, between=()):
    vrows = [R.v_low[s, :, 128 * g:128 * (g + 1)].T for g in range(CG)]

    def probs(g, p):
        at = slice(128 * g, 128 * (g + 1))
        ds, stack = [], []
        for h in (2 * p, 2 * p + 1):
            a = slab_at(h)
            d = own_rows(do[a:a + 24, at], h) * R.rsum[s, h, :, at]
            parts = ([jnp.zeros((a, 128), F32)] if a else []) + [d] + ([jnp.zeros((104 - a, 128), F32)])
            ds.append(low(d))
            stack.append(low(jnp.concatenate(parts, axis=0)))
        return ds, nn(vrows[g], jnp.concatenate(stack, axis=1))[0:GT]

    def inner(g, p, d, dp):
        at = slice(128 * g, 128 * (g + 1))
        e = R.prob[s, g, :, 256 * p:256 * (p + 1)]
        r = jnp.concatenate([R.rsum[s, 2 * p, :, at], R.rsum[s, 2 * p + 1, :, at]], axis=1)
        total = jnp.sum(e * dp, axis=0, keepdims=True) * r
        ds = low(pad8(e * (dp - total)))
        for i in range(2):
            cols = slice(128 * i, 128 * (i + 1))
            R.ds_t[3 * g + p, :, cols] = ds[:, cols].T
        return d, ds

    def outer(g, p, d, ds):
        at = slice(128 * g, 128 * (g + 1))
        out = []
        for i in range(2):
            h = 2 * p + i
            dsh = ds[:, 128 * i:128 * (i + 1)]
            out.append((nn(R.k_low[s, h, :, at], dsh), nn(R.q_low[s, h, :, at], R.ds_t[3 * g + p, :, 128 * i:128 * (i + 1)]),
                        nn(d[i], R.prob_low[s, g, :, 128 * h:128 * (h + 1)])))
        return out

    items = [(g, p) for g in range(CG) for p in range(H // 2)]
    slabs = pipeline(items, probs, inner, outer, BAHEAD, between)
    slabs = [t for pair in slabs for t in pair]
    out = []
    for i in range(3):
        out.append(jnp.concatenate(
            [join_slabs([t[i] for t in slabs[H * g:H * (g + 1)]]) for g in range(CG)], axis=1))
    return out[0] * SCALE, out[1], out[2]


def turn(R, i, v):
    for g in range(CG):
        R.turned[i, 128 * g:128 * (g + 1), :] = v[:, 128 * g:128 * (g + 1)].T


def embed(R, obs, c):
    rows = nn(jnp.concatenate(obs, axis=1), R.w_obs[...])
    parts = []
    for g in range(CG):
        r = rows[GT * g:GT * (g + 1)] + R.posb[...]
        parts.append(pad8(r).T[0:D])
    return jnp.concatenate(parts, axis=1)


def layer_fwd(R, l, c, s, x):
    def vec(i):
        return tile4(R.bc[l, i])

    xh, r = normed(x)
    R.xh1[s] = xh
    R.r1[s] = r
    n1 = low(ones8(xh * vec(G1) + vec(B1)))
    R.n1[s] = n1
    mix = nn(R.qkv_t[l], n1)
    q = mix[0:D] * SCALE
    k = mix[128:128 + D]
    v = mix[256:256 + D]
    for h in range(H):
        a = slab_at(h)
        R.q_low[s, h] = low(q[a:a + 24])
        R.k_low[s, h] = low(k[a:a + 24])
    R.v_low[s] = low(pad8(v))
    att = low(ones8(attend(R, s, c, q * LOG2E, k, v)))
    R.att[l] = att
    x1 = x + nn(R.out_t[l], att)[0:D]
    xh, r = normed(x1)
    R.xh2[l] = xh
    R.r2[l] = r
    n2 = low(ones8(xh * vec(G2) + vec(B2)))
    R.n2[l] = n2
    pre = nn(R.fc_t[l], n2)
    parts = []
    for j in range(4):
        pj = pre[128 * j:128 * j + D]
        half = gelu_half(pj)
        R.pre[l, D * j:D * (j + 1)] = pj
        R.half[l, D * j:D * (j + 1)] = half
        parts.append(low(ones8(pj * half) if j == 0 else pad8(pj * half)))
    inner = jnp.concatenate(parts, axis=0)
    R.inner[l] = inner
    return x1 + nn(R.proj_t[l], inner)[0:D]


def head_step(R, c, x, live_total, valid_total):
    xh, r = normed(x)
    fin = low(pad8(xh * tile4(R.bcf[0]) + tile4(R.bcf[1])))
    hd = nn(R.head_t[...], fin) + tile4(R.bch[...])
    live = R.live[c]
    lw = live * (1.0 / live_total)
    rows = iota((CODES, L), 0).astype(F32)
    grads = []
    csum = jnp.zeros((1, L), F32)
    for b in range(BOOKS):
        lg = hd[CODES * b:CODES * (b + 1)]
        m = jnp.max(lg, axis=0, keepdims=True)
        e = jnp.exp(lg - m)
        s = jnp.sum(e, axis=0, keepdims=True)
        hot = rows == R.code[c, b:b + 1, :]
        picked = jnp.sum(jnp.where(hot, lg, 0.0), axis=0, keepdims=True)
        csum = csum + (jnp.log(s) + m - picked) * live
        grads.append((e * (1.0 / s) - jnp.where(hot, 1.0, 0.0)) * lw)
    diff = hd[32:72] - R.act[c]
    val = R.val[c]
    sq = diff * diff + 1.0
    ri = lax.rsqrt(sq)
    asum = val * (sq * ri)
    grads.append((val * (1.0 / valid_total)) * (diff * ri))
    R.loss[0, 0:1] += fold4(csum)
    af = fold4(asum)
    R.loss[1] += af[0:8] + af[8:16] + af[16:24] + af[24:32] + af[32:40]
    dh = jnp.concatenate(grads, axis=0)
    R.a_hb[0:72] += fold4(dh)
    dhl = low(jnp.concatenate([dh, jnp.zeros((56, L), F32)], axis=0))
    turn(R, 4, dhl)
    R.a_head[...] += nn(fin, R.turned[4])
    df = nn(R.head[...], dhl)[0:D]
    R.a_fin[0, 0:D] += fold4(df * xh)
    R.a_fin[1, 0:D] += fold4(df)
    return normed_back(df * tile4(R.bcf[0]), xh, r)


def add_bias(R, l, i, v):
    R.a_bias[l, i, 0:D] += fold4(v)


def mlp_bwd(R, l, dout):
    outl = low(pad8(dout))
    add_bias(R, l, PB, dout)
    parts = []
    for j in range(4):
        rows = slice(D * j, D * (j + 1))
        dj = nn(R.proj[l, 128 * j:128 * (j + 1)], outl)
        parts.append(low(pad8(dj[0:D] * gelu_slope(R.pre[l, rows], R.half[l, rows]))))
    prel = jnp.concatenate(parts, axis=0)
    dn = nn(R.fc[l], prel)[0:D]
    xh = R.xh2[l]
    add_bias(R, l, G2, dn * xh)
    add_bias(R, l, B2, dn)
    dmid = normed_back(dn * tile4(R.bc[l, G2]), xh, R.r2[l]) + dout
    midl = low(pad8(dmid))
    add_bias(R, l, OB, dmid)
    da = nn(R.out[l], midl)[0:D]

    turn(R, 0, outl)
    turn(R, 1, R.n2[l])
    turn(R, 2, midl)

    def a_proj(j):
        def run():
            rows = slice(256 * j, 256 * (j + 1))
            R.a_proj[l, rows] += nn(R.inner[l, rows], R.turned[0])
        return run

    def a_fc(j):
        def run():
            rows = slice(256 * j, 256 * (j + 1))
            R.a_fc[l, rows] += nn(prel[rows], R.turned[1])
        return run

    def a_out():
        R.a_out[l] += nn(R.att[l], R.turned[2])

    return dmid, da, [a_proj(0), a_proj(1), a_fc(0), a_fc(1), a_out]


def att_bwd(R, l, s, dmid, da, between):
    turn(R, 3, R.n1[s])
    dq, dk, dv = attend_back(R, s, da, between)
    mixl = jnp.concatenate([low(pad8(dq)), low(pad8(dk)), low(pad8(dv))], axis=0)
    dn = nn(R.qkv[l], mixl)[0:D]
    add_bias(R, l, QB, dq)
    add_bias(R, l, VB, dv)
    R.a_qkv[l] += nn(mixl, R.turned[3])
    xh = R.xh1[s]
    add_bias(R, l, G1, dn * xh)
    add_bias(R, l, B1, dn)
    return normed_back(dn * tile4(R.bc[l, G1]), xh, R.r1[s]) + dmid


def embed_bwd(R, obs, c, dx):
    R.a_x[0:D] += fold4(dx)
    lanes = iota((D, 128), 1)
    tiles = []
    gs = [dx[:, 128 * g:128 * (g + 1)] for g in range(CG)]
    for t in range(CG):
        a = shifted(gs[t], -8 * t)
        b = shifted(gs[t + 1], 120 - 8 * t) if t + 1 < CG else jnp.zeros((D, 128), F32)
        tiles.append(jnp.where(lanes < GT - 8 * t, a, b))
    gl = low(pad8(jnp.concatenate(tiles, axis=1)))
    R.a_obs[...] += nn(gl, jnp.concatenate(obs, axis=1))


def zero_grads(R):
    for name in ("a_qkv", "a_out", "a_fc", "a_proj", "a_bias", "a_obs", "a_x", "a_fin", "a_head", "a_hb", "loss"):
        ref = getattr(R, name)
        ref[...] = jnp.zeros(ref.shape, F32)


HIGH = lax.Precision.HIGHEST


LATE = 364
EARLY_ROWS = (OB, G2, B2, PB)


def lane_sums(v):
    return jnp.sum(v.T, axis=0, keepdims=True)


def pack_vectors(R, rg, l, which):
    b = BASE + LROW * l
    for i in which:
        rg[pl.ds(b + VROWS[i], 1), :] = lane_sums(R.a_bias[l, i])


def pack_early(R, rg, l):
    b = BASE + LROW * l
    rg[pl.ds(b + 364, D), :] = R.a_out[l, 0:D]
    for j in range(4):
        fc = R.a_fc[l, 128 * j:128 * (j + 1), :].T
        rg[pl.ds(b + 487 + j, D, stride=4), :] = fc[0:D]
        rg[pl.ds(b + 967 + j, 1), :] = fc[D:D + 1]
        rg[pl.ds(b + 971 + D * j, D), :] = R.a_proj[l, 128 * j:128 * j + D, :]
    pack_vectors(R, rg, l, EARLY_ROWS)


def pack_late(R, rg, l):
    b = BASE + LROW * l
    for j in range(3):
        rg[pl.ds(b + 2 + j, D, stride=3), :] = R.a_qkv[l, 128 * j:128 * (j + 1), :].T[0:D]
    pack_vectors(R, rg, l, (G1, B1, QB, VB))


def pack_embed(R, rg):
    for f in range(OBS // 128):
        rg[128 * f:128 * (f + 1), :] = R.a_obs[:, 128 * f:128 * (f + 1)].T
    slot, lane = iota((32, 128), 0), iota((32, 128), 1)
    sel = jnp.where((slot == 0) | (lane % WIN == slot - 1), 1.0, 0.0)
    sel = jnp.where(lane < GT, sel, 0.0)
    rows = nt(sel, R.a_x[...], HIGH)
    rg[pl.ds(OBS, 1 + WIN), :] = rows[0:1 + WIN]


def pack_head(R, rg):
    for i in range(2):
        rg[pl.ds(HEAD + i, 1), :] = lane_sums(R.a_fin[i])
    lanes8 = iota((8, 128), 1)
    grad = R.a_head[...]
    R.hc[...] = jnp.where(iota((128, 128), 1) < 32, grad, 0.0)
    R.ho[...] = jnp.where(iota((128, 128), 1) < OFFS, shifted(grad, -32), 0.0)
    c0 = HEAD + 2
    o0 = c0 + 32

    def put(phases, src, rows_n, stride, width, count):
        acc = [jnp.zeros((rows_n, 128), F32) for _ in range(count + 1)]
        lanes = iota((rows_n, 128), 1)
        for p, a, s in phases:
            v = src[pl.ds(p, rows_n, stride=stride), :]
            first = shifted(v, s)
            if s + width > D:
                acc[a] = acc[a] + jnp.where((lanes >= s) & (lanes < D), first, 0.0)
                acc[a + 1] = acc[a + 1] + jnp.where(lanes < s + width - D, shifted(v, s - D), 0.0)
            else:
                acc[a] = acc[a] + first
        return acc

    acc = put(code_phases(), R.hc, 8, 15, 32, 4)
    for a in range(4):
        rg[pl.ds(c0 + a, 8, stride=4), :] = acc[a]
    hb = lane_sums(R.a_hb[...])
    lane1 = iota((1, 128), 1)
    rg[pl.ds(o0, 48), :] = jnp.zeros((48, 128), F32)
    acc = put(off_phases(), R.ho, 5, 24, OFFS, 7)
    for a in range(7):
        rg[pl.ds(o0 + a, 5, stride=7), :] = acc[a]
    rg[pl.ds(o0 + 7, 5, stride=7), :] = rg[pl.ds(o0 + 7, 5, stride=7), :] + acc[7]
    rg[pl.ds(o0, 1), :] = rg[pl.ds(o0, 1), :] + jnp.where(lane1 < 32, hb, 0.0)
    a, s = (D * OFFS + 32) // D, (D * OFFS + 32) % D
    ob = jnp.where(lane1 < OFFS, shifted(hb, -32), 0.0)
    rg[pl.ds(o0 + a, 1), :] = rg[pl.ds(o0 + a, 1), :] + shifted(ob, s)


MESH = pl.DeviceIdType.MESH


def round_up(n, m):
    return -(-n // m) * m


class Plan:
    def __init__(self, feats, toks, shard, tok_rows):
        self.feats, self.toks, self.chips = feats, toks, toks // 2
        self.shard = shard
        self.block = round_up(-(-(shard + 112) // D), 16)
        self.flat_rows = self.block // 16 * 15
        self.local = round_up(-(-shard // 1024), 1) * 8
        self.work = round_up(max(self.flat_rows, self.local + 1), 8)
        self.own_rows = tok_rows // feats
        self.chunks = self.own_rows // CT
        self.early = [f for f in range(feats) if shard * toks * f // D >= BASE + LATE]
        self.grid = round_up(-(-(shard * feats * toks) // D) + self.block, 8)


def comm_scratch(P):
    dma = pltpu.SemaphoreType.DMA
    B, C, Fn = P.block, P.chips, P.feats
    return dict(
        rg=pltpu.VMEM((P.grid, 128), F32),
        ob=pltpu.VMEM((P.chunks, Fn, L, 128), BF),
        pg=pltpu.VMEM((2, C, Fn, B, 128), BF),
        loc=pltpu.VMEM((P.work, 128), F32),
        rblk=pltpu.VMEM((B, 128), F32),
        codes_in=pltpu.VMEM((BOOKS, P.own_rows), jnp.int32),
        act_in=pltpu.VMEM((OFFS, P.own_rows), F32),
        val_in=pltpu.VMEM((OFFS, P.own_rows), jnp.int32),
        tz=pltpu.VMEM((2, Fn, 8, 128), F32),
        tc=pltpu.VMEM((2, C, 8, 128), F32),
        ts=pltpu.VMEM((2, 2, 8, 128), F32),
        sb1=pltpu.VMEM((C, Fn, B, 128), F32),
        rb1=pltpu.VMEM((C, Fn, B, 128), F32),
        sb2=pltpu.VMEM((C, Fn, B, 128), BF),
        rb2=pltpu.VMEM((C, Fn, B, 128), BF),
        col=pltpu.VMEM((Fn, B, 128), F32),
        sb3=pltpu.VMEM((Fn, B, 128), F32),
        rb3=pltpu.VMEM((Fn, B, 128), F32),
        s_p1=dma((2, Fn)), s_p2=dma((2, C)), s_p3=dma((2, C)),
        s_tz=dma((2, 2, Fn)), s_tc=dma((2, 2, C)), s_ts=dma((2, 2)),
        s_ob=dma((2, 2 * P.chunks, Fn)),
        s_own=dma((P.chunks,)),
        s_in=dma((3,)),
        s_r1=dma((3, 2, C)), s_r2=dma((2, Fn, C)), s_r3=dma((2, Fn)),
    )


def to_rows(loc, rblk, delta, P):
    v = loc[...]
    lanes = iota(v.shape, 1)
    moved = pltpu.roll(v, delta, 1)
    loc[...] = jnp.where(lanes >= delta, moved, pltpu.roll(moved, 1, 0))
    n = P.block // 16
    lane = iota((n, 128), 1)
    for j in range(16):
        if j < 15:
            a = shifted(loc[pl.ds(j, n, stride=15), :], 8 * j)
        if j > 0:
            b = shifted(loc[pl.ds(j - 1, n, stride=15), :], 8 * j)
            a = jnp.where(lane < 8 * j, b, a) if j < 15 else b
        rblk[pl.ds(j, n, stride=16), :] = jnp.where(lane < D, a, 0.0)


def from_rows(rblk, loc, delta, P):
    n = P.block // 16
    lane = iota((n, 128), 1)
    loc[...] = jnp.zeros(loc.shape, F32)
    for i in range(15):
        a = shifted(rblk[pl.ds(i, n, stride=16), :], -8 * i)
        b = shifted(rblk[pl.ds(i + 1, n, stride=16), :], D - 8 * i)
        loc[pl.ds(i, n, stride=15), :] = jnp.where(lane < D - 8 * i, a, b)
    v = loc[...]
    lanes = iota(v.shape, 1)
    moved = pltpu.roll(v, lax.rem(128 - delta, 128), 1)
    v = jnp.where(lanes < 128 - delta, moved, pltpu.roll(moved, P.work - 1, 0))
    return v[0:P.local]


def step_kernel(P, names, master, obs, counts, codes, actions, valid, grad, sums, *scratch):
    R = Refs()
    for name, ref in zip(names, scratch):
        setattr(R, name, ref)
    Fn, C, B = P.feats, P.chips, P.block
    feat = lax.axis_index("feat")
    tok = lax.axis_index("tok")
    chip = tok // 2
    core = tok % 2
    me = feat * P.toks + tok
    delta = lax.rem(me * P.shard, D)

    def z_peer(i):
        return lax.rem(feat + i, Fn)

    def z_from(i):
        return lax.rem(feat + Fn - i, Fn)

    def c_peer(i):
        return lax.rem(chip + i, C)

    def c_from(i):
        return lax.rem(chip + C - i, C)

    def to_z(i):
        return (z_peer(i), tok)

    def to_c(i):
        return (feat, 2 * c_peer(i) + core)

    sibling = (feat, 2 * chip + 1 - core)

    def send(src, dst, sems, at, dev):
        return pltpu.make_async_remote_copy(
            src_ref=src, dst_ref=dst, send_sem=sems.at[(0,) + at], recv_sem=sems.at[(1,) + at],
            device_id=dev, device_id_type=MESH)

    n = P.own_rows
    ins = []
    for i, (src, dst) in enumerate(((codes, R.codes_in), (actions, R.act_in), (valid, R.val_in))):
        ins.append(pltpu.make_async_copy(src.at[:, pl.ds(pl.multiple_of(feat * n, 128), n)], dst, R.s_in.at[i]))
        ins[-1].start()

    barrier = pltpu.get_barrier_semaphore()
    peers = [to_z(i) for i in range(1, Fn)] + [to_c(i) for i in range(1, C)] + [sibling]
    for dev in peers:
        pl.semaphore_signal(barrier, inc=1, device_id=dev, device_id_type=MESH)

    R.loc[...] = jnp.zeros(R.loc.shape, F32)
    whole = P.shard // 1024
    R.loc[0:8 * whole, :] = master[pl.ds(0, 1024 * whole)].reshape(8 * whole, 128)
    rest = P.shard - 1024 * whole
    last = jnp.concatenate([master[pl.ds(1024 * whole, rest)], jnp.zeros((1024 - rest,), F32)])
    R.loc[8 * whole:8 * whole + 8, :] = last.reshape(8, 128)
    to_rows(R.loc, R.rblk, delta, P)
    R.pg[core, chip, feat] = low(R.rblk[...])
    pl.semaphore_wait(barrier, len(peers))

    p1 = []
    for i in range(1, Fn):
        blk = R.pg.at[core, chip, feat]
        p1.append(send(blk, blk, R.s_p1, (i,), to_z(i)))
        p1[-1].start()

    half = CT // 2

    def obs_copies(p):
        cps = []
        for i in range(1, Fn):
            src = obs.at[pl.ds(pl.multiple_of(z_peer(i) * n + half * p, 16), half), :]
            dst = R.ob.at[p // 2, feat, pl.ds(pl.multiple_of(half * (p % 2), 16), half), :]
            cps.append(send(src, dst, R.s_ob, (p, i), to_z(i)))
        return cps

    def start_obs(p):
        for cp in obs_copies(p):
            cp.start()

    own = []
    for c in range(P.chunks):
        src = obs.at[pl.ds(pl.multiple_of(feat * n + CT * c, 16), CT), :]
        own.append(pltpu.make_async_copy(src, R.ob.at[c, feat, pl.ds(0, CT), :], R.s_own.at[c]))
        own[-1].start()
    for cp in ins:
        cp.wait()
    zero_grads(R)
    for c in range(P.chunks):
        for f in range(Fn):
            R.ob[c, f, CT:L, :] = jnp.zeros((L - CT, 128), BF)
    live_n, valid_n = prep_tokens(R, counts, R.codes_in, R.act_in, R.val_in, feat, P.chunks)

    def two_rows(a, b):
        return jnp.concatenate([jnp.broadcast_to(a, (1, 128)), jnp.broadcast_to(b, (1, 128)),
                                jnp.zeros((6, 128), F32)], axis=0)

    def z_copies(w):
        return [send(R.tz.at[w, feat], R.tz.at[w, feat], R.s_tz.at[w], (i,), to_z(i)) for i in range(1, Fn)]

    def c_copies(w):
        return [send(R.tc.at[w, chip], R.tc.at[w, chip], R.s_tc.at[w], (i,), to_c(i)) for i in range(1, C)]

    def s_copies(w):
        return [send(R.ts.at[w, core], R.ts.at[w, core], R.s_ts.at[w], (), sibling)]

    def start_all(cps):
        for cp in cps:
            cp.start()

    def total(ref, w, count):
        v = ref[w, 0]
        for i in range(1, count):
            v = v + ref[w, i]
        return v

    def wait_all(cps):
        for cp in cps:
            cp.wait()

    R.tz[0, feat] = two_rows(live_n, valid_n)
    start_all(z_copies(0))
    wait_all(p1)
    start_obs(0)
    start_obs(1)
    p2 = []
    for i in range(1, C):
        blk = R.pg.at[core, chip]
        p2.append(send(blk, blk, R.s_p2, (i,), to_c(i)))
        p2[-1].start()
    p3 = [send(R.pg.at[core, chip], R.pg.at[core, chip], R.s_p3, (0,), sibling)]
    p3[0].start()
    wait_all(z_copies(0))
    R.tc[0, chip] = total(R.tz, 0, Fn)
    start_all(c_copies(0))
    for i in range(1, C):
        p2[i - 1].wait_recv()
        blk = R.pg.at[core, c_from(i)]
        p3.append(send(blk, blk, R.s_p3, (i,), sibling))
        p3[-1].start()
    wait_all(c_copies(0))
    R.ts[0, core] = total(R.tc, 0, C)
    start_all(s_copies(0))
    for cp in p2:
        cp.wait_send()
    wait_all(p3)
    R.rg[0:8, :] = jnp.zeros((8, 128), F32)

    def place(d, _):
        r0 = (P.shard * d) // D
        f, t = d // P.toks, d % P.toks
        blk = R.pg[t % 2, t // 2, f].astype(F32)
        before = R.rg[pl.ds(r0, 1), :]
        R.rg[pl.ds(r0, B), :] = blk
        R.rg[pl.ds(r0, 1), :] = blk[0:1] + before
        return 0

    lax.fori_loop(0, Fn * P.toks, place, 0)
    prep_weights(R.rg, R)
    wait_all(s_copies(0))
    counted = total(R.ts, 0, 2)
    live_total = counted[0:1, 0:1]
    valid_total = counted[1:2, 0:1]

    for cp in own:
        cp.wait()


    def rows_of(f, ch, co):
        return (P.shard * (f * P.toks + 2 * ch + co)) // D

    early = P.early[0] if P.early else Fn
    planes = [slice(Fn - 1, Fn), slice(early, Fn - 1), slice(0, early)]

    def r1_copy(w, i):
        at = pl.ds(planes[w].start, planes[w].stop - planes[w].start)
        return send(R.sb1.at[i, at], R.rb1.at[i, at], R.s_r1.at[w], (i,), sibling)

    def r2_copy(f, i):
        return send(R.sb2.at[i, f], R.rb2.at[i, f], R.s_r2.at[:, f], (i,), to_c(i))

    def r3_copy(i):
        return send(R.sb3.at[i], R.rb3.at[i], R.s_r3, (i,), to_z(i))

    order = list(range(1, C)) + [0]

    def sum_cores(w):
        for i in order:
            for f in range(planes[w].start, planes[w].stop):
                R.sb1[i, f] = R.rg[pl.ds(rows_of(f, c_peer(i), 1 - core), B), :]
            r1_copy(w, i).start()

    def sum_chips(w):
        for i in order:
            r1_copy(w, i).wait_recv()
            for f in range(planes[w].start, planes[w].stop):
                v = R.rg[pl.ds(rows_of(f, c_peer(i), core), B), :] + R.rb1[i, f]
                if i:
                    R.sb2[i, f] = low(v)
                    r2_copy(f, i).start()
                else:
                    R.col[f] = v

    def sum_column(f):
        v = R.col[f]
        for i in range(1, C):
            r2_copy(f, i).wait_recv()
            v = v + R.rb2[i, f].astype(F32)
        R.col[f] = v
        for i in range(1, Fn):
            @pl.when(z_peer(i) == f)
            def _():
                R.sb3[i] = v
                r3_copy(i).start()

    def chunk(c, _):
        for p in (2 * c, 2 * c + 1):
            for cp in obs_copies(p):
                cp.wait_recv()

        @pl.when(c + 1 < P.chunks)
        def _():
            start_obs(2 * c + 2)
            start_obs(2 * c + 3)

        R.x[...] = embed(R, [R.ob[c, f, 0:CT, :] for f in range(Fn)], c)

        def lay(l, _):
            R.x[...] = layer_fwd(R, l, c, l, R.x[...])
            return 0

        lax.fori_loop(0, LAYERS, lay, 0)

        dx = head_step(R, c, R.x[...], live_total, valid_total)
        dmid, da, rest = mlp_bwd(R, 1, dx)
        R.x[...] = att_bwd(R, 1, 1, dmid, da, rest)
        @pl.when(c == P.chunks - 1)
        def _():
            R.rg[pl.ds(HEAD + 32, P.grid - HEAD - 32), :] = jnp.zeros((P.grid - HEAD - 32, 128), F32)
            pack_head(R, R.rg)
            pack_late(R, R.rg, 1)
            pack_early(R, R.rg, 1)
            R.ts[1, core] = two_rows(jnp.sum(R.loss[0], keepdims=True), jnp.sum(R.loss[1], keepdims=True))
            sum_cores(0)
            start_all(s_copies(1))

        dmid, da, rest = mlp_bwd(R, 0, R.x[...])
        R.dmid[...] = dmid
        R.da[...] = da
        for run in rest:
            run()

        @pl.when(c == P.chunks - 1)
        def _():
            pack_early(R, R.rg, 0)
            sum_cores(1)
            sum_chips(0)
            wait_all(s_copies(1))
            R.tc[1, chip] = total(R.ts, 1, 2)
            start_all(c_copies(1))

        dx = att_bwd(R, 0, 0, R.dmid[...], R.da[...], [])

        @pl.when(c == P.chunks - 1)
        def _():
            sum_chips(1)

        embed_bwd(R, [R.ob[c, f] for f in range(Fn)], c, dx)
        return 0

    lax.fori_loop(0, P.chunks, chunk, 0)
    pack_embed(R, R.rg)
    pack_late(R, R.rg, 0)
    sum_cores(2)
    wait_all(c_copies(1))
    R.tz[1, feat] = total(R.tc, 1, C)
    start_all(z_copies(1))
    sum_column(Fn - 1)
    sum_chips(2)
    for f in (*range(early, Fn - 1), *range(early)):
        sum_column(f)
    for i in range(1, Fn):
        r3_copy(i).wait_recv()
    v = R.col[feat]
    for i in range(1, Fn):
        v = v + R.rb3[i]
    R.rblk[...] = v
    grad[...] = from_rows(R.rblk, R.loc, delta, P)
    wait_all(z_copies(1))
    lost = total(R.tz, 1, Fn)
    sums[...] = jnp.concatenate([lost[0:1], counted[0:1], lost[1:2], counted[1:2], jnp.zeros((4, 128), F32)], axis=0)
    for p in range(2 * P.chunks):
        for cp in obs_copies(p):
            cp.wait_send()
    for w in range(3):
        for i in range(C):
            r1_copy(w, i).wait_send()
    for i in range(1, C):
        for f in range(Fn):
            r2_copy(f, i).wait_send()
    for i in range(1, Fn):
        r3_copy(i).wait_send()


def solution(mesh):
    feats, toks = mesh.shape["feat"], mesh.shape["tok"]

    def shards(master, first, second, obs, counts, codes, actions, valid):
        P_ = Plan(feats, toks, master.shape[0], obs.shape[0])
        scratch = dict(scratch_list(P_.chunks))
        scratch.update(comm_scratch(P_))
        vmem = pl.BlockSpec(memory_space=pltpu.VMEM)
        hbm = pl.BlockSpec(memory_space=pl.ANY)
        grad, sums = pl.pallas_call(
            functools.partial(step_kernel, P_, list(scratch)),
            out_shape=(jax.ShapeDtypeStruct((P_.local, 128), F32), jax.ShapeDtypeStruct((8, 128), F32)),
            in_specs=[vmem, hbm, vmem, hbm, hbm, hbm],
            out_specs=(vmem, vmem),
            scratch_shapes=list(scratch.values()),
            compiler_params=pltpu.CompilerParams(
                collective_id=0, has_side_effects=True, vmem_limit_bytes=60 * 2 ** 20),
        )(master, obs, counts.T, codes.T, actions, valid)
        grad = grad.reshape(-1)[:P_.shard]
        f_new = BETA_ONE * first + (1.0 - BETA_ONE) * grad
        s_new = BETA_TWO * second + (1.0 - BETA_TWO) * grad * grad
        f_hat = f_new / (1.0 - BETA_ONE ** STEP_NO)
        s_hat = s_new / (1.0 - BETA_TWO ** STEP_NO)
        new = master - LEARN_RATE * (f_hat / (jnp.sqrt(s_hat) + ADAM_EPS) + DECAY_RATE * master)
        return new, f_new, s_new, sums[0:4, 0]

    weights = PSpec(("feat", "tok"))
    return jax.shard_map(
        shards, mesh=mesh,
        in_specs=(weights, weights, weights, PSpec("tok", "feat"), PSpec("tok", None), PSpec("tok", None),
                  PSpec(None, "tok"), PSpec(None, "tok")),
        out_specs=(weights, weights, weights, PSpec()), check_vma=False)
```

```python
import functools
import math

import jax
import jax.numpy as jnp
from jax import lax
from jax.experimental import pallas as pl
from jax.experimental.pallas import tpu as pltpu
from jax.sharding import PartitionSpec as PSpec

D = 120
H = 6
HD = 20
FF = 480
OBS = 512
LAYERS = 2
CAMS = 3
BOOKS = 2
CODES = 16
SPAN = 5
ACT = 7
WIN = 30
OFFS = SPAN * ACT
NORM_EPS = 1e-05
STEP_NO = 10
BETA_ONE = 0.9
BETA_TWO = 0.999
ADAM_EPS = 1e-08
DECAY_RATE = 0.1
LEARN_RATE = 0.05
GW = 4
GT = GW * WIN
CG = 4
L = CG * 128
CT = CG * GT
F32 = jnp.float32
BF = jnp.bfloat16
SCALE = HD ** (-0.5)
LROW = 2 * 1 + 3 * D + 2 + D + 1 + 2 + 4 * D + 4 + 4 * D + 1
BASE = OBS + 1 + WIN
HEAD = BASE + LAYERS * LROW
NV = 13
VROWS = [0, 1, 362, 363, 484, 485, 486, 967, 968, 969, 970, 1451]
(G1, B1, QB, VB, OB, G2, B2, FB0, FB1, FB2, FB3, PB) = range(12)


def nn(a, b):
    return lax.dot_general(a, b, (((1,), (0,)), ((), ())), preferred_element_type=F32)


def nt(a, b, precision=None):
    return lax.dot_general(a, b, (((1,), (1,)), ((), ())), preferred_element_type=F32, precision=precision)


def low(v):
    return v.astype(BF)


def pad8(v):
    return jnp.concatenate([v, jnp.zeros((8, v.shape[1]), v.dtype)], axis=0)


def tile4(v):
    return jnp.concatenate([v] * CG, axis=1)


def fold4(v):
    out = v[:, 0:128]
    for g in range(1, CG):
        out = out + v[:, 128 * g:128 * (g + 1)]
    return out


def iota(shape, axis):
    return lax.broadcasted_iota(jnp.int32, shape, axis)


def slab_at(h):
    return 20 * h - (4 if h % 2 else 0)


def head_stack(v):
    rows = iota((8, 128), 0)
    cols = []
    for h in range(H):
        a = slab_at(h)
        if h % 2 == 0:
            parts = [v[a:a + 16], jnp.where(rows < 4, v[a + 16:a + 24], 0.0)]
        else:
            parts = [jnp.where(rows >= 4, v[a:a + 8], 0.0), v[a + 8:a + 24]]
        if a > 0:
            parts = [jnp.zeros((a, 128), F32)] + parts
        if a + 24 < 128:
            parts = parts + [jnp.zeros((128 - a - 24, 128), F32)]
        cols.append(jnp.concatenate(parts, axis=0))
    return jnp.concatenate(cols, axis=1)


def join_slabs(slabs):
    rows = iota((8, 128), 0)
    parts = []
    for p in range(3):
        a, b = slabs[2 * p], slabs[2 * p + 1]
        parts += [a[0:16], jnp.where(rows < 4, a[16:24], b[0:8]), b[8:24]]
    return jnp.concatenate(parts, axis=0)


def slabs_of(v):
    return [v[slab_at(h):slab_at(h) + 24] for h in range(H)]


def hi_lo(v):
    hi = low(v)
    return hi, low(v - hi.astype(F32))


def normed(x):
    mean = jnp.sum(x, axis=0, keepdims=True) * (1.0 / D)
    c = x - mean
    var = jnp.sum(c * c, axis=0, keepdims=True) * (1.0 / D)
    r = lax.rsqrt(var + NORM_EPS)
    return c * r, r


def normed_back(d, xh, r):
    m0 = jnp.sum(d, axis=0, keepdims=True) * (1.0 / D)
    m1 = jnp.sum(d * xh, axis=0, keepdims=True) * (1.0 / D)
    return r * (d - m0 - xh * m1)


GA = math.sqrt(2.0 / math.pi)
GB = 0.044715


def gelu_half(x):
    return 0.5 + 0.5 * jnp.tanh(x * (GA + (GA * GB) * (x * x)))


def gelu_slope(x, s):
    return s + (x * s) * (1.0 - s) * (2.0 * GA + (6.0 * GA * GB) * (x * x))


LOG2E = math.log2(math.e)
BIG = 1e30


class Refs:
    pass


def scratch_list(chunks):
    groups = chunks * CG
    return dict(
        w_obs=pltpu.VMEM((OBS, 128), BF),
        posb=pltpu.VMEM((GT, 128), F32),
        qkv_t=pltpu.VMEM((LAYERS, 384, 128), BF),
        qkv=pltpu.VMEM((LAYERS, 128, 384), BF),
        out_t=pltpu.VMEM((LAYERS, 128, 128), BF),
        out=pltpu.VMEM((LAYERS, 128, 128), BF),
        fc_t=pltpu.VMEM((LAYERS, 512, 128), BF),
        fc=pltpu.VMEM((LAYERS, 128, 512), BF),
        proj_t=pltpu.VMEM((LAYERS, 128, 512), BF),
        proj=pltpu.VMEM((LAYERS, 512, 128), BF),
        head_t=pltpu.VMEM((72, 128), BF),
        head=pltpu.VMEM((128, 128), BF),
        vec=pltpu.VMEM((32, 128), F32),
        bc=pltpu.VMEM((LAYERS, 12, GT, 128), F32),
        bcf=pltpu.VMEM((2, GT, 128), F32),
        bch=pltpu.VMEM((72, 128), F32),
        hc=pltpu.VMEM((128, 128), F32),
        ho=pltpu.VMEM((128, 128), F32),
        cnt=pltpu.VMEM((16, 256), F32),
        live=pltpu.VMEM((chunks, 1, L), F32),
        act=pltpu.VMEM((chunks, 40, L), F32),
        val=pltpu.VMEM((chunks, 40, L), F32),
        code=pltpu.VMEM((chunks, 2, L), F32),
        x=pltpu.VMEM((D, L), F32),
        dmid=pltpu.VMEM((D, L), F32),
        da=pltpu.VMEM((D, L), F32),
        xh1=pltpu.VMEM((LAYERS, D, L), F32),
        r1=pltpu.VMEM((LAYERS, 1, L), F32),
        xh2=pltpu.VMEM((LAYERS, D, L), F32),
        r2=pltpu.VMEM((LAYERS, 1, L), F32),
        n1=pltpu.VMEM((LAYERS, 128, L), BF),
        n2=pltpu.VMEM((LAYERS, 128, L), BF),
        att=pltpu.VMEM((LAYERS, 128, L), BF),
        q_low=pltpu.VMEM((LAYERS, H, 24, L), BF),
        k_low=pltpu.VMEM((LAYERS, H, 24, L), BF),
        v_low=pltpu.VMEM((LAYERS, 128, L), BF),
        rsum=pltpu.VMEM((LAYERS, H, 1, L), F32),
        prob=pltpu.VMEM((LAYERS, CG, GT, H * 128), F32),
        prob_low=pltpu.VMEM((LAYERS, CG, 128, H * 128), BF),
        k_mask=pltpu.VMEM((48, 128), BF),
        q_mask=pltpu.VMEM((48, 128), BF),
        dead=pltpu.VMEM((groups, 8, 128), F32),
        pre=pltpu.VMEM((LAYERS, FF, L), F32),
        half=pltpu.VMEM((LAYERS, FF, L), F32),
        inner=pltpu.VMEM((LAYERS, 512, L), BF),
        a_qkv=pltpu.VMEM((LAYERS, 384, 128), F32),
        ds_t=pltpu.VMEM((CG * H // 2, 128, 256), BF),
        turned=pltpu.VMEM((5, L, 128), BF),
        a_out=pltpu.VMEM((LAYERS, 128, 128), F32),
        a_fc=pltpu.VMEM((LAYERS, 512, 128), F32),
        a_proj=pltpu.VMEM((LAYERS, 512, 128), F32),
        a_bias=pltpu.VMEM((LAYERS, 12, 128, 128), F32),
        a_obs=pltpu.VMEM((128, 512), F32),
        a_x=pltpu.VMEM((128, 128), F32),
        a_fin=pltpu.VMEM((2, 128, 128), F32),
        a_head=pltpu.VMEM((128, 128), F32),
        a_hb=pltpu.VMEM((128, 128), F32),
        loss=pltpu.VMEM((2, 8, 128), F32),
    )


def code_phases():
    for p in range(15):
        yield p, (32 * p) // D, (32 * p) % D


def off_phases():
    for p in range(24):
        yield p, (35 * p + 32) // D, (35 * p + 32) % D


def shifted(v, by):
    by %= 128
    return v if by == 0 else pltpu.roll(v, by, 1)


def take_phase(load, a, s, width, rows):
    lanes = iota((rows, 128), 1)
    first = shifted(load(a), -s)
    if s + width > D:
        second = shifted(load(a + 1), D - s)
        first = jnp.where(lanes < D - s, first, second)
    return jnp.where(lanes < width, first, 0.0)


def with_bias(w, bias):
    if bias is not None:
        w = jnp.where(iota((128, 128), 0) == D, bias, w)
    return low(w.T)


def ones8(v):
    return jnp.concatenate([v, jnp.where(iota((8, v.shape[1]), 0) == 0, 1.0, 0.0)], axis=0)


def prep_weights(rg, R):
    R.w_obs[...] = low(rg[0:OBS, :])
    for w in range(GW):
        R.posb[pl.ds(WIN * w, WIN), :] = rg[OBS + 1:OBS + 1 + WIN, :] + rg[OBS:OBS + 1, :]
    R.vec[...] = jnp.zeros((32, 128), F32)
    for l in range(LAYERS):
        b = BASE + LROW * l
        for j in range(3):
            w = pad8(rg[pl.ds(b + 2 + j, D, stride=3), :])
            R.qkv[l, :, 128 * j:128 * (j + 1)] = low(w)
            R.qkv_t[l, 128 * j:128 * (j + 1), :] = with_bias(w, None if j == 1 else rg[pl.ds(b + 362 + j // 2, 1), :])
        w = pad8(rg[pl.ds(b + 364, D), :])
        R.out[l] = low(w)
        R.out_t[l] = with_bias(w, rg[pl.ds(b + 484, 1), :])
        for j in range(4):
            w = pad8(rg[pl.ds(b + 487 + j, D, stride=4), :])
            R.fc[l, :, 128 * j:128 * (j + 1)] = low(w)
            R.fc_t[l, 128 * j:128 * (j + 1), :] = with_bias(w, rg[pl.ds(b + 967 + j, 1), :])
            w = pad8(rg[pl.ds(b + 971 + D * j, D), :])
            R.proj[l, 128 * j:128 * (j + 1), :] = low(w)
            R.proj_t[l, :, 128 * j:128 * (j + 1)] = with_bias(w, None if j else rg[pl.ds(b + 1451, 1), :])
        for i, r in enumerate(VROWS):
            R.vec[pl.ds(12 * l + i, 1), :] = rg[pl.ds(b + r, 1), :]
    R.vec[24:26, :] = rg[pl.ds(HEAD, 2), :]
    R.hc[...] = jnp.zeros((128, 128), F32)
    R.ho[...] = jnp.zeros((128, 128), F32)
    c0 = HEAD + 2
    for p, a, s in code_phases():
        R.hc[pl.ds(p, 8, stride=15), :] = take_phase(
            lambda i: rg[pl.ds(c0 + i, 8, stride=4), :], a, s, 32, 8)
    o0 = c0 + 32
    for p, a, s in off_phases():
        R.ho[pl.ds(p, 5, stride=24), :] = take_phase(
            lambda i: rg[pl.ds(o0 + i, 5, stride=7), :], a, s, OFFS, 5)
    hw = R.hc[...] + shifted(R.ho[...], 32)
    R.head[...] = low(hw)
    R.head_t[...] = low(hw.T[0:72])
    lanes = iota((1, 128), 1)
    hb = jnp.where(lanes < 32, rg[pl.ds(o0, 1), :], 0.0)
    a, s = (D * OFFS + 32) // D, (D * OFFS + 32) % D
    ob = take_phase(lambda i: rg[pl.ds(o0 + i, 1), :], a, s, OFFS, 1)
    R.vec[26:27, :] = hb + shifted(ob, 32)
    columns = jnp.concatenate([R.vec[...], jnp.zeros((96, 128), F32)], axis=0).T
    for l in range(LAYERS):
        for i in range(12):
            R.bc[l, i] = jnp.broadcast_to(columns[0:D, 12 * l + i:12 * l + i + 1], (D, 128))
    for i in range(2):
        R.bcf[i] = jnp.broadcast_to(columns[0:D, 24 + i:25 + i], (D, 128))
    R.bch[...] = jnp.broadcast_to(columns[0:72, 26:27], (72, 128))


def spread_groups(v, groups, width):
    rows = v.shape[0]
    lanes = iota((rows, 128), 1)
    out = []
    for g in range(groups):
        t, o = (GT * g) // 128, (GT * g) % 128
        a = shifted(v[:, 128 * t:128 * (t + 1)], -o)
        if o + GT > 128:
            b = shifted(v[:, 128 * (t + 1):128 * (t + 2)], -o)
            a = jnp.where(lanes < 128 - o, a, b)
        out.append(jnp.where(lanes < GT, a, 0))
    return out


def prep_tokens(R, counts, codes, actions, valid, feat, chunks):
    groups = chunks * CG
    wins = counts.shape[1]
    R.cnt[...] = jnp.zeros(R.cnt.shape, F32)
    R.cnt[0:WIN // CAMS, :] = counts[...].astype(F32)
    k = iota((GT, 16), 0)
    step = (k % WIN) // CAMS
    sel = jnp.where(step == iota((GT, 16), 1), 1.0, 0.0)
    x = nn(low(sel), low(R.cnt[...]))
    y = jnp.where(iota((GT, wins), 1) % GW == iota((GT, wins), 0) // WIN, x, 0.0)
    pick = jnp.where(iota((wins, 128), 0) // GW == iota((wins, 128), 1) + groups * feat, 1.0, 0.0)
    z = nn(low(y), low(pick))
    kk = iota((GT, 128), 0)
    alive = jnp.where((kk % CAMS).astype(F32) < z, 1.0, 0.0)
    steps = WIN // CAMS
    j, at = iota((48, 128), 0), iota((48, 128), 1)
    own = (at // WIN == j // steps) & ((at % WIN) // CAMS == j % steps) & (at < GT)
    R.k_mask[...] = low(jnp.where(own, 1.0, 0.0))
    may = (at // WIN == j // steps) & ((at % WIN) // CAMS >= j % steps)
    R.q_mask[...] = low(jnp.where(may | (j >= GW * steps), 0.0, -BIG))
    rows = pad8(alive).T
    for g in range(groups):
        R.live[g // CG, :, 128 * (g % CG):128 * (g % CG + 1)] = rows[g:g + 1, :]
        R.dead[g] = jnp.where(iota((8, 128), 0) == 0, 1.0 - rows[g:g + 1, :], 0.0)
    for name, src in (("code", codes), ("act", actions), ("val", valid)):
        parts = spread_groups(src[...].astype(F32), groups, GT)
        dst = getattr(R, name)
        for g in range(groups):
            c, lo = g // CG, 128 * (g % CG)
            part = parts[g]
            if name == "val":
                part = part * rows[g:g + 1, :]
            if name != "code":
                dst[c, 32:40, lo:lo + 128] = jnp.zeros((8, 128), F32)
            dst[c, 0:part.shape[0], lo:lo + 128] = part
    lanes = iota((GT, 128), 1)
    live_total = jnp.sum(jnp.where(lanes < groups, alive, 0.0), keepdims=True)
    v = jnp.zeros((40, L), F32)
    for c in range(chunks):
        v = v + R.val[c]
    valid_total = jnp.sum(v, keepdims=True)
    return live_total, valid_total


def own_rows(slab, h):
    rows = iota((8, 128), 0)
    if h % 2 == 0:
        return jnp.concatenate([slab[0:16], jnp.where(rows < 4, slab[16:24], 0.0)], axis=0)
    return jnp.concatenate([jnp.where(rows >= 4, slab[0:8], 0.0), slab[8:24]], axis=0)


def split(v):
    hi = low(v).astype(F32)
    return hi, v - hi


def attend(R, s, c, q, k, v):
    qh, ql = split(q)
    kh, kl = split(k)
    vh, vl = split(v)
    minus = jnp.where(iota((8, 128), 0) == 0, -BIG, 0.0)

    none = jnp.zeros((128, 128), BF)

    def scores(g, p):
        at = slice(128 * g, 128 * (g + 1))
        qs, ks = [], []
        for h in (2 * p, 2 * p + 1):
            sl = slice(slab_at(h), slab_at(h) + 24)
            hi = own_rows(qh[sl, at], h)
            qd = low(jnp.concatenate([hi, hi, own_rows(ql[sl, at], h), minus], axis=0))
            kd = low(jnp.concatenate([kh[sl, at], kl[sl, at], kh[sl, at], R.dead[c * CG + g]], axis=0))
            qs.append(jnp.concatenate([qd, R.q_mask[...]], axis=0))
            ks.append(jnp.concatenate([kd, R.k_mask[...]], axis=0).T)
        if PAIR:
            both = jnp.concatenate([jnp.concatenate([qs[0], none], axis=1),
                                    jnp.concatenate([none, qs[1]], axis=1)], axis=0)
            return nn(jnp.concatenate(ks, axis=1), both)[0:GT]
        return jnp.concatenate([nn(ks[0], qs[0])[0:GT], nn(ks[1], qs[1])[0:GT]], axis=1)

    def soft(g, p, sc):
        at = slice(128 * g, 128 * (g + 1))
        e = jnp.exp2(sc - jnp.max(sc, axis=0, keepdims=True))
        r = 1.0 / jnp.sum(e, axis=0, keepdims=True)
        e8 = pad8(e)
        eh = low(e8)
        el = low(e8 - eh.astype(F32))
        cols = slice(256 * p, 256 * (p + 1))
        R.prob[s, g, :, cols] = e
        for i in range(2):
            at_h = slice(256 * p + 128 * i, 256 * p + 128 * (i + 1))
            R.prob_low[s, g, :, at_h] = eh[:, 128 * i:128 * (i + 1)].T
        R.rsum[s, 2 * p, :, at] = r[:, 0:128]
        R.rsum[s, 2 * p + 1, :, at] = r[:, 128:256]
        return r, eh, el

    def values(g, p, r, eh, el):
        at = slice(128 * g, 128 * (g + 1))
        out = []
        for i in range(2):
            sl = slice(slab_at(2 * p + i), slab_at(2 * p + i) + 24)
            cols = slice(128 * i, 128 * (i + 1))
            vs = low(jnp.concatenate([vh[sl, at], vl[sl, at]], axis=0))
            o = nn(jnp.concatenate([vs, vs], axis=1), jnp.concatenate([eh[:, cols], el[:, cols]], axis=0))
            out.append((o[0:24] + o[24:48]) * r[:, cols])
        return out

    items = [(g, p) for g in range(CG) for p in range(H // 2)]
    slabs = pipeline(items, scores, soft, values, FAHEAD)
    slabs = [t for pair in slabs for t in pair]
    return jnp.concatenate([join_slabs(slabs[H * g:H * (g + 1)]) for g in range(CG)], axis=1)


PAIR = True
FAHEAD = 2
BAHEAD = 2


def pipeline(items, first, second, third, ahead, between=()):
    n = len(items)
    a, b, out = {}, {}, []
    between = list(between)
    done = 0
    for t in range(n + ahead):
        if t < n:
            a[t] = first(*items[t])
        m = t - ahead + 1
        if 0 <= m < n:
            b[m] = second(*items[m], *(a.pop(m) if isinstance(a[m], tuple) else (a.pop(m),)))
        m = t - ahead
        if 0 <= m < n:
            out.append(third(*items[m], *b.pop(m)))
        while done < len(between) * (t + 1) // (n + ahead):
            between[done]()
            done += 1
    return out


def attend_back(R, s, do, between=()):
    vrows = [R.v_low[s, :, 128 * g:128 * (g + 1)].T for g in range(CG)]

    def probs(g, p):
        at = slice(128 * g, 128 * (g + 1))
        ds, stack = [], []
        for h in (2 * p, 2 * p + 1):
            a = slab_at(h)
            d = own_rows(do[a:a + 24, at], h) * R.rsum[s, h, :, at]
            parts = ([jnp.zeros((a, 128), F32)] if a else []) + [d] + ([jnp.zeros((104 - a, 128), F32)])
            ds.append(low(d))
            stack.append(low(jnp.concatenate(parts, axis=0)))
        return ds, nn(vrows[g], jnp.concatenate(stack, axis=1))[0:GT]

    def inner(g, p, d, dp):
        at = slice(128 * g, 128 * (g + 1))
        e = R.prob[s, g, :, 256 * p:256 * (p + 1)]
        r = jnp.concatenate([R.rsum[s, 2 * p, :, at], R.rsum[s, 2 * p + 1, :, at]], axis=1)
        total = jnp.sum(e * dp, axis=0, keepdims=True) * r
        ds = low(pad8(e * (dp - total)))
        for i in range(2):
            cols = slice(128 * i, 128 * (i + 1))
            R.ds_t[3 * g + p, :, cols] = ds[:, cols].T
        return d, ds

    def outer(g, p, d, ds):
        at = slice(128 * g, 128 * (g + 1))
        out = []
        for i in range(2):
            h = 2 * p + i
            dsh = ds[:, 128 * i:128 * (i + 1)]
            out.append((nn(R.k_low[s, h, :, at], dsh), nn(R.q_low[s, h, :, at], R.ds_t[3 * g + p, :, 128 * i:128 * (i + 1)]),
                        nn(d[i], R.prob_low[s, g, :, 128 * h:128 * (h + 1)])))
        return out

    items = [(g, p) for g in range(CG) for p in range(H // 2)]
    slabs = pipeline(items, probs, inner, outer, BAHEAD, between)
    slabs = [t for pair in slabs for t in pair]
    out = []
    for i in range(3):
        out.append(jnp.concatenate(
            [join_slabs([t[i] for t in slabs[H * g:H * (g + 1)]]) for g in range(CG)], axis=1))
    return out[0] * SCALE, out[1], out[2]


def turn(R, i, v):
    for g in range(CG):
        R.turned[i, 128 * g:128 * (g + 1), :] = v[:, 128 * g:128 * (g + 1)].T


def embed(R, obs, c):
    rows = nn(jnp.concatenate(obs, axis=1), R.w_obs[...])
    parts = []
    for g in range(CG):
        r = rows[GT * g:GT * (g + 1)] + R.posb[...]
        parts.append(pad8(r).T[0:D])
    return jnp.concatenate(parts, axis=1)


def layer_fwd(R, l, c, s, x):
    def vec(i):
        return tile4(R.bc[l, i])

    xh, r = normed(x)
    R.xh1[s] = xh
    R.r1[s] = r
    n1 = low(ones8(xh * vec(G1) + vec(B1)))
    R.n1[s] = n1
    mix = nn(R.qkv_t[l], n1)
    q = mix[0:D] * SCALE
    k = mix[128:128 + D]
    v = mix[256:256 + D]
    for h in range(H):
        a = slab_at(h)
        R.q_low[s, h] = low(q[a:a + 24])
        R.k_low[s, h] = low(k[a:a + 24])
    R.v_low[s] = low(pad8(v))
    att = low(ones8(attend(R, s, c, q * LOG2E, k, v)))
    R.att[l] = att
    x1 = x + nn(R.out_t[l], att)[0:D]
    xh, r = normed(x1)
    R.xh2[l] = xh
    R.r2[l] = r
    n2 = low(ones8(xh * vec(G2) + vec(B2)))
    R.n2[l] = n2
    pre = nn(R.fc_t[l], n2)
    parts = []
    for j in range(4):
        pj = pre[128 * j:128 * j + D]
        half = gelu_half(pj)
        R.pre[l, D * j:D * (j + 1)] = pj
        R.half[l, D * j:D * (j + 1)] = half
        parts.append(low(ones8(pj * half) if j == 0 else pad8(pj * half)))
    inner = jnp.concatenate(parts, axis=0)
    R.inner[l] = inner
    return x1 + nn(R.proj_t[l], inner)[0:D]


def head_step(R, c, x, live_total, valid_total):
    xh, r = normed(x)
    fin = low(pad8(xh * tile4(R.bcf[0]) + tile4(R.bcf[1])))
    hd = nn(R.head_t[...], fin) + tile4(R.bch[...])
    live = R.live[c]
    lw = live * (1.0 / live_total)
    rows = iota((CODES, L), 0).astype(F32)
    grads = []
    csum = jnp.zeros((1, L), F32)
    for b in range(BOOKS):
        lg = hd[CODES * b:CODES * (b + 1)]
        m = jnp.max(lg, axis=0, keepdims=True)
        e = jnp.exp(lg - m)
        s = jnp.sum(e, axis=0, keepdims=True)
        hot = rows == R.code[c, b:b + 1, :]
        picked = jnp.sum(jnp.where(hot, lg, 0.0), axis=0, keepdims=True)
        csum = csum + (jnp.log(s) + m - picked) * live
        grads.append((e * (1.0 / s) - jnp.where(hot, 1.0, 0.0)) * lw)
    diff = hd[32:72] - R.act[c]
    val = R.val[c]
    sq = diff * diff + 1.0
    ri = lax.rsqrt(sq)
    asum = val * (sq * ri)
    grads.append((val * (1.0 / valid_total)) * (diff * ri))
    R.loss[0, 0:1] += fold4(csum)
    af = fold4(asum)
    R.loss[1] += af[0:8] + af[8:16] + af[16:24] + af[24:32] + af[32:40]
    dh = jnp.concatenate(grads, axis=0)
    R.a_hb[0:72] += fold4(dh)
    dhl = low(jnp.concatenate([dh, jnp.zeros((56, L), F32)], axis=0))
    turn(R, 4, dhl)
    R.a_head[...] += nn(fin, R.turned[4])
    df = nn(R.head[...], dhl)[0:D]
    R.a_fin[0, 0:D] += fold4(df * xh)
    R.a_fin[1, 0:D] += fold4(df)
    return normed_back(df * tile4(R.bcf[0]), xh, r)


def add_bias(R, l, i, v):
    R.a_bias[l, i, 0:D] += fold4(v)


def mlp_bwd(R, l, dout):
    outl = low(pad8(dout))
    add_bias(R, l, PB, dout)
    parts = []
    for j in range(4):
        rows = slice(D * j, D * (j + 1))
        dj = nn(R.proj[l, 128 * j:128 * (j + 1)], outl)
        parts.append(low(pad8(dj[0:D] * gelu_slope(R.pre[l, rows], R.half[l, rows]))))
    prel = jnp.concatenate(parts, axis=0)
    dn = nn(R.fc[l], prel)[0:D]
    xh = R.xh2[l]
    add_bias(R, l, G2, dn * xh)
    add_bias(R, l, B2, dn)
    dmid = normed_back(dn * tile4(R.bc[l, G2]), xh, R.r2[l]) + dout
    midl = low(pad8(dmid))
    add_bias(R, l, OB, dmid)
    da = nn(R.out[l], midl)[0:D]

    turn(R, 0, outl)
    turn(R, 1, R.n2[l])
    turn(R, 2, midl)

    def a_proj(j):
        def run():
            rows = slice(256 * j, 256 * (j + 1))
            R.a_proj[l, rows] += nn(R.inner[l, rows], R.turned[0])
        return run

    def a_fc(j):
        def run():
            rows = slice(256 * j, 256 * (j + 1))
            R.a_fc[l, rows] += nn(prel[rows], R.turned[1])
        return run

    def a_out():
        R.a_out[l] += nn(R.att[l], R.turned[2])

    return dmid, da, [a_proj(0), a_proj(1), a_fc(0), a_fc(1), a_out]


def att_bwd(R, l, s, dmid, da, between):
    turn(R, 3, R.n1[s])
    dq, dk, dv = attend_back(R, s, da, between)
    mixl = jnp.concatenate([low(pad8(dq)), low(pad8(dk)), low(pad8(dv))], axis=0)
    dn = nn(R.qkv[l], mixl)[0:D]
    add_bias(R, l, QB, dq)
    add_bias(R, l, VB, dv)
    R.a_qkv[l] += nn(mixl, R.turned[3])
    xh = R.xh1[s]
    add_bias(R, l, G1, dn * xh)
    add_bias(R, l, B1, dn)
    return normed_back(dn * tile4(R.bc[l, G1]), xh, R.r1[s]) + dmid


def embed_bwd(R, obs, c, dx):
    R.a_x[0:D] += fold4(dx)
    lanes = iota((D, 128), 1)
    tiles = []
    gs = [dx[:, 128 * g:128 * (g + 1)] for g in range(CG)]
    for t in range(CG):
        a = shifted(gs[t], -8 * t)
        b = shifted(gs[t + 1], 120 - 8 * t) if t + 1 < CG else jnp.zeros((D, 128), F32)
        tiles.append(jnp.where(lanes < GT - 8 * t, a, b))
    gl = low(pad8(jnp.concatenate(tiles, axis=1)))
    R.a_obs[...] += nn(gl, jnp.concatenate(obs, axis=1))


def zero_grads(R):
    for name in ("a_qkv", "a_out", "a_fc", "a_proj", "a_bias", "a_obs", "a_x", "a_fin", "a_head", "a_hb", "loss"):
        ref = getattr(R, name)
        ref[...] = jnp.zeros(ref.shape, F32)


HIGH = lax.Precision.HIGHEST


LATE = 364
EARLY_ROWS = (OB, G2, B2, PB)


def lane_sums(v):
    return jnp.sum(v.T, axis=0, keepdims=True)


def pack_vectors(R, rg, l, which):
    b = BASE + LROW * l
    for i in which:
        rg[pl.ds(b + VROWS[i], 1), :] = lane_sums(R.a_bias[l, i])


def pack_early(R, rg, l):
    b = BASE + LROW * l
    rg[pl.ds(b + 364, D), :] = R.a_out[l, 0:D]
    for j in range(4):
        fc = R.a_fc[l, 128 * j:128 * (j + 1), :].T
        rg[pl.ds(b + 487 + j, D, stride=4), :] = fc[0:D]
        rg[pl.ds(b + 967 + j, 1), :] = fc[D:D + 1]
        rg[pl.ds(b + 971 + D * j, D), :] = R.a_proj[l, 128 * j:128 * j + D, :]
    pack_vectors(R, rg, l, EARLY_ROWS)


def pack_late(R, rg, l):
    b = BASE + LROW * l
    for j in range(3):
        rg[pl.ds(b + 2 + j, D, stride=3), :] = R.a_qkv[l, 128 * j:128 * (j + 1), :].T[0:D]
    pack_vectors(R, rg, l, (G1, B1, QB, VB))


def pack_embed(R, rg):
    for f in range(OBS // 128):
        rg[128 * f:128 * (f + 1), :] = R.a_obs[:, 128 * f:128 * (f + 1)].T
    slot, lane = iota((32, 128), 0), iota((32, 128), 1)
    sel = jnp.where((slot == 0) | (lane % WIN == slot - 1), 1.0, 0.0)
    sel = jnp.where(lane < GT, sel, 0.0)
    rows = nt(sel, R.a_x[...], HIGH)
    rg[pl.ds(OBS, 1 + WIN), :] = rows[0:1 + WIN]


def pack_head(R, rg):
    for i in range(2):
        rg[pl.ds(HEAD + i, 1), :] = lane_sums(R.a_fin[i])
    lanes8 = iota((8, 128), 1)
    grad = R.a_head[...]
    R.hc[...] = jnp.where(iota((128, 128), 1) < 32, grad, 0.0)
    R.ho[...] = jnp.where(iota((128, 128), 1) < OFFS, shifted(grad, -32), 0.0)
    c0 = HEAD + 2
    o0 = c0 + 32

    def put(phases, src, rows_n, stride, width, count):
        acc = [jnp.zeros((rows_n, 128), F32) for _ in range(count + 1)]
        lanes = iota((rows_n, 128), 1)
        for p, a, s in phases:
            v = src[pl.ds(p, rows_n, stride=stride), :]
            first = shifted(v, s)
            if s + width > D:
                acc[a] = acc[a] + jnp.where((lanes >= s) & (lanes < D), first, 0.0)
                acc[a + 1] = acc[a + 1] + jnp.where(lanes < s + width - D, shifted(v, s - D), 0.0)
            else:
                acc[a] = acc[a] + first
        return acc

    acc = put(code_phases(), R.hc, 8, 15, 32, 4)
    for a in range(4):
        rg[pl.ds(c0 + a, 8, stride=4), :] = acc[a]
    hb = lane_sums(R.a_hb[...])
    lane1 = iota((1, 128), 1)
    rg[pl.ds(o0, 48), :] = jnp.zeros((48, 128), F32)
    acc = put(off_phases(), R.ho, 5, 24, OFFS, 7)
    for a in range(7):
        rg[pl.ds(o0 + a, 5, stride=7), :] = acc[a]
    rg[pl.ds(o0 + 7, 5, stride=7), :] = rg[pl.ds(o0 + 7, 5, stride=7), :] + acc[7]
    rg[pl.ds(o0, 1), :] = rg[pl.ds(o0, 1), :] + jnp.where(lane1 < 32, hb, 0.0)
    a, s = (D * OFFS + 32) // D, (D * OFFS + 32) % D
    ob = jnp.where(lane1 < OFFS, shifted(hb, -32), 0.0)
    rg[pl.ds(o0 + a, 1), :] = rg[pl.ds(o0 + a, 1), :] + shifted(ob, s)


MESH = pl.DeviceIdType.MESH


def round_up(n, m):
    return -(-n // m) * m


class Plan:
    def __init__(self, feats, toks, shard, tok_rows):
        self.feats, self.toks, self.chips = feats, toks, toks // 2
        self.shard = shard
        self.block = round_up(-(-(shard + 112) // D), 16)
        self.flat_rows = self.block // 16 * 15
        self.local = round_up(-(-shard // 1024), 1) * 8
        self.work = round_up(max(self.flat_rows, self.local + 1), 8)
        self.own_rows = tok_rows // feats
        self.chunks = self.own_rows // CT
        self.early = [f for f in range(feats) if shard * toks * f // D >= BASE + LATE]
        self.grid = round_up(-(-(shard * feats * toks) // D) + self.block, 8)


def comm_scratch(P):
    dma = pltpu.SemaphoreType.DMA
    B, C, Fn = P.block, P.chips, P.feats
    return dict(
        rg=pltpu.VMEM((P.grid, 128), F32),
        ob=pltpu.VMEM((P.chunks, Fn, L, 128), BF),
        pg=pltpu.VMEM((2, C, Fn, B, 128), BF),
        loc=pltpu.VMEM((P.work, 128), F32),
        rblk=pltpu.VMEM((B, 128), F32),
        codes_in=pltpu.VMEM((BOOKS, P.own_rows), jnp.int32),
        act_in=pltpu.VMEM((OFFS, P.own_rows), F32),
        val_in=pltpu.VMEM((OFFS, P.own_rows), jnp.int32),
        tz=pltpu.VMEM((2, Fn, 8, 128), F32),
        tc=pltpu.VMEM((2, C, 8, 128), F32),
        ts=pltpu.VMEM((2, 2, 8, 128), F32),
        sb1=pltpu.VMEM((C, Fn, B, 128), F32),
        rb1=pltpu.VMEM((C, Fn, B, 128), F32),
        sb2=pltpu.VMEM((C, Fn, B, 128), BF),
        rb2=pltpu.VMEM((C, Fn, B, 128), BF),
        col=pltpu.VMEM((Fn, B, 128), F32),
        sb3=pltpu.VMEM((Fn, B, 128), F32),
        rb3=pltpu.VMEM((Fn, B, 128), F32),
        s_p1=dma((2, Fn)), s_p2=dma((2, C)), s_p3=dma((2, C)),
        s_tz=dma((2, 2, Fn)), s_tc=dma((2, 2, C)), s_ts=dma((2, 2)),
        s_ob=dma((2, 2 * P.chunks, Fn)),
        s_own=dma((P.chunks,)),
        s_in=dma((3,)),
        s_r1=dma((3, 2, C)), s_r2=dma((2, Fn, C)), s_r3=dma((2, Fn)),
    )


def to_rows(loc, rblk, delta, P):
    v = loc[...]
    lanes = iota(v.shape, 1)
    moved = pltpu.roll(v, delta, 1)
    loc[...] = jnp.where(lanes >= delta, moved, pltpu.roll(moved, 1, 0))
    n = P.block // 16
    lane = iota((n, 128), 1)
    for j in range(16):
        if j < 15:
            a = shifted(loc[pl.ds(j, n, stride=15), :], 8 * j)
        if j > 0:
            b = shifted(loc[pl.ds(j - 1, n, stride=15), :], 8 * j)
            a = jnp.where(lane < 8 * j, b, a) if j < 15 else b
        rblk[pl.ds(j, n, stride=16), :] = jnp.where(lane < D, a, 0.0)


def from_rows(rblk, loc, delta, P):
    n = P.block // 16
    lane = iota((n, 128), 1)
    loc[...] = jnp.zeros(loc.shape, F32)
    for i in range(15):
        a = shifted(rblk[pl.ds(i, n, stride=16), :], -8 * i)
        b = shifted(rblk[pl.ds(i + 1, n, stride=16), :], D - 8 * i)
        loc[pl.ds(i, n, stride=15), :] = jnp.where(lane < D - 8 * i, a, b)
    v = loc[...]
    lanes = iota(v.shape, 1)
    moved = pltpu.roll(v, lax.rem(128 - delta, 128), 1)
    v = jnp.where(lanes < 128 - delta, moved, pltpu.roll(moved, P.work - 1, 0))
    return v[0:P.local]


def step_kernel(P, names, master, obs, counts, codes, actions, valid, grad, sums, *scratch):
    R = Refs()
    for name, ref in zip(names, scratch):
        setattr(R, name, ref)
    Fn, C, B = P.feats, P.chips, P.block
    feat = lax.axis_index("feat")
    tok = lax.axis_index("tok")
    chip = tok // 2
    core = tok % 2
    me = feat * P.toks + tok
    delta = lax.rem(me * P.shard, D)

    def z_peer(i):
        return lax.rem(feat + i, Fn)

    def z_from(i):
        return lax.rem(feat + Fn - i, Fn)

    def c_peer(i):
        return lax.rem(chip + i, C)

    def c_from(i):
        return lax.rem(chip + C - i, C)

    def to_z(i):
        return (z_peer(i), tok)

    def to_c(i):
        return (feat, 2 * c_peer(i) + core)

    sibling = (feat, 2 * chip + 1 - core)

    def send(src, dst, sems, at, dev):
        return pltpu.make_async_remote_copy(
            src_ref=src, dst_ref=dst, send_sem=sems.at[(0,) + at], recv_sem=sems.at[(1,) + at],
            device_id=dev, device_id_type=MESH)

    n = P.own_rows
    ins = []
    for i, (src, dst) in enumerate(((codes, R.codes_in), (actions, R.act_in), (valid, R.val_in))):
        ins.append(pltpu.make_async_copy(src.at[:, pl.ds(pl.multiple_of(feat * n, 128), n)], dst, R.s_in.at[i]))
        ins[-1].start()

    barrier = pltpu.get_barrier_semaphore()
    peers = [to_z(i) for i in range(1, Fn)] + [to_c(i) for i in range(1, C)] + [sibling]
    for dev in peers:
        pl.semaphore_signal(barrier, inc=1, device_id=dev, device_id_type=MESH)

    R.loc[...] = jnp.zeros(R.loc.shape, F32)
    whole = P.shard // 1024
    R.loc[0:8 * whole, :] = master[pl.ds(0, 1024 * whole)].reshape(8 * whole, 128)
    rest = P.shard - 1024 * whole
    last = jnp.concatenate([master[pl.ds(1024 * whole, rest)], jnp.zeros((1024 - rest,), F32)])
    R.loc[8 * whole:8 * whole + 8, :] = last.reshape(8, 128)
    to_rows(R.loc, R.rblk, delta, P)
    R.pg[core, chip, feat] = low(R.rblk[...])
    pl.semaphore_wait(barrier, len(peers))

    p1 = []
    for i in range(1, Fn):
        blk = R.pg.at[core, chip, feat]
        p1.append(send(blk, blk, R.s_p1, (i,), to_z(i)))
        p1[-1].start()

    half = CT // 2

    def obs_copies(p):
        cps = []
        for i in range(1, Fn):
            src = obs.at[pl.ds(pl.multiple_of(z_peer(i) * n + half * p, 16), half), :]
            dst = R.ob.at[p // 2, feat, pl.ds(pl.multiple_of(half * (p % 2), 16), half), :]
            cps.append(send(src, dst, R.s_ob, (p, i), to_z(i)))
        return cps

    def start_obs(p):
        for cp in obs_copies(p):
            cp.start()

    own = []
    for c in range(P.chunks):
        src = obs.at[pl.ds(pl.multiple_of(feat * n + CT * c, 16), CT), :]
        own.append(pltpu.make_async_copy(src, R.ob.at[c, feat, pl.ds(0, CT), :], R.s_own.at[c]))
        own[-1].start()
    for cp in ins:
        cp.wait()
    zero_grads(R)
    for c in range(P.chunks):
        for f in range(Fn):
            R.ob[c, f, CT:L, :] = jnp.zeros((L - CT, 128), BF)
    live_n, valid_n = prep_tokens(R, counts, R.codes_in, R.act_in, R.val_in, feat, P.chunks)

    def two_rows(a, b):
        return jnp.concatenate([jnp.broadcast_to(a, (1, 128)), jnp.broadcast_to(b, (1, 128)),
                                jnp.zeros((6, 128), F32)], axis=0)

    def z_copies(w):
        return [send(R.tz.at[w, feat], R.tz.at[w, feat], R.s_tz.at[w], (i,), to_z(i)) for i in range(1, Fn)]

    def c_copies(w):
        return [send(R.tc.at[w, chip], R.tc.at[w, chip], R.s_tc.at[w], (i,), to_c(i)) for i in range(1, C)]

    def s_copies(w):
        return [send(R.ts.at[w, core], R.ts.at[w, core], R.s_ts.at[w], (), sibling)]

    def start_all(cps):
        for cp in cps:
            cp.start()

    def total(ref, w, count):
        v = ref[w, 0]
        for i in range(1, count):
            v = v + ref[w, i]
        return v

    def wait_all(cps):
        for cp in cps:
            cp.wait()

    R.tz[0, feat] = two_rows(live_n, valid_n)
    start_all(z_copies(0))
    wait_all(p1)
    start_obs(0)
    start_obs(1)
    p2 = []
    for i in range(1, C):
        blk = R.pg.at[core, chip]
        p2.append(send(blk, blk, R.s_p2, (i,), to_c(i)))
        p2[-1].start()
    p3 = [send(R.pg.at[core, chip], R.pg.at[core, chip], R.s_p3, (0,), sibling)]
    p3[0].start()
    wait_all(z_copies(0))
    R.tc[0, chip] = total(R.tz, 0, Fn)
    start_all(c_copies(0))
    for i in range(1, C):
        p2[i - 1].wait_recv()
        blk = R.pg.at[core, c_from(i)]
        p3.append(send(blk, blk, R.s_p3, (i,), sibling))
        p3[-1].start()
    wait_all(c_copies(0))
    R.ts[0, core] = total(R.tc, 0, C)
    start_all(s_copies(0))
    for cp in p2:
        cp.wait_send()
    wait_all(p3)
    R.rg[0:8, :] = jnp.zeros((8, 128), F32)

    def place(d, _):
        r0 = (P.shard * d) // D
        f, t = d // P.toks, d % P.toks
        blk = R.pg[t % 2, t // 2, f].astype(F32)
        before = R.rg[pl.ds(r0, 1), :]
        R.rg[pl.ds(r0, B), :] = blk
        R.rg[pl.ds(r0, 1), :] = blk[0:1] + before
        return 0

    lax.fori_loop(0, Fn * P.toks, place, 0)
    prep_weights(R.rg, R)
    wait_all(s_copies(0))
    counted = total(R.ts, 0, 2)
    live_total = counted[0:1, 0:1]
    valid_total = counted[1:2, 0:1]

    for cp in own:
        cp.wait()


    def rows_of(f, ch, co):
        return (P.shard * (f * P.toks + 2 * ch + co)) // D

    early = P.early[0] if P.early else Fn
    planes = [slice(Fn - 1, Fn), slice(early, Fn - 1), slice(0, early)]

    def r1_copy(w, i):
        at = pl.ds(planes[w].start, planes[w].stop - planes[w].start)
        return send(R.sb1.at[i, at], R.rb1.at[i, at], R.s_r1.at[w], (i,), sibling)

    def r2_copy(f, i):
        return send(R.sb2.at[i, f], R.rb2.at[i, f], R.s_r2.at[:, f], (i,), to_c(i))

    def r3_copy(i):
        return send(R.sb3.at[i], R.rb3.at[i], R.s_r3, (i,), to_z(i))

    order = list(range(1, C)) + [0]

    def sum_cores(w):
        for i in order:
            for f in range(planes[w].start, planes[w].stop):
                R.sb1[i, f] = R.rg[pl.ds(rows_of(f, c_peer(i), 1 - core), B), :]
            r1_copy(w, i).start()

    def sum_chips(w):
        for i in order:
            r1_copy(w, i).wait_recv()
            for f in range(planes[w].start, planes[w].stop):
                v = R.rg[pl.ds(rows_of(f, c_peer(i), core), B), :] + R.rb1[i, f]
                if i:
                    R.sb2[i, f] = low(v)
                    r2_copy(f, i).start()
                else:
                    R.col[f] = v

    def sum_column(f):
        v = R.col[f]
        for i in range(1, C):
            r2_copy(f, i).wait_recv()
            v = v + R.rb2[i, f].astype(F32)
        R.col[f] = v
        for i in range(1, Fn):
            @pl.when(z_peer(i) == f)
            def _():
                R.sb3[i] = v
                r3_copy(i).start()

    def chunk(c, _):
        for p in (2 * c, 2 * c + 1):
            for cp in obs_copies(p):
                cp.wait_recv()

        @pl.when(c + 1 < P.chunks)
        def _():
            start_obs(2 * c + 2)
            start_obs(2 * c + 3)

        R.x[...] = embed(R, [R.ob[c, f, 0:CT, :] for f in range(Fn)], c)

        def lay(l, _):
            R.x[...] = layer_fwd(R, l, c, l, R.x[...])
            return 0

        lax.fori_loop(0, LAYERS, lay, 0)

        dx = head_step(R, c, R.x[...], live_total, valid_total)
        dmid, da, rest = mlp_bwd(R, 1, dx)
        R.x[...] = att_bwd(R, 1, 1, dmid, da, rest)
        @pl.when(c == P.chunks - 1)
        def _():
            R.rg[pl.ds(HEAD + 32, P.grid - HEAD - 32), :] = jnp.zeros((P.grid - HEAD - 32, 128), F32)
            pack_head(R, R.rg)
            pack_late(R, R.rg, 1)
            pack_early(R, R.rg, 1)
            R.ts[1, core] = two_rows(jnp.sum(R.loss[0], keepdims=True), jnp.sum(R.loss[1], keepdims=True))
            sum_cores(0)
            start_all(s_copies(1))

        dmid, da, rest = mlp_bwd(R, 0, R.x[...])
        R.dmid[...] = dmid
        R.da[...] = da
        for run in rest:
            run()

        @pl.when(c == P.chunks - 1)
        def _():
            pack_early(R, R.rg, 0)
            sum_cores(1)
            sum_chips(0)
            wait_all(s_copies(1))
            R.tc[1, chip] = total(R.ts, 1, 2)
            start_all(c_copies(1))

        dx = att_bwd(R, 0, 0, R.dmid[...], R.da[...], [])

        @pl.when(c == P.chunks - 1)
        def _():
            sum_chips(1)

        embed_bwd(R, [R.ob[c, f] for f in range(Fn)], c, dx)
        return 0

    lax.fori_loop(0, P.chunks, chunk, 0)
    pack_embed(R, R.rg)
    pack_late(R, R.rg, 0)
    sum_cores(2)
    wait_all(c_copies(1))
    R.tz[1, feat] = total(R.tc, 1, C)
    start_all(z_copies(1))
    sum_column(Fn - 1)
    sum_chips(2)
    for f in (*range(early, Fn - 1), *range(early)):
        sum_column(f)
    for i in range(1, Fn):
        r3_copy(i).wait_recv()
    v = R.col[feat]
    for i in range(1, Fn):
        v = v + R.rb3[i]
    R.rblk[...] = v
    grad[...] = from_rows(R.rblk, R.loc, delta, P)
    wait_all(z_copies(1))
    lost = total(R.tz, 1, Fn)
    sums[...] = jnp.concatenate([lost[0:1], counted[0:1], lost[1:2], counted[1:2], jnp.zeros((4, 128), F32)], axis=0)
    for p in range(2 * P.chunks):
        for cp in obs_copies(p):
            cp.wait_send()
    for w in range(3):
        for i in range(C):
            r1_copy(w, i).wait_send()
    for i in range(1, C):
        for f in range(Fn):
            r2_copy(f, i).wait_send()
    for i in range(1, Fn):
        r3_copy(i).wait_send()


def adam_kernel(shard, grad, sums, master, first, second, new_master, new_first, new_second, parts):
    whole = shard // 1024
    for lo, hi in ((0, whole), (whole, whole + 1)):
        n = min(1024 * hi, shard) - 1024 * lo
        at = pl.ds(1024 * lo, n)
        g = grad[8 * lo:8 * hi].reshape(1024 * (hi - lo))[0:n]
        old = master[at]
        f_new = BETA_ONE * first[at] + (1.0 - BETA_ONE) * g
        s_new = BETA_TWO * second[at] + (1.0 - BETA_TWO) * g * g
        f_hat = f_new / (1.0 - BETA_ONE ** STEP_NO)
        s_hat = s_new / (1.0 - BETA_TWO ** STEP_NO)
        new_first[at] = f_new
        new_second[at] = s_new
        new_master[at] = old - LEARN_RATE * (f_hat / (jnp.sqrt(s_hat) + ADAM_EPS) + DECAY_RATE * old)
    for i in range(4):
        parts[i] = sums[i, 0]


def solution(mesh):
    feats, toks = mesh.shape["feat"], mesh.shape["tok"]

    def shards(master, first, second, obs, counts, codes, actions, valid):
        P_ = Plan(feats, toks, master.shape[0], obs.shape[0])
        scratch = dict(scratch_list(P_.chunks))
        scratch.update(comm_scratch(P_))
        vmem = pl.BlockSpec(memory_space=pltpu.VMEM)
        hbm = pl.BlockSpec(memory_space=pl.ANY)
        grad, sums = pl.pallas_call(
            functools.partial(step_kernel, P_, list(scratch)),
            out_shape=(jax.ShapeDtypeStruct((P_.local, 128), F32), jax.ShapeDtypeStruct((8, 128), F32)),
            in_specs=[vmem, hbm, vmem, hbm, hbm, hbm],
            out_specs=(vmem, vmem),
            scratch_shapes=list(scratch.values()),
            compiler_params=pltpu.CompilerParams(
                collective_id=0, has_side_effects=True, vmem_limit_bytes=60 * 2 ** 20),
        )(master, obs, counts.T, codes.T, actions, valid)
        flat = jax.ShapeDtypeStruct((P_.shard,), F32)
        return pl.pallas_call(
            functools.partial(adam_kernel, P_.shard),
            out_shape=(flat, flat, flat, jax.ShapeDtypeStruct((4,), F32)),
            in_specs=[vmem] * 5,
            out_specs=(vmem, vmem, vmem, pl.BlockSpec(memory_space=pltpu.SMEM)),
        )(grad, sums, master, first, second)

    weights = PSpec(("feat", "tok"))
    return jax.shard_map(
        shards, mesh=mesh,
        in_specs=(weights, weights, weights, PSpec("tok", "feat"), PSpec("tok", None), PSpec("tok", None),
                  PSpec(None, "tok"), PSpec(None, "tok")),
        out_specs=(weights, weights, weights, PSpec()), check_vma=False)
```

```python
import functools
import math

import jax
import jax.numpy as jnp
from jax import lax
from jax.experimental import pallas as pl
from jax.experimental.pallas import tpu as pltpu
from jax.sharding import PartitionSpec as PSpec

D = 120
H = 6
HD = 20
FF = 480
OBS = 512
LAYERS = 2
CAMS = 3
BOOKS = 2
CODES = 16
SPAN = 5
ACT = 7
WIN = 30
OFFS = SPAN * ACT
NORM_EPS = 1e-05
STEP_NO = 10
BETA_ONE = 0.9
BETA_TWO = 0.999
ADAM_EPS = 1e-08
DECAY_RATE = 0.1
LEARN_RATE = 0.05
GW = 4
GT = GW * WIN
CG = 4
L = CG * 128
CT = CG * GT
F32 = jnp.float32
BF = jnp.bfloat16
SCALE = HD ** (-0.5)
LROW = 2 * 1 + 3 * D + 2 + D + 1 + 2 + 4 * D + 4 + 4 * D + 1
BASE = OBS + 1 + WIN
HEAD = BASE + LAYERS * LROW
NV = 13
VROWS = [0, 1, 362, 363, 484, 485, 486, 967, 968, 969, 970, 1451]
(G1, B1, QB, VB, OB, G2, B2, FB0, FB1, FB2, FB3, PB) = range(12)


def nn(a, b):
    return lax.dot_general(a, b, (((1,), (0,)), ((), ())), preferred_element_type=F32)


def nt(a, b, precision=None):
    return lax.dot_general(a, b, (((1,), (1,)), ((), ())), preferred_element_type=F32, precision=precision)


def low(v):
    return v.astype(BF)


def pad8(v):
    return jnp.concatenate([v, jnp.zeros((8, v.shape[1]), v.dtype)], axis=0)


def tile4(v):
    return jnp.concatenate([v] * CG, axis=1)


def fold4(v):
    out = v[:, 0:128]
    for g in range(1, CG):
        out = out + v[:, 128 * g:128 * (g + 1)]
    return out


def iota(shape, axis):
    return lax.broadcasted_iota(jnp.int32, shape, axis)


def slab_at(h):
    return 20 * h - (4 if h % 2 else 0)


def head_stack(v):
    rows = iota((8, 128), 0)
    cols = []
    for h in range(H):
        a = slab_at(h)
        if h % 2 == 0:
            parts = [v[a:a + 16], jnp.where(rows < 4, v[a + 16:a + 24], 0.0)]
        else:
            parts = [jnp.where(rows >= 4, v[a:a + 8], 0.0), v[a + 8:a + 24]]
        if a > 0:
            parts = [jnp.zeros((a, 128), F32)] + parts
        if a + 24 < 128:
            parts = parts + [jnp.zeros((128 - a - 24, 128), F32)]
        cols.append(jnp.concatenate(parts, axis=0))
    return jnp.concatenate(cols, axis=1)


def join_slabs(slabs):
    rows = iota((8, 128), 0)
    parts = []
    for p in range(3):
        a, b = slabs[2 * p], slabs[2 * p + 1]
        parts += [a[0:16], jnp.where(rows < 4, a[16:24], b[0:8]), b[8:24]]
    return jnp.concatenate(parts, axis=0)


def slabs_of(v):
    return [v[slab_at(h):slab_at(h) + 24] for h in range(H)]


def hi_lo(v):
    hi = low(v)
    return hi, low(v - hi.astype(F32))


def normed(x):
    mean = jnp.sum(x, axis=0, keepdims=True) * (1.0 / D)
    c = x - mean
    var = jnp.sum(c * c, axis=0, keepdims=True) * (1.0 / D)
    r = lax.rsqrt(var + NORM_EPS)
    return c * r, r


def normed_back(d, xh, r):
    m0 = jnp.sum(d, axis=0, keepdims=True) * (1.0 / D)
    m1 = jnp.sum(d * xh, axis=0, keepdims=True) * (1.0 / D)
    return r * (d - m0 - xh * m1)


GA = math.sqrt(2.0 / math.pi)
GB = 0.044715


def gelu_half(x):
    return 0.5 + 0.5 * jnp.tanh(x * (GA + (GA * GB) * (x * x)))


def gelu_slope(x, s):
    return s + (x * s) * (1.0 - s) * (2.0 * GA + (6.0 * GA * GB) * (x * x))


LOG2E = math.log2(math.e)
BIG = 1e30


class Refs:
    pass


def scratch_list(chunks):
    groups = chunks * CG
    return dict(
        w_obs=pltpu.VMEM((OBS, 128), BF),
        posb=pltpu.VMEM((GT, 128), F32),
        qkv_t=pltpu.VMEM((LAYERS, 384, 128), BF),
        qkv=pltpu.VMEM((LAYERS, 128, 384), BF),
        out_t=pltpu.VMEM((LAYERS, 128, 128), BF),
        out=pltpu.VMEM((LAYERS, 128, 128), BF),
        fc_t=pltpu.VMEM((LAYERS, 512, 128), BF),
        fc=pltpu.VMEM((LAYERS, 128, 512), BF),
        proj_t=pltpu.VMEM((LAYERS, 128, 512), BF),
        proj=pltpu.VMEM((LAYERS, 512, 128), BF),
        head_t=pltpu.VMEM((72, 128), BF),
        head=pltpu.VMEM((128, 128), BF),
        vec=pltpu.VMEM((32, 128), F32),
        bc=pltpu.VMEM((LAYERS, 12, GT, 128), F32),
        bcf=pltpu.VMEM((2, GT, 128), F32),
        bch=pltpu.VMEM((72, 128), F32),
        hc=pltpu.VMEM((128, 128), F32),
        ho=pltpu.VMEM((128, 128), F32),
        cnt=pltpu.VMEM((16, 256), F32),
        live=pltpu.VMEM((chunks, 1, L), F32),
        act=pltpu.VMEM((chunks, 40, L), F32),
        val=pltpu.VMEM((chunks, 40, L), F32),
        code=pltpu.VMEM((chunks, 2, L), F32),
        x=pltpu.VMEM((D, L), F32),
        dmid=pltpu.VMEM((D, L), F32),
        da=pltpu.VMEM((D, L), F32),
        xh1=pltpu.VMEM((LAYERS, D, L), F32),
        r1=pltpu.VMEM((LAYERS, 1, L), F32),
        xh2=pltpu.VMEM((LAYERS, D, L), F32),
        r2=pltpu.VMEM((LAYERS, 1, L), F32),
        n1=pltpu.VMEM((LAYERS, 128, L), BF),
        n2=pltpu.VMEM((LAYERS, 128, L), BF),
        att=pltpu.VMEM((LAYERS, 128, L), BF),
        q_low=pltpu.VMEM((LAYERS, H, 24, L), BF),
        k_low=pltpu.VMEM((LAYERS, H, 24, L), BF),
        v_low=pltpu.VMEM((LAYERS, 128, L), BF),
        rsum=pltpu.VMEM((LAYERS, H, 1, L), F32),
        prob=pltpu.VMEM((LAYERS, CG, GT, H * 128), F32),
        prob_low=pltpu.VMEM((LAYERS, CG, 128, H * 128), BF),
        k_mask=pltpu.VMEM((48, 128), BF),
        q_mask=pltpu.VMEM((48, 128), BF),
        dead=pltpu.VMEM((groups, 8, 128), F32),
        pre=pltpu.VMEM((LAYERS, FF, L), F32),
        half=pltpu.VMEM((LAYERS, FF, L), F32),
        inner=pltpu.VMEM((LAYERS, 512, L), BF),
        a_qkv=pltpu.VMEM((LAYERS, 384, 128), F32),
        ds_t=pltpu.VMEM((CG * H // 2, 128, 256), BF),
        turned=pltpu.VMEM((5, L, 128), BF),
        a_out=pltpu.VMEM((LAYERS, 128, 128), F32),
        a_fc=pltpu.VMEM((LAYERS, 512, 128), F32),
        a_proj=pltpu.VMEM((LAYERS, 512, 128), F32),
        a_bias=pltpu.VMEM((LAYERS, 12, 128, 128), F32),
        a_obs=pltpu.VMEM((128, 512), F32),
        a_x=pltpu.VMEM((128, 128), F32),
        a_fin=pltpu.VMEM((2, 128, 128), F32),
        a_head=pltpu.VMEM((128, 128), F32),
        a_hb=pltpu.VMEM((128, 128), F32),
        loss=pltpu.VMEM((2, 8, 128), F32),
    )


def code_phases():
    for p in range(15):
        yield p, (32 * p) // D, (32 * p) % D


def off_phases():
    for p in range(24):
        yield p, (35 * p + 32) // D, (35 * p + 32) % D


def shifted(v, by):
    by %= 128
    return v if by == 0 else pltpu.roll(v, by, 1)


def take_phase(load, a, s, width, rows):
    lanes = iota((rows, 128), 1)
    first = shifted(load(a), -s)
    if s + width > D:
        second = shifted(load(a + 1), D - s)
        first = jnp.where(lanes < D - s, first, second)
    return jnp.where(lanes < width, first, 0.0)


def with_bias(w, bias):
    if bias is not None:
        w = jnp.where(iota((128, 128), 0) == D, bias, w)
    return low(w.T)


def ones8(v):
    return jnp.concatenate([v, jnp.where(iota((8, v.shape[1]), 0) == 0, 1.0, 0.0)], axis=0)


def prep_weights(rg, R):
    R.w_obs[...] = low(rg[0:OBS, :])
    for w in range(GW):
        R.posb[pl.ds(WIN * w, WIN), :] = rg[OBS + 1:OBS + 1 + WIN, :] + rg[OBS:OBS + 1, :]
    R.vec[...] = jnp.zeros((32, 128), F32)
    for l in range(LAYERS):
        b = BASE + LROW * l
        for j in range(3):
            w = pad8(rg[pl.ds(b + 2 + j, D, stride=3), :])
            R.qkv[l, :, 128 * j:128 * (j + 1)] = low(w)
            R.qkv_t[l, 128 * j:128 * (j + 1), :] = with_bias(w, None if j == 1 else rg[pl.ds(b + 362 + j // 2, 1), :])
        w = pad8(rg[pl.ds(b + 364, D), :])
        R.out[l] = low(w)
        R.out_t[l] = with_bias(w, rg[pl.ds(b + 484, 1), :])
        for j in range(4):
            w = pad8(rg[pl.ds(b + 487 + j, D, stride=4), :])
            R.fc[l, :, 128 * j:128 * (j + 1)] = low(w)
            R.fc_t[l, 128 * j:128 * (j + 1), :] = with_bias(w, rg[pl.ds(b + 967 + j, 1), :])
            w = pad8(rg[pl.ds(b + 971 + D * j, D), :])
            R.proj[l, 128 * j:128 * (j + 1), :] = low(w)
            R.proj_t[l, :, 128 * j:128 * (j + 1)] = with_bias(w, None if j else rg[pl.ds(b + 1451, 1), :])
        for i, r in enumerate(VROWS):
            R.vec[pl.ds(12 * l + i, 1), :] = rg[pl.ds(b + r, 1), :]
    R.vec[24:26, :] = rg[pl.ds(HEAD, 2), :]
    R.hc[...] = jnp.zeros((128, 128), F32)
    R.ho[...] = jnp.zeros((128, 128), F32)
    c0 = HEAD + 2
    for p, a, s in code_phases():
        R.hc[pl.ds(p, 8, stride=15), :] = take_phase(
            lambda i: rg[pl.ds(c0 + i, 8, stride=4), :], a, s, 32, 8)
    o0 = c0 + 32
    for p, a, s in off_phases():
        R.ho[pl.ds(p, 5, stride=24), :] = take_phase(
            lambda i: rg[pl.ds(o0 + i, 5, stride=7), :], a, s, OFFS, 5)
    hw = R.hc[...] + shifted(R.ho[...], 32)
    R.head[...] = low(hw)
    R.head_t[...] = low(hw.T[0:72])
    lanes = iota((1, 128), 1)
    hb = jnp.where(lanes < 32, rg[pl.ds(o0, 1), :], 0.0)
    a, s = (D * OFFS + 32) // D, (D * OFFS + 32) % D
    ob = take_phase(lambda i: rg[pl.ds(o0 + i, 1), :], a, s, OFFS, 1)
    R.vec[26:27, :] = hb + shifted(ob, 32)
    columns = jnp.concatenate([R.vec[...], jnp.zeros((96, 128), F32)], axis=0).T
    for l in range(LAYERS):
        for i in range(12):
            R.bc[l, i] = jnp.broadcast_to(columns[0:D, 12 * l + i:12 * l + i + 1], (D, 128))
    for i in range(2):
        R.bcf[i] = jnp.broadcast_to(columns[0:D, 24 + i:25 + i], (D, 128))
    R.bch[...] = jnp.broadcast_to(columns[0:72, 26:27], (72, 128))


def spread_groups(v, groups, width):
    rows = v.shape[0]
    lanes = iota((rows, 128), 1)
    out = []
    for g in range(groups):
        t, o = (GT * g) // 128, (GT * g) % 128
        a = shifted(v[:, 128 * t:128 * (t + 1)], -o)
        if o + GT > 128:
            b = shifted(v[:, 128 * (t + 1):128 * (t + 2)], -o)
            a = jnp.where(lanes < 128 - o, a, b)
        out.append(jnp.where(lanes < GT, a, 0))
    return out


def prep_tokens(R, counts, codes, actions, valid, feat, chunks):
    groups = chunks * CG
    wins = counts.shape[1]
    R.cnt[...] = jnp.zeros(R.cnt.shape, F32)
    R.cnt[0:WIN // CAMS, :] = counts[...].astype(F32)
    k = iota((GT, 16), 0)
    step = (k % WIN) // CAMS
    sel = jnp.where(step == iota((GT, 16), 1), 1.0, 0.0)
    x = nn(low(sel), low(R.cnt[...]))
    y = jnp.where(iota((GT, wins), 1) % GW == iota((GT, wins), 0) // WIN, x, 0.0)
    pick = jnp.where(iota((wins, 128), 0) // GW == iota((wins, 128), 1) + groups * feat, 1.0, 0.0)
    z = nn(low(y), low(pick))
    kk = iota((GT, 128), 0)
    alive = jnp.where((kk % CAMS).astype(F32) < z, 1.0, 0.0)
    steps = WIN // CAMS
    j, at = iota((48, 128), 0), iota((48, 128), 1)
    own = (at // WIN == j // steps) & ((at % WIN) // CAMS == j % steps) & (at < GT)
    R.k_mask[...] = low(jnp.where(own, 1.0, 0.0))
    may = (at // WIN == j // steps) & ((at % WIN) // CAMS >= j % steps)
    R.q_mask[...] = low(jnp.where(may | (j >= GW * steps), 0.0, -BIG))
    rows = pad8(alive).T
    for g in range(groups):
        R.live[g // CG, :, 128 * (g % CG):128 * (g % CG + 1)] = rows[g:g + 1, :]
        R.dead[g] = jnp.where(iota((8, 128), 0) == 0, 1.0 - rows[g:g + 1, :], 0.0)
    for name, src in (("code", codes), ("act", actions), ("val", valid)):
        parts = spread_groups(src[...].astype(F32), groups, GT)
        dst = getattr(R, name)
        for g in range(groups):
            c, lo = g // CG, 128 * (g % CG)
            part = parts[g]
            if name == "val":
                part = part * rows[g:g + 1, :]
            if name != "code":
                dst[c, 32:40, lo:lo + 128] = jnp.zeros((8, 128), F32)
            dst[c, 0:part.shape[0], lo:lo + 128] = part
    lanes = iota((GT, 128), 1)
    live_total = jnp.sum(jnp.where(lanes < groups, alive, 0.0), keepdims=True)
    v = jnp.zeros((40, L), F32)
    for c in range(chunks):
        v = v + R.val[c]
    valid_total = jnp.sum(v, keepdims=True)
    return live_total, valid_total


def own_rows(slab, h):
    rows = iota((8, 128), 0)
    if h % 2 == 0:
        return jnp.concatenate([slab[0:16], jnp.where(rows < 4, slab[16:24], 0.0)], axis=0)
    return jnp.concatenate([jnp.where(rows >= 4, slab[0:8], 0.0), slab[8:24]], axis=0)


def split(v):
    hi = low(v).astype(F32)
    return hi, v - hi


def attend(R, s, c, q, k, v):
    qh, ql = split(q)
    kh, kl = split(k)
    vh, vl = split(v)
    minus = jnp.where(iota((8, 128), 0) == 0, -BIG, 0.0)

    none = jnp.zeros((128, 128), BF)

    def scores(g, p):
        at = slice(128 * g, 128 * (g + 1))
        qs, ks = [], []
        for h in (2 * p, 2 * p + 1):
            sl = slice(slab_at(h), slab_at(h) + 24)
            hi = own_rows(qh[sl, at], h)
            qd = low(jnp.concatenate([hi, hi, own_rows(ql[sl, at], h), minus], axis=0))
            kd = low(jnp.concatenate([kh[sl, at], kl[sl, at], kh[sl, at], R.dead[c * CG + g]], axis=0))
            qs.append(jnp.concatenate([qd, R.q_mask[...]], axis=0))
            ks.append(jnp.concatenate([kd, R.k_mask[...]], axis=0).T)
        if PAIR:
            both = jnp.concatenate([jnp.concatenate([qs[0], none], axis=1),
                                    jnp.concatenate([none, qs[1]], axis=1)], axis=0)
            return nn(jnp.concatenate(ks, axis=1), both)[0:GT]
        return jnp.concatenate([nn(ks[0], qs[0])[0:GT], nn(ks[1], qs[1])[0:GT]], axis=1)

    def soft(g, p, sc):
        at = slice(128 * g, 128 * (g + 1))
        e = jnp.exp2(sc - jnp.max(sc, axis=0, keepdims=True))
        r = 1.0 / jnp.sum(e, axis=0, keepdims=True)
        e8 = pad8(e)
        eh = low(e8)
        el = low(e8 - eh.astype(F32))
        cols = slice(256 * p, 256 * (p + 1))
        R.prob[s, g, :, cols] = e
        for i in range(2):
            at_h = slice(256 * p + 128 * i, 256 * p + 128 * (i + 1))
            R.prob_low[s, g, :, at_h] = eh[:, 128 * i:128 * (i + 1)].T
        R.rsum[s, 2 * p, :, at] = r[:, 0:128]
        R.rsum[s, 2 * p + 1, :, at] = r[:, 128:256]
        return r, eh, el

    def values(g, p, r, eh, el):
        at = slice(128 * g, 128 * (g + 1))
        out = []
        for i in range(2):
            sl = slice(slab_at(2 * p + i), slab_at(2 * p + i) + 24)
            cols = slice(128 * i, 128 * (i + 1))
            vs = low(jnp.concatenate([vh[sl, at], vl[sl, at]], axis=0))
            o = nn(jnp.concatenate([vs, vs], axis=1), jnp.concatenate([eh[:, cols], el[:, cols]], axis=0))
            out.append((o[0:24] + o[24:48]) * r[:, cols])
        return out

    items = [(g, p) for g in range(CG) for p in range(H // 2)]
    slabs = pipeline(items, scores, soft, values, FAHEAD)
    slabs = [t for pair in slabs for t in pair]
    return jnp.concatenate([join_slabs(slabs[H * g:H * (g + 1)]) for g in range(CG)], axis=1)


PAIR = True
FAHEAD = 2
BAHEAD = 2


def pipeline(items, first, second, third, ahead, between=()):
    n = len(items)
    a, b, out = {}, {}, []
    between = list(between)
    done = 0
    for t in range(n + ahead):
        if t < n:
            a[t] = first(*items[t])
        m = t - ahead + 1
        if 0 <= m < n:
            b[m] = second(*items[m], *(a.pop(m) if isinstance(a[m], tuple) else (a.pop(m),)))
        m = t - ahead
        if 0 <= m < n:
            out.append(third(*items[m], *b.pop(m)))
        while done < len(between) * (t + 1) // (n + ahead):
            between[done]()
            done += 1
    return out


def attend_back(R, s, do, between=()):
    vrows = [R.v_low[s, :, 128 * g:128 * (g + 1)].T for g in range(CG)]

    def probs(g, p):
        at = slice(128 * g, 128 * (g + 1))
        ds, stack = [], []
        for h in (2 * p, 2 * p + 1):
            a = slab_at(h)
            d = own_rows(do[a:a + 24, at], h) * R.rsum[s, h, :, at]
            parts = ([jnp.zeros((a, 128), F32)] if a else []) + [d] + ([jnp.zeros((104 - a, 128), F32)])
            ds.append(low(d))
            stack.append(low(jnp.concatenate(parts, axis=0)))
        return ds, nn(vrows[g], jnp.concatenate(stack, axis=1))[0:GT]

    def inner(g, p, d, dp):
        at = slice(128 * g, 128 * (g + 1))
        e = R.prob[s, g, :, 256 * p:256 * (p + 1)]
        r = jnp.concatenate([R.rsum[s, 2 * p, :, at], R.rsum[s, 2 * p + 1, :, at]], axis=1)
        total = jnp.sum(e * dp, axis=0, keepdims=True) * r
        ds = low(pad8(e * (dp - total)))
        for i in range(2):
            cols = slice(128 * i, 128 * (i + 1))
            R.ds_t[3 * g + p, :, cols] = ds[:, cols].T
        return d, ds

    def outer(g, p, d, ds):
        at = slice(128 * g, 128 * (g + 1))
        out = []
        for i in range(2):
            h = 2 * p + i
            dsh = ds[:, 128 * i:128 * (i + 1)]
            out.append((nn(R.k_low[s, h, :, at], dsh), nn(R.q_low[s, h, :, at], R.ds_t[3 * g + p, :, 128 * i:128 * (i + 1)]),
                        nn(d[i], R.prob_low[s, g, :, 128 * h:128 * (h + 1)])))
        return out

    items = [(g, p) for g in range(CG) for p in range(H // 2)]
    slabs = pipeline(items, probs, inner, outer, BAHEAD, between)
    slabs = [t for pair in slabs for t in pair]
    out = []
    for i in range(3):
        out.append(jnp.concatenate(
            [join_slabs([t[i] for t in slabs[H * g:H * (g + 1)]]) for g in range(CG)], axis=1))
    return out[0] * SCALE, out[1], out[2]


def turn(R, i, v):
    for g in range(CG):
        R.turned[i, 128 * g:128 * (g + 1), :] = v[:, 128 * g:128 * (g + 1)].T


def embed(R, obs, c):
    rows = nn(jnp.concatenate(obs, axis=1), R.w_obs[...])
    parts = []
    for g in range(CG):
        r = rows[GT * g:GT * (g + 1)] + R.posb[...]
        parts.append(pad8(r).T[0:D])
    return jnp.concatenate(parts, axis=1)


def layer_fwd(R, l, c, s, x):
    def vec(i):
        return tile4(R.bc[l, i])

    xh, r = normed(x)
    R.xh1[s] = xh
    R.r1[s] = r
    n1 = low(ones8(xh * vec(G1) + vec(B1)))
    R.n1[s] = n1
    mix = nn(R.qkv_t[l], n1)
    q = mix[0:D] * SCALE
    k = mix[128:128 + D]
    v = mix[256:256 + D]
    for h in range(H):
        a = slab_at(h)
        R.q_low[s, h] = low(q[a:a + 24])
        R.k_low[s, h] = low(k[a:a + 24])
    R.v_low[s] = low(pad8(v))
    att = low(ones8(attend(R, s, c, q * LOG2E, k, v)))
    R.att[l] = att
    x1 = x + nn(R.out_t[l], att)[0:D]
    xh, r = normed(x1)
    R.xh2[l] = xh
    R.r2[l] = r
    n2 = low(ones8(xh * vec(G2) + vec(B2)))
    R.n2[l] = n2
    pre = nn(R.fc_t[l], n2)
    parts = []
    for j in range(4):
        pj = pre[128 * j:128 * j + D]
        half = gelu_half(pj)
        R.pre[l, D * j:D * (j + 1)] = pj
        R.half[l, D * j:D * (j + 1)] = half
        parts.append(low(ones8(pj * half) if j == 0 else pad8(pj * half)))
    inner = jnp.concatenate(parts, axis=0)
    R.inner[l] = inner
    return x1 + nn(R.proj_t[l], inner)[0:D]


def head_step(R, c, x, live_total, valid_total):
    xh, r = normed(x)
    fin = low(pad8(xh * tile4(R.bcf[0]) + tile4(R.bcf[1])))
    hd = nn(R.head_t[...], fin) + tile4(R.bch[...])
    live = R.live[c]
    lw = live * (1.0 / live_total)
    rows = iota((CODES, L), 0).astype(F32)
    grads = []
    csum = jnp.zeros((1, L), F32)
    for b in range(BOOKS):
        lg = hd[CODES * b:CODES * (b + 1)]
        m = jnp.max(lg, axis=0, keepdims=True)
        e = jnp.exp(lg - m)
        s = jnp.sum(e, axis=0, keepdims=True)
        hot = rows == R.code[c, b:b + 1, :]
        picked = jnp.sum(jnp.where(hot, lg, 0.0), axis=0, keepdims=True)
        csum = csum + (jnp.log(s) + m - picked) * live
        grads.append((e * (1.0 / s) - jnp.where(hot, 1.0, 0.0)) * lw)
    diff = hd[32:72] - R.act[c]
    val = R.val[c]
    sq = diff * diff + 1.0
    ri = lax.rsqrt(sq)
    asum = val * (sq * ri)
    grads.append((val * (1.0 / valid_total)) * (diff * ri))
    R.loss[0, 0:1] += fold4(csum)
    af = fold4(asum)
    R.loss[1] += af[0:8] + af[8:16] + af[16:24] + af[24:32] + af[32:40]
    dh = jnp.concatenate(grads, axis=0)
    R.a_hb[0:72] += fold4(dh)
    dhl = low(jnp.concatenate([dh, jnp.zeros((56, L), F32)], axis=0))
    turn(R, 4, dhl)
    R.a_head[...] += nn(fin, R.turned[4])
    df = nn(R.head[...], dhl)[0:D]
    R.a_fin[0, 0:D] += fold4(df * xh)
    R.a_fin[1, 0:D] += fold4(df)
    return normed_back(df * tile4(R.bcf[0]), xh, r)


def add_bias(R, l, i, v):
    R.a_bias[l, i, 0:D] += fold4(v)


def mlp_bwd(R, l, dout):
    outl = low(pad8(dout))
    add_bias(R, l, PB, dout)
    parts = []
    for j in range(4):
        rows = slice(D * j, D * (j + 1))
        dj = nn(R.proj[l, 128 * j:128 * (j + 1)], outl)
        parts.append(low(pad8(dj[0:D] * gelu_slope(R.pre[l, rows], R.half[l, rows]))))
    prel = jnp.concatenate(parts, axis=0)
    dn = nn(R.fc[l], prel)[0:D]
    xh = R.xh2[l]
    add_bias(R, l, G2, dn * xh)
    add_bias(R, l, B2, dn)
    dmid = normed_back(dn * tile4(R.bc[l, G2]), xh, R.r2[l]) + dout
    midl = low(pad8(dmid))
    add_bias(R, l, OB, dmid)
    da = nn(R.out[l], midl)[0:D]

    turn(R, 0, outl)
    turn(R, 1, R.n2[l])
    turn(R, 2, midl)

    def a_proj(j):
        def run():
            rows = slice(256 * j, 256 * (j + 1))
            R.a_proj[l, rows] += nn(R.inner[l, rows], R.turned[0])
        return run

    def a_fc(j):
        def run():
            rows = slice(256 * j, 256 * (j + 1))
            R.a_fc[l, rows] += nn(prel[rows], R.turned[1])
        return run

    def a_out():
        R.a_out[l] += nn(R.att[l], R.turned[2])

    return dmid, da, [a_proj(0), a_proj(1), a_fc(0), a_fc(1), a_out]


def att_bwd(R, l, s, dmid, da, between):
    turn(R, 3, R.n1[s])
    dq, dk, dv = attend_back(R, s, da, between)
    mixl = jnp.concatenate([low(pad8(dq)), low(pad8(dk)), low(pad8(dv))], axis=0)
    dn = nn(R.qkv[l], mixl)[0:D]
    add_bias(R, l, QB, dq)
    add_bias(R, l, VB, dv)
    R.a_qkv[l] += nn(mixl, R.turned[3])
    xh = R.xh1[s]
    add_bias(R, l, G1, dn * xh)
    add_bias(R, l, B1, dn)
    return normed_back(dn * tile4(R.bc[l, G1]), xh, R.r1[s]) + dmid


def embed_bwd(R, obs, c, dx):
    R.a_x[0:D] += fold4(dx)
    lanes = iota((D, 128), 1)
    tiles = []
    gs = [dx[:, 128 * g:128 * (g + 1)] for g in range(CG)]
    for t in range(CG):
        a = shifted(gs[t], -8 * t)
        b = shifted(gs[t + 1], 120 - 8 * t) if t + 1 < CG else jnp.zeros((D, 128), F32)
        tiles.append(jnp.where(lanes < GT - 8 * t, a, b))
    gl = low(pad8(jnp.concatenate(tiles, axis=1)))
    R.a_obs[...] += nn(gl, jnp.concatenate(obs, axis=1))


def zero_grads(R):
    for name in ("a_qkv", "a_out", "a_fc", "a_proj", "a_bias", "a_obs", "a_x", "a_fin", "a_head", "a_hb", "loss"):
        ref = getattr(R, name)
        ref[...] = jnp.zeros(ref.shape, F32)


HIGH = lax.Precision.HIGHEST


LATE = 364
EARLY_ROWS = (OB, G2, B2, PB)


def lane_sums(v):
    return jnp.sum(v.T, axis=0, keepdims=True)


def pack_vectors(R, rg, l, which):
    b = BASE + LROW * l
    for i in which:
        rg[pl.ds(b + VROWS[i], 1), :] = lane_sums(R.a_bias[l, i])


def pack_early(R, rg, l):
    b = BASE + LROW * l
    rg[pl.ds(b + 364, D), :] = R.a_out[l, 0:D]
    for j in range(4):
        fc = R.a_fc[l, 128 * j:128 * (j + 1), :].T
        rg[pl.ds(b + 487 + j, D, stride=4), :] = fc[0:D]
        rg[pl.ds(b + 967 + j, 1), :] = fc[D:D + 1]
        rg[pl.ds(b + 971 + D * j, D), :] = R.a_proj[l, 128 * j:128 * j + D, :]
    pack_vectors(R, rg, l, EARLY_ROWS)


def pack_late(R, rg, l):
    b = BASE + LROW * l
    for j in range(3):
        rg[pl.ds(b + 2 + j, D, stride=3), :] = R.a_qkv[l, 128 * j:128 * (j + 1), :].T[0:D]
    pack_vectors(R, rg, l, (G1, B1, QB, VB))


def pack_embed(R, rg):
    for f in range(OBS // 128):
        rg[128 * f:128 * (f + 1), :] = R.a_obs[:, 128 * f:128 * (f + 1)].T
    slot, lane = iota((32, 128), 0), iota((32, 128), 1)
    sel = jnp.where((slot == 0) | (lane % WIN == slot - 1), 1.0, 0.0)
    sel = jnp.where(lane < GT, sel, 0.0)
    rows = nt(sel, R.a_x[...], HIGH)
    rg[pl.ds(OBS, 1 + WIN), :] = rows[0:1 + WIN]


def pack_head(R, rg):
    for i in range(2):
        rg[pl.ds(HEAD + i, 1), :] = lane_sums(R.a_fin[i])
    lanes8 = iota((8, 128), 1)
    grad = R.a_head[...]
    R.hc[...] = jnp.where(iota((128, 128), 1) < 32, grad, 0.0)
    R.ho[...] = jnp.where(iota((128, 128), 1) < OFFS, shifted(grad, -32), 0.0)
    c0 = HEAD + 2
    o0 = c0 + 32

    def put(phases, src, rows_n, stride, width, count):
        acc = [jnp.zeros((rows_n, 128), F32) for _ in range(count + 1)]
        lanes = iota((rows_n, 128), 1)
        for p, a, s in phases:
            v = src[pl.ds(p, rows_n, stride=stride), :]
            first = shifted(v, s)
            if s + width > D:
                acc[a] = acc[a] + jnp.where((lanes >= s) & (lanes < D), first, 0.0)
                acc[a + 1] = acc[a + 1] + jnp.where(lanes < s + width - D, shifted(v, s - D), 0.0)
            else:
                acc[a] = acc[a] + first
        return acc

    acc = put(code_phases(), R.hc, 8, 15, 32, 4)
    for a in range(4):
        rg[pl.ds(c0 + a, 8, stride=4), :] = acc[a]
    hb = lane_sums(R.a_hb[...])
    lane1 = iota((1, 128), 1)
    rg[pl.ds(o0, 48), :] = jnp.zeros((48, 128), F32)
    acc = put(off_phases(), R.ho, 5, 24, OFFS, 7)
    for a in range(7):
        rg[pl.ds(o0 + a, 5, stride=7), :] = acc[a]
    rg[pl.ds(o0 + 7, 5, stride=7), :] = rg[pl.ds(o0 + 7, 5, stride=7), :] + acc[7]
    rg[pl.ds(o0, 1), :] = rg[pl.ds(o0, 1), :] + jnp.where(lane1 < 32, hb, 0.0)
    a, s = (D * OFFS + 32) // D, (D * OFFS + 32) % D
    ob = jnp.where(lane1 < OFFS, shifted(hb, -32), 0.0)
    rg[pl.ds(o0 + a, 1), :] = rg[pl.ds(o0 + a, 1), :] + shifted(ob, s)


MESH = pl.DeviceIdType.MESH


def round_up(n, m):
    return -(-n // m) * m


class Plan:
    def __init__(self, feats, toks, shard, tok_rows):
        self.feats, self.toks, self.chips = feats, toks, toks // 2
        self.shard = shard
        self.block = round_up(-(-(shard + 112) // D), 16)
        self.flat_rows = self.block // 16 * 15
        self.local = round_up(-(-shard // 1024), 1) * 8
        self.work = round_up(max(self.flat_rows, self.local + 1), 8)
        self.own_rows = tok_rows // feats
        self.chunks = self.own_rows // CT
        self.early = [f for f in range(feats) if shard * toks * f // D >= BASE + LATE]
        self.grid = round_up(-(-(shard * feats * toks) // D) + self.block, 8)


def comm_scratch(P):
    dma = pltpu.SemaphoreType.DMA
    B, C, Fn = P.block, P.chips, P.feats
    return dict(
        rg=pltpu.VMEM((P.grid, 128), F32),
        ob=pltpu.VMEM((P.chunks, Fn, L, 128), BF),
        pg=pltpu.VMEM((2, C, Fn, B, 128), BF),
        loc=pltpu.VMEM((P.work, 128), F32),
        rblk=pltpu.VMEM((B, 128), F32),
        codes_in=pltpu.VMEM((BOOKS, P.own_rows), jnp.int32),
        act_in=pltpu.VMEM((OFFS, P.own_rows), F32),
        val_in=pltpu.VMEM((OFFS, P.own_rows), jnp.int32),
        tz=pltpu.VMEM((2, Fn, 8, 128), F32),
        tc=pltpu.VMEM((2, C, 8, 128), F32),
        ts=pltpu.VMEM((2, 2, 8, 128), F32),
        sb1=pltpu.VMEM((C, Fn, B, 128), F32),
        rb1=pltpu.VMEM((C, Fn, B, 128), F32),
        sb2=pltpu.VMEM((C, Fn, B, 128), BF),
        rb2=pltpu.VMEM((C, Fn, B, 128), BF),
        col=pltpu.VMEM((Fn, B, 128), F32),
        sb3=pltpu.VMEM((Fn, B, 128), F32),
        rb3=pltpu.VMEM((Fn, B, 128), F32),
        s_p1=dma((2, Fn)), s_p2=dma((2, C)), s_p3=dma((2, C)),
        s_tz=dma((2, 2, Fn)), s_tc=dma((2, 2, C)), s_ts=dma((2, 2)),
        s_ob=dma((2, 2 * P.chunks, Fn)),
        s_own=dma((P.chunks,)),
        s_in=dma((3,)),
        s_r1=dma((3, 2, C)), s_r2=dma((2, Fn, C)), s_r3=dma((2, Fn)),
    )


def to_rows(loc, rblk, delta, P):
    v = loc[...]
    lanes = iota(v.shape, 1)
    moved = pltpu.roll(v, delta, 1)
    loc[...] = jnp.where(lanes >= delta, moved, pltpu.roll(moved, 1, 0))
    n = P.block // 16
    lane = iota((n, 128), 1)
    for j in range(16):
        if j < 15:
            a = shifted(loc[pl.ds(j, n, stride=15), :], 8 * j)
        if j > 0:
            b = shifted(loc[pl.ds(j - 1, n, stride=15), :], 8 * j)
            a = jnp.where(lane < 8 * j, b, a) if j < 15 else b
        rblk[pl.ds(j, n, stride=16), :] = jnp.where(lane < D, a, 0.0)


def from_rows(rblk, loc, delta, P):
    n = P.block // 16
    lane = iota((n, 128), 1)
    loc[...] = jnp.zeros(loc.shape, F32)
    for i in range(15):
        a = shifted(rblk[pl.ds(i, n, stride=16), :], -8 * i)
        b = shifted(rblk[pl.ds(i + 1, n, stride=16), :], D - 8 * i)
        loc[pl.ds(i, n, stride=15), :] = jnp.where(lane < D - 8 * i, a, b)
    v = loc[...]
    lanes = iota(v.shape, 1)
    moved = pltpu.roll(v, lax.rem(128 - delta, 128), 1)
    v = jnp.where(lanes < 128 - delta, moved, pltpu.roll(moved, P.work - 1, 0))
    return v[0:P.local]


def step_kernel(P, names, master, obs, counts, codes, actions, valid, grad, sums, *scratch):
    R = Refs()
    for name, ref in zip(names, scratch):
        setattr(R, name, ref)
    Fn, C, B = P.feats, P.chips, P.block
    feat = lax.axis_index("feat")
    tok = lax.axis_index("tok")
    chip = tok // 2
    core = tok % 2
    me = feat * P.toks + tok
    delta = lax.rem(me * P.shard, D)

    def z_peer(i):
        return lax.rem(feat + i, Fn)

    def z_from(i):
        return lax.rem(feat + Fn - i, Fn)

    def c_peer(i):
        return lax.rem(chip + i, C)

    def c_from(i):
        return lax.rem(chip + C - i, C)

    def to_z(i):
        return (z_peer(i), tok)

    def to_c(i):
        return (feat, 2 * c_peer(i) + core)

    sibling = (feat, 2 * chip + 1 - core)

    def send(src, dst, sems, at, dev):
        return pltpu.make_async_remote_copy(
            src_ref=src, dst_ref=dst, send_sem=sems.at[(0,) + at], recv_sem=sems.at[(1,) + at],
            device_id=dev, device_id_type=MESH)

    barrier = pltpu.get_barrier_semaphore()
    peers = [to_z(i) for i in range(1, Fn)] + [to_c(i) for i in range(1, C)] + [sibling]
    for dev in peers:
        pl.semaphore_signal(barrier, inc=1, device_id=dev, device_id_type=MESH)

    n = P.own_rows
    ins = []
    for i, (src, dst) in enumerate(((codes, R.codes_in), (actions, R.act_in), (valid, R.val_in))):
        ins.append(pltpu.make_async_copy(src.at[:, pl.ds(pl.multiple_of(feat * n, 128), n)], dst, R.s_in.at[i]))
        ins[-1].start()

    R.loc[...] = jnp.zeros(R.loc.shape, F32)
    whole = P.shard // 1024
    R.loc[0:8 * whole, :] = master[pl.ds(0, 1024 * whole)].reshape(8 * whole, 128)
    rest = P.shard - 1024 * whole
    last = jnp.concatenate([master[pl.ds(1024 * whole, rest)], jnp.zeros((1024 - rest,), F32)])
    R.loc[8 * whole:8 * whole + 8, :] = last.reshape(8, 128)
    to_rows(R.loc, R.rblk, delta, P)
    R.pg[core, chip, feat] = low(R.rblk[...])
    pl.semaphore_wait(barrier, len(peers))

    p1 = []
    for i in range(1, Fn):
        blk = R.pg.at[core, chip, feat]
        p1.append(send(blk, blk, R.s_p1, (i,), to_z(i)))
        p1[-1].start()

    half = CT // 2

    def obs_copies(p):
        cps = []
        for i in range(1, Fn):
            src = obs.at[pl.ds(pl.multiple_of(z_peer(i) * n + half * p, 16), half), :]
            dst = R.ob.at[p // 2, feat, pl.ds(pl.multiple_of(half * (p % 2), 16), half), :]
            cps.append(send(src, dst, R.s_ob, (p, i), to_z(i)))
        return cps

    def start_obs(p):
        for cp in obs_copies(p):
            cp.start()

    own = []
    for c in range(P.chunks):
        src = obs.at[pl.ds(pl.multiple_of(feat * n + CT * c, 16), CT), :]
        own.append(pltpu.make_async_copy(src, R.ob.at[c, feat, pl.ds(0, CT), :], R.s_own.at[c]))
        own[-1].start()
    for cp in ins:
        cp.wait()
    zero_grads(R)
    for c in range(P.chunks):
        for f in range(Fn):
            R.ob[c, f, CT:L, :] = jnp.zeros((L - CT, 128), BF)
    live_n, valid_n = prep_tokens(R, counts, R.codes_in, R.act_in, R.val_in, feat, P.chunks)

    def two_rows(a, b):
        return jnp.concatenate([jnp.broadcast_to(a, (1, 128)), jnp.broadcast_to(b, (1, 128)),
                                jnp.zeros((6, 128), F32)], axis=0)

    def z_copies(w):
        return [send(R.tz.at[w, feat], R.tz.at[w, feat], R.s_tz.at[w], (i,), to_z(i)) for i in range(1, Fn)]

    def c_copies(w):
        return [send(R.tc.at[w, chip], R.tc.at[w, chip], R.s_tc.at[w], (i,), to_c(i)) for i in range(1, C)]

    def s_copies(w):
        return [send(R.ts.at[w, core], R.ts.at[w, core], R.s_ts.at[w], (), sibling)]

    def start_all(cps):
        for cp in cps:
            cp.start()

    def total(ref, w, count):
        v = ref[w, 0]
        for i in range(1, count):
            v = v + ref[w, i]
        return v

    def wait_all(cps):
        for cp in cps:
            cp.wait()

    R.tz[0, feat] = two_rows(live_n, valid_n)
    start_all(z_copies(0))
    wait_all(p1)
    start_obs(0)
    start_obs(1)
    p2 = []
    for i in range(1, C):
        blk = R.pg.at[core, chip]
        p2.append(send(blk, blk, R.s_p2, (i,), to_c(i)))
        p2[-1].start()
    p3 = [send(R.pg.at[core, chip], R.pg.at[core, chip], R.s_p3, (0,), sibling)]
    p3[0].start()
    wait_all(z_copies(0))
    R.tc[0, chip] = total(R.tz, 0, Fn)
    start_all(c_copies(0))
    for i in range(1, C):
        p2[i - 1].wait_recv()
        blk = R.pg.at[core, c_from(i)]
        p3.append(send(blk, blk, R.s_p3, (i,), sibling))
        p3[-1].start()
    wait_all(c_copies(0))
    R.ts[0, core] = total(R.tc, 0, C)
    start_all(s_copies(0))
    for cp in p2:
        cp.wait_send()
    wait_all(p3)
    R.rg[0:8, :] = jnp.zeros((8, 128), F32)

    def place(d, _):
        r0 = (P.shard * d) // D
        f, t = d // P.toks, d % P.toks
        blk = R.pg[t % 2, t // 2, f].astype(F32)
        before = R.rg[pl.ds(r0, 1), :]
        R.rg[pl.ds(r0, B), :] = blk
        R.rg[pl.ds(r0, 1), :] = blk[0:1] + before
        return 0

    lax.fori_loop(0, Fn * P.toks, place, 0)
    prep_weights(R.rg, R)
    wait_all(s_copies(0))
    counted = total(R.ts, 0, 2)
    live_total = counted[0:1, 0:1]
    valid_total = counted[1:2, 0:1]

    for cp in own:
        cp.wait()


    def rows_of(f, ch, co):
        return (P.shard * (f * P.toks + 2 * ch + co)) // D

    early = P.early[0] if P.early else Fn
    planes = [slice(Fn - 1, Fn), slice(early, Fn - 1), slice(0, early)]

    def r1_copy(w, i):
        at = pl.ds(planes[w].start, planes[w].stop - planes[w].start)
        return send(R.sb1.at[i, at], R.rb1.at[i, at], R.s_r1.at[w], (i,), sibling)

    def r2_copy(f, i):
        return send(R.sb2.at[i, f], R.rb2.at[i, f], R.s_r2.at[:, f], (i,), to_c(i))

    def r3_copy(i):
        return send(R.sb3.at[i], R.rb3.at[i], R.s_r3, (i,), to_z(i))

    order = list(range(1, C)) + [0]

    def sum_cores(w):
        for i in order:
            for f in range(planes[w].start, planes[w].stop):
                R.sb1[i, f] = R.rg[pl.ds(rows_of(f, c_peer(i), 1 - core), B), :]
            r1_copy(w, i).start()

    def sum_chips(w):
        for i in order:
            r1_copy(w, i).wait_recv()
            for f in range(planes[w].start, planes[w].stop):
                v = R.rg[pl.ds(rows_of(f, c_peer(i), core), B), :] + R.rb1[i, f]
                if i:
                    R.sb2[i, f] = low(v)
                    r2_copy(f, i).start()
                else:
                    R.col[f] = v

    def sum_column(f):
        v = R.col[f]
        for i in range(1, C):
            r2_copy(f, i).wait_recv()
            v = v + R.rb2[i, f].astype(F32)
        R.col[f] = v
        for i in range(1, Fn):
            @pl.when(z_peer(i) == f)
            def _():
                R.sb3[i] = v
                r3_copy(i).start()

    def chunk(c, _):
        for p in (2 * c, 2 * c + 1):
            for cp in obs_copies(p):
                cp.wait_recv()

            @pl.when(c + 1 < P.chunks)
            def _():
                start_obs(p + 2)

        R.x[...] = embed(R, [R.ob[c, f, 0:CT, :] for f in range(Fn)], c)

        def lay(l, _):
            R.x[...] = layer_fwd(R, l, c, l, R.x[...])
            return 0

        lax.fori_loop(0, LAYERS, lay, 0)

        dx = head_step(R, c, R.x[...], live_total, valid_total)
        dmid, da, rest = mlp_bwd(R, 1, dx)
        R.x[...] = att_bwd(R, 1, 1, dmid, da, rest)
        @pl.when(c == P.chunks - 1)
        def _():
            R.rg[pl.ds(HEAD + 32, P.grid - HEAD - 32), :] = jnp.zeros((P.grid - HEAD - 32, 128), F32)
            pack_head(R, R.rg)
            pack_late(R, R.rg, 1)
            pack_early(R, R.rg, 1)
            R.ts[1, core] = two_rows(jnp.sum(R.loss[0], keepdims=True), jnp.sum(R.loss[1], keepdims=True))
            sum_cores(0)
            start_all(s_copies(1))

        dmid, da, rest = mlp_bwd(R, 0, R.x[...])
        R.dmid[...] = dmid
        R.da[...] = da
        for run in rest:
            run()

        @pl.when(c == P.chunks - 1)
        def _():
            pack_early(R, R.rg, 0)
            sum_cores(1)
            sum_chips(0)
            wait_all(s_copies(1))
            R.tc[1, chip] = total(R.ts, 1, 2)
            start_all(c_copies(1))

        dx = att_bwd(R, 0, 0, R.dmid[...], R.da[...], [])

        @pl.when(c == P.chunks - 1)
        def _():
            pack_late(R, R.rg, 0)
            sum_chips(1)

        embed_bwd(R, [R.ob[c, f] for f in range(Fn)], c, dx)
        return 0

    lax.fori_loop(0, P.chunks, chunk, 0)
    pack_embed(R, R.rg)
    sum_cores(2)
    wait_all(c_copies(1))
    R.tz[1, feat] = total(R.tc, 1, C)
    start_all(z_copies(1))
    sum_column(Fn - 1)
    sum_chips(2)
    for f in (*range(early, Fn - 1), *range(early)):
        sum_column(f)
    for i in range(1, Fn):
        r3_copy(i).wait_recv()
    v = R.col[feat]
    for i in range(1, Fn):
        v = v + R.rb3[i]
    R.rblk[...] = v
    grad[...] = from_rows(R.rblk, R.loc, delta, P)
    wait_all(z_copies(1))
    lost = total(R.tz, 1, Fn)
    sums[...] = jnp.concatenate([lost[0:1], counted[0:1], lost[1:2], counted[1:2], jnp.zeros((4, 128), F32)], axis=0)
    for p in range(2 * P.chunks):
        for cp in obs_copies(p):
            cp.wait_send()
    for w in range(3):
        for i in range(C):
            r1_copy(w, i).wait_send()
    for i in range(1, C):
        for f in range(Fn):
            r2_copy(f, i).wait_send()
    for i in range(1, Fn):
        r3_copy(i).wait_send()


def adam_kernel(shard, grad, sums, master, first, second, new_master, new_first, new_second, parts):
    whole = shard // 1024
    for lo, hi in ((0, whole), (whole, whole + 1)):
        n = min(1024 * hi, shard) - 1024 * lo
        at = pl.ds(1024 * lo, n)
        g = grad[8 * lo:8 * hi].reshape(1024 * (hi - lo))[0:n]
        old = master[at]
        f_new = BETA_ONE * first[at] + (1.0 - BETA_ONE) * g
        s_new = BETA_TWO * second[at] + (1.0 - BETA_TWO) * g * g
        f_hat = f_new / (1.0 - BETA_ONE ** STEP_NO)
        s_hat = s_new / (1.0 - BETA_TWO ** STEP_NO)
        new_first[at] = f_new
        new_second[at] = s_new
        new_master[at] = old - LEARN_RATE * (f_hat / (jnp.sqrt(s_hat) + ADAM_EPS) + DECAY_RATE * old)
    for i in range(4):
        parts[i] = sums[i, 0]


def solution(mesh):
    feats, toks = mesh.shape["feat"], mesh.shape["tok"]

    def shards(master, first, second, obs, counts, codes, actions, valid):
        P_ = Plan(feats, toks, master.shape[0], obs.shape[0])
        scratch = dict(scratch_list(P_.chunks))
        scratch.update(comm_scratch(P_))
        vmem = pl.BlockSpec(memory_space=pltpu.VMEM)
        hbm = pl.BlockSpec(memory_space=pl.ANY)
        grad, sums = pl.pallas_call(
            functools.partial(step_kernel, P_, list(scratch)),
            out_shape=(jax.ShapeDtypeStruct((P_.local, 128), F32), jax.ShapeDtypeStruct((8, 128), F32)),
            in_specs=[vmem, hbm, vmem, hbm, hbm, hbm],
            out_specs=(vmem, vmem),
            scratch_shapes=list(scratch.values()),
            compiler_params=pltpu.CompilerParams(
                collective_id=0, has_side_effects=True, vmem_limit_bytes=60 * 2 ** 20),
        )(master, obs, counts.T, codes.T, actions, valid)
        flat = jax.ShapeDtypeStruct((P_.shard,), F32)
        return pl.pallas_call(
            functools.partial(adam_kernel, P_.shard),
            out_shape=(flat, flat, flat, jax.ShapeDtypeStruct((4,), F32)),
            in_specs=[vmem] * 5,
            out_specs=(vmem, vmem, vmem, pl.BlockSpec(memory_space=pltpu.SMEM)),
        )(grad, sums, master, first, second)

    weights = PSpec(("feat", "tok"))
    return jax.shard_map(
        shards, mesh=mesh,
        in_specs=(weights, weights, weights, PSpec("tok", "feat"), PSpec("tok", None), PSpec("tok", None),
                  PSpec(None, "tok"), PSpec(None, "tok")),
        out_specs=(weights, weights, weights, PSpec()), check_vma=False)
```

```python
import functools
import math

import jax
import jax.numpy as jnp
from jax import lax
from jax.experimental import pallas as pl
from jax.experimental.pallas import tpu as pltpu
from jax.sharding import PartitionSpec as PSpec

D = 120
H = 6
HD = 20
FF = 480
OBS = 512
LAYERS = 2
CAMS = 3
BOOKS = 2
CODES = 16
SPAN = 5
ACT = 7
WIN = 30
OFFS = SPAN * ACT
NORM_EPS = 1e-05
STEP_NO = 10
BETA_ONE = 0.9
BETA_TWO = 0.999
ADAM_EPS = 1e-08
DECAY_RATE = 0.1
LEARN_RATE = 0.05
GW = 4
GT = GW * WIN
CG = 4
L = CG * 128
CT = CG * GT
F32 = jnp.float32
BF = jnp.bfloat16
SCALE = HD ** (-0.5)
LROW = 2 * 1 + 3 * D + 2 + D + 1 + 2 + 4 * D + 4 + 4 * D + 1
BASE = OBS + 1 + WIN
HEAD = BASE + LAYERS * LROW
NV = 13
VROWS = [0, 1, 362, 363, 484, 485, 486, 967, 968, 969, 970, 1451]
(G1, B1, QB, VB, OB, G2, B2, FB0, FB1, FB2, FB3, PB) = range(12)


def nn(a, b):
    return lax.dot_general(a, b, (((1,), (0,)), ((), ())), preferred_element_type=F32)


def nt(a, b, precision=None):
    return lax.dot_general(a, b, (((1,), (1,)), ((), ())), preferred_element_type=F32, precision=precision)


def low(v):
    return v.astype(BF)


def pad8(v):
    return jnp.concatenate([v, jnp.zeros((8, v.shape[1]), v.dtype)], axis=0)


def tile4(v):
    return jnp.concatenate([v] * CG, axis=1)


def fold4(v):
    out = v[:, 0:128]
    for g in range(1, CG):
        out = out + v[:, 128 * g:128 * (g + 1)]
    return out


def iota(shape, axis):
    return lax.broadcasted_iota(jnp.int32, shape, axis)


def slab_at(h):
    return 20 * h - (4 if h % 2 else 0)


def head_stack(v):
    rows = iota((8, 128), 0)
    cols = []
    for h in range(H):
        a = slab_at(h)
        if h % 2 == 0:
            parts = [v[a:a + 16], jnp.where(rows < 4, v[a + 16:a + 24], 0.0)]
        else:
            parts = [jnp.where(rows >= 4, v[a:a + 8], 0.0), v[a + 8:a + 24]]
        if a > 0:
            parts = [jnp.zeros((a, 128), F32)] + parts
        if a + 24 < 128:
            parts = parts + [jnp.zeros((128 - a - 24, 128), F32)]
        cols.append(jnp.concatenate(parts, axis=0))
    return jnp.concatenate(cols, axis=1)


def join_slabs(slabs):
    rows = iota((8, 128), 0)
    parts = []
    for p in range(3):
        a, b = slabs[2 * p], slabs[2 * p + 1]
        parts += [a[0:16], jnp.where(rows < 4, a[16:24], b[0:8]), b[8:24]]
    return jnp.concatenate(parts, axis=0)


def slabs_of(v):
    return [v[slab_at(h):slab_at(h) + 24] for h in range(H)]


def hi_lo(v):
    hi = low(v)
    return hi, low(v - hi.astype(F32))


def normed(x):
    mean = jnp.sum(x, axis=0, keepdims=True) * (1.0 / D)
    c = x - mean
    var = jnp.sum(c * c, axis=0, keepdims=True) * (1.0 / D)
    r = lax.rsqrt(var + NORM_EPS)
    return c * r, r


def normed_back(d, xh, r):
    m0 = jnp.sum(d, axis=0, keepdims=True) * (1.0 / D)
    m1 = jnp.sum(d * xh, axis=0, keepdims=True) * (1.0 / D)
    return r * (d - m0 - xh * m1)


GA = math.sqrt(2.0 / math.pi)
GB = 0.044715


def gelu_half(x):
    return 0.5 + 0.5 * jnp.tanh(x * (GA + (GA * GB) * (x * x)))


def gelu_slope(x, s):
    return s + (x * s) * (1.0 - s) * (2.0 * GA + (6.0 * GA * GB) * (x * x))


LOG2E = math.log2(math.e)
BIG = 1e30


class Refs:
    pass


def scratch_list(chunks):
    groups = chunks * CG
    return dict(
        w_obs=pltpu.VMEM((OBS, 128), BF),
        posb=pltpu.VMEM((GT, 128), F32),
        qkv_t=pltpu.VMEM((LAYERS, 384, 128), BF),
        qkv=pltpu.VMEM((LAYERS, 128, 384), BF),
        out_t=pltpu.VMEM((LAYERS, 128, 128), BF),
        out=pltpu.VMEM((LAYERS, 128, 128), BF),
        fc_t=pltpu.VMEM((LAYERS, 512, 128), BF),
        fc=pltpu.VMEM((LAYERS, 128, 512), BF),
        proj_t=pltpu.VMEM((LAYERS, 128, 512), BF),
        proj=pltpu.VMEM((LAYERS, 512, 128), BF),
        head_t=pltpu.VMEM((72, 128), BF),
        head=pltpu.VMEM((128, 128), BF),
        vec=pltpu.VMEM((32, 128), F32),
        bc=pltpu.VMEM((LAYERS, 12, GT, 128), F32),
        bcf=pltpu.VMEM((2, GT, 128), F32),
        bch=pltpu.VMEM((72, 128), F32),
        hc=pltpu.VMEM((128, 128), F32),
        ho=pltpu.VMEM((128, 128), F32),
        cnt=pltpu.VMEM((16, 256), F32),
        live=pltpu.VMEM((chunks, 1, L), F32),
        act=pltpu.VMEM((chunks, 40, L), F32),
        val=pltpu.VMEM((chunks, 40, L), F32),
        code=pltpu.VMEM((chunks, 2, L), F32),
        x=pltpu.VMEM((D, L), F32),
        dmid=pltpu.VMEM((D, L), F32),
        da=pltpu.VMEM((D, L), F32),
        xh1=pltpu.VMEM((LAYERS, D, L), F32),
        r1=pltpu.VMEM((LAYERS, 1, L), F32),
        xh2=pltpu.VMEM((LAYERS, D, L), F32),
        r2=pltpu.VMEM((LAYERS, 1, L), F32),
        n1=pltpu.VMEM((LAYERS, 128, L), BF),
        n2=pltpu.VMEM((LAYERS, 128, L), BF),
        att=pltpu.VMEM((LAYERS, 128, L), BF),
        q_low=pltpu.VMEM((LAYERS, H, 24, L), BF),
        k_low=pltpu.VMEM((LAYERS, H, 24, L), BF),
        v_low=pltpu.VMEM((LAYERS, 128, L), BF),
        rsum=pltpu.VMEM((LAYERS, H, 1, L), F32),
        prob=pltpu.VMEM((LAYERS, CG, GT, H * 128), F32),
        prob_low=pltpu.VMEM((LAYERS, CG, 128, H * 128), BF),
        k_mask=pltpu.VMEM((48, 128), BF),
        q_mask=pltpu.VMEM((48, 128), BF),
        dead=pltpu.VMEM((groups, 8, 128), F32),
        pre=pltpu.VMEM((LAYERS, FF, L), F32),
        half=pltpu.VMEM((LAYERS, FF, L), F32),
        inner=pltpu.VMEM((LAYERS, 512, L), BF),
        a_qkv=pltpu.VMEM((LAYERS, 384, 128), F32),
        ds_t=pltpu.VMEM((CG * H // 2, 128, 256), BF),
        turned=pltpu.VMEM((5, L, 128), BF),
        a_out=pltpu.VMEM((LAYERS, 128, 128), F32),
        a_fc=pltpu.VMEM((LAYERS, 512, 128), F32),
        a_proj=pltpu.VMEM((LAYERS, 512, 128), F32),
        a_bias=pltpu.VMEM((LAYERS, 12, 128, 128), F32),
        a_obs=pltpu.VMEM((128, 512), F32),
        a_x=pltpu.VMEM((128, 128), F32),
        a_fin=pltpu.VMEM((2, 128, 128), F32),
        a_head=pltpu.VMEM((128, 128), F32),
        a_hb=pltpu.VMEM((128, 128), F32),
        loss=pltpu.VMEM((2, 8, 128), F32),
    )


def code_phases():
    for p in range(15):
        yield p, (32 * p) // D, (32 * p) % D


def off_phases():
    for p in range(24):
        yield p, (35 * p + 32) // D, (35 * p + 32) % D


def shifted(v, by):
    by %= 128
    return v if by == 0 else pltpu.roll(v, by, 1)


def take_phase(load, a, s, width, rows):
    lanes = iota((rows, 128), 1)
    first = shifted(load(a), -s)
    if s + width > D:
        second = shifted(load(a + 1), D - s)
        first = jnp.where(lanes < D - s, first, second)
    return jnp.where(lanes < width, first, 0.0)


def with_bias(w, bias):
    if bias is not None:
        w = jnp.where(iota((128, 128), 0) == D, bias, w)
    return low(w.T)


def ones8(v):
    return jnp.concatenate([v, jnp.where(iota((8, v.shape[1]), 0) == 0, 1.0, 0.0)], axis=0)


def prep_weights(rg, R):
    R.w_obs[...] = low(rg[0:OBS, :])
    for w in range(GW):
        R.posb[pl.ds(WIN * w, WIN), :] = rg[OBS + 1:OBS + 1 + WIN, :] + rg[OBS:OBS + 1, :]
    R.vec[...] = jnp.zeros((32, 128), F32)
    for l in range(LAYERS):
        b = BASE + LROW * l
        for j in range(3):
            w = pad8(rg[pl.ds(b + 2 + j, D, stride=3), :])
            R.qkv[l, :, 128 * j:128 * (j + 1)] = low(w)
            R.qkv_t[l, 128 * j:128 * (j + 1), :] = with_bias(w, None if j == 1 else rg[pl.ds(b + 362 + j // 2, 1), :])
        w = pad8(rg[pl.ds(b + 364, D), :])
        R.out[l] = low(w)
        R.out_t[l] = with_bias(w, rg[pl.ds(b + 484, 1), :])
        for j in range(4):
            w = pad8(rg[pl.ds(b + 487 + j, D, stride=4), :])
            R.fc[l, :, 128 * j:128 * (j + 1)] = low(w)
            R.fc_t[l, 128 * j:128 * (j + 1), :] = with_bias(w, rg[pl.ds(b + 967 + j, 1), :])
            w = pad8(rg[pl.ds(b + 971 + D * j, D), :])
            R.proj[l, 128 * j:128 * (j + 1), :] = low(w)
            R.proj_t[l, :, 128 * j:128 * (j + 1)] = with_bias(w, None if j else rg[pl.ds(b + 1451, 1), :])
        for i, r in enumerate(VROWS):
            R.vec[pl.ds(12 * l + i, 1), :] = rg[pl.ds(b + r, 1), :]
    R.vec[24:26, :] = rg[pl.ds(HEAD, 2), :]
    R.hc[...] = jnp.zeros((128, 128), F32)
    R.ho[...] = jnp.zeros((128, 128), F32)
    c0 = HEAD + 2
    for p, a, s in code_phases():
        R.hc[pl.ds(p, 8, stride=15), :] = take_phase(
            lambda i: rg[pl.ds(c0 + i, 8, stride=4), :], a, s, 32, 8)
    o0 = c0 + 32
    for p, a, s in off_phases():
        R.ho[pl.ds(p, 5, stride=24), :] = take_phase(
            lambda i: rg[pl.ds(o0 + i, 5, stride=7), :], a, s, OFFS, 5)
    hw = R.hc[...] + shifted(R.ho[...], 32)
    R.head[...] = low(hw)
    R.head_t[...] = low(hw.T[0:72])
    lanes = iota((1, 128), 1)
    hb = jnp.where(lanes < 32, rg[pl.ds(o0, 1), :], 0.0)
    a, s = (D * OFFS + 32) // D, (D * OFFS + 32) % D
    ob = take_phase(lambda i: rg[pl.ds(o0 + i, 1), :], a, s, OFFS, 1)
    R.vec[26:27, :] = hb + shifted(ob, 32)
    columns = jnp.concatenate([R.vec[...], jnp.zeros((96, 128), F32)], axis=0).T
    for l in range(LAYERS):
        for i in range(12):
            R.bc[l, i] = jnp.broadcast_to(columns[0:D, 12 * l + i:12 * l + i + 1], (D, 128))
    for i in range(2):
        R.bcf[i] = jnp.broadcast_to(columns[0:D, 24 + i:25 + i], (D, 128))
    R.bch[...] = jnp.broadcast_to(columns[0:72, 26:27], (72, 128))


def spread_groups(v, groups, width):
    rows = v.shape[0]
    lanes = iota((rows, 128), 1)
    out = []
    for g in range(groups):
        t, o = (GT * g) // 128, (GT * g) % 128
        a = shifted(v[:, 128 * t:128 * (t + 1)], -o)
        if o + GT > 128:
            b = shifted(v[:, 128 * (t + 1):128 * (t + 2)], -o)
            a = jnp.where(lanes < 128 - o, a, b)
        out.append(jnp.where(lanes < GT, a, 0))
    return out


def prep_tokens(R, counts, codes, actions, valid, feat, chunks):
    groups = chunks * CG
    wins = counts.shape[1]
    R.cnt[...] = jnp.zeros(R.cnt.shape, F32)
    R.cnt[0:WIN // CAMS, :] = counts[...].astype(F32)
    k = iota((GT, 16), 0)
    step = (k % WIN) // CAMS
    sel = jnp.where(step == iota((GT, 16), 1), 1.0, 0.0)
    x = nn(low(sel), low(R.cnt[...]))
    y = jnp.where(iota((GT, wins), 1) % GW == iota((GT, wins), 0) // WIN, x, 0.0)
    pick = jnp.where(iota((wins, 128), 0) // GW == iota((wins, 128), 1) + groups * feat, 1.0, 0.0)
    z = nn(low(y), low(pick))
    kk = iota((GT, 128), 0)
    alive = jnp.where((kk % CAMS).astype(F32) < z, 1.0, 0.0)
    steps = WIN // CAMS
    j, at = iota((48, 128), 0), iota((48, 128), 1)
    own = (at // WIN == j // steps) & ((at % WIN) // CAMS == j % steps) & (at < GT)
    R.k_mask[...] = low(jnp.where(own, 1.0, 0.0))
    may = (at // WIN == j // steps) & ((at % WIN) // CAMS >= j % steps)
    R.q_mask[...] = low(jnp.where(may | (j >= GW * steps), 0.0, -BIG))
    rows = pad8(alive).T
    for g in range(groups):
        R.live[g // CG, :, 128 * (g % CG):128 * (g % CG + 1)] = rows[g:g + 1, :]
        R.dead[g] = jnp.where(iota((8, 128), 0) == 0, 1.0 - rows[g:g + 1, :], 0.0)
    for name, src in (("code", codes), ("act", actions), ("val", valid)):
        parts = spread_groups(src[...].astype(F32), groups, GT)
        dst = getattr(R, name)
        for g in range(groups):
            c, lo = g // CG, 128 * (g % CG)
            part = parts[g]
            if name == "val":
                part = part * rows[g:g + 1, :]
            if name != "code":
                dst[c, 32:40, lo:lo + 128] = jnp.zeros((8, 128), F32)
            dst[c, 0:part.shape[0], lo:lo + 128] = part
    lanes = iota((GT, 128), 1)
    live_total = jnp.sum(jnp.where(lanes < groups, alive, 0.0), keepdims=True)
    v = jnp.zeros((40, L), F32)
    for c in range(chunks):
        v = v + R.val[c]
    valid_total = jnp.sum(v, keepdims=True)
    return live_total, valid_total


def own_rows(slab, h):
    rows = iota((8, 128), 0)
    if h % 2 == 0:
        return jnp.concatenate([slab[0:16], jnp.where(rows < 4, slab[16:24], 0.0)], axis=0)
    return jnp.concatenate([jnp.where(rows >= 4, slab[0:8], 0.0), slab[8:24]], axis=0)


def split(v):
    hi = low(v).astype(F32)
    return hi, v - hi


def attend(R, s, c, q, k, v):
    qh, ql = split(q)
    kh, kl = split(k)
    vh, vl = split(v)
    minus = jnp.where(iota((8, 128), 0) == 0, -BIG, 0.0)

    none = jnp.zeros((128, 128), BF)

    def scores(g, p):
        at = slice(128 * g, 128 * (g + 1))
        qs, ks = [], []
        for h in (2 * p, 2 * p + 1):
            sl = slice(slab_at(h), slab_at(h) + 24)
            hi = own_rows(qh[sl, at], h)
            qd = low(jnp.concatenate([hi, hi, own_rows(ql[sl, at], h), minus], axis=0))
            kd = low(jnp.concatenate([kh[sl, at], kl[sl, at], kh[sl, at], R.dead[c * CG + g]], axis=0))
            qs.append(jnp.concatenate([qd, R.q_mask[...]], axis=0))
            ks.append(jnp.concatenate([kd, R.k_mask[...]], axis=0).T)
        if PAIR:
            both = jnp.concatenate([jnp.concatenate([qs[0], none], axis=1),
                                    jnp.concatenate([none, qs[1]], axis=1)], axis=0)
            return nn(jnp.concatenate(ks, axis=1), both)[0:GT]
        return jnp.concatenate([nn(ks[0], qs[0])[0:GT], nn(ks[1], qs[1])[0:GT]], axis=1)

    def soft(g, p, sc):
        at = slice(128 * g, 128 * (g + 1))
        e = jnp.exp2(sc - jnp.max(sc, axis=0, keepdims=True))
        r = 1.0 / jnp.sum(e, axis=0, keepdims=True)
        e8 = pad8(e)
        eh = low(e8)
        el = low(e8 - eh.astype(F32))
        cols = slice(256 * p, 256 * (p + 1))
        R.prob[s, g, :, cols] = e
        for i in range(2):
            at_h = slice(256 * p + 128 * i, 256 * p + 128 * (i + 1))
            R.prob_low[s, g, :, at_h] = eh[:, 128 * i:128 * (i + 1)].T
        R.rsum[s, 2 * p, :, at] = r[:, 0:128]
        R.rsum[s, 2 * p + 1, :, at] = r[:, 128:256]
        return r, eh, el

    def values(g, p, r, eh, el):
        at = slice(128 * g, 128 * (g + 1))
        out = []
        for i in range(2):
            sl = slice(slab_at(2 * p + i), slab_at(2 * p + i) + 24)
            cols = slice(128 * i, 128 * (i + 1))
            vs = low(jnp.concatenate([vh[sl, at], vl[sl, at]], axis=0))
            o = nn(jnp.concatenate([vs, vs], axis=1), jnp.concatenate([eh[:, cols], el[:, cols]], axis=0))
            out.append((o[0:24] + o[24:48]) * r[:, cols])
        return out

    items = [(g, p) for g in range(CG) for p in range(H // 2)]
    slabs = pipeline(items, scores, soft, values, FAHEAD)
    slabs = [t for pair in slabs for t in pair]
    return jnp.concatenate([join_slabs(slabs[H * g:H * (g + 1)]) for g in range(CG)], axis=1)


PAIR = True
FAHEAD = 2
BAHEAD = 6


def pipeline(items, first, second, third, ahead, between=()):
    n = len(items)
    a, b, out = {}, {}, []
    between = list(between)
    done = 0
    for t in range(n + ahead):
        if t < n:
            a[t] = first(*items[t])
        m = t - ahead + 1
        if 0 <= m < n:
            b[m] = second(*items[m], *(a.pop(m) if isinstance(a[m], tuple) else (a.pop(m),)))
        m = t - ahead
        if 0 <= m < n:
            out.append(third(*items[m], *b.pop(m)))
        while done < len(between) * (t + 1) // (n + ahead):
            between[done]()
            done += 1
    return out


def attend_back(R, s, do, between=()):
    vrows = [R.v_low[s, :, 128 * g:128 * (g + 1)].T for g in range(CG)]

    def probs(g, p):
        at = slice(128 * g, 128 * (g + 1))
        ds, stack = [], []
        for h in (2 * p, 2 * p + 1):
            a = slab_at(h)
            d = own_rows(do[a:a + 24, at], h) * R.rsum[s, h, :, at]
            parts = ([jnp.zeros((a, 128), F32)] if a else []) + [d] + ([jnp.zeros((104 - a, 128), F32)])
            ds.append(low(d))
            stack.append(low(jnp.concatenate(parts, axis=0)))
        return ds, nn(vrows[g], jnp.concatenate(stack, axis=1))[0:GT]

    def inner(g, p, d, dp):
        at = slice(128 * g, 128 * (g + 1))
        e = R.prob[s, g, :, 256 * p:256 * (p + 1)]
        r = jnp.concatenate([R.rsum[s, 2 * p, :, at], R.rsum[s, 2 * p + 1, :, at]], axis=1)
        total = jnp.sum(e * dp, axis=0, keepdims=True) * r
        ds = low(pad8(e * (dp - total)))
        for i in range(2):
            cols = slice(128 * i, 128 * (i + 1))
            R.ds_t[3 * g + p, :, cols] = ds[:, cols].T
        return d, ds

    def outer(g, p, d, ds):
        at = slice(128 * g, 128 * (g + 1))
        out = []
        for i in range(2):
            h = 2 * p + i
            dsh = ds[:, 128 * i:128 * (i + 1)]
            out.append((nn(R.k_low[s, h, :, at], dsh), nn(R.q_low[s, h, :, at], R.ds_t[3 * g + p, :, 128 * i:128 * (i + 1)]),
                        nn(d[i], R.prob_low[s, g, :, 128 * h:128 * (h + 1)])))
        return out

    items = [(g, p) for g in range(CG) for p in range(H // 2)]
    slabs = pipeline(items, probs, inner, outer, BAHEAD, between)
    slabs = [t for pair in slabs for t in pair]
    out = []
    for i in range(3):
        out.append(jnp.concatenate(
            [join_slabs([t[i] for t in slabs[H * g:H * (g + 1)]]) for g in range(CG)], axis=1))
    return out[0] * SCALE, out[1], out[2]


def turn(R, i, v):
    for g in range(CG):
        R.turned[i, 128 * g:128 * (g + 1), :] = v[:, 128 * g:128 * (g + 1)].T


def embed(R, obs, c):
    rows = nn(jnp.concatenate(obs, axis=1), R.w_obs[...])
    parts = []
    for g in range(CG):
        r = rows[GT * g:GT * (g + 1)] + R.posb[...]
        parts.append(pad8(r).T[0:D])
    return jnp.concatenate(parts, axis=1)


def layer_fwd(R, l, c, s, x):
    def vec(i):
        return tile4(R.bc[l, i])

    xh, r = normed(x)
    R.xh1[s] = xh
    R.r1[s] = r
    n1 = low(ones8(xh * vec(G1) + vec(B1)))
    R.n1[s] = n1
    mix = nn(R.qkv_t[l], n1)
    q = mix[0:D] * SCALE
    k = mix[128:128 + D]
    v = mix[256:256 + D]
    for h in range(H):
        a = slab_at(h)
        R.q_low[s, h] = low(q[a:a + 24])
        R.k_low[s, h] = low(k[a:a + 24])
    R.v_low[s] = low(pad8(v))
    att = low(ones8(attend(R, s, c, q * LOG2E, k, v)))
    R.att[l] = att
    x1 = x + nn(R.out_t[l], att)[0:D]
    xh, r = normed(x1)
    R.xh2[l] = xh
    R.r2[l] = r
    n2 = low(ones8(xh * vec(G2) + vec(B2)))
    R.n2[l] = n2
    pre = nn(R.fc_t[l], n2)
    parts = []
    for j in range(4):
        pj = pre[128 * j:128 * j + D]
        half = gelu_half(pj)
        R.pre[l, D * j:D * (j + 1)] = pj
        R.half[l, D * j:D * (j + 1)] = half
        parts.append(low(ones8(pj * half) if j == 0 else pad8(pj * half)))
    inner = jnp.concatenate(parts, axis=0)
    R.inner[l] = inner
    return x1 + nn(R.proj_t[l], inner)[0:D]


def head_step(R, c, x, live_total, valid_total):
    xh, r = normed(x)
    fin = low(pad8(xh * tile4(R.bcf[0]) + tile4(R.bcf[1])))
    hd = nn(R.head_t[...], fin) + tile4(R.bch[...])
    live = R.live[c]
    lw = live * (1.0 / live_total)
    rows = iota((CODES, L), 0).astype(F32)
    grads = []
    csum = jnp.zeros((1, L), F32)
    for b in range(BOOKS):
        lg = hd[CODES * b:CODES * (b + 1)]
        m = jnp.max(lg, axis=0, keepdims=True)
        e = jnp.exp(lg - m)
        s = jnp.sum(e, axis=0, keepdims=True)
        hot = rows == R.code[c, b:b + 1, :]
        picked = jnp.sum(jnp.where(hot, lg, 0.0), axis=0, keepdims=True)
        csum = csum + (jnp.log(s) + m - picked) * live
        grads.append((e * (1.0 / s) - jnp.where(hot, 1.0, 0.0)) * lw)
    diff = hd[32:72] - R.act[c]
    val = R.val[c]
    sq = diff * diff + 1.0
    ri = lax.rsqrt(sq)
    asum = val * (sq * ri)
    grads.append((val * (1.0 / valid_total)) * (diff * ri))
    R.loss[0, 0:1] += fold4(csum)
    af = fold4(asum)
    R.loss[1] += af[0:8] + af[8:16] + af[16:24] + af[24:32] + af[32:40]
    dh = jnp.concatenate(grads, axis=0)
    R.a_hb[0:72] += fold4(dh)
    dhl = low(jnp.concatenate([dh, jnp.zeros((56, L), F32)], axis=0))
    turn(R, 4, dhl)
    R.a_head[...] += nn(fin, R.turned[4])
    df = nn(R.head[...], dhl)[0:D]
    R.a_fin[0, 0:D] += fold4(df * xh)
    R.a_fin[1, 0:D] += fold4(df)
    return normed_back(df * tile4(R.bcf[0]), xh, r)


def add_bias(R, l, i, v):
    R.a_bias[l, i, 0:D] += fold4(v)


def mlp_bwd(R, l, dout):
    outl = low(pad8(dout))
    add_bias(R, l, PB, dout)
    parts = []
    for j in range(4):
        rows = slice(D * j, D * (j + 1))
        dj = nn(R.proj[l, 128 * j:128 * (j + 1)], outl)
        parts.append(low(pad8(dj[0:D] * gelu_slope(R.pre[l, rows], R.half[l, rows]))))
    prel = jnp.concatenate(parts, axis=0)
    dn = nn(R.fc[l], prel)[0:D]
    xh = R.xh2[l]
    add_bias(R, l, G2, dn * xh)
    add_bias(R, l, B2, dn)
    dmid = normed_back(dn * tile4(R.bc[l, G2]), xh, R.r2[l]) + dout
    midl = low(pad8(dmid))
    add_bias(R, l, OB, dmid)
    da = nn(R.out[l], midl)[0:D]

    turn(R, 0, outl)
    turn(R, 1, R.n2[l])
    turn(R, 2, midl)

    def a_proj(j):
        def run():
            rows = slice(256 * j, 256 * (j + 1))
            R.a_proj[l, rows] += nn(R.inner[l, rows], R.turned[0])
        return run

    def a_fc(j):
        def run():
            rows = slice(256 * j, 256 * (j + 1))
            R.a_fc[l, rows] += nn(prel[rows], R.turned[1])
        return run

    def a_out():
        R.a_out[l] += nn(R.att[l], R.turned[2])

    return dmid, da, [a_proj(0), a_proj(1), a_fc(0), a_fc(1), a_out]


def att_bwd(R, l, s, dmid, da, between):
    turn(R, 3, R.n1[s])
    dq, dk, dv = attend_back(R, s, da, between)
    mixl = jnp.concatenate([low(pad8(dq)), low(pad8(dk)), low(pad8(dv))], axis=0)
    dn = nn(R.qkv[l], mixl)[0:D]
    add_bias(R, l, QB, dq)
    add_bias(R, l, VB, dv)
    R.a_qkv[l] += nn(mixl, R.turned[3])
    xh = R.xh1[s]
    add_bias(R, l, G1, dn * xh)
    add_bias(R, l, B1, dn)
    return normed_back(dn * tile4(R.bc[l, G1]), xh, R.r1[s]) + dmid


def embed_bwd(R, obs, c, dx):
    R.a_x[0:D] += fold4(dx)
    lanes = iota((D, 128), 1)
    tiles = []
    gs = [dx[:, 128 * g:128 * (g + 1)] for g in range(CG)]
    for t in range(CG):
        a = shifted(gs[t], -8 * t)
        b = shifted(gs[t + 1], 120 - 8 * t) if t + 1 < CG else jnp.zeros((D, 128), F32)
        tiles.append(jnp.where(lanes < GT - 8 * t, a, b))
    gl = low(pad8(jnp.concatenate(tiles, axis=1)))
    R.a_obs[...] += nn(gl, jnp.concatenate(obs, axis=1))


def zero_grads(R):
    for name in ("a_qkv", "a_out", "a_fc", "a_proj", "a_bias", "a_obs", "a_x", "a_fin", "a_head", "a_hb", "loss"):
        ref = getattr(R, name)
        ref[...] = jnp.zeros(ref.shape, F32)


HIGH = lax.Precision.HIGHEST


LATE = 364
EARLY_ROWS = (OB, G2, B2, PB)


def lane_sums(v):
    return jnp.sum(v.T, axis=0, keepdims=True)


def pack_vectors(R, rg, l, which):
    b = BASE + LROW * l
    for i in which:
        rg[pl.ds(b + VROWS[i], 1), :] = lane_sums(R.a_bias[l, i])


def pack_early(R, rg, l):
    b = BASE + LROW * l
    rg[pl.ds(b + 364, D), :] = R.a_out[l, 0:D]
    for j in range(4):
        fc = R.a_fc[l, 128 * j:128 * (j + 1), :].T
        rg[pl.ds(b + 487 + j, D, stride=4), :] = fc[0:D]
        rg[pl.ds(b + 967 + j, 1), :] = fc[D:D + 1]
        rg[pl.ds(b + 971 + D * j, D), :] = R.a_proj[l, 128 * j:128 * j + D, :]
    pack_vectors(R, rg, l, EARLY_ROWS)


def pack_late(R, rg, l):
    b = BASE + LROW * l
    for j in range(3):
        rg[pl.ds(b + 2 + j, D, stride=3), :] = R.a_qkv[l, 128 * j:128 * (j + 1), :].T[0:D]
    pack_vectors(R, rg, l, (G1, B1, QB, VB))


def pack_embed(R, rg):
    for f in range(OBS // 128):
        rg[128 * f:128 * (f + 1), :] = R.a_obs[:, 128 * f:128 * (f + 1)].T
    slot, lane = iota((32, 128), 0), iota((32, 128), 1)
    sel = jnp.where((slot == 0) | (lane % WIN == slot - 1), 1.0, 0.0)
    sel = jnp.where(lane < GT, sel, 0.0)
    rows = nt(sel, R.a_x[...], HIGH)
    rg[pl.ds(OBS, 1 + WIN), :] = rows[0:1 + WIN]


def pack_head(R, rg):
    for i in range(2):
        rg[pl.ds(HEAD + i, 1), :] = lane_sums(R.a_fin[i])
    lanes8 = iota((8, 128), 1)
    grad = R.a_head[...]
    R.hc[...] = jnp.where(iota((128, 128), 1) < 32, grad, 0.0)
    R.ho[...] = jnp.where(iota((128, 128), 1) < OFFS, shifted(grad, -32), 0.0)
    c0 = HEAD + 2
    o0 = c0 + 32

    def put(phases, src, rows_n, stride, width, count):
        acc = [jnp.zeros((rows_n, 128), F32) for _ in range(count + 1)]
        lanes = iota((rows_n, 128), 1)
        for p, a, s in phases:
            v = src[pl.ds(p, rows_n, stride=stride), :]
            first = shifted(v, s)
            if s + width > D:
                acc[a] = acc[a] + jnp.where((lanes >= s) & (lanes < D), first, 0.0)
                acc[a + 1] = acc[a + 1] + jnp.where(lanes < s + width - D, shifted(v, s - D), 0.0)
            else:
                acc[a] = acc[a] + first
        return acc

    acc = put(code_phases(), R.hc, 8, 15, 32, 4)
    for a in range(4):
        rg[pl.ds(c0 + a, 8, stride=4), :] = acc[a]
    hb = lane_sums(R.a_hb[...])
    lane1 = iota((1, 128), 1)
    rg[pl.ds(o0, 48), :] = jnp.zeros((48, 128), F32)
    acc = put(off_phases(), R.ho, 5, 24, OFFS, 7)
    for a in range(7):
        rg[pl.ds(o0 + a, 5, stride=7), :] = acc[a]
    rg[pl.ds(o0 + 7, 5, stride=7), :] = rg[pl.ds(o0 + 7, 5, stride=7), :] + acc[7]
    rg[pl.ds(o0, 1), :] = rg[pl.ds(o0, 1), :] + jnp.where(lane1 < 32, hb, 0.0)
    a, s = (D * OFFS + 32) // D, (D * OFFS + 32) % D
    ob = jnp.where(lane1 < OFFS, shifted(hb, -32), 0.0)
    rg[pl.ds(o0 + a, 1), :] = rg[pl.ds(o0 + a, 1), :] + shifted(ob, s)


MESH = pl.DeviceIdType.MESH


def round_up(n, m):
    return -(-n // m) * m


class Plan:
    def __init__(self, feats, toks, shard, tok_rows):
        self.feats, self.toks, self.chips = feats, toks, toks // 2
        self.shard = shard
        self.block = round_up(-(-(shard + 112) // D), 16)
        self.flat_rows = self.block // 16 * 15
        self.local = round_up(-(-shard // 1024), 1) * 8
        self.work = round_up(max(self.flat_rows, self.local + 1), 8)
        self.own_rows = tok_rows // feats
        self.chunks = self.own_rows // CT
        self.early = [f for f in range(feats) if shard * toks * f // D >= BASE + LATE]
        self.grid = round_up(-(-(shard * feats * toks) // D) + self.block, 8)


def comm_scratch(P):
    dma = pltpu.SemaphoreType.DMA
    B, C, Fn = P.block, P.chips, P.feats
    return dict(
        rg=pltpu.VMEM((P.grid, 128), F32),
        ob=pltpu.VMEM((P.chunks, Fn, L, 128), BF),
        pg=pltpu.VMEM((2, C, Fn, B, 128), BF),
        loc=pltpu.VMEM((P.work, 128), F32),
        rblk=pltpu.VMEM((B, 128), F32),
        codes_in=pltpu.VMEM((BOOKS, P.own_rows), jnp.int32),
        act_in=pltpu.VMEM((OFFS, P.own_rows), F32),
        val_in=pltpu.VMEM((OFFS, P.own_rows), jnp.int32),
        tz=pltpu.VMEM((2, Fn, 8, 128), F32),
        tc=pltpu.VMEM((2, C, 8, 128), F32),
        ts=pltpu.VMEM((2, 2, 8, 128), F32),
        sb1=pltpu.VMEM((C, Fn, B, 128), F32),
        rb1=pltpu.VMEM((C, Fn, B, 128), F32),
        sb2=pltpu.VMEM((C, Fn, B, 128), BF),
        rb2=pltpu.VMEM((C, Fn, B, 128), BF),
        col=pltpu.VMEM((Fn, B, 128), F32),
        sb3=pltpu.VMEM((Fn, B, 128), F32),
        rb3=pltpu.VMEM((Fn, B, 128), F32),
        s_p1=dma((2, Fn)), s_p2=dma((2, C)), s_p3=dma((2, C)),
        s_tz=dma((2, 2, Fn)), s_tc=dma((2, 2, C)), s_ts=dma((2, 2)),
        s_ob=dma((2, 2 * P.chunks, Fn)),
        s_own=dma((P.chunks,)),
        s_in=dma((3,)),
        s_r1=dma((3, 2, C)), s_r2=dma((2, Fn, C)), s_r3=dma((2, Fn)),
    )


def to_rows(loc, rblk, delta, P):
    v = loc[...]
    lanes = iota(v.shape, 1)
    moved = pltpu.roll(v, delta, 1)
    loc[...] = jnp.where(lanes >= delta, moved, pltpu.roll(moved, 1, 0))
    n = P.block // 16
    lane = iota((n, 128), 1)
    for j in range(16):
        if j < 15:
            a = shifted(loc[pl.ds(j, n, stride=15), :], 8 * j)
        if j > 0:
            b = shifted(loc[pl.ds(j - 1, n, stride=15), :], 8 * j)
            a = jnp.where(lane < 8 * j, b, a) if j < 15 else b
        rblk[pl.ds(j, n, stride=16), :] = jnp.where(lane < D, a, 0.0)


def from_rows(rblk, loc, delta, P):
    n = P.block // 16
    lane = iota((n, 128), 1)
    loc[...] = jnp.zeros(loc.shape, F32)
    for i in range(15):
        a = shifted(rblk[pl.ds(i, n, stride=16), :], -8 * i)
        b = shifted(rblk[pl.ds(i + 1, n, stride=16), :], D - 8 * i)
        loc[pl.ds(i, n, stride=15), :] = jnp.where(lane < D - 8 * i, a, b)
    v = loc[...]
    lanes = iota(v.shape, 1)
    moved = pltpu.roll(v, lax.rem(128 - delta, 128), 1)
    v = jnp.where(lanes < 128 - delta, moved, pltpu.roll(moved, P.work - 1, 0))
    return v[0:P.local]


def step_kernel(P, names, master, obs, counts, codes, actions, valid, grad, sums, *scratch):
    R = Refs()
    for name, ref in zip(names, scratch):
        setattr(R, name, ref)
    Fn, C, B = P.feats, P.chips, P.block
    feat = lax.axis_index("feat")
    tok = lax.axis_index("tok")
    chip = tok // 2
    core = tok % 2
    me = feat * P.toks + tok
    delta = lax.rem(me * P.shard, D)

    def z_peer(i):
        return lax.rem(feat + i, Fn)

    def z_from(i):
        return lax.rem(feat + Fn - i, Fn)

    def c_peer(i):
        return lax.rem(chip + i, C)

    def c_from(i):
        return lax.rem(chip + C - i, C)

    def to_z(i):
        return (z_peer(i), tok)

    def to_c(i):
        return (feat, 2 * c_peer(i) + core)

    sibling = (feat, 2 * chip + 1 - core)

    def send(src, dst, sems, at, dev):
        return pltpu.make_async_remote_copy(
            src_ref=src, dst_ref=dst, send_sem=sems.at[(0,) + at], recv_sem=sems.at[(1,) + at],
            device_id=dev, device_id_type=MESH)

    barrier = pltpu.get_barrier_semaphore()
    peers = [to_z(i) for i in range(1, Fn)] + [to_c(i) for i in range(1, C)] + [sibling]
    for dev in peers:
        pl.semaphore_signal(barrier, inc=1, device_id=dev, device_id_type=MESH)

    n = P.own_rows
    ins = []
    for i, (src, dst) in enumerate(((codes, R.codes_in), (actions, R.act_in), (valid, R.val_in))):
        ins.append(pltpu.make_async_copy(src.at[:, pl.ds(pl.multiple_of(feat * n, 128), n)], dst, R.s_in.at[i]))
        ins[-1].start()

    R.loc[...] = jnp.zeros(R.loc.shape, F32)
    whole = P.shard // 1024
    R.loc[0:8 * whole, :] = master[pl.ds(0, 1024 * whole)].reshape(8 * whole, 128)
    rest = P.shard - 1024 * whole
    last = jnp.concatenate([master[pl.ds(1024 * whole, rest)], jnp.zeros((1024 - rest,), F32)])
    R.loc[8 * whole:8 * whole + 8, :] = last.reshape(8, 128)
    to_rows(R.loc, R.rblk, delta, P)
    R.pg[core, chip, feat] = low(R.rblk[...])
    pl.semaphore_wait(barrier, len(peers))

    p1 = []
    for i in range(1, Fn):
        blk = R.pg.at[core, chip, feat]
        p1.append(send(blk, blk, R.s_p1, (i,), to_z(i)))
        p1[-1].start()

    half = CT // 2

    def obs_copies(p):
        cps = []
        for i in range(1, Fn):
            src = obs.at[pl.ds(pl.multiple_of(z_peer(i) * n + half * p, 16), half), :]
            dst = R.ob.at[p // 2, feat, pl.ds(pl.multiple_of(half * (p % 2), 16), half), :]
            cps.append(send(src, dst, R.s_ob, (p, i), to_z(i)))
        return cps

    def start_obs(p):
        for cp in obs_copies(p):
            cp.start()

    own = []
    for c in range(P.chunks):
        src = obs.at[pl.ds(pl.multiple_of(feat * n + CT * c, 16), CT), :]
        own.append(pltpu.make_async_copy(src, R.ob.at[c, feat, pl.ds(0, CT), :], R.s_own.at[c]))
        own[-1].start()
    for cp in ins:
        cp.wait()
    zero_grads(R)
    for c in range(P.chunks):
        for f in range(Fn):
            R.ob[c, f, CT:L, :] = jnp.zeros((L - CT, 128), BF)
    live_n, valid_n = prep_tokens(R, counts, R.codes_in, R.act_in, R.val_in, feat, P.chunks)

    def two_rows(a, b):
        return jnp.concatenate([jnp.broadcast_to(a, (1, 128)), jnp.broadcast_to(b, (1, 128)),
                                jnp.zeros((6, 128), F32)], axis=0)

    def z_copies(w):
        return [send(R.tz.at[w, feat], R.tz.at[w, feat], R.s_tz.at[w], (i,), to_z(i)) for i in range(1, Fn)]

    def c_copies(w):
        return [send(R.tc.at[w, chip], R.tc.at[w, chip], R.s_tc.at[w], (i,), to_c(i)) for i in range(1, C)]

    def s_copies(w):
        return [send(R.ts.at[w, core], R.ts.at[w, core], R.s_ts.at[w], (), sibling)]

    def start_all(cps):
        for cp in cps:
            cp.start()

    def total(ref, w, count):
        v = ref[w, 0]
        for i in range(1, count):
            v = v + ref[w, i]
        return v

    def wait_all(cps):
        for cp in cps:
            cp.wait()

    R.tz[0, feat] = two_rows(live_n, valid_n)
    start_all(z_copies(0))
    wait_all(p1)
    start_obs(0)
    start_obs(1)
    p2 = []
    for i in range(1, C):
        blk = R.pg.at[core, chip]
        p2.append(send(blk, blk, R.s_p2, (i,), to_c(i)))
        p2[-1].start()
    p3 = [send(R.pg.at[core, chip], R.pg.at[core, chip], R.s_p3, (0,), sibling)]
    p3[0].start()
    wait_all(z_copies(0))
    R.tc[0, chip] = total(R.tz, 0, Fn)
    start_all(c_copies(0))
    for i in range(1, C):
        p2[i - 1].wait_recv()
        blk = R.pg.at[core, c_from(i)]
        p3.append(send(blk, blk, R.s_p3, (i,), sibling))
        p3[-1].start()
    wait_all(c_copies(0))
    R.ts[0, core] = total(R.tc, 0, C)
    start_all(s_copies(0))
    for cp in p2:
        cp.wait_send()
    wait_all(p3)
    R.rg[0:8, :] = jnp.zeros((8, 128), F32)

    def place(d, _):
        r0 = (P.shard * d) // D
        f, t = d // P.toks, d % P.toks
        blk = R.pg[t % 2, t // 2, f].astype(F32)
        before = R.rg[pl.ds(r0, 1), :]
        R.rg[pl.ds(r0, B), :] = blk
        R.rg[pl.ds(r0, 1), :] = blk[0:1] + before
        return 0

    lax.fori_loop(0, Fn * P.toks, place, 0)
    prep_weights(R.rg, R)
    wait_all(s_copies(0))
    counted = total(R.ts, 0, 2)
    live_total = counted[0:1, 0:1]
    valid_total = counted[1:2, 0:1]

    for cp in own:
        cp.wait()


    def rows_of(f, ch, co):
        return (P.shard * (f * P.toks + 2 * ch + co)) // D

    early = P.early[0] if P.early else Fn
    planes = [slice(Fn - 1, Fn), slice(early, Fn - 1), slice(0, early)]

    def r1_copy(w, i):
        at = pl.ds(planes[w].start, planes[w].stop - planes[w].start)
        return send(R.sb1.at[i, at], R.rb1.at[i, at], R.s_r1.at[w], (i,), sibling)

    def r2_copy(f, i):
        return send(R.sb2.at[i, f], R.rb2.at[i, f], R.s_r2.at[:, f], (i,), to_c(i))

    def r3_copy(i):
        return send(R.sb3.at[i], R.rb3.at[i], R.s_r3, (i,), to_z(i))

    order = list(range(1, C)) + [0]

    def sum_cores(w):
        for i in order:
            for f in range(planes[w].start, planes[w].stop):
                R.sb1[i, f] = R.rg[pl.ds(rows_of(f, c_peer(i), 1 - core), B), :]
            r1_copy(w, i).start()

    def sum_chips(w):
        for i in order:
            r1_copy(w, i).wait_recv()
            for f in range(planes[w].start, planes[w].stop):
                v = R.rg[pl.ds(rows_of(f, c_peer(i), core), B), :] + R.rb1[i, f]
                if i:
                    R.sb2[i, f] = low(v)
                    r2_copy(f, i).start()
                else:
                    R.col[f] = v

    def sum_column(f):
        v = R.col[f]
        for i in range(1, C):
            r2_copy(f, i).wait_recv()
            v = v + R.rb2[i, f].astype(F32)
        R.col[f] = v
        for i in range(1, Fn):
            @pl.when(z_peer(i) == f)
            def _():
                R.sb3[i] = v
                r3_copy(i).start()

    def chunk(c, _):
        for p in (2 * c, 2 * c + 1):
            for cp in obs_copies(p):
                cp.wait_recv()

            @pl.when(c + 1 < P.chunks)
            def _():
                start_obs(p + 2)

        R.x[...] = embed(R, [R.ob[c, f, 0:CT, :] for f in range(Fn)], c)

        def lay(l, _):
            R.x[...] = layer_fwd(R, l, c, l, R.x[...])
            return 0

        lax.fori_loop(0, LAYERS, lay, 0)

        dx = head_step(R, c, R.x[...], live_total, valid_total)
        dmid, da, rest = mlp_bwd(R, 1, dx)
        R.x[...] = att_bwd(R, 1, 1, dmid, da, rest)
        @pl.when(c == P.chunks - 1)
        def _():
            R.rg[pl.ds(HEAD + 32, P.grid - HEAD - 32), :] = jnp.zeros((P.grid - HEAD - 32, 128), F32)
            pack_head(R, R.rg)
            pack_late(R, R.rg, 1)
            pack_early(R, R.rg, 1)
            R.ts[1, core] = two_rows(jnp.sum(R.loss[0], keepdims=True), jnp.sum(R.loss[1], keepdims=True))
            sum_cores(0)
            start_all(s_copies(1))

        dmid, da, rest = mlp_bwd(R, 0, R.x[...])
        R.dmid[...] = dmid
        R.da[...] = da
        for run in rest:
            run()

        @pl.when(c == P.chunks - 1)
        def _():
            pack_early(R, R.rg, 0)
            sum_cores(1)
            sum_chips(0)
            wait_all(s_copies(1))
            R.tc[1, chip] = total(R.ts, 1, 2)
            start_all(c_copies(1))

        dx = att_bwd(R, 0, 0, R.dmid[...], R.da[...], [])

        @pl.when(c == P.chunks - 1)
        def _():
            pack_late(R, R.rg, 0)
            sum_chips(1)

        embed_bwd(R, [R.ob[c, f] for f in range(Fn)], c, dx)
        return 0

    lax.fori_loop(0, P.chunks, chunk, 0)
    pack_embed(R, R.rg)
    sum_cores(2)
    wait_all(c_copies(1))
    R.tz[1, feat] = total(R.tc, 1, C)
    start_all(z_copies(1))
    sum_column(Fn - 1)
    sum_chips(2)
    for f in (*range(early, Fn - 1), *range(early)):
        sum_column(f)
    for i in range(1, Fn):
        r3_copy(i).wait_recv()
    v = R.col[feat]
    for i in range(1, Fn):
        v = v + R.rb3[i]
    R.rblk[...] = v
    grad[...] = from_rows(R.rblk, R.loc, delta, P)
    wait_all(z_copies(1))
    lost = total(R.tz, 1, Fn)
    sums[...] = jnp.concatenate([lost[0:1], counted[0:1], lost[1:2], counted[1:2], jnp.zeros((4, 128), F32)], axis=0)
    for p in range(2 * P.chunks):
        for cp in obs_copies(p):
            cp.wait_send()
    for w in range(3):
        for i in range(C):
            r1_copy(w, i).wait_send()
    for i in range(1, C):
        for f in range(Fn):
            r2_copy(f, i).wait_send()
    for i in range(1, Fn):
        r3_copy(i).wait_send()


def adam_kernel(shard, grad, sums, master, first, second, new_master, new_first, new_second, parts):
    whole = shard // 1024
    for lo, hi in ((0, whole), (whole, whole + 1)):
        n = min(1024 * hi, shard) - 1024 * lo
        at = pl.ds(1024 * lo, n)
        g = grad[8 * lo:8 * hi].reshape(1024 * (hi - lo))[0:n]
        old = master[at]
        f_new = BETA_ONE * first[at] + (1.0 - BETA_ONE) * g
        s_new = BETA_TWO * second[at] + (1.0 - BETA_TWO) * g * g
        f_hat = f_new / (1.0 - BETA_ONE ** STEP_NO)
        s_hat = s_new / (1.0 - BETA_TWO ** STEP_NO)
        new_first[at] = f_new
        new_second[at] = s_new
        new_master[at] = old - LEARN_RATE * (f_hat / (jnp.sqrt(s_hat) + ADAM_EPS) + DECAY_RATE * old)
    for i in range(4):
        parts[i] = sums[i, 0]


def solution(mesh):
    feats, toks = mesh.shape["feat"], mesh.shape["tok"]

    def shards(master, first, second, obs, counts, codes, actions, valid):
        P_ = Plan(feats, toks, master.shape[0], obs.shape[0])
        scratch = dict(scratch_list(P_.chunks))
        scratch.update(comm_scratch(P_))
        vmem = pl.BlockSpec(memory_space=pltpu.VMEM)
        hbm = pl.BlockSpec(memory_space=pl.ANY)
        grad, sums = pl.pallas_call(
            functools.partial(step_kernel, P_, list(scratch)),
            out_shape=(jax.ShapeDtypeStruct((P_.local, 128), F32), jax.ShapeDtypeStruct((8, 128), F32)),
            in_specs=[vmem, hbm, vmem, hbm, hbm, hbm],
            out_specs=(vmem, vmem),
            scratch_shapes=list(scratch.values()),
            compiler_params=pltpu.CompilerParams(
                collective_id=0, has_side_effects=True, vmem_limit_bytes=60 * 2 ** 20),
        )(master, obs, counts.T, codes.T, actions, valid)
        flat = jax.ShapeDtypeStruct((P_.shard,), F32)
        return pl.pallas_call(
            functools.partial(adam_kernel, P_.shard),
            out_shape=(flat, flat, flat, jax.ShapeDtypeStruct((4,), F32)),
            in_specs=[vmem] * 5,
            out_specs=(vmem, vmem, vmem, pl.BlockSpec(memory_space=pltpu.SMEM)),
        )(grad, sums, master, first, second)

    weights = PSpec(("feat", "tok"))
    return jax.shard_map(
        shards, mesh=mesh,
        in_specs=(weights, weights, weights, PSpec("tok", "feat"), PSpec("tok", None), PSpec("tok", None),
                  PSpec(None, "tok"), PSpec(None, "tok")),
        out_specs=(weights, weights, weights, PSpec()), check_vma=False)
```

```python
import functools
import math

import jax
import jax.numpy as jnp
from jax import lax
from jax.experimental import pallas as pl
from jax.experimental.pallas import tpu as pltpu
from jax.sharding import PartitionSpec as PSpec

D = 120
H = 6
HD = 20
FF = 480
OBS = 512
LAYERS = 2
CAMS = 3
BOOKS = 2
CODES = 16
SPAN = 5
ACT = 7
WIN = 30
OFFS = SPAN * ACT
NORM_EPS = 1e-05
STEP_NO = 10
BETA_ONE = 0.9
BETA_TWO = 0.999
ADAM_EPS = 1e-08
DECAY_RATE = 0.1
LEARN_RATE = 0.05
GW = 4
GT = GW * WIN
CG = 4
L = CG * 128
CT = CG * GT
F32 = jnp.float32
BF = jnp.bfloat16
SCALE = HD ** (-0.5)
LROW = 2 * 1 + 3 * D + 2 + D + 1 + 2 + 4 * D + 4 + 4 * D + 1
BASE = OBS + 1 + WIN
HEAD = BASE + LAYERS * LROW
NV = 13
VROWS = [0, 1, 362, 363, 484, 485, 486, 967, 968, 969, 970, 1451]
(G1, B1, QB, VB, OB, G2, B2, FB0, FB1, FB2, FB3, PB) = range(12)


def nn(a, b):
    return lax.dot_general(a, b, (((1,), (0,)), ((), ())), preferred_element_type=F32)


def nt(a, b, precision=None):
    return lax.dot_general(a, b, (((1,), (1,)), ((), ())), preferred_element_type=F32, precision=precision)


def low(v):
    return v.astype(BF)


def pad8(v):
    return jnp.concatenate([v, jnp.zeros((8, v.shape[1]), v.dtype)], axis=0)


def tile4(v):
    return jnp.concatenate([v] * CG, axis=1)


def fold4(v):
    out = v[:, 0:128]
    for g in range(1, CG):
        out = out + v[:, 128 * g:128 * (g + 1)]
    return out


def iota(shape, axis):
    return lax.broadcasted_iota(jnp.int32, shape, axis)


def slab_at(h):
    return 20 * h - (4 if h % 2 else 0)


def head_stack(v):
    rows = iota((8, 128), 0)
    cols = []
    for h in range(H):
        a = slab_at(h)
        if h % 2 == 0:
            parts = [v[a:a + 16], jnp.where(rows < 4, v[a + 16:a + 24], 0.0)]
        else:
            parts = [jnp.where(rows >= 4, v[a:a + 8], 0.0), v[a + 8:a + 24]]
        if a > 0:
            parts = [jnp.zeros((a, 128), F32)] + parts
        if a + 24 < 128:
            parts = parts + [jnp.zeros((128 - a - 24, 128), F32)]
        cols.append(jnp.concatenate(parts, axis=0))
    return jnp.concatenate(cols, axis=1)


def join_slabs(slabs):
    rows = iota((8, 128), 0)
    parts = []
    for p in range(3):
        a, b = slabs[2 * p], slabs[2 * p + 1]
        parts += [a[0:16], jnp.where(rows < 4, a[16:24], b[0:8]), b[8:24]]
    return jnp.concatenate(parts, axis=0)


def slabs_of(v):
    return [v[slab_at(h):slab_at(h) + 24] for h in range(H)]


def hi_lo(v):
    hi = low(v)
    return hi, low(v - hi.astype(F32))


def normed(x):
    mean = jnp.sum(x, axis=0, keepdims=True) * (1.0 / D)
    c = x - mean
    var = jnp.sum(c * c, axis=0, keepdims=True) * (1.0 / D)
    r = lax.rsqrt(var + NORM_EPS)
    return c * r, r


def normed_back(d, xh, r):
    m0 = jnp.sum(d, axis=0, keepdims=True) * (1.0 / D)
    m1 = jnp.sum(d * xh, axis=0, keepdims=True) * (1.0 / D)
    return r * (d - m0 - xh * m1)


GA = math.sqrt(2.0 / math.pi)
GB = 0.044715


def gelu_half(x):
    return 0.5 + 0.5 * jnp.tanh(x * (GA + (GA * GB) * (x * x)))


def gelu_slope(x, s):
    return s + (x * s) * (1.0 - s) * (2.0 * GA + (6.0 * GA * GB) * (x * x))


LOG2E = math.log2(math.e)
BIG = 1e30


class Refs:
    pass


def scratch_list(chunks):
    groups = chunks * CG
    return dict(
        w_obs=pltpu.VMEM((OBS, 128), BF),
        posb=pltpu.VMEM((GT, 128), F32),
        qkv_t=pltpu.VMEM((LAYERS, 384, 128), BF),
        qkv=pltpu.VMEM((LAYERS, 128, 384), BF),
        out_t=pltpu.VMEM((LAYERS, 128, 128), BF),
        out=pltpu.VMEM((LAYERS, 128, 128), BF),
        fc_t=pltpu.VMEM((LAYERS, 512, 128), BF),
        fc=pltpu.VMEM((LAYERS, 128, 512), BF),
        proj_t=pltpu.VMEM((LAYERS, 128, 512), BF),
        proj=pltpu.VMEM((LAYERS, 512, 128), BF),
        head_t=pltpu.VMEM((72, 128), BF),
        head=pltpu.VMEM((128, 128), BF),
        vec=pltpu.VMEM((32, 128), F32),
        bc=pltpu.VMEM((LAYERS, 12, GT, 128), F32),
        bcf=pltpu.VMEM((2, GT, 128), F32),
        bch=pltpu.VMEM((72, 128), F32),
        hc=pltpu.VMEM((128, 128), F32),
        ho=pltpu.VMEM((128, 128), F32),
        cnt=pltpu.VMEM((16, 256), F32),
        live=pltpu.VMEM((chunks, 1, L), F32),
        act=pltpu.VMEM((chunks, 40, L), F32),
        val=pltpu.VMEM((chunks, 40, L), F32),
        code=pltpu.VMEM((chunks, 2, L), F32),
        x=pltpu.VMEM((D, L), F32),
        dmid=pltpu.VMEM((D, L), F32),
        da=pltpu.VMEM((D, L), F32),
        xh1=pltpu.VMEM((LAYERS, D, L), F32),
        r1=pltpu.VMEM((LAYERS, 1, L), F32),
        xh2=pltpu.VMEM((LAYERS, D, L), F32),
        r2=pltpu.VMEM((LAYERS, 1, L), F32),
        n1=pltpu.VMEM((LAYERS, 128, L), BF),
        n2=pltpu.VMEM((LAYERS, 128, L), BF),
        att=pltpu.VMEM((LAYERS, 128, L), BF),
        q_low=pltpu.VMEM((LAYERS, H, 24, L), BF),
        k_low=pltpu.VMEM((LAYERS, H, 24, L), BF),
        v_low=pltpu.VMEM((LAYERS, 128, L), BF),
        rsum=pltpu.VMEM((LAYERS, H, 1, L), F32),
        prob=pltpu.VMEM((LAYERS, CG, GT, H * 128), F32),
        prob_low=pltpu.VMEM((LAYERS, CG, 128, H * 128), BF),
        k_mask=pltpu.VMEM((48, 128), BF),
        q_mask=pltpu.VMEM((48, 128), BF),
        dead=pltpu.VMEM((groups, 8, 128), F32),
        pre=pltpu.VMEM((LAYERS, FF, L), F32),
        half=pltpu.VMEM((LAYERS, FF, L), F32),
        inner=pltpu.VMEM((LAYERS, 512, L), BF),
        a_qkv=pltpu.VMEM((LAYERS, 384, 128), F32),
        ds_t=pltpu.VMEM((CG * H // 2, 128, 256), BF),
        turned=pltpu.VMEM((5, L, 128), BF),
        a_out=pltpu.VMEM((LAYERS, 128, 128), F32),
        a_fc=pltpu.VMEM((LAYERS, 512, 128), F32),
        a_proj=pltpu.VMEM((LAYERS, 512, 128), F32),
        a_bias=pltpu.VMEM((LAYERS, 12, 128, 128), F32),
        a_obs=pltpu.VMEM((128, 512), F32),
        a_x=pltpu.VMEM((128, 128), F32),
        a_fin=pltpu.VMEM((2, 128, 128), F32),
        a_head=pltpu.VMEM((128, 128), F32),
        a_hb=pltpu.VMEM((128, 128), F32),
        loss=pltpu.VMEM((2, 8, 128), F32),
    )


def code_phases():
    for p in range(15):
        yield p, (32 * p) // D, (32 * p) % D


def off_phases():
    for p in range(24):
        yield p, (35 * p + 32) // D, (35 * p + 32) % D


def shifted(v, by):
    by %= 128
    return v if by == 0 else pltpu.roll(v, by, 1)


def take_phase(load, a, s, width, rows):
    lanes = iota((rows, 128), 1)
    first = shifted(load(a), -s)
    if s + width > D:
        second = shifted(load(a + 1), D - s)
        first = jnp.where(lanes < D - s, first, second)
    return jnp.where(lanes < width, first, 0.0)


def with_bias(w, bias):
    if bias is not None:
        w = jnp.where(iota((128, 128), 0) == D, bias, w)
    return low(w.T)


def ones8(v):
    return jnp.concatenate([v, jnp.where(iota((8, v.shape[1]), 0) == 0, 1.0, 0.0)], axis=0)


def prep_weights(rg, R):
    R.w_obs[...] = low(rg[0:OBS, :])
    for w in range(GW):
        R.posb[pl.ds(WIN * w, WIN), :] = rg[OBS + 1:OBS + 1 + WIN, :] + rg[OBS:OBS + 1, :]
    R.vec[...] = jnp.zeros((32, 128), F32)
    for l in range(LAYERS):
        b = BASE + LROW * l
        for j in range(3):
            w = pad8(rg[pl.ds(b + 2 + j, D, stride=3), :])
            R.qkv[l, :, 128 * j:128 * (j + 1)] = low(w)
            R.qkv_t[l, 128 * j:128 * (j + 1), :] = with_bias(w, None if j == 1 else rg[pl.ds(b + 362 + j // 2, 1), :])
        w = pad8(rg[pl.ds(b + 364, D), :])
        R.out[l] = low(w)
        R.out_t[l] = with_bias(w, rg[pl.ds(b + 484, 1), :])
        for j in range(4):
            w = pad8(rg[pl.ds(b + 487 + j, D, stride=4), :])
            R.fc[l, :, 128 * j:128 * (j + 1)] = low(w)
            R.fc_t[l, 128 * j:128 * (j + 1), :] = with_bias(w, rg[pl.ds(b + 967 + j, 1), :])
            w = pad8(rg[pl.ds(b + 971 + D * j, D), :])
            R.proj[l, 128 * j:128 * (j + 1), :] = low(w)
            R.proj_t[l, :, 128 * j:128 * (j + 1)] = with_bias(w, None if j else rg[pl.ds(b + 1451, 1), :])
        for i, r in enumerate(VROWS):
            R.vec[pl.ds(12 * l + i, 1), :] = rg[pl.ds(b + r, 1), :]
    R.vec[24:26, :] = rg[pl.ds(HEAD, 2), :]
    R.hc[...] = jnp.zeros((128, 128), F32)
    R.ho[...] = jnp.zeros((128, 128), F32)
    c0 = HEAD + 2
    for p, a, s in code_phases():
        R.hc[pl.ds(p, 8, stride=15), :] = take_phase(
            lambda i: rg[pl.ds(c0 + i, 8, stride=4), :], a, s, 32, 8)
    o0 = c0 + 32
    for p, a, s in off_phases():
        R.ho[pl.ds(p, 5, stride=24), :] = take_phase(
            lambda i: rg[pl.ds(o0 + i, 5, stride=7), :], a, s, OFFS, 5)
    hw = R.hc[...] + shifted(R.ho[...], 32)
    R.head[...] = low(hw)
    R.head_t[...] = low(hw.T[0:72])
    lanes = iota((1, 128), 1)
    hb = jnp.where(lanes < 32, rg[pl.ds(o0, 1), :], 0.0)
    a, s = (D * OFFS + 32) // D, (D * OFFS + 32) % D
    ob = take_phase(lambda i: rg[pl.ds(o0 + i, 1), :], a, s, OFFS, 1)
    R.vec[26:27, :] = hb + shifted(ob, 32)
    columns = jnp.concatenate([R.vec[...], jnp.zeros((96, 128), F32)], axis=0).T
    for l in range(LAYERS):
        for i in range(12):
            R.bc[l, i] = jnp.broadcast_to(columns[0:D, 12 * l + i:12 * l + i + 1], (D, 128))
    for i in range(2):
        R.bcf[i] = jnp.broadcast_to(columns[0:D, 24 + i:25 + i], (D, 128))
    R.bch[...] = jnp.broadcast_to(columns[0:72, 26:27], (72, 128))


def spread_groups(v, groups, width):
    rows = v.shape[0]
    lanes = iota((rows, 128), 1)
    out = []
    for g in range(groups):
        t, o = (GT * g) // 128, (GT * g) % 128
        a = shifted(v[:, 128 * t:128 * (t + 1)], -o)
        if o + GT > 128:
            b = shifted(v[:, 128 * (t + 1):128 * (t + 2)], -o)
            a = jnp.where(lanes < 128 - o, a, b)
        out.append(jnp.where(lanes < GT, a, 0))
    return out


def prep_tokens(R, counts, codes, actions, valid, feat, chunks):
    groups = chunks * CG
    wins = counts.shape[1]
    R.cnt[...] = jnp.zeros(R.cnt.shape, F32)
    R.cnt[0:WIN // CAMS, :] = counts[...].astype(F32)
    k = iota((GT, 16), 0)
    step = (k % WIN) // CAMS
    sel = jnp.where(step == iota((GT, 16), 1), 1.0, 0.0)
    x = nn(low(sel), low(R.cnt[...]))
    y = jnp.where(iota((GT, wins), 1) % GW == iota((GT, wins), 0) // WIN, x, 0.0)
    pick = jnp.where(iota((wins, 128), 0) // GW == iota((wins, 128), 1) + groups * feat, 1.0, 0.0)
    z = nn(low(y), low(pick))
    kk = iota((GT, 128), 0)
    alive = jnp.where((kk % CAMS).astype(F32) < z, 1.0, 0.0)
    steps = WIN // CAMS
    j, at = iota((48, 128), 0), iota((48, 128), 1)
    own = (at // WIN == j // steps) & ((at % WIN) // CAMS == j % steps) & (at < GT)
    R.k_mask[...] = low(jnp.where(own, 1.0, 0.0))
    may = (at // WIN == j // steps) & ((at % WIN) // CAMS >= j % steps)
    R.q_mask[...] = low(jnp.where(may | (j >= GW * steps), 0.0, -BIG))
    rows = pad8(alive).T
    for g in range(groups):
        R.live[g // CG, :, 128 * (g % CG):128 * (g % CG + 1)] = rows[g:g + 1, :]
        R.dead[g] = jnp.where(iota((8, 128), 0) == 0, 1.0 - rows[g:g + 1, :], 0.0)
    for name, src in (("code", codes), ("act", actions), ("val", valid)):
        parts = spread_groups(src[...].astype(F32), groups, GT)
        dst = getattr(R, name)
        for g in range(groups):
            c, lo = g // CG, 128 * (g % CG)
            part = parts[g]
            if name == "val":
                part = part * rows[g:g + 1, :]
            if name != "code":
                dst[c, 32:40, lo:lo + 128] = jnp.zeros((8, 128), F32)
            dst[c, 0:part.shape[0], lo:lo + 128] = part
    lanes = iota((GT, 128), 1)
    live_total = jnp.sum(jnp.where(lanes < groups, alive, 0.0), keepdims=True)
    v = jnp.zeros((40, L), F32)
    for c in range(chunks):
        v = v + R.val[c]
    valid_total = jnp.sum(v, keepdims=True)
    return live_total, valid_total


def own_rows(slab, h):
    rows = iota((8, 128), 0)
    if h % 2 == 0:
        return jnp.concatenate([slab[0:16], jnp.where(rows < 4, slab[16:24], 0.0)], axis=0)
    return jnp.concatenate([jnp.where(rows >= 4, slab[0:8], 0.0), slab[8:24]], axis=0)


def split(v):
    hi = low(v).astype(F32)
    return hi, v - hi


def attend(R, s, c, q, k, v):
    qh, ql = split(q)
    kh, kl = split(k)
    vh, vl = split(v)
    minus = jnp.where(iota((8, 128), 0) == 0, -BIG, 0.0)

    none = jnp.zeros((128, 128), BF)

    def scores(g, p):
        at = slice(128 * g, 128 * (g + 1))
        qs, ks = [], []
        for h in (2 * p, 2 * p + 1):
            sl = slice(slab_at(h), slab_at(h) + 24)
            hi = own_rows(qh[sl, at], h)
            qd = low(jnp.concatenate([hi, hi, own_rows(ql[sl, at], h), minus], axis=0))
            kd = low(jnp.concatenate([kh[sl, at], kl[sl, at], kh[sl, at], R.dead[c * CG + g]], axis=0))
            qs.append(jnp.concatenate([qd, R.q_mask[...]], axis=0))
            ks.append(jnp.concatenate([kd, R.k_mask[...]], axis=0).T)
        if PAIR:
            both = jnp.concatenate([jnp.concatenate([qs[0], none], axis=1),
                                    jnp.concatenate([none, qs[1]], axis=1)], axis=0)
            return nn(jnp.concatenate(ks, axis=1), both)[0:GT]
        return jnp.concatenate([nn(ks[0], qs[0])[0:GT], nn(ks[1], qs[1])[0:GT]], axis=1)

    def soft(g, p, sc):
        at = slice(128 * g, 128 * (g + 1))
        e = jnp.exp2(sc - jnp.max(sc, axis=0, keepdims=True))
        r = 1.0 / jnp.sum(e, axis=0, keepdims=True)
        e8 = pad8(e)
        eh = low(e8)
        cols = slice(256 * p, 256 * (p + 1))
        R.prob[s, g, :, cols] = e
        for i in range(2):
            at_h = slice(256 * p + 128 * i, 256 * p + 128 * (i + 1))
            R.prob_low[s, g, :, at_h] = eh[:, 128 * i:128 * (i + 1)].T
        R.rsum[s, 2 * p, :, at] = r[:, 0:128]
        R.rsum[s, 2 * p + 1, :, at] = r[:, 128:256]
        return r, eh

    def values(g, p, r, eh):
        at = slice(128 * g, 128 * (g + 1))
        out = []
        for i in range(2):
            sl = slice(slab_at(2 * p + i), slab_at(2 * p + i) + 24)
            cols = slice(128 * i, 128 * (i + 1))
            vs = low(jnp.concatenate([vh[sl, at], vl[sl, at]], axis=0))
            o = nn(vs, eh[:, cols])
            out.append((o[0:24] + o[24:48]) * r[:, cols])
        return out

    items = [(g, p) for g in range(CG) for p in range(H // 2)]
    slabs = pipeline(items, scores, soft, values, FAHEAD)
    slabs = [t for pair in slabs for t in pair]
    return jnp.concatenate([join_slabs(slabs[H * g:H * (g + 1)]) for g in range(CG)], axis=1)


PAIR = True
FAHEAD = 2
BAHEAD = 6


def pipeline(items, first, second, third, ahead, between=()):
    n = len(items)
    a, b, out = {}, {}, []
    between = list(between)
    done = 0
    for t in range(n + ahead):
        if t < n:
            a[t] = first(*items[t])
        m = t - ahead + 1
        if 0 <= m < n:
            b[m] = second(*items[m], *(a.pop(m) if isinstance(a[m], tuple) else (a.pop(m),)))
        m = t - ahead
        if 0 <= m < n:
            out.append(third(*items[m], *b.pop(m)))
        while done < len(between) * (t + 1) // (n + ahead):
            between[done]()
            done += 1
    return out


def attend_back(R, s, do, between=()):
    vrows = [R.v_low[s, :, 128 * g:128 * (g + 1)].T for g in range(CG)]

    def probs(g, p):
        at = slice(128 * g, 128 * (g + 1))
        ds, stack = [], []
        for h in (2 * p, 2 * p + 1):
            a = slab_at(h)
            d = own_rows(do[a:a + 24, at], h) * R.rsum[s, h, :, at]
            parts = ([jnp.zeros((a, 128), F32)] if a else []) + [d] + ([jnp.zeros((104 - a, 128), F32)])
            ds.append(low(d))
            stack.append(low(jnp.concatenate(parts, axis=0)))
        return ds, nn(vrows[g], jnp.concatenate(stack, axis=1))[0:GT]

    def inner(g, p, d, dp):
        at = slice(128 * g, 128 * (g + 1))
        e = R.prob[s, g, :, 256 * p:256 * (p + 1)]
        r = jnp.concatenate([R.rsum[s, 2 * p, :, at], R.rsum[s, 2 * p + 1, :, at]], axis=1)
        total = jnp.sum(e * dp, axis=0, keepdims=True) * r
        ds = low(pad8(e * (dp - total)))
        for i in range(2):
            cols = slice(128 * i, 128 * (i + 1))
            R.ds_t[3 * g + p, :, cols] = ds[:, cols].T
        return d, ds

    def outer(g, p, d, ds):
        at = slice(128 * g, 128 * (g + 1))
        out = []
        for i in range(2):
            h = 2 * p + i
            dsh = ds[:, 128 * i:128 * (i + 1)]
            out.append((nn(R.k_low[s, h, :, at], dsh), nn(R.q_low[s, h, :, at], R.ds_t[3 * g + p, :, 128 * i:128 * (i + 1)]),
                        nn(d[i], R.prob_low[s, g, :, 128 * h:128 * (h + 1)])))
        return out

    items = [(g, p) for g in range(CG) for p in range(H // 2)]
    slabs = pipeline(items, probs, inner, outer, BAHEAD, between)
    slabs = [t for pair in slabs for t in pair]
    out = []
    for i in range(3):
        out.append(jnp.concatenate(
            [join_slabs([t[i] for t in slabs[H * g:H * (g + 1)]]) for g in range(CG)], axis=1))
    return out[0] * SCALE, out[1], out[2]


def turn(R, i, v):
    for g in range(CG):
        R.turned[i, 128 * g:128 * (g + 1), :] = v[:, 128 * g:128 * (g + 1)].T


def embed(R, obs, c):
    rows = nn(jnp.concatenate(obs, axis=1), R.w_obs[...])
    parts = []
    for g in range(CG):
        r = rows[GT * g:GT * (g + 1)] + R.posb[...]
        parts.append(pad8(r).T[0:D])
    return jnp.concatenate(parts, axis=1)


def layer_fwd(R, l, c, s, x):
    def vec(i):
        return tile4(R.bc[l, i])

    xh, r = normed(x)
    R.xh1[s] = xh
    R.r1[s] = r
    n1 = low(ones8(xh * vec(G1) + vec(B1)))
    R.n1[s] = n1
    mix = nn(R.qkv_t[l], n1)
    q = mix[0:D] * SCALE
    k = mix[128:128 + D]
    v = mix[256:256 + D]
    for h in range(H):
        a = slab_at(h)
        R.q_low[s, h] = low(q[a:a + 24])
        R.k_low[s, h] = low(k[a:a + 24])
    R.v_low[s] = low(pad8(v))
    att = low(ones8(attend(R, s, c, q * LOG2E, k, v)))
    R.att[l] = att
    x1 = x + nn(R.out_t[l], att)[0:D]
    xh, r = normed(x1)
    R.xh2[l] = xh
    R.r2[l] = r
    n2 = low(ones8(xh * vec(G2) + vec(B2)))
    R.n2[l] = n2
    pre = nn(R.fc_t[l], n2)
    parts = []
    for j in range(4):
        pj = pre[128 * j:128 * j + D]
        half = gelu_half(pj)
        R.pre[l, D * j:D * (j + 1)] = pj
        R.half[l, D * j:D * (j + 1)] = half
        parts.append(low(ones8(pj * half) if j == 0 else pad8(pj * half)))
    inner = jnp.concatenate(parts, axis=0)
    R.inner[l] = inner
    return x1 + nn(R.proj_t[l], inner)[0:D]


def head_step(R, c, x, live_total, valid_total):
    xh, r = normed(x)
    fin = low(pad8(xh * tile4(R.bcf[0]) + tile4(R.bcf[1])))
    hd = nn(R.head_t[...], fin) + tile4(R.bch[...])
    live = R.live[c]
    lw = live * (1.0 / live_total)
    rows = iota((CODES, L), 0).astype(F32)
    grads = []
    csum = jnp.zeros((1, L), F32)
    for b in range(BOOKS):
        lg = hd[CODES * b:CODES * (b + 1)]
        m = jnp.max(lg, axis=0, keepdims=True)
        e = jnp.exp(lg - m)
        s = jnp.sum(e, axis=0, keepdims=True)
        hot = rows == R.code[c, b:b + 1, :]
        picked = jnp.sum(jnp.where(hot, lg, 0.0), axis=0, keepdims=True)
        csum = csum + (jnp.log(s) + m - picked) * live
        grads.append((e * (1.0 / s) - jnp.where(hot, 1.0, 0.0)) * lw)
    diff = hd[32:72] - R.act[c]
    val = R.val[c]
    sq = diff * diff + 1.0
    ri = lax.rsqrt(sq)
    asum = val * (sq * ri)
    grads.append((val * (1.0 / valid_total)) * (diff * ri))
    R.loss[0, 0:1] += fold4(csum)
    af = fold4(asum)
    R.loss[1] += af[0:8] + af[8:16] + af[16:24] + af[24:32] + af[32:40]
    dh = jnp.concatenate(grads, axis=0)
    R.a_hb[0:72] += fold4(dh)
    dhl = low(jnp.concatenate([dh, jnp.zeros((56, L), F32)], axis=0))
    turn(R, 4, dhl)
    R.a_head[...] += nn(fin, R.turned[4])
    df = nn(R.head[...], dhl)[0:D]
    R.a_fin[0, 0:D] += fold4(df * xh)
    R.a_fin[1, 0:D] += fold4(df)
    return normed_back(df * tile4(R.bcf[0]), xh, r)


def add_bias(R, l, i, v):
    R.a_bias[l, i, 0:D] += fold4(v)


def mlp_bwd(R, l, dout):
    outl = low(pad8(dout))
    add_bias(R, l, PB, dout)
    parts = []
    for j in range(4):
        rows = slice(D * j, D * (j + 1))
        dj = nn(R.proj[l, 128 * j:128 * (j + 1)], outl)
        parts.append(low(pad8(dj[0:D] * gelu_slope(R.pre[l, rows], R.half[l, rows]))))
    prel = jnp.concatenate(parts, axis=0)
    dn = nn(R.fc[l], prel)[0:D]
    xh = R.xh2[l]
    add_bias(R, l, G2, dn * xh)
    add_bias(R, l, B2, dn)
    dmid = normed_back(dn * tile4(R.bc[l, G2]), xh, R.r2[l]) + dout
    midl = low(pad8(dmid))
    add_bias(R, l, OB, dmid)
    da = nn(R.out[l], midl)[0:D]

    turn(R, 0, outl)
    turn(R, 1, R.n2[l])
    turn(R, 2, midl)

    def a_proj(j):
        def run():
            rows = slice(256 * j, 256 * (j + 1))
            R.a_proj[l, rows] += nn(R.inner[l, rows], R.turned[0])
        return run

    def a_fc(j):
        def run():
            rows = slice(256 * j, 256 * (j + 1))
            R.a_fc[l, rows] += nn(prel[rows], R.turned[1])
        return run

    def a_out():
        R.a_out[l] += nn(R.att[l], R.turned[2])

    return dmid, da, [a_proj(0), a_proj(1), a_fc(0), a_fc(1), a_out]


def att_bwd(R, l, s, dmid, da, between):
    turn(R, 3, R.n1[s])
    dq, dk, dv = attend_back(R, s, da, between)
    mixl = jnp.concatenate([low(pad8(dq)), low(pad8(dk)), low(pad8(dv))], axis=0)
    dn = nn(R.qkv[l], mixl)[0:D]
    add_bias(R, l, QB, dq)
    add_bias(R, l, VB, dv)
    R.a_qkv[l] += nn(mixl, R.turned[3])
    xh = R.xh1[s]
    add_bias(R, l, G1, dn * xh)
    add_bias(R, l, B1, dn)
    return normed_back(dn * tile4(R.bc[l, G1]), xh, R.r1[s]) + dmid


def embed_bwd(R, obs, c, dx):
    R.a_x[0:D] += fold4(dx)
    lanes = iota((D, 128), 1)
    tiles = []
    gs = [dx[:, 128 * g:128 * (g + 1)] for g in range(CG)]
    for t in range(CG):
        a = shifted(gs[t], -8 * t)
        b = shifted(gs[t + 1], 120 - 8 * t) if t + 1 < CG else jnp.zeros((D, 128), F32)
        tiles.append(jnp.where(lanes < GT - 8 * t, a, b))
    gl = low(pad8(jnp.concatenate(tiles, axis=1)))
    R.a_obs[...] += nn(gl, jnp.concatenate(obs, axis=1))


def zero_grads(R):
    for name in ("a_qkv", "a_out", "a_fc", "a_proj", "a_bias", "a_obs", "a_x", "a_fin", "a_head", "a_hb", "loss"):
        ref = getattr(R, name)
        ref[...] = jnp.zeros(ref.shape, F32)


HIGH = lax.Precision.HIGHEST


LATE = 364
EARLY_ROWS = (OB, G2, B2, PB)


def lane_sums(v):
    return jnp.sum(v.T, axis=0, keepdims=True)


def pack_vectors(R, rg, l, which):
    b = BASE + LROW * l
    for i in which:
        rg[pl.ds(b + VROWS[i], 1), :] = lane_sums(R.a_bias[l, i])


def pack_early(R, rg, l):
    b = BASE + LROW * l
    rg[pl.ds(b + 364, D), :] = R.a_out[l, 0:D]
    for j in range(4):
        fc = R.a_fc[l, 128 * j:128 * (j + 1), :].T
        rg[pl.ds(b + 487 + j, D, stride=4), :] = fc[0:D]
        rg[pl.ds(b + 967 + j, 1), :] = fc[D:D + 1]
        rg[pl.ds(b + 971 + D * j, D), :] = R.a_proj[l, 128 * j:128 * j + D, :]
    pack_vectors(R, rg, l, EARLY_ROWS)


def pack_late(R, rg, l):
    b = BASE + LROW * l
    for j in range(3):
        rg[pl.ds(b + 2 + j, D, stride=3), :] = R.a_qkv[l, 128 * j:128 * (j + 1), :].T[0:D]
    pack_vectors(R, rg, l, (G1, B1, QB, VB))


def pack_embed(R, rg):
    for f in range(OBS // 128):
        rg[128 * f:128 * (f + 1), :] = R.a_obs[:, 128 * f:128 * (f + 1)].T
    slot, lane = iota((32, 128), 0), iota((32, 128), 1)
    sel = jnp.where((slot == 0) | (lane % WIN == slot - 1), 1.0, 0.0)
    sel = jnp.where(lane < GT, sel, 0.0)
    rows = nt(sel, R.a_x[...], HIGH)
    rg[pl.ds(OBS, 1 + WIN), :] = rows[0:1 + WIN]


def pack_head(R, rg):
    for i in range(2):
        rg[pl.ds(HEAD + i, 1), :] = lane_sums(R.a_fin[i])
    lanes8 = iota((8, 128), 1)
    grad = R.a_head[...]
    R.hc[...] = jnp.where(iota((128, 128), 1) < 32, grad, 0.0)
    R.ho[...] = jnp.where(iota((128, 128), 1) < OFFS, shifted(grad, -32), 0.0)
    c0 = HEAD + 2
    o0 = c0 + 32

    def put(phases, src, rows_n, stride, width, count):
        acc = [jnp.zeros((rows_n, 128), F32) for _ in range(count + 1)]
        lanes = iota((rows_n, 128), 1)
        for p, a, s in phases:
            v = src[pl.ds(p, rows_n, stride=stride), :]
            first = shifted(v, s)
            if s + width > D:
                acc[a] = acc[a] + jnp.where((lanes >= s) & (lanes < D), first, 0.0)
                acc[a + 1] = acc[a + 1] + jnp.where(lanes < s + width - D, shifted(v, s - D), 0.0)
            else:
                acc[a] = acc[a] + first
        return acc

    acc = put(code_phases(), R.hc, 8, 15, 32, 4)
    for a in range(4):
        rg[pl.ds(c0 + a, 8, stride=4), :] = acc[a]
    hb = lane_sums(R.a_hb[...])
    lane1 = iota((1, 128), 1)
    rg[pl.ds(o0, 48), :] = jnp.zeros((48, 128), F32)
    acc = put(off_phases(), R.ho, 5, 24, OFFS, 7)
    for a in range(7):
        rg[pl.ds(o0 + a, 5, stride=7), :] = acc[a]
    rg[pl.ds(o0 + 7, 5, stride=7), :] = rg[pl.ds(o0 + 7, 5, stride=7), :] + acc[7]
    rg[pl.ds(o0, 1), :] = rg[pl.ds(o0, 1), :] + jnp.where(lane1 < 32, hb, 0.0)
    a, s = (D * OFFS + 32) // D, (D * OFFS + 32) % D
    ob = jnp.where(lane1 < OFFS, shifted(hb, -32), 0.0)
    rg[pl.ds(o0 + a, 1), :] = rg[pl.ds(o0 + a, 1), :] + shifted(ob, s)


MESH = pl.DeviceIdType.MESH


def round_up(n, m):
    return -(-n // m) * m


class Plan:
    def __init__(self, feats, toks, shard, tok_rows):
        self.feats, self.toks, self.chips = feats, toks, toks // 2
        self.shard = shard
        self.block = round_up(-(-(shard + 112) // D), 16)
        self.flat_rows = self.block // 16 * 15
        self.local = round_up(-(-shard // 1024), 1) * 8
        self.work = round_up(max(self.flat_rows, self.local + 1), 8)
        self.own_rows = tok_rows // feats
        self.chunks = self.own_rows // CT
        self.early = [f for f in range(feats) if shard * toks * f // D >= BASE + LATE]
        self.grid = round_up(-(-(shard * feats * toks) // D) + self.block, 8)


def comm_scratch(P):
    dma = pltpu.SemaphoreType.DMA
    B, C, Fn = P.block, P.chips, P.feats
    return dict(
        rg=pltpu.VMEM((P.grid, 128), F32),
        ob=pltpu.VMEM((P.chunks, Fn, L, 128), BF),
        pg=pltpu.VMEM((2, C, Fn, B, 128), BF),
        loc=pltpu.VMEM((P.work, 128), F32),
        rblk=pltpu.VMEM((B, 128), F32),
        codes_in=pltpu.VMEM((BOOKS, P.own_rows), jnp.int32),
        act_in=pltpu.VMEM((OFFS, P.own_rows), F32),
        val_in=pltpu.VMEM((OFFS, P.own_rows), jnp.int32),
        tz=pltpu.VMEM((2, Fn, 8, 128), F32),
        tc=pltpu.VMEM((2, C, 8, 128), F32),
        ts=pltpu.VMEM((2, 2, 8, 128), F32),
        sb1=pltpu.VMEM((C, Fn, B, 128), F32),
        rb1=pltpu.VMEM((C, Fn, B, 128), F32),
        sb2=pltpu.VMEM((C, Fn, B, 128), BF),
        rb2=pltpu.VMEM((C, Fn, B, 128), BF),
        col=pltpu.VMEM((Fn, B, 128), F32),
        sb3=pltpu.VMEM((Fn, B, 128), F32),
        rb3=pltpu.VMEM((Fn, B, 128), F32),
        s_p1=dma((2, Fn)), s_p2=dma((2, C)), s_p3=dma((2, C)),
        s_tz=dma((2, 2, Fn)), s_tc=dma((2, 2, C)), s_ts=dma((2, 2)),
        s_ob=dma((2, 2 * P.chunks, Fn)),
        s_own=dma((P.chunks,)),
        s_in=dma((3,)),
        s_r1=dma((3, 2, C)), s_r2=dma((2, Fn, C)), s_r3=dma((2, Fn)),
    )


def to_rows(loc, rblk, delta, P):
    v = loc[...]
    lanes = iota(v.shape, 1)
    moved = pltpu.roll(v, delta, 1)
    loc[...] = jnp.where(lanes >= delta, moved, pltpu.roll(moved, 1, 0))
    n = P.block // 16
    lane = iota((n, 128), 1)
    for j in range(16):
        if j < 15:
            a = shifted(loc[pl.ds(j, n, stride=15), :], 8 * j)
        if j > 0:
            b = shifted(loc[pl.ds(j - 1, n, stride=15), :], 8 * j)
            a = jnp.where(lane < 8 * j, b, a) if j < 15 else b
        rblk[pl.ds(j, n, stride=16), :] = jnp.where(lane < D, a, 0.0)


def from_rows(rblk, loc, delta, P):
    n = P.block // 16
    lane = iota((n, 128), 1)
    loc[...] = jnp.zeros(loc.shape, F32)
    for i in range(15):
        a = shifted(rblk[pl.ds(i, n, stride=16), :], -8 * i)
        b = shifted(rblk[pl.ds(i + 1, n, stride=16), :], D - 8 * i)
        loc[pl.ds(i, n, stride=15), :] = jnp.where(lane < D - 8 * i, a, b)
    v = loc[...]
    lanes = iota(v.shape, 1)
    moved = pltpu.roll(v, lax.rem(128 - delta, 128), 1)
    v = jnp.where(lanes < 128 - delta, moved, pltpu.roll(moved, P.work - 1, 0))
    return v[0:P.local]


def step_kernel(P, names, master, obs, counts, codes, actions, valid, grad, sums, *scratch):
    R = Refs()
    for name, ref in zip(names, scratch):
        setattr(R, name, ref)
    Fn, C, B = P.feats, P.chips, P.block
    feat = lax.axis_index("feat")
    tok = lax.axis_index("tok")
    chip = tok // 2
    core = tok % 2
    me = feat * P.toks + tok
    delta = lax.rem(me * P.shard, D)

    def z_peer(i):
        return lax.rem(feat + i, Fn)

    def z_from(i):
        return lax.rem(feat + Fn - i, Fn)

    def c_peer(i):
        return lax.rem(chip + i, C)

    def c_from(i):
        return lax.rem(chip + C - i, C)

    def to_z(i):
        return (z_peer(i), tok)

    def to_c(i):
        return (feat, 2 * c_peer(i) + core)

    sibling = (feat, 2 * chip + 1 - core)

    def send(src, dst, sems, at, dev):
        return pltpu.make_async_remote_copy(
            src_ref=src, dst_ref=dst, send_sem=sems.at[(0,) + at], recv_sem=sems.at[(1,) + at],
            device_id=dev, device_id_type=MESH)

    barrier = pltpu.get_barrier_semaphore()
    peers = [to_z(i) for i in range(1, Fn)] + [to_c(i) for i in range(1, C)] + [sibling]
    for dev in peers:
        pl.semaphore_signal(barrier, inc=1, device_id=dev, device_id_type=MESH)

    n = P.own_rows
    ins = []
    for i, (src, dst) in enumerate(((codes, R.codes_in), (actions, R.act_in), (valid, R.val_in))):
        ins.append(pltpu.make_async_copy(src.at[:, pl.ds(pl.multiple_of(feat * n, 128), n)], dst, R.s_in.at[i]))
        ins[-1].start()

    R.loc[...] = jnp.zeros(R.loc.shape, F32)
    whole = P.shard // 1024
    R.loc[0:8 * whole, :] = master[pl.ds(0, 1024 * whole)].reshape(8 * whole, 128)
    rest = P.shard - 1024 * whole
    last = jnp.concatenate([master[pl.ds(1024 * whole, rest)], jnp.zeros((1024 - rest,), F32)])
    R.loc[8 * whole:8 * whole + 8, :] = last.reshape(8, 128)
    to_rows(R.loc, R.rblk, delta, P)
    R.pg[core, chip, feat] = low(R.rblk[...])
    pl.semaphore_wait(barrier, len(peers))

    p1 = []
    for i in range(1, Fn):
        blk = R.pg.at[core, chip, feat]
        p1.append(send(blk, blk, R.s_p1, (i,), to_z(i)))
        p1[-1].start()

    half = CT // 2

    def obs_copies(p):
        cps = []
        for i in range(1, Fn):
            src = obs.at[pl.ds(pl.multiple_of(z_peer(i) * n + half * p, 16), half), :]
            dst = R.ob.at[p // 2, feat, pl.ds(pl.multiple_of(half * (p % 2), 16), half), :]
            cps.append(send(src, dst, R.s_ob, (p, i), to_z(i)))
        return cps

    def start_obs(p):
        for cp in obs_copies(p):
            cp.start()

    own = []
    for c in range(P.chunks):
        src = obs.at[pl.ds(pl.multiple_of(feat * n + CT * c, 16), CT), :]
        own.append(pltpu.make_async_copy(src, R.ob.at[c, feat, pl.ds(0, CT), :], R.s_own.at[c]))
        own[-1].start()
    for cp in ins:
        cp.wait()
    zero_grads(R)
    for c in range(P.chunks):
        for f in range(Fn):
            R.ob[c, f, CT:L, :] = jnp.zeros((L - CT, 128), BF)
    live_n, valid_n = prep_tokens(R, counts, R.codes_in, R.act_in, R.val_in, feat, P.chunks)

    def two_rows(a, b):
        return jnp.concatenate([jnp.broadcast_to(a, (1, 128)), jnp.broadcast_to(b, (1, 128)),
                                jnp.zeros((6, 128), F32)], axis=0)

    def z_copies(w):
        return [send(R.tz.at[w, feat], R.tz.at[w, feat], R.s_tz.at[w], (i,), to_z(i)) for i in range(1, Fn)]

    def c_copies(w):
        return [send(R.tc.at[w, chip], R.tc.at[w, chip], R.s_tc.at[w], (i,), to_c(i)) for i in range(1, C)]

    def s_copies(w):
        return [send(R.ts.at[w, core], R.ts.at[w, core], R.s_ts.at[w], (), sibling)]

    def start_all(cps):
        for cp in cps:
            cp.start()

    def total(ref, w, count):
        v = ref[w, 0]
        for i in range(1, count):
            v = v + ref[w, i]
        return v

    def wait_all(cps):
        for cp in cps:
            cp.wait()

    R.tz[0, feat] = two_rows(live_n, valid_n)
    start_all(z_copies(0))
    wait_all(p1)
    start_obs(0)
    start_obs(1)
    p2 = []
    for i in range(1, C):
        blk = R.pg.at[core, chip]
        p2.append(send(blk, blk, R.s_p2, (i,), to_c(i)))
        p2[-1].start()
    p3 = [send(R.pg.at[core, chip], R.pg.at[core, chip], R.s_p3, (0,), sibling)]
    p3[0].start()
    wait_all(z_copies(0))
    R.tc[0, chip] = total(R.tz, 0, Fn)
    start_all(c_copies(0))
    for i in range(1, C):
        p2[i - 1].wait_recv()
        blk = R.pg.at[core, c_from(i)]
        p3.append(send(blk, blk, R.s_p3, (i,), sibling))
        p3[-1].start()
    wait_all(c_copies(0))
    R.ts[0, core] = total(R.tc, 0, C)
    start_all(s_copies(0))
    for cp in p2:
        cp.wait_send()
    wait_all(p3)
    R.rg[0:8, :] = jnp.zeros((8, 128), F32)

    def place(d, _):
        r0 = (P.shard * d) // D
        f, t = d // P.toks, d % P.toks
        blk = R.pg[t % 2, t // 2, f].astype(F32)
        before = R.rg[pl.ds(r0, 1), :]
        R.rg[pl.ds(r0, B), :] = blk
        R.rg[pl.ds(r0, 1), :] = blk[0:1] + before
        return 0

    lax.fori_loop(0, Fn * P.toks, place, 0)
    prep_weights(R.rg, R)
    wait_all(s_copies(0))
    counted = total(R.ts, 0, 2)
    live_total = counted[0:1, 0:1]
    valid_total = counted[1:2, 0:1]

    for cp in own:
        cp.wait()


    def rows_of(f, ch, co):
        return (P.shard * (f * P.toks + 2 * ch + co)) // D

    early = P.early[0] if P.early else Fn
    planes = [slice(Fn - 1, Fn), slice(early, Fn - 1), slice(0, early)]

    def r1_copy(w, i):
        at = pl.ds(planes[w].start, planes[w].stop - planes[w].start)
        return send(R.sb1.at[i, at], R.rb1.at[i, at], R.s_r1.at[w], (i,), sibling)

    def r2_copy(f, i):
        return send(R.sb2.at[i, f], R.rb2.at[i, f], R.s_r2.at[:, f], (i,), to_c(i))

    def r3_copy(i):
        return send(R.sb3.at[i], R.rb3.at[i], R.s_r3, (i,), to_z(i))

    order = list(range(1, C)) + [0]

    def sum_cores(w):
        for i in order:
            for f in range(planes[w].start, planes[w].stop):
                R.sb1[i, f] = R.rg[pl.ds(rows_of(f, c_peer(i), 1 - core), B), :]
            r1_copy(w, i).start()

    def sum_chips(w):
        for i in order:
            r1_copy(w, i).wait_recv()
            for f in range(planes[w].start, planes[w].stop):
                v = R.rg[pl.ds(rows_of(f, c_peer(i), core), B), :] + R.rb1[i, f]
                if i:
                    R.sb2[i, f] = low(v)
                    r2_copy(f, i).start()
                else:
                    R.col[f] = v

    def sum_column(f):
        v = R.col[f]
        for i in range(1, C):
            r2_copy(f, i).wait_recv()
            v = v + R.rb2[i, f].astype(F32)
        R.col[f] = v
        for i in range(1, Fn):
            @pl.when(z_peer(i) == f)
            def _():
                R.sb3[i] = v
                r3_copy(i).start()

    def chunk(c, _):
        for p in (2 * c, 2 * c + 1):
            for cp in obs_copies(p):
                cp.wait_recv()

            @pl.when(c + 1 < P.chunks)
            def _():
                start_obs(p + 2)

        R.x[...] = embed(R, [R.ob[c, f, 0:CT, :] for f in range(Fn)], c)

        def lay(l, _):
            R.x[...] = layer_fwd(R, l, c, l, R.x[...])
            return 0

        lax.fori_loop(0, LAYERS, lay, 0)

        dx = head_step(R, c, R.x[...], live_total, valid_total)
        dmid, da, rest = mlp_bwd(R, 1, dx)
        R.x[...] = att_bwd(R, 1, 1, dmid, da, rest)
        @pl.when(c == P.chunks - 1)
        def _():
            R.rg[pl.ds(HEAD + 32, P.grid - HEAD - 32), :] = jnp.zeros((P.grid - HEAD - 32, 128), F32)
            pack_head(R, R.rg)
            pack_late(R, R.rg, 1)
            pack_early(R, R.rg, 1)
            R.ts[1, core] = two_rows(jnp.sum(R.loss[0], keepdims=True), jnp.sum(R.loss[1], keepdims=True))
            sum_cores(0)
            start_all(s_copies(1))

        dmid, da, rest = mlp_bwd(R, 0, R.x[...])
        R.dmid[...] = dmid
        R.da[...] = da
        for run in rest:
            run()

        @pl.when(c == P.chunks - 1)
        def _():
            pack_early(R, R.rg, 0)
            sum_cores(1)
            sum_chips(0)
            wait_all(s_copies(1))
            R.tc[1, chip] = total(R.ts, 1, 2)
            start_all(c_copies(1))

        dx = att_bwd(R, 0, 0, R.dmid[...], R.da[...], [])

        @pl.when(c == P.chunks - 1)
        def _():
            pack_late(R, R.rg, 0)
            sum_chips(1)

        embed_bwd(R, [R.ob[c, f] for f in range(Fn)], c, dx)
        return 0

    lax.fori_loop(0, P.chunks, chunk, 0)
    pack_embed(R, R.rg)
    sum_cores(2)
    wait_all(c_copies(1))
    R.tz[1, feat] = total(R.tc, 1, C)
    start_all(z_copies(1))
    sum_column(Fn - 1)
    sum_chips(2)
    for f in (*range(early, Fn - 1), *range(early)):
        sum_column(f)
    for i in range(1, Fn):
        r3_copy(i).wait_recv()
    v = R.col[feat]
    for i in range(1, Fn):
        v = v + R.rb3[i]
    R.rblk[...] = v
    grad[...] = from_rows(R.rblk, R.loc, delta, P)
    wait_all(z_copies(1))
    lost = total(R.tz, 1, Fn)
    sums[...] = jnp.concatenate([lost[0:1], counted[0:1], lost[1:2], counted[1:2], jnp.zeros((4, 128), F32)], axis=0)
    for p in range(2 * P.chunks):
        for cp in obs_copies(p):
            cp.wait_send()
    for w in range(3):
        for i in range(C):
            r1_copy(w, i).wait_send()
    for i in range(1, C):
        for f in range(Fn):
            r2_copy(f, i).wait_send()
    for i in range(1, Fn):
        r3_copy(i).wait_send()


def adam_kernel(shard, grad, sums, master, first, second, new_master, new_first, new_second, parts):
    whole = shard // 1024
    for lo, hi in ((0, whole), (whole, whole + 1)):
        n = min(1024 * hi, shard) - 1024 * lo
        at = pl.ds(1024 * lo, n)
        g = grad[8 * lo:8 * hi].reshape(1024 * (hi - lo))[0:n]
        old = master[at]
        f_new = BETA_ONE * first[at] + (1.0 - BETA_ONE) * g
        s_new = BETA_TWO * second[at] + (1.0 - BETA_TWO) * g * g
        f_hat = f_new / (1.0 - BETA_ONE ** STEP_NO)
        s_hat = s_new / (1.0 - BETA_TWO ** STEP_NO)
        new_first[at] = f_new
        new_second[at] = s_new
        new_master[at] = old - LEARN_RATE * (f_hat / (jnp.sqrt(s_hat) + ADAM_EPS) + DECAY_RATE * old)
    for i in range(4):
        parts[i] = sums[i, 0]


def solution(mesh):
    feats, toks = mesh.shape["feat"], mesh.shape["tok"]

    def shards(master, first, second, obs, counts, codes, actions, valid):
        P_ = Plan(feats, toks, master.shape[0], obs.shape[0])
        scratch = dict(scratch_list(P_.chunks))
        scratch.update(comm_scratch(P_))
        vmem = pl.BlockSpec(memory_space=pltpu.VMEM)
        hbm = pl.BlockSpec(memory_space=pl.ANY)
        grad, sums = pl.pallas_call(
            functools.partial(step_kernel, P_, list(scratch)),
            out_shape=(jax.ShapeDtypeStruct((P_.local, 128), F32), jax.ShapeDtypeStruct((8, 128), F32)),
            in_specs=[vmem, hbm, vmem, hbm, hbm, hbm],
            out_specs=(vmem, vmem),
            scratch_shapes=list(scratch.values()),
            compiler_params=pltpu.CompilerParams(
                collective_id=0, has_side_effects=True, vmem_limit_bytes=60 * 2 ** 20),
        )(master, obs, counts.T, codes.T, actions, valid)
        flat = jax.ShapeDtypeStruct((P_.shard,), F32)
        return pl.pallas_call(
            functools.partial(adam_kernel, P_.shard),
            out_shape=(flat, flat, flat, jax.ShapeDtypeStruct((4,), F32)),
            in_specs=[vmem] * 5,
            out_specs=(vmem, vmem, vmem, pl.BlockSpec(memory_space=pltpu.SMEM)),
        )(grad, sums, master, first, second)

    weights = PSpec(("feat", "tok"))
    return jax.shard_map(
        shards, mesh=mesh,
        in_specs=(weights, weights, weights, PSpec("tok", "feat"), PSpec("tok", None), PSpec("tok", None),
                  PSpec(None, "tok"), PSpec(None, "tok")),
        out_specs=(weights, weights, weights, PSpec()), check_vma=False)
```

```python
import functools
import math

import jax
import jax.numpy as jnp
from jax import lax
from jax.experimental import pallas as pl
from jax.experimental.pallas import tpu as pltpu
from jax.sharding import PartitionSpec as PSpec

D = 120
H = 6
HD = 20
FF = 480
OBS = 512
LAYERS = 2
CAMS = 3
BOOKS = 2
CODES = 16
SPAN = 5
ACT = 7
WIN = 30
OFFS = SPAN * ACT
NORM_EPS = 1e-05
STEP_NO = 10
BETA_ONE = 0.9
BETA_TWO = 0.999
ADAM_EPS = 1e-08
DECAY_RATE = 0.1
LEARN_RATE = 0.05
GW = 4
GT = GW * WIN
CG = 4
L = CG * 128
CT = CG * GT
F32 = jnp.float32
BF = jnp.bfloat16
SCALE = HD ** (-0.5)
LROW = 2 * 1 + 3 * D + 2 + D + 1 + 2 + 4 * D + 4 + 4 * D + 1
BASE = OBS + 1 + WIN
HEAD = BASE + LAYERS * LROW
NV = 13
VROWS = [0, 1, 362, 363, 484, 485, 486, 967, 968, 969, 970, 1451]
(G1, B1, QB, VB, OB, G2, B2, FB0, FB1, FB2, FB3, PB) = range(12)


def nn(a, b):
    return lax.dot_general(a, b, (((1,), (0,)), ((), ())), preferred_element_type=F32)


def nt(a, b, precision=None):
    return lax.dot_general(a, b, (((1,), (1,)), ((), ())), preferred_element_type=F32, precision=precision)


def low(v):
    return v.astype(BF)


def pad8(v):
    return jnp.concatenate([v, jnp.zeros((8, v.shape[1]), v.dtype)], axis=0)


def tile4(v):
    return jnp.concatenate([v] * CG, axis=1)


def fold4(v):
    out = v[:, 0:128]
    for g in range(1, CG):
        out = out + v[:, 128 * g:128 * (g + 1)]
    return out


def iota(shape, axis):
    return lax.broadcasted_iota(jnp.int32, shape, axis)


def slab_at(h):
    return 20 * h - (4 if h % 2 else 0)


def head_stack(v):
    rows = iota((8, 128), 0)
    cols = []
    for h in range(H):
        a = slab_at(h)
        if h % 2 == 0:
            parts = [v[a:a + 16], jnp.where(rows < 4, v[a + 16:a + 24], 0.0)]
        else:
            parts = [jnp.where(rows >= 4, v[a:a + 8], 0.0), v[a + 8:a + 24]]
        if a > 0:
            parts = [jnp.zeros((a, 128), F32)] + parts
        if a + 24 < 128:
            parts = parts + [jnp.zeros((128 - a - 24, 128), F32)]
        cols.append(jnp.concatenate(parts, axis=0))
    return jnp.concatenate(cols, axis=1)


def join_slabs(slabs):
    rows = iota((8, 128), 0)
    parts = []
    for p in range(3):
        a, b = slabs[2 * p], slabs[2 * p + 1]
        parts += [a[0:16], jnp.where(rows < 4, a[16:24], b[0:8]), b[8:24]]
    return jnp.concatenate(parts, axis=0)


def slabs_of(v):
    return [v[slab_at(h):slab_at(h) + 24] for h in range(H)]


def hi_lo(v):
    hi = low(v)
    return hi, low(v - hi.astype(F32))


def normed(x):
    mean = jnp.sum(x, axis=0, keepdims=True) * (1.0 / D)
    c = x - mean
    var = jnp.sum(c * c, axis=0, keepdims=True) * (1.0 / D)
    r = lax.rsqrt(var + NORM_EPS)
    return c * r, r


def normed_back(d, xh, r):
    m0 = jnp.sum(d, axis=0, keepdims=True) * (1.0 / D)
    m1 = jnp.sum(d * xh, axis=0, keepdims=True) * (1.0 / D)
    return r * (d - m0 - xh * m1)


GA = math.sqrt(2.0 / math.pi)
GB = 0.044715


def gelu_half(x):
    return 0.5 + 0.5 * jnp.tanh(x * (GA + (GA * GB) * (x * x)))


def gelu_slope(x, s):
    return s + (x * s) * (1.0 - s) * (2.0 * GA + (6.0 * GA * GB) * (x * x))


LOG2E = math.log2(math.e)
BIG = 1e30


class Refs:
    pass


def scratch_list(chunks):
    groups = chunks * CG
    return dict(
        w_obs=pltpu.VMEM((OBS, 128), BF),
        posb=pltpu.VMEM((GT, 128), F32),
        qkv_t=pltpu.VMEM((LAYERS, 384, 128), BF),
        qkv=pltpu.VMEM((LAYERS, 128, 384), BF),
        out_t=pltpu.VMEM((LAYERS, 128, 128), BF),
        out=pltpu.VMEM((LAYERS, 128, 128), BF),
        fc_t=pltpu.VMEM((LAYERS, 512, 128), BF),
        fc=pltpu.VMEM((LAYERS, 128, 512), BF),
        proj_t=pltpu.VMEM((LAYERS, 128, 512), BF),
        proj=pltpu.VMEM((LAYERS, 512, 128), BF),
        head_t=pltpu.VMEM((72, 128), BF),
        head=pltpu.VMEM((128, 128), BF),
        vec=pltpu.VMEM((32, 128), F32),
        bc=pltpu.VMEM((LAYERS, 12, GT, 128), F32),
        bcf=pltpu.VMEM((2, GT, 128), F32),
        bch=pltpu.VMEM((72, 128), F32),
        hc=pltpu.VMEM((128, 128), F32),
        ho=pltpu.VMEM((128, 128), F32),
        cnt=pltpu.VMEM((16, 256), F32),
        live=pltpu.VMEM((chunks, 1, L), F32),
        act=pltpu.VMEM((chunks, 40, L), F32),
        val=pltpu.VMEM((chunks, 40, L), F32),
        code=pltpu.VMEM((chunks, 2, L), F32),
        x=pltpu.VMEM((D, L), F32),
        dmid=pltpu.VMEM((D, L), F32),
        da=pltpu.VMEM((D, L), F32),
        xh1=pltpu.VMEM((LAYERS, D, L), F32),
        r1=pltpu.VMEM((LAYERS, 1, L), F32),
        xh2=pltpu.VMEM((LAYERS, D, L), F32),
        r2=pltpu.VMEM((LAYERS, 1, L), F32),
        n1=pltpu.VMEM((LAYERS, 128, L), BF),
        n2=pltpu.VMEM((LAYERS, 128, L), BF),
        att=pltpu.VMEM((LAYERS, 128, L), BF),
        q_low=pltpu.VMEM((LAYERS, H, 24, L), BF),
        k_low=pltpu.VMEM((LAYERS, H, 24, L), BF),
        v_low=pltpu.VMEM((LAYERS, 128, L), BF),
        rsum=pltpu.VMEM((LAYERS, H, 1, L), F32),
        prob=pltpu.VMEM((LAYERS, CG, GT, H * 128), F32),
        prob_low=pltpu.VMEM((LAYERS, CG, 128, H * 128), BF),
        k_mask=pltpu.VMEM((48, 128), BF),
        q_mask=pltpu.VMEM((48, 128), BF),
        dead=pltpu.VMEM((groups, 8, 128), F32),
        pre=pltpu.VMEM((LAYERS, FF, L), F32),
        half=pltpu.VMEM((LAYERS, FF, L), F32),
        inner=pltpu.VMEM((LAYERS, 512, L), BF),
        a_qkv=pltpu.VMEM((LAYERS, 384, 128), F32),
        ds_t=pltpu.VMEM((CG * H // 2, 128, 256), BF),
        turned=pltpu.VMEM((5, L, 128), BF),
        a_out=pltpu.VMEM((LAYERS, 128, 128), F32),
        a_fc=pltpu.VMEM((LAYERS, 512, 128), F32),
        a_proj=pltpu.VMEM((LAYERS, 512, 128), F32),
        a_bias=pltpu.VMEM((LAYERS, 12, 128, 128), F32),
        a_obs=pltpu.VMEM((128, 512), F32),
        a_x=pltpu.VMEM((128, 128), F32),
        a_fin=pltpu.VMEM((2, 128, 128), F32),
        a_head=pltpu.VMEM((128, 128), F32),
        a_hb=pltpu.VMEM((128, 128), F32),
        loss=pltpu.VMEM((2, 8, 128), F32),
    )


def code_phases():
    for p in range(15):
        yield p, (32 * p) // D, (32 * p) % D


def off_phases():
    for p in range(24):
        yield p, (35 * p + 32) // D, (35 * p + 32) % D


def shifted(v, by):
    by %= 128
    return v if by == 0 else pltpu.roll(v, by, 1)


def take_phase(load, a, s, width, rows):
    lanes = iota((rows, 128), 1)
    first = shifted(load(a), -s)
    if s + width > D:
        second = shifted(load(a + 1), D - s)
        first = jnp.where(lanes < D - s, first, second)
    return jnp.where(lanes < width, first, 0.0)


def with_bias(w, bias):
    if bias is not None:
        w = jnp.where(iota((128, 128), 0) == D, bias, w)
    return low(w.T)


def ones8(v):
    return jnp.concatenate([v, jnp.where(iota((8, v.shape[1]), 0) == 0, 1.0, 0.0)], axis=0)


def prep_weights(rg, R):
    R.w_obs[...] = low(rg[0:OBS, :])
    for w in range(GW):
        R.posb[pl.ds(WIN * w, WIN), :] = rg[OBS + 1:OBS + 1 + WIN, :] + rg[OBS:OBS + 1, :]
    R.vec[...] = jnp.zeros((32, 128), F32)
    for l in range(LAYERS):
        b = BASE + LROW * l
        for j in range(3):
            w = pad8(rg[pl.ds(b + 2 + j, D, stride=3), :])
            R.qkv[l, :, 128 * j:128 * (j + 1)] = low(w)
            R.qkv_t[l, 128 * j:128 * (j + 1), :] = with_bias(w, None if j == 1 else rg[pl.ds(b + 362 + j // 2, 1), :])
        w = pad8(rg[pl.ds(b + 364, D), :])
        R.out[l] = low(w)
        R.out_t[l] = with_bias(w, rg[pl.ds(b + 484, 1), :])
        for j in range(4):
            w = pad8(rg[pl.ds(b + 487 + j, D, stride=4), :])
            R.fc[l, :, 128 * j:128 * (j + 1)] = low(w)
            R.fc_t[l, 128 * j:128 * (j + 1), :] = with_bias(w, rg[pl.ds(b + 967 + j, 1), :])
            w = pad8(rg[pl.ds(b + 971 + D * j, D), :])
            R.proj[l, 128 * j:128 * (j + 1), :] = low(w)
            R.proj_t[l, :, 128 * j:128 * (j + 1)] = with_bias(w, None if j else rg[pl.ds(b + 1451, 1), :])
        for i, r in enumerate(VROWS):
            R.vec[pl.ds(12 * l + i, 1), :] = rg[pl.ds(b + r, 1), :]
    R.vec[24:26, :] = rg[pl.ds(HEAD, 2), :]
    R.hc[...] = jnp.zeros((128, 128), F32)
    R.ho[...] = jnp.zeros((128, 128), F32)
    c0 = HEAD + 2
    for p, a, s in code_phases():
        R.hc[pl.ds(p, 8, stride=15), :] = take_phase(
            lambda i: rg[pl.ds(c0 + i, 8, stride=4), :], a, s, 32, 8)
    o0 = c0 + 32
    for p, a, s in off_phases():
        R.ho[pl.ds(p, 5, stride=24), :] = take_phase(
            lambda i: rg[pl.ds(o0 + i, 5, stride=7), :], a, s, OFFS, 5)
    hw = R.hc[...] + shifted(R.ho[...], 32)
    R.head[...] = low(hw)
    R.head_t[...] = low(hw.T[0:72])
    lanes = iota((1, 128), 1)
    hb = jnp.where(lanes < 32, rg[pl.ds(o0, 1), :], 0.0)
    a, s = (D * OFFS + 32) // D, (D * OFFS + 32) % D
    ob = take_phase(lambda i: rg[pl.ds(o0 + i, 1), :], a, s, OFFS, 1)
    R.vec[26:27, :] = hb + shifted(ob, 32)
    columns = jnp.concatenate([R.vec[...], jnp.zeros((96, 128), F32)], axis=0).T
    for l in range(LAYERS):
        for i in range(12):
            R.bc[l, i] = jnp.broadcast_to(columns[0:D, 12 * l + i:12 * l + i + 1], (D, 128))
    for i in range(2):
        R.bcf[i] = jnp.broadcast_to(columns[0:D, 24 + i:25 + i], (D, 128))
    R.bch[...] = jnp.broadcast_to(columns[0:72, 26:27], (72, 128))


def spread_groups(v, groups, width):
    rows = v.shape[0]
    lanes = iota((rows, 128), 1)
    out = []
    for g in range(groups):
        t, o = (GT * g) // 128, (GT * g) % 128
        a = shifted(v[:, 128 * t:128 * (t + 1)], -o)
        if o + GT > 128:
            b = shifted(v[:, 128 * (t + 1):128 * (t + 2)], -o)
            a = jnp.where(lanes < 128 - o, a, b)
        out.append(jnp.where(lanes < GT, a, 0))
    return out


def prep_tokens(R, counts, codes, actions, valid, feat, chunks):
    groups = chunks * CG
    wins = counts.shape[1]
    R.cnt[...] = jnp.zeros(R.cnt.shape, F32)
    R.cnt[0:WIN // CAMS, :] = counts[...].astype(F32)
    k = iota((GT, 16), 0)
    step = (k % WIN) // CAMS
    sel = jnp.where(step == iota((GT, 16), 1), 1.0, 0.0)
    x = nn(low(sel), low(R.cnt[...]))
    y = jnp.where(iota((GT, wins), 1) % GW == iota((GT, wins), 0) // WIN, x, 0.0)
    pick = jnp.where(iota((wins, 128), 0) // GW == iota((wins, 128), 1) + groups * feat, 1.0, 0.0)
    z = nn(low(y), low(pick))
    kk = iota((GT, 128), 0)
    alive = jnp.where((kk % CAMS).astype(F32) < z, 1.0, 0.0)
    steps = WIN // CAMS
    j, at = iota((48, 128), 0), iota((48, 128), 1)
    own = (at // WIN == j // steps) & ((at % WIN) // CAMS == j % steps) & (at < GT)
    R.k_mask[...] = low(jnp.where(own, 1.0, 0.0))
    may = (at // WIN == j // steps) & ((at % WIN) // CAMS >= j % steps)
    R.q_mask[...] = low(jnp.where(may | (j >= GW * steps), 0.0, -BIG))
    rows = pad8(alive).T
    for g in range(groups):
        R.live[g // CG, :, 128 * (g % CG):128 * (g % CG + 1)] = rows[g:g + 1, :]
        R.dead[g] = jnp.where(iota((8, 128), 0) == 0, 1.0 - rows[g:g + 1, :], 0.0)
    for name, src in (("code", codes), ("act", actions), ("val", valid)):
        parts = spread_groups(src[...].astype(F32), groups, GT)
        dst = getattr(R, name)
        for g in range(groups):
            c, lo = g // CG, 128 * (g % CG)
            part = parts[g]
            if name == "val":
                part = part * rows[g:g + 1, :]
            if name != "code":
                dst[c, 32:40, lo:lo + 128] = jnp.zeros((8, 128), F32)
            dst[c, 0:part.shape[0], lo:lo + 128] = part
    lanes = iota((GT, 128), 1)
    live_total = jnp.sum(jnp.where(lanes < groups, alive, 0.0), keepdims=True)
    v = jnp.zeros((40, L), F32)
    for c in range(chunks):
        v = v + R.val[c]
    valid_total = jnp.sum(v, keepdims=True)
    return live_total, valid_total


def own_rows(slab, h):
    rows = iota((8, 128), 0)
    if h % 2 == 0:
        return jnp.concatenate([slab[0:16], jnp.where(rows < 4, slab[16:24], 0.0)], axis=0)
    return jnp.concatenate([jnp.where(rows >= 4, slab[0:8], 0.0), slab[8:24]], axis=0)


def split(v):
    hi = low(v).astype(F32)
    return hi, v - hi


def attend(R, s, c, q, k, v):
    qh, ql = split(q)
    kh, kl = split(k)
    vh, vl = split(v)
    minus = jnp.where(iota((8, 128), 0) == 0, -BIG, 0.0)

    none = jnp.zeros((128, 128), BF)

    def scores(g, p):
        at = slice(128 * g, 128 * (g + 1))
        qs, ks = [], []
        for h in (2 * p, 2 * p + 1):
            sl = slice(slab_at(h), slab_at(h) + 24)
            hi = own_rows(qh[sl, at], h)
            qd = low(jnp.concatenate([hi, hi, own_rows(ql[sl, at], h), minus], axis=0))
            kd = low(jnp.concatenate([kh[sl, at], kl[sl, at], kh[sl, at], R.dead[c * CG + g]], axis=0))
            qs.append(jnp.concatenate([qd, R.q_mask[...]], axis=0))
            ks.append(jnp.concatenate([kd, R.k_mask[...]], axis=0).T)
        if PAIR:
            both = jnp.concatenate([jnp.concatenate([qs[0], none], axis=1),
                                    jnp.concatenate([none, qs[1]], axis=1)], axis=0)
            return nn(jnp.concatenate(ks, axis=1), both)[0:GT]
        return jnp.concatenate([nn(ks[0], qs[0])[0:GT], nn(ks[1], qs[1])[0:GT]], axis=1)

    def soft(g, p, sc):
        at = slice(128 * g, 128 * (g + 1))
        e = jnp.exp2(sc - jnp.max(sc, axis=0, keepdims=True))
        r = 1.0 / jnp.sum(e, axis=0, keepdims=True)
        e8 = pad8(e)
        eh = low(e8)
        cols = slice(256 * p, 256 * (p + 1))
        R.prob[s, g, :, cols] = e
        for i in range(2):
            at_h = slice(256 * p + 128 * i, 256 * p + 128 * (i + 1))
            R.prob_low[s, g, :, at_h] = eh[:, 128 * i:128 * (i + 1)].T
        R.rsum[s, 2 * p, :, at] = r[:, 0:128]
        R.rsum[s, 2 * p + 1, :, at] = r[:, 128:256]
        return r, eh

    def values(g, p, r, eh):
        at = slice(128 * g, 128 * (g + 1))
        out = []
        for i in range(2):
            sl = slice(slab_at(2 * p + i), slab_at(2 * p + i) + 24)
            cols = slice(128 * i, 128 * (i + 1))
            vs = low(jnp.concatenate([vh[sl, at], vl[sl, at]], axis=0))
            o = nn(vs, eh[:, cols])
            out.append((o[0:24] + o[24:48]) * r[:, cols])
        return out

    items = [(g, p) for g in range(CG) for p in range(H // 2)]
    slabs = pipeline(items, scores, soft, values, FAHEAD)
    slabs = [t for pair in slabs for t in pair]
    return jnp.concatenate([join_slabs(slabs[H * g:H * (g + 1)]) for g in range(CG)], axis=1)


PAIR = True
FAHEAD = 2
BAHEAD = 4


def pipeline(items, first, second, third, ahead, between=()):
    n = len(items)
    a, b, out = {}, {}, []
    between = list(between)
    done = 0
    for t in range(n + ahead):
        if t < n:
            a[t] = first(*items[t])
        m = t - ahead + 1
        if 0 <= m < n:
            b[m] = second(*items[m], *(a.pop(m) if isinstance(a[m], tuple) else (a.pop(m),)))
        m = t - ahead
        if 0 <= m < n:
            out.append(third(*items[m], *b.pop(m)))
        while done < len(between) * (t + 1) // (n + ahead):
            between[done]()
            done += 1
    return out


def attend_back(R, s, do, between=()):
    vrows = [R.v_low[s, :, 128 * g:128 * (g + 1)].T for g in range(CG)]

    def probs(g, p):
        at = slice(128 * g, 128 * (g + 1))
        ds, stack = [], []
        for h in (2 * p, 2 * p + 1):
            a = slab_at(h)
            d = own_rows(do[a:a + 24, at], h) * R.rsum[s, h, :, at]
            parts = ([jnp.zeros((a, 128), F32)] if a else []) + [d] + ([jnp.zeros((104 - a, 128), F32)])
            ds.append(low(d))
            stack.append(low(jnp.concatenate(parts, axis=0)))
        return ds, nn(vrows[g], jnp.concatenate(stack, axis=1))[0:GT]

    def inner(g, p, d, dp):
        at = slice(128 * g, 128 * (g + 1))
        e = R.prob[s, g, :, 256 * p:256 * (p + 1)]
        r = jnp.concatenate([R.rsum[s, 2 * p, :, at], R.rsum[s, 2 * p + 1, :, at]], axis=1)
        total = jnp.sum(e * dp, axis=0, keepdims=True) * r
        ds = low(pad8(e * (dp - total)))
        for i in range(2):
            cols = slice(128 * i, 128 * (i + 1))
            R.ds_t[3 * g + p, :, cols] = ds[:, cols].T
        return d, ds

    def outer(g, p, d, ds):
        at = slice(128 * g, 128 * (g + 1))
        out = []
        for i in range(2):
            h = 2 * p + i
            dsh = ds[:, 128 * i:128 * (i + 1)]
            out.append((nn(R.k_low[s, h, :, at], dsh), nn(R.q_low[s, h, :, at], R.ds_t[3 * g + p, :, 128 * i:128 * (i + 1)]),
                        nn(d[i], R.prob_low[s, g, :, 128 * h:128 * (h + 1)])))
        return out

    items = [(g, p) for g in range(CG) for p in range(H // 2)]
    slabs = pipeline(items, probs, inner, outer, BAHEAD, between)
    slabs = [t for pair in slabs for t in pair]
    out = []
    for i in range(3):
        out.append(jnp.concatenate(
            [join_slabs([t[i] for t in slabs[H * g:H * (g + 1)]]) for g in range(CG)], axis=1))
    return out[0] * SCALE, out[1], out[2]


def turn(R, i, v):
    for g in range(CG):
        R.turned[i, 128 * g:128 * (g + 1), :] = v[:, 128 * g:128 * (g + 1)].T


def embed(R, obs, c):
    rows = nn(jnp.concatenate(obs, axis=1), R.w_obs[...])
    parts = []
    for g in range(CG):
        r = rows[GT * g:GT * (g + 1)] + R.posb[...]
        parts.append(pad8(r).T[0:D])
    return jnp.concatenate(parts, axis=1)


def layer_fwd(R, l, c, s, x):
    def vec(i):
        return tile4(R.bc[l, i])

    xh, r = normed(x)
    R.xh1[s] = xh
    R.r1[s] = r
    n1 = low(ones8(xh * vec(G1) + vec(B1)))
    R.n1[s] = n1
    mix = nn(R.qkv_t[l], n1)
    q = mix[0:D] * SCALE
    k = mix[128:128 + D]
    v = mix[256:256 + D]
    for h in range(H):
        a = slab_at(h)
        R.q_low[s, h] = low(q[a:a + 24])
        R.k_low[s, h] = low(k[a:a + 24])
    R.v_low[s] = low(pad8(v))
    att = low(ones8(attend(R, s, c, q * LOG2E, k, v)))
    R.att[l] = att
    x1 = x + nn(R.out_t[l], att)[0:D]
    xh, r = normed(x1)
    R.xh2[l] = xh
    R.r2[l] = r
    n2 = low(ones8(xh * vec(G2) + vec(B2)))
    R.n2[l] = n2
    pre = nn(R.fc_t[l], n2)
    parts = []
    for j in range(4):
        pj = pre[128 * j:128 * j + D]
        half = gelu_half(pj)
        R.pre[l, D * j:D * (j + 1)] = pj
        R.half[l, D * j:D * (j + 1)] = half
        parts.append(low(ones8(pj * half) if j == 0 else pad8(pj * half)))
    inner = jnp.concatenate(parts, axis=0)
    R.inner[l] = inner
    return x1 + nn(R.proj_t[l], inner)[0:D]


def head_step(R, c, x, live_total, valid_total):
    xh, r = normed(x)
    fin = low(pad8(xh * tile4(R.bcf[0]) + tile4(R.bcf[1])))
    hd = nn(R.head_t[...], fin) + tile4(R.bch[...])
    live = R.live[c]
    lw = live * (1.0 / live_total)
    rows = iota((CODES, L), 0).astype(F32)
    grads = []
    csum = jnp.zeros((1, L), F32)
    for b in range(BOOKS):
        lg = hd[CODES * b:CODES * (b + 1)]
        m = jnp.max(lg, axis=0, keepdims=True)
        e = jnp.exp(lg - m)
        s = jnp.sum(e, axis=0, keepdims=True)
        hot = rows == R.code[c, b:b + 1, :]
        picked = jnp.sum(jnp.where(hot, lg, 0.0), axis=0, keepdims=True)
        csum = csum + (jnp.log(s) + m - picked) * live
        grads.append((e * (1.0 / s) - jnp.where(hot, 1.0, 0.0)) * lw)
    diff = hd[32:72] - R.act[c]
    val = R.val[c]
    sq = diff * diff + 1.0
    ri = lax.rsqrt(sq)
    asum = val * (sq * ri)
    grads.append((val * (1.0 / valid_total)) * (diff * ri))
    R.loss[0, 0:1] += fold4(csum)
    af = fold4(asum)
    R.loss[1] += af[0:8] + af[8:16] + af[16:24] + af[24:32] + af[32:40]
    dh = jnp.concatenate(grads, axis=0)
    R.a_hb[0:72] += fold4(dh)
    dhl = low(jnp.concatenate([dh, jnp.zeros((56, L), F32)], axis=0))
    turn(R, 4, dhl)
    R.a_head[...] += nn(fin, R.turned[4])
    df = nn(R.head[...], dhl)[0:D]
    R.a_fin[0, 0:D] += fold4(df * xh)
    R.a_fin[1, 0:D] += fold4(df)
    return normed_back(df * tile4(R.bcf[0]), xh, r)


def add_bias(R, l, i, v):
    R.a_bias[l, i, 0:D] += fold4(v)


def mlp_bwd(R, l, dout):
    outl = low(pad8(dout))
    add_bias(R, l, PB, dout)
    parts = []
    for j in range(4):
        rows = slice(D * j, D * (j + 1))
        dj = nn(R.proj[l, 128 * j:128 * (j + 1)], outl)
        parts.append(low(pad8(dj[0:D] * gelu_slope(R.pre[l, rows], R.half[l, rows]))))
    prel = jnp.concatenate(parts, axis=0)
    dn = nn(R.fc[l], prel)[0:D]
    xh = R.xh2[l]
    add_bias(R, l, G2, dn * xh)
    add_bias(R, l, B2, dn)
    dmid = normed_back(dn * tile4(R.bc[l, G2]), xh, R.r2[l]) + dout
    midl = low(pad8(dmid))
    add_bias(R, l, OB, dmid)
    da = nn(R.out[l], midl)[0:D]

    turn(R, 0, outl)
    turn(R, 1, R.n2[l])
    turn(R, 2, midl)

    def a_proj(j):
        def run():
            rows = slice(256 * j, 256 * (j + 1))
            R.a_proj[l, rows] += nn(R.inner[l, rows], R.turned[0])
        return run

    def a_fc(j):
        def run():
            rows = slice(256 * j, 256 * (j + 1))
            R.a_fc[l, rows] += nn(prel[rows], R.turned[1])
        return run

    def a_out():
        R.a_out[l] += nn(R.att[l], R.turned[2])

    return dmid, da, [a_proj(0), a_proj(1), a_fc(0), a_fc(1), a_out]


def att_bwd(R, l, s, dmid, da, between):
    turn(R, 3, R.n1[s])
    dq, dk, dv = attend_back(R, s, da, between)
    mixl = jnp.concatenate([low(pad8(dq)), low(pad8(dk)), low(pad8(dv))], axis=0)
    dn = nn(R.qkv[l], mixl)[0:D]
    add_bias(R, l, QB, dq)
    add_bias(R, l, VB, dv)
    R.a_qkv[l] += nn(mixl, R.turned[3])
    xh = R.xh1[s]
    add_bias(R, l, G1, dn * xh)
    add_bias(R, l, B1, dn)
    return normed_back(dn * tile4(R.bc[l, G1]), xh, R.r1[s]) + dmid


def embed_bwd(R, obs, c, dx):
    R.a_x[0:D] += fold4(dx)
    lanes = iota((D, 128), 1)
    tiles = []
    gs = [dx[:, 128 * g:128 * (g + 1)] for g in range(CG)]
    for t in range(CG):
        a = shifted(gs[t], -8 * t)
        b = shifted(gs[t + 1], 120 - 8 * t) if t + 1 < CG else jnp.zeros((D, 128), F32)
        tiles.append(jnp.where(lanes < GT - 8 * t, a, b))
    gl = low(pad8(jnp.concatenate(tiles, axis=1)))
    R.a_obs[...] += nn(gl, jnp.concatenate(obs, axis=1))


def zero_grads(R):
    for name in ("a_qkv", "a_out", "a_fc", "a_proj", "a_bias", "a_obs", "a_x", "a_fin", "a_head", "a_hb", "loss"):
        ref = getattr(R, name)
        ref[...] = jnp.zeros(ref.shape, F32)


HIGH = lax.Precision.HIGHEST


LATE = 364
EARLY_ROWS = (OB, G2, B2, PB)


def lane_sums(v):
    return jnp.sum(v.T, axis=0, keepdims=True)


def pack_vectors(R, rg, l, which):
    b = BASE + LROW * l
    for i in which:
        rg[pl.ds(b + VROWS[i], 1), :] = lane_sums(R.a_bias[l, i])


def pack_early(R, rg, l):
    b = BASE + LROW * l
    rg[pl.ds(b + 364, D), :] = R.a_out[l, 0:D]
    for j in range(4):
        fc = R.a_fc[l, 128 * j:128 * (j + 1), :].T
        rg[pl.ds(b + 487 + j, D, stride=4), :] = fc[0:D]
        rg[pl.ds(b + 967 + j, 1), :] = fc[D:D + 1]
        rg[pl.ds(b + 971 + D * j, D), :] = R.a_proj[l, 128 * j:128 * j + D, :]
    pack_vectors(R, rg, l, EARLY_ROWS)


def pack_late(R, rg, l):
    b = BASE + LROW * l
    for j in range(3):
        rg[pl.ds(b + 2 + j, D, stride=3), :] = R.a_qkv[l, 128 * j:128 * (j + 1), :].T[0:D]
    pack_vectors(R, rg, l, (G1, B1, QB, VB))


def pack_embed(R, rg):
    for f in range(OBS // 128):
        rg[128 * f:128 * (f + 1), :] = R.a_obs[:, 128 * f:128 * (f + 1)].T
    slot, lane = iota((32, 128), 0), iota((32, 128), 1)
    sel = jnp.where((slot == 0) | (lane % WIN == slot - 1), 1.0, 0.0)
    sel = jnp.where(lane < GT, sel, 0.0)
    rows = nt(sel, R.a_x[...], HIGH)
    rg[pl.ds(OBS, 1 + WIN), :] = rows[0:1 + WIN]


def pack_head(R, rg):
    for i in range(2):
        rg[pl.ds(HEAD + i, 1), :] = lane_sums(R.a_fin[i])
    lanes8 = iota((8, 128), 1)
    grad = R.a_head[...]
    R.hc[...] = jnp.where(iota((128, 128), 1) < 32, grad, 0.0)
    R.ho[...] = jnp.where(iota((128, 128), 1) < OFFS, shifted(grad, -32), 0.0)
    c0 = HEAD + 2
    o0 = c0 + 32

    def put(phases, src, rows_n, stride, width, count):
        acc = [jnp.zeros((rows_n, 128), F32) for _ in range(count + 1)]
        lanes = iota((rows_n, 128), 1)
        for p, a, s in phases:
            v = src[pl.ds(p, rows_n, stride=stride), :]
            first = shifted(v, s)
            if s + width > D:
                acc[a] = acc[a] + jnp.where((lanes >= s) & (lanes < D), first, 0.0)
                acc[a + 1] = acc[a + 1] + jnp.where(lanes < s + width - D, shifted(v, s - D), 0.0)
            else:
                acc[a] = acc[a] + first
        return acc

    acc = put(code_phases(), R.hc, 8, 15, 32, 4)
    for a in range(4):
        rg[pl.ds(c0 + a, 8, stride=4), :] = acc[a]
    hb = lane_sums(R.a_hb[...])
    lane1 = iota((1, 128), 1)
    rg[pl.ds(o0, 48), :] = jnp.zeros((48, 128), F32)
    acc = put(off_phases(), R.ho, 5, 24, OFFS, 7)
    for a in range(7):
        rg[pl.ds(o0 + a, 5, stride=7), :] = acc[a]
    rg[pl.ds(o0 + 7, 5, stride=7), :] = rg[pl.ds(o0 + 7, 5, stride=7), :] + acc[7]
    rg[pl.ds(o0, 1), :] = rg[pl.ds(o0, 1), :] + jnp.where(lane1 < 32, hb, 0.0)
    a, s = (D * OFFS + 32) // D, (D * OFFS + 32) % D
    ob = jnp.where(lane1 < OFFS, shifted(hb, -32), 0.0)
    rg[pl.ds(o0 + a, 1), :] = rg[pl.ds(o0 + a, 1), :] + shifted(ob, s)


MESH = pl.DeviceIdType.MESH


def round_up(n, m):
    return -(-n // m) * m


class Plan:
    def __init__(self, feats, toks, shard, tok_rows):
        self.feats, self.toks, self.chips = feats, toks, toks // 2
        self.shard = shard
        self.block = round_up(-(-(shard + 112) // D), 16)
        self.flat_rows = self.block // 16 * 15
        self.local = round_up(-(-shard // 1024), 1) * 8
        self.work = round_up(max(self.flat_rows, self.local + 1), 8)
        self.own_rows = tok_rows // feats
        self.chunks = self.own_rows // CT
        self.early = [f for f in range(feats) if shard * toks * f // D >= BASE + LATE]
        self.grid = round_up(-(-(shard * feats * toks) // D) + self.block, 8)


def comm_scratch(P):
    dma = pltpu.SemaphoreType.DMA
    B, C, Fn = P.block, P.chips, P.feats
    return dict(
        rg=pltpu.VMEM((P.grid, 128), F32),
        ob=pltpu.VMEM((P.chunks, Fn, L, 128), BF),
        pg=pltpu.VMEM((2, C, Fn, B, 128), BF),
        loc=pltpu.VMEM((P.work, 128), F32),
        rblk=pltpu.VMEM((B, 128), F32),
        codes_in=pltpu.VMEM((BOOKS, P.own_rows), jnp.int32),
        act_in=pltpu.VMEM((OFFS, P.own_rows), F32),
        val_in=pltpu.VMEM((OFFS, P.own_rows), jnp.int32),
        tz=pltpu.VMEM((2, Fn, 8, 128), F32),
        tc=pltpu.VMEM((2, C, 8, 128), F32),
        ts=pltpu.VMEM((2, 2, 8, 128), F32),
        sb1=pltpu.VMEM((C, Fn, B, 128), F32),
        rb1=pltpu.VMEM((C, Fn, B, 128), F32),
        sb2=pltpu.VMEM((C, Fn, B, 128), BF),
        rb2=pltpu.VMEM((C, Fn, B, 128), BF),
        col=pltpu.VMEM((Fn, B, 128), F32),
        sb3=pltpu.VMEM((Fn, B, 128), F32),
        rb3=pltpu.VMEM((Fn, B, 128), F32),
        s_p1=dma((2, Fn)), s_p2=dma((2, C)), s_p3=dma((2, C)),
        s_tz=dma((2, 2, Fn)), s_tc=dma((2, 2, C)), s_ts=dma((2, 2)),
        s_ob=dma((2, 2 * P.chunks, Fn)),
        s_own=dma((P.chunks,)),
        s_in=dma((3,)),
        s_r1=dma((3, 2, C)), s_r2=dma((2, Fn, C)), s_r3=dma((2, Fn)),
    )


def to_rows(loc, rblk, delta, P):
    v = loc[...]
    lanes = iota(v.shape, 1)
    moved = pltpu.roll(v, delta, 1)
    loc[...] = jnp.where(lanes >= delta, moved, pltpu.roll(moved, 1, 0))
    n = P.block // 16
    lane = iota((n, 128), 1)
    for j in range(16):
        if j < 15:
            a = shifted(loc[pl.ds(j, n, stride=15), :], 8 * j)
        if j > 0:
            b = shifted(loc[pl.ds(j - 1, n, stride=15), :], 8 * j)
            a = jnp.where(lane < 8 * j, b, a) if j < 15 else b
        rblk[pl.ds(j, n, stride=16), :] = jnp.where(lane < D, a, 0.0)


def from_rows(rblk, loc, delta, P):
    n = P.block // 16
    lane = iota((n, 128), 1)
    loc[...] = jnp.zeros(loc.shape, F32)
    for i in range(15):
        a = shifted(rblk[pl.ds(i, n, stride=16), :], -8 * i)
        b = shifted(rblk[pl.ds(i + 1, n, stride=16), :], D - 8 * i)
        loc[pl.ds(i, n, stride=15), :] = jnp.where(lane < D - 8 * i, a, b)
    v = loc[...]
    lanes = iota(v.shape, 1)
    moved = pltpu.roll(v, lax.rem(128 - delta, 128), 1)
    v = jnp.where(lanes < 128 - delta, moved, pltpu.roll(moved, P.work - 1, 0))
    return v[0:P.local]


def step_kernel(P, names, master, obs, counts, codes, actions, valid, grad, sums, *scratch):
    R = Refs()
    for name, ref in zip(names, scratch):
        setattr(R, name, ref)
    Fn, C, B = P.feats, P.chips, P.block
    feat = lax.axis_index("feat")
    tok = lax.axis_index("tok")
    chip = tok // 2
    core = tok % 2
    me = feat * P.toks + tok
    delta = lax.rem(me * P.shard, D)

    def z_peer(i):
        return lax.rem(feat + i, Fn)

    def z_from(i):
        return lax.rem(feat + Fn - i, Fn)

    def c_peer(i):
        return lax.rem(chip + i, C)

    def c_from(i):
        return lax.rem(chip + C - i, C)

    def to_z(i):
        return (z_peer(i), tok)

    def to_c(i):
        return (feat, 2 * c_peer(i) + core)

    sibling = (feat, 2 * chip + 1 - core)

    def send(src, dst, sems, at, dev):
        return pltpu.make_async_remote_copy(
            src_ref=src, dst_ref=dst, send_sem=sems.at[(0,) + at], recv_sem=sems.at[(1,) + at],
            device_id=dev, device_id_type=MESH)

    barrier = pltpu.get_barrier_semaphore()
    peers = [to_z(i) for i in range(1, Fn)] + [to_c(i) for i in range(1, C)] + [sibling]
    for dev in peers:
        pl.semaphore_signal(barrier, inc=1, device_id=dev, device_id_type=MESH)

    n = P.own_rows
    ins = []
    for i, (src, dst) in enumerate(((codes, R.codes_in), (actions, R.act_in), (valid, R.val_in))):
        ins.append(pltpu.make_async_copy(src.at[:, pl.ds(pl.multiple_of(feat * n, 128), n)], dst, R.s_in.at[i]))
        ins[-1].start()

    R.loc[...] = jnp.zeros(R.loc.shape, F32)
    whole = P.shard // 1024
    R.loc[0:8 * whole, :] = master[pl.ds(0, 1024 * whole)].reshape(8 * whole, 128)
    rest = P.shard - 1024 * whole
    last = jnp.concatenate([master[pl.ds(1024 * whole, rest)], jnp.zeros((1024 - rest,), F32)])
    R.loc[8 * whole:8 * whole + 8, :] = last.reshape(8, 128)
    to_rows(R.loc, R.rblk, delta, P)
    R.pg[core, chip, feat] = low(R.rblk[...])
    pl.semaphore_wait(barrier, len(peers))

    p1 = []
    for i in range(1, Fn):
        blk = R.pg.at[core, chip, feat]
        p1.append(send(blk, blk, R.s_p1, (i,), to_z(i)))
        p1[-1].start()

    half = CT // 2

    def obs_copies(p):
        cps = []
        for i in range(1, Fn):
            src = obs.at[pl.ds(pl.multiple_of(z_peer(i) * n + half * p, 16), half), :]
            dst = R.ob.at[p // 2, feat, pl.ds(pl.multiple_of(half * (p % 2), 16), half), :]
            cps.append(send(src, dst, R.s_ob, (p, i), to_z(i)))
        return cps

    def start_obs(p):
        for cp in obs_copies(p):
            cp.start()

    own = []
    for c in range(P.chunks):
        src = obs.at[pl.ds(pl.multiple_of(feat * n + CT * c, 16), CT), :]
        own.append(pltpu.make_async_copy(src, R.ob.at[c, feat, pl.ds(0, CT), :], R.s_own.at[c]))
        own[-1].start()
    for cp in ins:
        cp.wait()
    zero_grads(R)
    for c in range(P.chunks):
        for f in range(Fn):
            R.ob[c, f, CT:L, :] = jnp.zeros((L - CT, 128), BF)
    live_n, valid_n = prep_tokens(R, counts, R.codes_in, R.act_in, R.val_in, feat, P.chunks)

    def two_rows(a, b):
        return jnp.concatenate([jnp.broadcast_to(a, (1, 128)), jnp.broadcast_to(b, (1, 128)),
                                jnp.zeros((6, 128), F32)], axis=0)

    def z_copies(w):
        return [send(R.tz.at[w, feat], R.tz.at[w, feat], R.s_tz.at[w], (i,), to_z(i)) for i in range(1, Fn)]

    def c_copies(w):
        return [send(R.tc.at[w, chip], R.tc.at[w, chip], R.s_tc.at[w], (i,), to_c(i)) for i in range(1, C)]

    def s_copies(w):
        return [send(R.ts.at[w, core], R.ts.at[w, core], R.s_ts.at[w], (), sibling)]

    def start_all(cps):
        for cp in cps:
            cp.start()

    def total(ref, w, count):
        v = ref[w, 0]
        for i in range(1, count):
            v = v + ref[w, i]
        return v

    def wait_all(cps):
        for cp in cps:
            cp.wait()

    R.tz[0, feat] = two_rows(live_n, valid_n)
    start_all(z_copies(0))
    wait_all(p1)
    start_obs(0)
    start_obs(1)
    p2 = []
    for i in range(1, C):
        blk = R.pg.at[core, chip]
        p2.append(send(blk, blk, R.s_p2, (i,), to_c(i)))
        p2[-1].start()
    p3 = [send(R.pg.at[core, chip], R.pg.at[core, chip], R.s_p3, (0,), sibling)]
    p3[0].start()
    wait_all(z_copies(0))
    R.tc[0, chip] = total(R.tz, 0, Fn)
    start_all(c_copies(0))
    for i in range(1, C):
        p2[i - 1].wait_recv()
        blk = R.pg.at[core, c_from(i)]
        p3.append(send(blk, blk, R.s_p3, (i,), sibling))
        p3[-1].start()
    wait_all(c_copies(0))
    R.ts[0, core] = total(R.tc, 0, C)
    start_all(s_copies(0))
    for cp in p2:
        cp.wait_send()
    wait_all(p3)
    R.rg[0:8, :] = jnp.zeros((8, 128), F32)

    def place(d, _):
        r0 = (P.shard * d) // D
        f, t = d // P.toks, d % P.toks
        blk = R.pg[t % 2, t // 2, f].astype(F32)
        before = R.rg[pl.ds(r0, 1), :]
        R.rg[pl.ds(r0, B), :] = blk
        R.rg[pl.ds(r0, 1), :] = blk[0:1] + before
        return 0

    lax.fori_loop(0, Fn * P.toks, place, 0)
    prep_weights(R.rg, R)
    wait_all(s_copies(0))
    counted = total(R.ts, 0, 2)
    live_total = counted[0:1, 0:1]
    valid_total = counted[1:2, 0:1]

    for cp in own:
        cp.wait()


    def rows_of(f, ch, co):
        return (P.shard * (f * P.toks + 2 * ch + co)) // D

    early = P.early[0] if P.early else Fn
    planes = [slice(Fn - 1, Fn), slice(early, Fn - 1), slice(0, early)]

    def r1_copy(w, i):
        at = pl.ds(planes[w].start, planes[w].stop - planes[w].start)
        return send(R.sb1.at[i, at], R.rb1.at[i, at], R.s_r1.at[w], (i,), sibling)

    def r2_copy(f, i):
        return send(R.sb2.at[i, f], R.rb2.at[i, f], R.s_r2.at[:, f], (i,), to_c(i))

    def r3_copy(i):
        return send(R.sb3.at[i], R.rb3.at[i], R.s_r3, (i,), to_z(i))

    order = list(range(1, C)) + [0]

    def sum_cores(w):
        for i in order:
            for f in range(planes[w].start, planes[w].stop):
                R.sb1[i, f] = R.rg[pl.ds(rows_of(f, c_peer(i), 1 - core), B), :]
            r1_copy(w, i).start()

    def sum_chips(w):
        for i in order:
            r1_copy(w, i).wait_recv()
            for f in range(planes[w].start, planes[w].stop):
                v = R.rg[pl.ds(rows_of(f, c_peer(i), core), B), :] + R.rb1[i, f]
                if i:
                    R.sb2[i, f] = low(v)
                    r2_copy(f, i).start()
                else:
                    R.col[f] = v

    def sum_column(f):
        v = R.col[f]
        for i in range(1, C):
            r2_copy(f, i).wait_recv()
            v = v + R.rb2[i, f].astype(F32)
        R.col[f] = v
        for i in range(1, Fn):
            @pl.when(z_peer(i) == f)
            def _():
                R.sb3[i] = v
                r3_copy(i).start()

    def chunk(c, _):
        for p in (2 * c, 2 * c + 1):
            for cp in obs_copies(p):
                cp.wait_recv()

            @pl.when(c + 1 < P.chunks)
            def _():
                start_obs(p + 2)

        R.x[...] = embed(R, [R.ob[c, f, 0:CT, :] for f in range(Fn)], c)

        def lay(l, _):
            R.x[...] = layer_fwd(R, l, c, l, R.x[...])
            return 0

        lax.fori_loop(0, LAYERS, lay, 0)

        dx = head_step(R, c, R.x[...], live_total, valid_total)
        dmid, da, rest = mlp_bwd(R, 1, dx)
        R.x[...] = att_bwd(R, 1, 1, dmid, da, rest)
        @pl.when(c == P.chunks - 1)
        def _():
            R.rg[pl.ds(HEAD + 32, P.grid - HEAD - 32), :] = jnp.zeros((P.grid - HEAD - 32, 128), F32)
            pack_head(R, R.rg)
            pack_late(R, R.rg, 1)
            pack_early(R, R.rg, 1)
            R.ts[1, core] = two_rows(jnp.sum(R.loss[0], keepdims=True), jnp.sum(R.loss[1], keepdims=True))
            sum_cores(0)
            start_all(s_copies(1))

        dmid, da, rest = mlp_bwd(R, 0, R.x[...])
        R.dmid[...] = dmid
        R.da[...] = da
        for run in rest:
            run()

        @pl.when(c == P.chunks - 1)
        def _():
            pack_early(R, R.rg, 0)
            sum_cores(1)
            sum_chips(0)
            wait_all(s_copies(1))
            R.tc[1, chip] = total(R.ts, 1, 2)
            start_all(c_copies(1))

        dx = att_bwd(R, 0, 0, R.dmid[...], R.da[...], [])

        @pl.when(c == P.chunks - 1)
        def _():
            pack_late(R, R.rg, 0)
            sum_chips(1)

        embed_bwd(R, [R.ob[c, f] for f in range(Fn)], c, dx)
        return 0

    lax.fori_loop(0, P.chunks, chunk, 0)
    pack_embed(R, R.rg)
    sum_cores(2)
    wait_all(c_copies(1))
    R.tz[1, feat] = total(R.tc, 1, C)
    start_all(z_copies(1))
    sum_column(Fn - 1)
    sum_chips(2)
    for f in (*range(early, Fn - 1), *range(early)):
        sum_column(f)
    for i in range(1, Fn):
        r3_copy(i).wait_recv()
    v = R.col[feat]
    for i in range(1, Fn):
        v = v + R.rb3[i]
    R.rblk[...] = v
    grad[...] = from_rows(R.rblk, R.loc, delta, P)
    wait_all(z_copies(1))
    lost = total(R.tz, 1, Fn)
    sums[...] = jnp.concatenate([lost[0:1], counted[0:1], lost[1:2], counted[1:2], jnp.zeros((4, 128), F32)], axis=0)
    for p in range(2 * P.chunks):
        for cp in obs_copies(p):
            cp.wait_send()
    for w in range(3):
        for i in range(C):
            r1_copy(w, i).wait_send()
    for i in range(1, C):
        for f in range(Fn):
            r2_copy(f, i).wait_send()
    for i in range(1, Fn):
        r3_copy(i).wait_send()


def adam_kernel(shard, grad, sums, master, first, second, new_master, new_first, new_second, parts):
    whole = shard // 1024
    for lo, hi in ((0, whole), (whole, whole + 1)):
        n = min(1024 * hi, shard) - 1024 * lo
        at = pl.ds(1024 * lo, n)
        g = grad[8 * lo:8 * hi].reshape(1024 * (hi - lo))[0:n]
        old = master[at]
        f_new = BETA_ONE * first[at] + (1.0 - BETA_ONE) * g
        s_new = BETA_TWO * second[at] + (1.0 - BETA_TWO) * g * g
        f_hat = f_new / (1.0 - BETA_ONE ** STEP_NO)
        s_hat = s_new / (1.0 - BETA_TWO ** STEP_NO)
        new_first[at] = f_new
        new_second[at] = s_new
        new_master[at] = old - LEARN_RATE * (f_hat / (jnp.sqrt(s_hat) + ADAM_EPS) + DECAY_RATE * old)
    for i in range(4):
        parts[i] = sums[i, 0]


def solution(mesh):
    feats, toks = mesh.shape["feat"], mesh.shape["tok"]

    def shards(master, first, second, obs, counts, codes, actions, valid):
        P_ = Plan(feats, toks, master.shape[0], obs.shape[0])
        scratch = dict(scratch_list(P_.chunks))
        scratch.update(comm_scratch(P_))
        vmem = pl.BlockSpec(memory_space=pltpu.VMEM)
        hbm = pl.BlockSpec(memory_space=pl.ANY)
        grad, sums = pl.pallas_call(
            functools.partial(step_kernel, P_, list(scratch)),
            out_shape=(jax.ShapeDtypeStruct((P_.local, 128), F32), jax.ShapeDtypeStruct((8, 128), F32)),
            in_specs=[vmem, hbm, vmem, hbm, hbm, hbm],
            out_specs=(vmem, vmem),
            scratch_shapes=list(scratch.values()),
            compiler_params=pltpu.CompilerParams(
                collective_id=0, has_side_effects=True, vmem_limit_bytes=60 * 2 ** 20),
        )(master, obs, counts.T, codes.T, actions, valid)
        flat = jax.ShapeDtypeStruct((P_.shard,), F32)
        return pl.pallas_call(
            functools.partial(adam_kernel, P_.shard),
            out_shape=(flat, flat, flat, jax.ShapeDtypeStruct((4,), F32)),
            in_specs=[vmem] * 5,
            out_specs=(vmem, vmem, vmem, pl.BlockSpec(memory_space=pltpu.SMEM)),
        )(grad, sums, master, first, second)

    weights = PSpec(("feat", "tok"))
    return jax.shard_map(
        shards, mesh=mesh,
        in_specs=(weights, weights, weights, PSpec("tok", "feat"), PSpec("tok", None), PSpec("tok", None),
                  PSpec(None, "tok"), PSpec(None, "tok")),
        out_specs=(weights, weights, weights, PSpec()), check_vma=False)
```
